128 devices in a mesh: seq: 2 (over y_hi), ctx: 32 (over x, z, core), tp: 2 (over y_lo).
Axes of the slice: x: 4, y: 4 (y_hi: 2, y_lo: 2; y = y_hi * 2 + y_lo), z: 4, core: 2. Of those that a mesh axis runs over, the one named last changes fastest.
Arguments:
- tokens: bfloat16 [8192, 1024], P(('seq', 'ctx')), may hold values from -6 to 6
- cotangent: bfloat16 [8192, 1024], P(('seq', 'ctx')), may hold values from -6 to 6
- group_order: int32 [2, 32], P('seq', 'ctx'), may hold values from 0 to 31, each once within a row
- input_weight: bfloat16 [2, 1024, 3, 1024], P(None, ('seq', 'ctx'), None, 'tp'), may hold values from -0.1875 to 0.1875
- output_weight: bfloat16 [2, 1024, 1024], P(None, ('seq', 'ctx'), 'tp'), may hold values from -3 to 3
- expand_weight: bfloat16 [2, 1024, 4096], P(None, ('seq', 'ctx'), 'tp'), may hold values from -0.1875 to 0.1875
- contract_weight: bfloat16 [2, 1024, 4096], P(None, ('seq', 'ctx'), 'tp'), may hold values from -0.09375 to 0.09375
- norm_gain: float32 [2, 2, 1024], P(None, None, ('seq', 'ctx', 'tp')), may hold values from 0.1 to 1.9
- norm_shift: float32 [2, 2, 1024], P(None, None, ('seq', 'ctx', 'tp')), may hold values from -3 to 3
- input_bias: float32 [2, 3, 1024], P(None, None, ('seq', 'ctx', 'tp')), may hold values from -3 to 3
- output_bias: float32 [2, 2, 1024], P(None, None, ('seq', 'ctx', 'tp')), may hold values from -3 to 3
- expand_bias: float32 [2, 4096], P(None, ('seq', 'ctx', 'tp')), may hold values from -4 to 4
Outputs:
- activations: bfloat16 [8192, 1024], P(('seq', 'ctx'))
- input_gradient: float32 [8192, 1024], P(('seq', 'ctx'))
- input_weight_gradient: float32 [2, 1024, 3, 1024], P(None, ('seq', 'ctx'), None, 'tp')
- output_weight_gradient: float32 [2, 1024, 1024], P(None, ('seq', 'ctx'), 'tp')
- expand_weight_gradient: float32 [2, 1024, 4096], P(None, ('seq', 'ctx'), 'tp')
- contract_weight_gradient: float32 [2, 1024, 4096], P(None, ('seq', 'ctx'), 'tp')
- norm_gain_gradient: float32 [2, 2, 1024], P(None, None, ('seq', 'ctx', 'tp'))
- norm_shift_gradient: float32 [2, 2, 1024], P(None, None, ('seq', 'ctx', 'tp'))
- input_bias_gradient: float32 [2, 3, 1024], P(None, None, ('seq', 'ctx', 'tp'))
- output_bias_gradient: float32 [2, 2, 1024], P(None, None, ('seq', 'ctx', 'tp'))
- expand_bias_gradient: float32 [2, 4096], P(None, ('seq', 'ctx', 'tp'))
The draws below stay inside these ranges and needn't reach their ends.
Inputs may be any that keep to these rules, and one draw needn't show every extreme that they name: `group_order`: each row holds every number 0 to 31 once.
All inputs are finite; a program needn't handle non-finite values.
Results may differ from the reference program's by a relative error of at most 0.024.
Values may be sent and summed in bfloat16 or wider, within the bound.
A program may use at most 192 MiB of HBM per device.

```python
import jax
import jax.numpy as jnp
from jax import lax

D = 1024
HEADS = 16
FF = 4096
ROWS = 128
LAYERS = 2
HEAD_DIM = 64
ROT = 16
SEQS = 2
TOKENS = 8192
N_CTX = 32


def shard_levels(rng, extent, shards, smallest, high):
    factor_of, own = 1.0, jax.random.fold_in(rng, 6)
    for axis_at, blocks in shards:
        heights = jnp.exp(jax.random.uniform(jax.random.fold_in(own, axis_at), (blocks,), jnp.float32, smallest / len(shards), high / len(shards)))
        factor_of = factor_of * jnp.repeat(heights, extent[axis_at] // blocks).reshape([-1 if axis == axis_at else 1 for axis in range(len(extent))])
    return factor_of


def noise(rng, dims, width, most, pieces=(), kind=jnp.bfloat16):
    level = shard_levels(rng, dims, pieces, -0.22, 0.18) if pieces else 1.0
    entries = jax.random.normal(rng, dims, jnp.float32) * width * level
    return jnp.minimum(jnp.maximum(entries, -most), most).astype(kind)


def setup_inputs(seed: int = 0) -> dict:
    streams_of = jax.random.split(jax.random.key(seed), 13)
    tokens = noise(streams_of[0], (TOKENS, D), 1.0, 6.0, ((0, 64),))
    cotangent = noise(streams_of[1], (TOKENS, D), 1.0, 6.0, ((0, 64),))
    group_order = jax.vmap(lambda own: jax.random.permutation(own, N_CTX))(jax.random.split(streams_of[2], SEQS)).reshape((SEQS, N_CTX)).astype(jnp.int32)
    input_weight = noise(streams_of[3], (LAYERS, D, 3, D), D ** -0.5, 0.1875, ((1, 64), (3, 2)))
    output_weight = noise(streams_of[4], (LAYERS, D, D), (max(D // 256, 2)) ** -0.5, 3.0, ((1, 64), (2, 2)))
    expand_weight = noise(streams_of[5], (LAYERS, D, FF), D ** -0.5, 0.1875, ((1, 64), (2, 2)))
    contract_weight = noise(streams_of[6], (LAYERS, D, FF), FF ** -0.5, 0.09375, ((1, 64), (2, 2)))
    norm_gain = jnp.clip(1.0 + 0.18 * jax.random.normal(streams_of[7], (LAYERS, 2, D), jnp.float32), 0.1, 1.9)
    norm_shift = noise(streams_of[8], (LAYERS, 2, D), 0.3, 3.0, ((2, 128),), jnp.float32)
    input_bias = noise(streams_of[9], (LAYERS, 3, D), 0.3, 3.0, ((2, 128),), jnp.float32)
    output_bias = noise(streams_of[10], (LAYERS, 2, D), 0.3, 3.0, ((2, 128),), jnp.float32)
    expand_bias = noise(streams_of[11], (LAYERS, FF), 0.5, 4.0, ((1, 128),), jnp.float32)
    return {"tokens": tokens, "cotangent": cotangent, "group_order": group_order, "input_weight": input_weight, "output_weight": output_weight, "expand_weight": expand_weight, "contract_weight": contract_weight, "norm_gain": norm_gain, "norm_shift": norm_shift, "input_bias": input_bias, "output_bias": output_bias, "expand_bias": expand_bias}


EPSILON = 1e-05
MASKED = -1e+30

@jax.custom_vjp
def low(v):
    return lax.optimization_barrier(v.astype(jnp.bfloat16)).astype(jnp.float32)

@jax.custom_vjp
def low_back(v):
    return v

def low_keep(v):
    return (low(v), None)

def low_pass(kept, grad):
    return (grad,)

def back_keep(v):
    return (v, None)

def back_low(kept, grad):
    return (low(grad),)
low.defvjp(low_keep, low_pass)
low_back.defvjp(back_keep, back_low)

def highest(left, right):
    return jnp.dot(left, right, precision=lax.Precision.HIGHEST)

def layer_norm(values, gain, shift):
    centre = lax.optimization_barrier(jnp.mean(values, axis=-1, keepdims=True))
    centred = values - centre
    spread = lax.optimization_barrier(jnp.mean(centred * centred, axis=-1, keepdims=True))
    return centred * lax.rsqrt(spread + EPSILON) * gain + shift

def rotary_tables(positions):
    half = ROT // 2
    freqs = 10000.0 ** (-(jnp.arange(half, dtype=jnp.float32) * 2.0 / ROT))
    angle = positions.astype(jnp.float32)[:, None] * freqs[None, :]
    cosine = jnp.concatenate([jnp.cos(angle), jnp.cos(angle)], axis=-1)
    sine = jnp.concatenate([jnp.sin(angle), jnp.sin(angle)], axis=-1)
    return (cosine, sine)

def rotate(values, cosine, sine):
    half = ROT // 2
    part = values[..., :ROT]
    turned = jnp.concatenate([-part[..., half:], part[..., :half]], axis=-1)
    return jnp.concatenate([part * cosine[:, None, :] + turned * sine[:, None, :], values[..., ROT:]], axis=-1)

def run_sequence(hidden, positions, params):
    input_weight, output_weight, expand_weight, contract_weight, norm_gain, norm_shift, input_bias, output_bias, expand_bias = params
    length = hidden.shape[0]
    cosine, sine = rotary_tables(positions)
    allowed = positions[None, :] <= positions[:, None]
    scale = HEAD_DIM ** (-0.5)

    def one_head(trio):
        queries, keys, values = trio
        scores = low_back(highest(queries, keys.T) * scale)
        scores = jnp.where(allowed, scores, MASKED)
        highest_score = lax.optimization_barrier(jnp.max(scores, axis=1, keepdims=True))
        exponent = jnp.exp(scores - highest_score)
        probs = exponent / lax.optimization_barrier(jnp.sum(exponent, axis=1, keepdims=True))
        return highest(low(probs), values)
    head_step = jax.checkpoint(one_head)
    for layer in range(LAYERS):
        first_in = low(layer_norm(hidden, norm_gain[layer, 0], norm_shift[layer, 0]))
        projected = low_back(jnp.einsum('ld,dtk->ltk', first_in, input_weight[layer], precision=lax.Precision.HIGHEST) + input_bias[layer])
        queries = low(rotate(projected[:, 0].reshape(length, HEADS, HEAD_DIM), cosine, sine))
        keys = low(rotate(projected[:, 1].reshape(length, HEADS, HEAD_DIM), cosine, sine))
        values = low(projected[:, 2].reshape(length, HEADS, HEAD_DIM))
        attended = lax.map(head_step, (queries.transpose(1, 0, 2), keys.transpose(1, 0, 2), values.transpose(1, 0, 2)))
        mixed = low(low_back(attended.transpose(1, 0, 2).reshape(length, D)))
        second_in = low(layer_norm(hidden, norm_gain[layer, 1], norm_shift[layer, 1]))
        inner = low_back(highest(second_in, expand_weight[layer]) + expand_bias[layer])
        activated = low(jax.nn.gelu(inner, approximate=False))
        branch = low_back(highest(mixed, output_weight[layer].T) + highest(activated, contract_weight[layer].T))
        hidden = hidden + branch + output_bias[layer, 0] + output_bias[layer, 1]
    return hidden

def reference(tokens, cotangent, group_order, input_weight, output_weight, expand_weight, contract_weight, norm_gain, norm_shift, input_bias, output_bias, expand_bias):
    length = ROWS * N_CTX
    params = (input_weight.astype(jnp.float32), output_weight.astype(jnp.float32), expand_weight.astype(jnp.float32), contract_weight.astype(jnp.float32), norm_gain.astype(jnp.float32), norm_shift.astype(jnp.float32), input_bias.astype(jnp.float32), output_bias.astype(jnp.float32), expand_bias.astype(jnp.float32))
    positions = (group_order[:, :, None] * ROWS + jnp.arange(ROWS, dtype=jnp.int32)[None, None, :]).astype(jnp.int32).reshape(SEQS, length)

    def forward(inputs, weights):
        blocks = inputs.reshape(SEQS, length, D)
        outcome = lax.map(lambda pair: run_sequence(pair[0], pair[1], weights), (blocks, positions))
        return outcome.reshape(SEQS * length, D)
    result, pull = jax.vjp(forward, tokens.astype(jnp.float32), params)
    input_gradient, weight_gradients = pull(cotangent.astype(jnp.float32))
    return (result.astype(jnp.bfloat16), input_gradient, weight_gradients[0], weight_gradients[1], weight_gradients[2], weight_gradients[3], weight_gradients[4], weight_gradients[5], weight_gradients[6], weight_gradients[7], weight_gradients[8])
```

```python
import functools

import jax
import jax.numpy as jnp
from jax import lax
from jax.experimental import pallas as pl
from jax.experimental.pallas import tpu as pltpu
from jax.sharding import PartitionSpec as P

MESH = pl.DeviceIdType.MESH
F32, BF16 = jnp.float32, jnp.bfloat16
D, HEAD_DIM, ROT, LAYERS = 1024, 64, 16, 2
ROWS = 128
GROUP = 512
WIN, WOUT, WFF = 384, 128, 512
COLS = WIN + WOUT + 2 * WFF
PARAMS = 208
EPSILON = 1e-05
MASKED = -1e30
VMEM_LIMIT = 56 * 1024 * 1024


def place():
    ctx = lax.axis_index("ctx")
    chip = lax.div(ctx, 2)
    y = lax.axis_index("seq") * 2 + lax.axis_index("tp")
    return y, lax.div(chip, 4), lax.rem(chip, 4), lax.rem(ctx, 2)


def device(y, x, z, core):
    return (lax.div(y, 2), (x * 4 + z) * 2 + core, lax.rem(y, 2))


def ring(index, step):
    return lax.rem(index + step, 4)


def enter(partners):
    barrier = pltpu.get_barrier_semaphore()
    for partner in partners:
        pl.semaphore_signal(barrier, inc=1, device_id=partner, device_id_type=MESH)
    pl.semaphore_wait(barrier, len(partners))


def plane_partners(y, x, z, core):
    return [
        device(y, ring(x, dx), ring(z, dz), core)
        for dx in range(4)
        for dz in range(4)
        if dx or dz
    ]


def column_partners(y, x, z, core):
    return [
        device(ring(y, dy), x, z, lax.rem(core + dc, 2))
        for dy in range(4)
        for dc in range(2)
        if dy or dc
    ]


def remote(source, target, send, receive, partner):
    return pltpu.make_async_remote_copy(
        src_ref=source,
        dst_ref=target,
        send_sem=send,
        recv_sem=receive,
        device_id=partner,
        device_id_type=MESH,
    )


HBM = pl.BlockSpec(memory_space=pl.ANY)
VMEM = pl.BlockSpec(memory_space=pltpu.VMEM)
SMEM = pl.BlockSpec(memory_space=pltpu.SMEM)


def dma(*shape):
    return pltpu.SemaphoreType.DMA(shape)


def params(number):
    return pltpu.CompilerParams(
        collective_id=number, has_side_effects=True, vmem_limit_bytes=VMEM_LIMIT
    )


def gather_kernel(
    w_ref, tok_ref, cot_ref, par_ref, g0_ref, g1_ref, t_ref, c_ref, s_ref,
    here, send_a, recv_a, send_s, recv_s, send_b, recv_b, column_s, joined, send_p, recv_p,
):
    y, x, z, core = place()
    seq, tp = lax.div(y, 2), lax.rem(y, 2)
    mine = seq * 2 + core
    chip = x * 4 + z
    full = (g0_ref, g1_ref)
    neighbours = {
        "x": (device(y, ring(x, 1), z, core), device(y, ring(x, 3), z, core)),
        "z": (device(y, x, ring(z, 1), core), device(y, x, ring(z, 3), core)),
    }
    column = column_partners(y, x, z, core)
    plane = plane_partners(y, x, z, core)
    enter(column + plane)

    quarter = pl.ds(pl.multiple_of(core * 16, 16), 16)
    local = [
        pltpu.make_async_copy(w_ref.at[0, mine], g0_ref.at[seq, x, z, quarter], here.at[0]),
        pltpu.make_async_copy(w_ref.at[1, mine], g1_ref.at[seq, x, z, quarter], here.at[1]),
        pltpu.make_async_copy(tok_ref, t_ref.at[mine], here.at[2]),
        pltpu.make_async_copy(cot_ref, c_ref.at[mine], here.at[3]),
        pltpu.make_async_copy(par_ref, column_s.at[y * 2 + core], here.at[4]),
    ]
    for copy in local:
        copy.start()
    weights = [[], []]
    others = []
    peers = []
    for k, (dh, dc) in enumerate(((0, 1), (1, 0), (1, 1))):
        seq_to, core_to = lax.rem(seq + dh, 2), lax.rem(core + dc, 2)
        peers.append((k, seq_to * 2 + core_to, device(seq_to * 2 + tp, x, z, core_to)))
    for layer in range(2):
        for k, theirs, peer in peers:
            weights[layer].append(
                remote(
                    w_ref.at[layer, theirs],
                    full[layer].at[seq, x, z, quarter],
                    send_a.at[layer, k],
                    recv_a.at[layer, k],
                    peer,
                )
            )
            weights[layer][-1].start()
    for k, theirs, peer in peers:
        others.append(remote(tok_ref, t_ref.at[mine], send_a.at[2, k], recv_a.at[2, k], peer))
        others.append(remote(cot_ref, c_ref.at[mine], send_a.at[3, k], recv_a.at[3, k], peer))
    smalls = [
        remote(par_ref, column_s.at[y * 2 + core], send_s.at[k], recv_s.at[k], peer)
        for k, peer in enumerate(column)
    ]
    for copy in smalls + others:
        copy.start()

    for copy in weights[0]:
        copy.wait_recv()
    local[0].wait()

    started = []

    def go(source, slot, partner):
        copy = remote(source, source, send_b.at[slot], recv_b.at[slot], partner)
        copy.start()
        started.append(copy)
        return copy

    low, high = pl.ds(0, 16), pl.ds(16, 16)
    two, more = pl.ds(0, 2), pl.ds(2, 2)

    def first(layer, half):
        base = (layer * 2 + half) * 8
        up, down = neighbours["xz"[half]]
        own = full[layer].at[half, x, z]
        return go(own, base, up), go(own, base + 1, down)

    def first_on(layer, half, copies):
        base = (layer * 2 + half) * 8
        up, down = neighbours["xz"[half]]
        for copy in copies:
            copy.wait_recv()
        whole = full[layer].at[half]
        if half == 0:
            before, after = whole.at[ring(x, 3), z], whole.at[ring(x, 1), z]
        else:
            before, after = whole.at[x, ring(z, 3)], whole.at[x, ring(z, 1)]
        return go(before.at[low], base + 2, up), go(after.at[high], base + 3, down)

    def second(layer, half, copies):
        base = (layer * 2 + half) * 8
        up, down = neighbours["zx"[half]]
        for copy in copies:
            copy.wait_recv()
        whole = full[layer].at[half]
        line = whole.at[:, z] if half == 0 else whole.at[x]
        return go(line, base + 4, up), go(line, base + 5, down)

    def second_on(layer, half, copies):
        base = (layer * 2 + half) * 8
        up, down = neighbours["zx"[half]]
        for copy in copies:
            copy.wait_recv()
        whole = full[layer].at[half]
        if half == 0:
            before, after = whole.at[two, ring(z, 3)], whole.at[more, ring(z, 1)]
        else:
            before, after = whole.at[ring(x, 3), two], whole.at[ring(x, 1), more]
        return go(before, base + 6, up), go(after, base + 7, down)

    def over(layer, steps, held=(None, None)):
        held = list(held)
        for step in steps:
            for half in range(2):
                held[half] = (
                    step(layer, half) if step is first else step(layer, half, held[half])
                )
        return held

    last0 = over(0, (first,))
    for copy in smalls:
        copy.wait_recv()
    local[4].wait()
    for k in range(2):
        joined[k] = column_s[:, k, :]
    spread = [pltpu.make_async_copy(joined, s_ref.at[chip], here.at[5])]
    spread += [
        remote(joined, s_ref.at[chip], send_p.at[k], recv_p.at[k], peer)
        for k, peer in enumerate(plane)
    ]
    for copy in spread:
        copy.start()
    last0 = over(0, (first_on, second, second_on), last0)
    for copy in weights[1]:
        copy.wait_recv()
    local[1].wait()
    last1 = over(1, (first, first_on, second, second_on))
    for held in (last0, last1):
        for pair in held:
            for copy in pair:
                copy.wait_recv()
    for copy in started:
        copy.wait_send()
    for copy in weights[0] + weights[1] + smalls:
        copy.wait_send()
    for copy in local[2:4] + others + spread:
        copy.wait()


def gather_all(packed, tokens, cotangent, small):
    full = jax.ShapeDtypeStruct((2, 4, 4, 32, COLS), BF16)
    rows = jax.ShapeDtypeStruct((4, ROWS, D), BF16)
    return pl.pallas_call(
        gather_kernel,
        out_shape=(full, full, rows, rows, jax.ShapeDtypeStruct((16, 2, 8, 128), F32)),
        in_specs=[HBM] * 4,
        out_specs=[HBM] * 5,
        scratch_shapes=[
            dma(6), dma(4, 3), dma(4, 3), dma(7), dma(7), dma(32), dma(32),
            pltpu.VMEM((8, 8, 128), F32), pltpu.VMEM((2, 8, 128), F32), dma(15), dma(15),
        ],
        compiler_params=params(0),
        name="gather_all",
    )(packed, tokens, cotangent, small)


def exchange_kernel(count, shared, *refs):
    sources, targets = refs[:count], refs[count : 2 * count]
    here, send, receive = refs[2 * count :]
    y, x, z, core = place()
    chip = x * 4 + z
    partners = plane_partners(y, x, z, core)
    enter(partners)
    copies = []
    steps = [(dx, dz) for dx in range(4) for dz in range(4) if dx or dz]
    for number, (source, target) in enumerate(zip(sources, targets)):
        own = pltpu.make_async_copy(
            source.at[x if shared[number] else chip], target.at[chip], here.at[number]
        )
        own.start()
        copies.append(own)
        for k, (dx, dz) in enumerate(steps):
            to_x, to_z = ring(x, dx), ring(z, dz)
            copy = remote(
                source.at[to_x if shared[number] else to_x * 4 + to_z],
                target.at[chip],
                send.at[number, k],
                receive.at[number, k],
                partners[k],
            )
            copy.start()
            copies.append(copy)
    for copy in copies:
        copy.wait()


def exchange(number, shared, *sources):
    count = len(sources)
    return pl.pallas_call(
        functools.partial(exchange_kernel, count, shared),
        out_shape=tuple(jax.ShapeDtypeStruct((16, *s.shape[1:]), s.dtype) for s in sources),
        in_specs=[HBM] * count,
        out_specs=[HBM] * count,
        scratch_shapes=[dma(count), dma(count, 15), dma(count, 15)],
        compiler_params=params(number),
        name="exchange",
    )(*sources)


def column_sum_kernel(
    everywhere, part_ref, out_ref, near, far, held, send1, recv1, send2, recv2, send3, recv3
):
    y, x, z, core = place()
    seq, tp = lax.div(y, 2), lax.rem(y, 2)
    other = lax.rem(core + 1, 2)
    sibling = device(y, x, z, other)
    partners = [device(ring(y, dy), x, z, core) for dy in (1, 2, 3)]
    enter([sibling, *partners])
    order = (2, 1, 3)
    copies = []
    nears = {}
    for dy in (*order, 0):
        to = ring(y, dy)
        nears[dy] = remote(
            part_ref.at[lax.div(to, 2), other, lax.rem(to, 2)],
            near.at[dy],
            send1.at[dy],
            recv1.at[dy],
            sibling,
        )
        nears[dy].start()
    fars = []
    for dy in order:
        to = ring(y, dy)
        nears[dy].wait_recv()
        held[dy - 1] = (
            part_ref[lax.div(to, 2), core, lax.rem(to, 2)].astype(F32) + near[dy].astype(F32)
        ).astype(BF16)
        copy = remote(
            held.at[dy - 1], far.at[dy - 1], send2.at[dy - 1], recv2.at[dy - 1], partners[dy - 1]
        )
        copy.start()
        fars.append(copy)
    nears[0].wait_recv()
    total = part_ref[seq, core, tp].astype(F32) + near[0].astype(F32)
    for copy in fars:
        copy.wait_recv()
    total = total + far[0].astype(F32) + far[1].astype(F32) + far[2].astype(F32)
    if everywhere:
        own = out_ref.at[seq, core, tp]
        out_ref[seq, core, tp] = total.astype(BF16)
        outs = []
        for dy in order:
            copy = remote(own, own, send3.at[dy - 1], recv3.at[dy - 1], partners[dy - 1])
            copy.start()
            outs.append(copy)
        copy = remote(own, own, send3.at[3], recv3.at[3], sibling)
        copy.start()
        copies.append(copy)
        for at, dy in enumerate(order):
            outs[at].wait_recv()
            source = ring(y, 4 - dy)
            block = out_ref.at[lax.div(source, 2), core, lax.rem(source, 2)]
            copy = remote(block, block, send3.at[3 + dy], recv3.at[3 + dy], sibling)
            copy.start()
            copies.append(copy)
        for copy in outs:
            copy.wait_send()
    else:
        out_ref[tp] = total.astype(BF16)
        own = out_ref.at[tp]
        copy = remote(
            own, own, send3.at[0], recv3.at[0], device(seq * 2 + lax.rem(tp + 1, 2), x, z, core)
        )
        copy.start()
        copies.append(copy)
    for copy in copies:
        copy.wait()
    for copy in [*nears.values(), *fars]:
        copy.wait_send()


def column_sum(number, part, everywhere):
    shape = (2, 2, 2, 64, D) if everywhere else (2, 64, D)
    out = pl.pallas_call(
        functools.partial(column_sum_kernel, everywhere),
        out_shape=jax.ShapeDtypeStruct(shape, BF16),
        in_specs=[VMEM],
        out_specs=VMEM,
        scratch_shapes=[
            pltpu.VMEM((4, 64, D), BF16),
            pltpu.VMEM((3, 64, D), BF16),
            pltpu.VMEM((3, 64, D), BF16),
            dma(4), dma(4), dma(3), dma(3), dma(7), dma(7),
        ],
        compiler_params=params(number),
        name="column_sum",
    )(part.reshape(2, 2, 2, 64, D))
    return out.reshape(-1, D)


def scatter_kernel(with_small, *refs):
    if with_small:
        dw_ref, small_ref, out_ref, small_out, *refs = refs
    else:
        dw_ref, out_ref, *refs = refs
    (opp1, dir1, comb1, mid, opp2, dir2, comb2, sent1, sent2, done, send, recv, here, send_f, recv_f,
     *small_scratch) = refs
    y, x, z, core = place()
    seq, tp = lax.div(y, 2), lax.rem(y, 2)
    mine = seq * 2 + core
    neighbours = {
        "x": (device(y, ring(x, 1), z, core), device(y, ring(x, 3), z, core)),
        "z": (device(y, x, ring(z, 1), core), device(y, x, ring(z, 3), core)),
    }
    column = column_partners(y, x, z, core)
    if with_small:
        plane = plane_partners(y, x, z, core)
        enter(column + plane)
    else:
        peers_now = []
        for dh, dc in ((0, 1), (1, 0), (1, 1)):
            peers_now.append(
                device(lax.rem(seq + dh, 2) * 2 + tp, x, z, lax.rem(core + dc, 2))
            )
        enter(peers_now + [*neighbours["x"], *neighbours["z"]])

    started = []

    def go(source, target, slot, partner):
        copy = remote(source, target, send.at[slot], recv.at[slot], partner)
        copy.start()
        started.append(copy)
        return copy

    two = (pl.ds(0, 2), pl.ds(2, 2))
    rows = (pl.ds(0, 16), pl.ds(16, 16))

    def part1(half, step, side):
        whole = dw_ref.at[half]
        if half == 0:
            return whole.at[two[side], ring(z, step)]
        return whole.at[ring(x, step), two[side]]

    def part2(half, step, side):
        at = ring(x, step) if half == 0 else ring(z, step)
        return mid.at[half, at].at[rows[side]]

    def begin(half, part, axis, opposite, direct, base):
        up, down = neighbours[axis]
        return (
            go(part(half, 2, 0), opposite.at[half, 0], base, up),
            go(part(half, 2, 1), opposite.at[half, 1], base + 1, down),
            go(part(half, 1, 1), direct.at[half, 0], base + 2, up),
            go(part(half, 3, 0), direct.at[half, 1], base + 3, down),
        )

    def onward(half, part, axis, opposite, combined, sent, base, copies):
        up, down = neighbours[axis]
        copies[0].wait_recv()
        sent[half, 0] = (
            part(half, 1, 0)[...].astype(F32) + opposite[half, 0].astype(F32)
        ).astype(BF16)
        first = go(sent.at[half, 0], combined.at[half, 0], base + 4, up)
        copies[1].wait_recv()
        sent[half, 1] = (
            part(half, 3, 1)[...].astype(F32) + opposite[half, 1].astype(F32)
        ).astype(BF16)
        return (*copies[2:], first, go(sent.at[half, 1], combined.at[half, 1], base + 5, down))

    def finish(half, part, direct, combined, copies):
        for copy in copies:
            copy.wait_recv()
        low = (
            part(half, 0, 0)[...].astype(F32)
            + combined[half, 0].astype(F32)
            + direct[half, 1].astype(F32)
        )
        high = (
            part(half, 0, 1)[...].astype(F32)
            + combined[half, 1].astype(F32)
            + direct[half, 0].astype(F32)
        )
        return low, high

    held = [None, None]
    for half in range(2):
        held[half] = begin(half, part1, "zx"[half], opp1, dir1, half * 12)
    if with_small:
        gathered, total, sent_s, recv_s, sent_t, recv_t, others = small_scratch
        chip = x * 4 + z
        steps = [(dx, dz) for dx in range(4) for dz in range(4) if dx or dz]
        spread = []
        for k, (dx, dz) in enumerate(steps):
            copy = remote(
                small_ref.at[ring(x, dx) * 4 + ring(z, dz)],
                gathered.at[k],
                sent_s.at[k],
                recv_s.at[k],
                plane[k],
            )
            copy.start()
            spread.append(copy)
    for half in range(2):
        held[half] = onward(half, part1, "zx"[half], opp1, comb1, sent1, half * 12, held[half])
    for half in range(2):
        low, high = finish(half, part1, dir1, comb1, held[half])
        mid[half, 0:2] = low.astype(BF16)
        mid[half, 2:4] = high.astype(BF16)
        held[half] = begin(half, part2, "xz"[half], opp2, dir2, half * 12 + 6)
    if with_small:
        for copy in spread:
            copy.wait_recv()
        total[...] = small_ref[chip] + jnp.sum(gathered[...], axis=0)
        shared = []
        for k, peer in enumerate(column):
            copy = remote(total, others.at[k], sent_t.at[k], recv_t.at[k], peer)
            copy.start()
            shared.append(copy)
    for half in range(2):
        held[half] = onward(half, part2, "xz"[half], opp2, comb2, sent2, half * 12 + 6, held[half])
    for half in range(2):
        low, high = finish(half, part2, dir2, comb2, held[half])
        done[half, 0] = low.astype(BF16)
        done[half, 1] = high.astype(BF16)
    own = pltpu.make_async_copy(done.at[seq, core], out_ref.at[mine], here)
    own.start()
    final = []
    for k, (dh, dc) in enumerate(((0, 1), (1, 0), (1, 1))):
        seq_to, core_to = lax.rem(seq + dh, 2), lax.rem(core + dc, 2)
        copy = remote(
            done.at[seq_to, core_to],
            out_ref.at[mine],
            send_f.at[k],
            recv_f.at[k],
            device(seq_to * 2 + tp, x, z, core_to),
        )
        copy.start()
        final.append(copy)
    if with_small:
        for copy in shared:
            copy.wait_recv()
        small_out[...] = total[...] + jnp.sum(others[...], axis=0)
        for copy in spread + shared:
            copy.wait_send()
    own.wait()
    for copy in final:
        copy.wait()
    for copy in started:
        copy.wait_send()


def scatter(number, grads, small=None):
    out = [jax.ShapeDtypeStruct((4, 16, COLS), BF16)]
    halves1 = pltpu.VMEM((2, 2, 2, 32, COLS), BF16)
    halves2 = pltpu.VMEM((2, 2, 16, COLS), BF16)
    scratch = [
        halves1, halves1, halves1, pltpu.VMEM((2, 4, 32, COLS), BF16),
        halves2, halves2, halves2, halves1, halves2, halves2,
        dma(24), dma(24), pltpu.SemaphoreType.DMA, dma(3), dma(3),
    ]
    args = [grads.reshape(2, 4, 4, 32, COLS)]
    if small is not None:
        args.append(small)
        out.append(jax.ShapeDtypeStruct((2, 8, 128), F32))
        scratch += [
            pltpu.VMEM((15, 2, 8, 128), F32), pltpu.VMEM((2, 8, 128), F32),
            dma(15), dma(15), dma(7), dma(7), pltpu.VMEM((7, 2, 8, 128), F32),
        ]
    return pl.pallas_call(
        functools.partial(scatter_kernel, small is not None),
        out_shape=tuple(out),
        in_specs=[VMEM] * len(args),
        out_specs=tuple([VMEM] * len(out)),
        scratch_shapes=scratch,
        compiler_params=params(number),
        name="scatter",
    )(*args)


TILE = 256
SPAN = 1024


def seen(quarter, tile):
    key = lax.broadcasted_iota(jnp.int32, (SPAN, TILE), 0)
    row = lax.broadcasted_iota(jnp.int32, (SPAN, TILE), 1)
    place_of = (row // 32) * ROWS + quarter * 32 + row % 32
    return key <= place_of


def attend_kernel(rank_ref, kv_ref, q_ref, m_ref, kvs_ref, kvt_ref, qs_ref, o_ref, lse_ref, score, rows):
    quarter = rank_ref[32]
    lane = lax.broadcasted_iota(jnp.int32, (32, 128), 1)

    def arrange(chip, carry):
        block = q_ref[chip].astype(F32) * (HEAD_DIM**-0.5)
        for core in range(2):
            rank = rank_ref[chip * 2 + core]
            keyed = kv_ref[chip * 2 + core]
            kvs_ref[pl.ds(pl.multiple_of(rank * ROWS, ROWS), ROWS), :] = keyed
            kvt_ref[rank] = keyed.astype(F32).T.astype(BF16)
            part = block if core == 0 else pltpu.roll(block, 64, 1)
            qs_ref[pl.ds(pl.multiple_of(rank * 32, 32), 32), :] = jnp.where(
                lane < 64, part, 0.0
            ).astype(BF16)
        return carry

    lax.fori_loop(0, 16, arrange, 0)

    for tile in range(4):
        queries = qs_ref[tile * TILE : (tile + 1) * TILE, :]
        highest = jnp.full((1, TILE), MASKED, F32)
        for span in range(tile + 1):
            block = lax.dot_general(
                kvs_ref[span * SPAN : (span + 1) * SPAN, :],
                queries,
                (((1,), (1,)), ((), ())),
                preferred_element_type=F32,
            )
            if span == tile:
                block = jnp.where(seen(quarter, tile), block, MASKED)
            score[span * SPAN : (span + 1) * SPAN, :] = block
            highest = jnp.maximum(highest, jnp.max(block, axis=0, keepdims=True))
        total = jnp.zeros((1, TILE), F32)
        mixed = jnp.zeros((128, TILE), F32)
        for span in range(tile + 1):
            weight = jnp.exp(score[span * SPAN : (span + 1) * SPAN, :] - highest)
            total = total + jnp.sum(weight, axis=0, keepdims=True)
            low = weight.astype(BF16)
            for part in range(8):
                mixed = mixed + jnp.dot(
                    kvt_ref[span * 8 + part],
                    low[part * ROWS : (part + 1) * ROWS],
                    preferred_element_type=F32,
                )
        mixed = mixed / total
        lse_ref[tile] = jnp.broadcast_to(highest + jnp.log(total), (8, TILE))
        o_ref[tile] = mixed
        rows[tile * TILE : (tile + 1) * TILE, :] = mixed.T

    def put_back(chip, carry):
        first = rows[pl.ds(pl.multiple_of(rank_ref[chip * 2] * 32, 32), 32), :]
        second = rows[pl.ds(pl.multiple_of(rank_ref[chip * 2 + 1] * 32, 32), 32), :]
        m_ref[chip] = jnp.where(lane < 64, pltpu.roll(first, 64, 1), second).astype(BF16)
        return carry

    lax.fori_loop(0, 16, put_back, 0)


def attend(rank, kv, q):
    return pl.pallas_call(
        attend_kernel,
        out_shape=(
            jax.ShapeDtypeStruct((16, 32, 128), BF16),
            jax.ShapeDtypeStruct((4096, 128), BF16),
            jax.ShapeDtypeStruct((32, 128, 128), BF16),
            jax.ShapeDtypeStruct((1024, 128), BF16),
            jax.ShapeDtypeStruct((4, 128, TILE), F32),
            jax.ShapeDtypeStruct((4, 8, TILE), F32),
        ),
        in_specs=[SMEM, VMEM, VMEM],
        out_specs=tuple([VMEM] * 6),
        scratch_shapes=[pltpu.VMEM((4096, TILE), F32), pltpu.VMEM((1024, 128), F32)],
        compiler_params=pltpu.CompilerParams(vmem_limit_bytes=VMEM_LIMIT),
        name="attend",
    )(rank, kv, q)


def attend_back_kernel(
    rank_ref, kvs_ref, kvt_ref, qs_ref, o_ref, lse_ref, dm_ref, dkv_ref, dq_ref, dos, acc, dqs
):
    quarter = rank_ref[32]
    lane = lax.broadcasted_iota(jnp.int32, (32, 128), 1)

    def arrange(chip, carry):
        block = dm_ref[chip].astype(F32)
        for core in range(2):
            rank = rank_ref[chip * 2 + core]
            part = pltpu.roll(block, 64, 1) if core == 0 else block
            dos[pl.ds(pl.multiple_of(rank * 32, 32), 32), :] = jnp.where(
                lane < 64, 0.0, part
            ).astype(BF16)
        return carry

    lax.fori_loop(0, 16, arrange, 0)

    for tile in range(4):
        queries = qs_ref[tile * TILE : (tile + 1) * TILE, :]
        outs = dos[tile * TILE : (tile + 1) * TILE, :]
        delta = jnp.sum(outs.astype(F32).T * o_ref[tile], axis=0, keepdims=True)
        lse = lse_ref[tile][0:1, :]
        query_grad = jnp.zeros((128, TILE), F32)
        for span in range(tile + 1):
            keyed = kvs_ref[span * SPAN : (span + 1) * SPAN, :]
            block = lax.dot_general(
                keyed, queries, (((1,), (1,)), ((), ())), preferred_element_type=F32
            )
            if span == tile:
                block = jnp.where(seen(quarter, tile), block, MASKED)
            probs = jnp.exp(block - lse)
            back = lax.dot_general(
                keyed, outs, (((1,), (1,)), ((), ())), preferred_element_type=F32
            )
            score_grad = (probs * (back - delta)).astype(BF16)
            pair = jnp.dot(score_grad, queries, preferred_element_type=F32) + jnp.dot(
                probs.astype(BF16), outs, preferred_element_type=F32
            )
            if span == tile:
                acc[span * SPAN : (span + 1) * SPAN, :] = pair
            else:
                acc[span * SPAN : (span + 1) * SPAN, :] += pair
            for part in range(8):
                query_grad = query_grad + jnp.dot(
                    kvt_ref[span * 8 + part],
                    score_grad[part * ROWS : (part + 1) * ROWS],
                    preferred_element_type=F32,
                )
        dqs[tile * TILE : (tile + 1) * TILE, :] = query_grad.T * (HEAD_DIM**-0.5)

    def put_back(chip, carry):
        first = dqs[pl.ds(pl.multiple_of(rank_ref[chip * 2] * 32, 32), 32), :]
        second = dqs[pl.ds(pl.multiple_of(rank_ref[chip * 2 + 1] * 32, 32), 32), :]
        dq_ref[chip] = jnp.where(lane < 64, first, pltpu.roll(second, 64, 1)).astype(BF16)
        for core in range(2):
            rank = rank_ref[chip * 2 + core]
            dkv_ref[chip, core] = acc[
                pl.ds(pl.multiple_of(rank * ROWS, ROWS), ROWS), :
            ].astype(BF16)
        return carry

    lax.fori_loop(0, 16, put_back, 0)


def attend_back(rank, kvs, kvt, qs, o, lse, dm):
    return pl.pallas_call(
        attend_back_kernel,
        out_shape=(
            jax.ShapeDtypeStruct((16, 2, 128, 128), BF16),
            jax.ShapeDtypeStruct((16, 32, 128), BF16),
        ),
        in_specs=[SMEM] + [VMEM] * 6,
        out_specs=tuple([VMEM] * 2),
        scratch_shapes=[
            pltpu.VMEM((1024, 128), BF16),
            pltpu.VMEM((4096, 128), F32),
            pltpu.VMEM((1024, 128), F32),
        ],
        compiler_params=pltpu.CompilerParams(vmem_limit_bytes=VMEM_LIMIT),
        name="attend_back",
    )(rank, kvs, kvt, qs, o, lse, dm)


def pack_rows(values):
    parts = values.reshape(2, 2, 4, 32, 2, HEAD_DIM)
    return parts.transpose(0, 4, 2, 3, 1, 5).reshape(16, 32, 128)


def unpack_rows(parts):
    values = parts.reshape(2, 2, 4, 32, 2, HEAD_DIM)
    return values.transpose(0, 4, 2, 3, 1, 5).reshape(GROUP, 128)


def pack_pairs(keys, values):
    pairs = jnp.concatenate(
        [keys.reshape(2, 256, 2, HEAD_DIM), values.reshape(2, 256, 2, HEAD_DIM)], axis=3
    )
    return pairs.transpose(0, 2, 1, 3).reshape(4, 256, 128)


def unpack_pairs(pairs):
    values = jnp.sum(pairs.reshape(2, 2, 4, 256, 128).astype(F32), axis=2)
    values = values.transpose(0, 2, 1, 3).reshape(GROUP, 2, 128)
    return (
        values[:, :, :HEAD_DIM].reshape(GROUP, 128),
        values[:, :, HEAD_DIM:].reshape(GROUP, 128),
    )


def rotary_tables(positions):
    half = ROT // 2
    freqs = 10000.0 ** (-(jnp.arange(half, dtype=F32) * 2.0 / ROT))
    angle = positions.astype(F32)[:, None] * freqs[None, :]
    cosine, sine = jnp.cos(angle), jnp.sin(angle)
    rows = positions.shape[0]
    rest = HEAD_DIM - ROT
    one = jnp.concatenate([cosine, cosine, jnp.ones((rows, rest), F32)], axis=1)
    right = jnp.concatenate([-sine, jnp.zeros((rows, rest + half), F32)], axis=1)
    left = jnp.concatenate(
        [jnp.zeros((rows, half), F32), sine, jnp.zeros((rows, rest), F32)], axis=1
    )
    return tuple(jnp.concatenate([t, t], axis=1) for t in (one, right, left))


def rotate(values, tables, sign):
    one, right, left = tables
    half = ROT // 2
    return (
        values * one
        + sign * jnp.roll(values, -half, axis=1) * right
        + sign * jnp.roll(values, half, axis=1) * left
    )


def normalize(values):
    centre = jnp.mean(values, axis=-1, keepdims=True)
    centred = values - centre
    spread = jnp.mean(centred * centred, axis=-1, keepdims=True)
    inverse = lax.rsqrt(spread + EPSILON)
    return centred * inverse, inverse


def matmul(left, right, dims):
    return lax.dot_general(left, right, (dims, ((), ())), preferred_element_type=F32)


def local(
    tokens, cotangent, group_order, input_weight, output_weight, expand_weight, contract_weight,
    norm_gain, norm_shift, input_bias, output_bias, expand_bias,
):
    y, x, z, core = place()
    seq, tp = lax.div(y, 2), lax.rem(y, 2)
    chip = x * 4 + z
    mine = seq * 2 + core

    def quarters(weight, width):
        shaped = weight.reshape(LAYERS, 16, -1, 4, width).transpose(0, 3, 1, 2, 4)
        return shaped.reshape(LAYERS, 4, 16, -1)

    packed = jnp.concatenate(
        [
            quarters(input_weight, 128),
            quarters(output_weight, 128),
            quarters(expand_weight, 512),
            quarters(contract_weight, 512),
        ],
        axis=3,
    )
    small = jnp.concatenate(
        [
            norm_gain.reshape(-1), norm_shift.reshape(-1), input_bias.reshape(-1),
            output_bias.reshape(-1), expand_bias.reshape(-1), group_order.reshape(-1).astype(F32),
            jnp.zeros((1024 - PARAMS - 1,), F32),
        ]
    ).reshape(8, 128)
    full0, full1, token_rows, grad_rows, smalls = gather_all(packed, tokens, cotangent, small)
    weights = (full0.reshape(D, COLS), full1.reshape(D, COLS))
    smalls = smalls.transpose(0, 2, 1, 3).reshape(16, 2, 2, 2, 256)[..., : PARAMS + 1]
    smalls = smalls.transpose(1, 0, 3, 2, 4).reshape(128, PARAMS + 1)
    gains = smalls[:, 0:32].reshape(128, 2, 2, 8).transpose(1, 2, 0, 3).reshape(2, 2, D)
    shifts = smalls[:, 32:64].reshape(128, 2, 2, 8).transpose(1, 2, 0, 3).reshape(2, 2, D)
    input_shifts = smalls[:, 64:112].reshape(128, 2, 3, 8).transpose(1, 2, 0, 3).reshape(2, 3, D)
    output_shifts = smalls[:, 112:144].reshape(128, 2, 2, 8).transpose(1, 2, 0, 3).reshape(2, 2, D)
    expand_shifts = smalls[:, 144:208].reshape(128, 2, 32).transpose(1, 0, 2).reshape(2, 4 * D)
    ranks = smalls.reshape(2, 32, 2, PARAMS + 1)[:, :, 0, PARAMS].astype(jnp.int32)
    input_at = tp * 512 + mine * 128
    expand_at = tp * 2048 + mine * 512
    input_shifts = lax.dynamic_slice_in_dim(input_shifts, input_at, 128, 2)
    expand_shifts = lax.dynamic_slice_in_dim(expand_shifts, expand_at, 512, 1)

    here = lax.dynamic_slice_in_dim(ranks, chip * 2, 2, 1)
    positions = (here[:, :, None] * ROWS + jnp.arange(ROWS, dtype=jnp.int32)).reshape(GROUP)
    tables = rotary_tables(positions)
    task = jnp.concatenate(
        [lax.dynamic_slice_in_dim(ranks, lax.div(x, 2), 1, 0).reshape(32), z.reshape(1)]
    )

    hidden = token_rows.reshape(GROUP, D).astype(F32)
    saved = []
    activations = None
    for layer in range(LAYERS):
        weight = weights[layer]
        input_full = weight[:, :WIN]
        output_full = weight[:, WIN : WIN + WOUT]
        expand_full = weight[:, WIN + WOUT : WIN + WOUT + WFF]
        contract_full = weight[:, WIN + WOUT + WFF :]
        normed, inverse = normalize(hidden)
        first_in = (normed * gains[layer, 0] + shifts[layer, 0]).astype(BF16)
        second_in = (normed * gains[layer, 1] + shifts[layer, 1]).astype(BF16)
        projected = matmul(first_in, input_full, ((1,), (0,))) + input_shifts[layer].reshape(-1)
        queries = rotate(projected[:, :128], tables, 1.0).astype(BF16)
        keys = rotate(projected[:, 128:256], tables, 1.0).astype(BF16)
        values = projected[:, 256:].astype(BF16)
        kv_parts, q_parts = exchange(
            1, (True, False), pack_pairs(keys, values), pack_rows(queries)
        )
        mixed_parts, kvs, kvt, qs, o, lse = attend(task, kv_parts.reshape(32, 128, 128), q_parts)
        (mixed_back,) = exchange(2, (False,), mixed_parts)
        mixed = unpack_rows(mixed_back)
        inner = matmul(second_in, expand_full, ((1,), (0,))) + expand_shifts[layer]
        activated = jax.nn.gelu(inner, approximate=False).astype(BF16)
        branch = matmul(mixed, output_full, ((1,), (1,))) + matmul(
            activated, contract_full, ((1,), (1,))
        )
        branch = branch.astype(BF16)
        shift = output_shifts[layer, 0] + output_shifts[layer, 1]
        if layer + 1 < LAYERS:
            hidden = hidden + column_sum(3, branch, True).astype(F32) + shift
        else:
            own = lax.dynamic_slice_in_dim(hidden, mine * ROWS, ROWS, 0)
            activations = (own + column_sum(4, branch, False).astype(F32) + shift).astype(BF16)
        saved.append(
            (normed, inverse, first_in, second_in, kvs, kvt, qs, o, lse, mixed, inner, activated)
        )

    grad = grad_rows.reshape(GROUP, D).astype(F32)
    gain_parts, shift_parts, input_shift_parts = [None] * 2, [None] * 2, [None] * 2
    output_shift_parts, expand_shift_parts = [None] * 2, [None] * 2
    weight_out = [None] * 2
    input_gradient = None
    small_out = None
    first_device = (y * 2 + core) == 0
    for layer in reversed(range(LAYERS)):
        weight = weights[layer]
        input_full = weight[:, :WIN]
        output_full = weight[:, WIN : WIN + WOUT]
        expand_full = weight[:, WIN + WOUT : WIN + WOUT + WFF]
        contract_full = weight[:, WIN + WOUT + WFF :]
        normed, inverse, first_in, second_in, kvs, kvt, qs, o, lse, mixed, inner, activated = saved[
            layer
        ]
        grad_low = grad.astype(BF16)
        column = jnp.where(first_device, jnp.sum(grad, axis=0), 0.0)
        output_shift_parts[layer] = jnp.stack([column, column], axis=0)
        mixed_grad = matmul(grad_low, output_full, ((1,), (0,))).astype(BF16)
        (mixed_grad_parts,) = exchange(2, (False,), pack_rows(mixed_grad))
        pair_parts, query_parts = attend_back(task, kvs, kvt, qs, o, lse, mixed_grad_parts)
        pair_back, query_back = exchange(
            5, (False, False), pair_parts.reshape(16, 256, 128), query_parts
        )
        activated_grad = matmul(grad_low, contract_full, ((1,), (0,)))
        _, gelu_pull = jax.vjp(functools.partial(jax.nn.gelu, approximate=False), inner)
        inner_grad = gelu_pull(activated_grad)[0].astype(BF16)
        expand_shift_parts[layer] = jnp.sum(inner_grad.astype(F32), axis=0)
        second_grad = matmul(inner_grad, expand_full, ((1,), (1,)))
        key_grad, value_grad = unpack_pairs(pair_back)
        projected_grad = jnp.concatenate(
            [
                rotate(unpack_rows(query_back).astype(F32), tables, -1.0),
                rotate(key_grad, tables, -1.0),
                value_grad,
            ],
            axis=1,
        ).astype(BF16)
        input_shift_parts[layer] = jnp.sum(projected_grad.astype(F32), axis=0).reshape(3, 128)
        first_grad = matmul(projected_grad, input_full, ((1,), (1,)))
        gain_parts[layer] = jnp.stack(
            [jnp.sum(first_grad * normed, axis=0), jnp.sum(second_grad * normed, axis=0)], axis=0
        )
        shift_parts[layer] = jnp.stack(
            [jnp.sum(first_grad, axis=0), jnp.sum(second_grad, axis=0)], axis=0
        )
        scaled = (first_grad * gains[layer, 0] + second_grad * gains[layer, 1]).astype(BF16)
        if layer:
            scaled = column_sum(3, scaled, True).astype(F32)
        else:
            scaled = column_sum(4, scaled, False).astype(F32)
            normed = lax.dynamic_slice_in_dim(normed, mine * ROWS, ROWS, 0)
            inverse = lax.dynamic_slice_in_dim(inverse, mine * ROWS, ROWS, 0)
            grad = lax.dynamic_slice_in_dim(grad, mine * ROWS, ROWS, 0)
        first_mean = jnp.mean(scaled, axis=-1, keepdims=True)
        second_mean = jnp.mean(scaled * normed, axis=-1, keepdims=True)
        grad = grad + inverse * (scaled - first_mean - normed * second_mean)
        weight_grad = jnp.concatenate(
            [
                matmul(first_in, projected_grad, ((0,), (0,))).astype(BF16),
                matmul(grad_low, mixed, ((0,), (0,))).astype(BF16),
                matmul(second_in, inner_grad, ((0,), (0,))).astype(BF16),
                matmul(grad_low, activated, ((0,), (0,))).astype(BF16),
            ],
            axis=1,
        )
        if layer:
            (weight_out[layer],) = scatter(6, weight_grad)
        else:
            input_gradient = grad
            input_full_shift = lax.dynamic_update_slice_in_dim(
                jnp.zeros((2, 3, D), F32), jnp.stack(input_shift_parts, axis=0), input_at, 2
            )
            expand_full_shift = lax.dynamic_update_slice_in_dim(
                jnp.zeros((2, 4 * D), F32), jnp.stack(expand_shift_parts, axis=0), expand_at, 1
            )

            def owners(values, width):
                parts = values.reshape(-1, 128, width).transpose(1, 0, 2)
                return parts.reshape(128, -1)

            every = jnp.concatenate(
                [
                    owners(jnp.stack(gain_parts, axis=0), 8),
                    owners(jnp.stack(shift_parts, axis=0), 8),
                    owners(input_full_shift, 8),
                    owners(jnp.stack(output_shift_parts, axis=0), 8),
                    owners(expand_full_shift, 32),
                    jnp.zeros((128, 256 - PARAMS), F32),
                ],
                axis=1,
            )
            every = every.reshape(2, 16, 2, 2, 2, 128).transpose(1, 4, 0, 3, 2, 5)
            weight_out[layer], small_out = scatter(7, weight_grad, every.reshape(16, 2, 8, 128))

    def whole(layer_grads, first, width, count):
        parts = [
            g[:, :, first : first + width * count].astype(F32).reshape(4, 16, count, width)
            for g in layer_grads
        ]
        return jnp.stack(parts, axis=0).transpose(0, 2, 3, 1, 4)

    input_out = whole(weight_out, 0, 128, 3).reshape(2, 16, 3, 512)
    output_out = whole(weight_out, WIN, 128, 1).reshape(2, 16, 512)
    expand_out = whole(weight_out, WIN + WOUT, WFF, 1).reshape(2, 16, 2048)
    contract_out = whole(weight_out, WIN + WOUT + WFF, WFF, 1).reshape(2, 16, 2048)
    own = lax.dynamic_slice_in_dim(small_out, y * 2 + core, 1, 1).reshape(256)
    return (
        activations,
        input_gradient,
        input_out,
        output_out,
        expand_out,
        contract_out,
        own[0:32].reshape(2, 2, 8),
        own[32:64].reshape(2, 2, 8),
        own[64:112].reshape(2, 3, 8),
        own[112:144].reshape(2, 2, 8),
        own[144:208].reshape(2, 32),
    )


def solution(mesh):
    rows, columns = P(("seq", "ctx"), None), P(None, None, ("seq", "ctx", "tp"))
    weight, flat = P(None, ("seq", "ctx"), "tp"), P(None, ("seq", "ctx", "tp"))
    first = P(None, ("seq", "ctx"), None, "tp")
    outs = (rows, rows, first, weight, weight, weight, columns, columns, columns, columns, flat)
    return jax.shard_map(
        local,
        mesh=mesh,
        in_specs=(rows, rows, P("seq", "ctx"), *outs[2:]),
        out_specs=outs,
        check_vma=False,
    )
```

```python
import functools

import jax
import jax.numpy as jnp
from jax import lax
from jax.experimental import pallas as pl
from jax.experimental.pallas import tpu as pltpu
from jax.sharding import PartitionSpec as P

MESH = pl.DeviceIdType.MESH
F32, BF16 = jnp.float32, jnp.bfloat16
D, HEAD_DIM, ROT, LAYERS = 1024, 64, 16, 2
ROWS = 128
GROUP = 512
WIN, WOUT, WFF = 384, 128, 512
COLS = WIN + WOUT + 2 * WFF
PARAMS = 208
EPSILON = 1e-05
MASKED = -1e30
VMEM_LIMIT = 56 * 1024 * 1024


def place():
    ctx = lax.axis_index("ctx")
    chip = lax.div(ctx, 2)
    y = lax.axis_index("seq") * 2 + lax.axis_index("tp")
    return y, lax.div(chip, 4), lax.rem(chip, 4), lax.rem(ctx, 2)


def device(y, x, z, core):
    return (lax.div(y, 2), (x * 4 + z) * 2 + core, lax.rem(y, 2))


def ring(index, step):
    return lax.rem(index + step, 4)


def enter(partners):
    barrier = pltpu.get_barrier_semaphore()
    for partner in partners:
        pl.semaphore_signal(barrier, inc=1, device_id=partner, device_id_type=MESH)
    pl.semaphore_wait(barrier, len(partners))


def plane_partners(y, x, z, core):
    return [
        device(y, ring(x, dx), ring(z, dz), core)
        for dx in range(4)
        for dz in range(4)
        if dx or dz
    ]


def column_partners(y, x, z, core):
    return [
        device(ring(y, dy), x, z, lax.rem(core + dc, 2))
        for dy in range(4)
        for dc in range(2)
        if dy or dc
    ]


def remote(source, target, send, receive, partner):
    return pltpu.make_async_remote_copy(
        src_ref=source,
        dst_ref=target,
        send_sem=send,
        recv_sem=receive,
        device_id=partner,
        device_id_type=MESH,
    )


HBM = pl.BlockSpec(memory_space=pl.ANY)
VMEM = pl.BlockSpec(memory_space=pltpu.VMEM)
SMEM = pl.BlockSpec(memory_space=pltpu.SMEM)


def dma(*shape):
    return pltpu.SemaphoreType.DMA(shape)


def params(number):
    return pltpu.CompilerParams(
        collective_id=number, has_side_effects=True, vmem_limit_bytes=VMEM_LIMIT
    )


PEERS = ((0, 1), (1, 0), (1, 1))
STEPS = tuple((dx, dz) for dx in range(4) for dz in range(4) if dx or dz)


def peer_at(y, x, z, core, step):
    seq, tp = lax.div(y, 2), lax.rem(y, 2)
    seq_to, core_to = lax.rem(seq + step[0], 2), lax.rem(core + step[1], 2)
    return seq_to * 2 + core_to, device(seq_to * 2 + tp, x, z, core_to)


class Gather:
    def __init__(self, full, where, send, recv):
        y, x, z, core = where
        self.full, self.x, self.z, self.send, self.recv = full, x, z, send, recv
        self.near = {
            "x": (device(y, ring(x, 1), z, core), device(y, ring(x, 3), z, core)),
            "z": (device(y, x, ring(z, 1), core), device(y, x, ring(z, 3), core)),
        }
        self.held = [(), ()]
        self.started = []

    def go(self, source, slot, partner):
        copy = remote(source, source, self.send.at[slot], self.recv.at[slot], partner)
        copy.start()
        self.started.append(copy)
        return copy

    def begin(self):
        for half in range(2):
            up, down = self.near["xz"[half]]
            own = self.full.at[half, self.x, self.z]
            self.held[half] = (self.go(own, half * 8, up), self.go(own, half * 8 + 1, down))

    def arrive(self, half):
        for copy in self.held[half]:
            copy.wait_recv()

    def pass_on(self):
        x, z = self.x, self.z
        for half in range(2):
            self.arrive(half)
            up, down = self.near["xz"[half]]
            whole = self.full.at[half]
            if half == 0:
                before, after = whole.at[ring(x, 3), z], whole.at[ring(x, 1), z]
            else:
                before, after = whole.at[x, ring(z, 3)], whole.at[x, ring(z, 1)]
            self.held[half] = (
                self.go(before.at[pl.ds(0, 16)], half * 8 + 2, up),
                self.go(after.at[pl.ds(16, 16)], half * 8 + 3, down),
            )

    def turn(self):
        for half in range(2):
            self.arrive(half)
            up, down = self.near["zx"[half]]
            whole = self.full.at[half]
            line = whole.at[:, self.z] if half == 0 else whole.at[self.x]
            self.held[half] = (self.go(line, half * 8 + 4, up), self.go(line, half * 8 + 5, down))

    def pass_line(self):
        x, z = self.x, self.z
        two, more = pl.ds(0, 2), pl.ds(2, 2)
        for half in range(2):
            self.arrive(half)
            up, down = self.near["zx"[half]]
            whole = self.full.at[half]
            if half == 0:
                before, after = whole.at[two, ring(z, 3)], whole.at[more, ring(z, 1)]
            else:
                before, after = whole.at[ring(x, 3), two], whole.at[ring(x, 1), more]
            self.held[half] = (
                self.go(before, half * 8 + 6, up),
                self.go(after, half * 8 + 7, down),
            )

    def end(self):
        for half in range(2):
            self.arrive(half)

    def sent(self):
        for copy in self.started:
            copy.wait_send()


def start_exchange(where, source, target, shared, send, recv):
    y, x, z, core = where
    chip = x * 4 + z
    target[chip] = source[x if shared else chip]
    copies = []
    for k, (dx, dz) in enumerate(STEPS):
        to_x, to_z = ring(x, dx), ring(z, dz)
        copy = remote(
            source.at[to_x if shared else to_x * 4 + to_z],
            target.at[chip],
            send.at[k],
            recv.at[k],
            device(y, to_x, to_z, core),
        )
        copy.start()
        copies.append(copy)
    return copies


def loop(count, body):
    def step(index, carry):
        body(index)
        return carry

    lax.fori_loop(0, count, step, 0)


def rows_at(index, count):
    return pl.ds(pl.multiple_of(index * count, count), count)


def turned(values, tables, sign):
    one, right, left = tables
    half = ROT // 2
    return values * one + sign * (
        pltpu.roll(values, 128 - half, 1) * right + pltpu.roll(values, half, 1) * left
    )


def low_lanes(shape):
    return lax.broadcasted_iota(jnp.int32, shape, 1) < HEAD_DIM


def swap(values):
    return pltpu.roll(values, HEAD_DIM, 1)


def heads_to_chips(values, target):
    def body(index):
        seq, quarter = lax.div(index, 4), lax.rem(index, 4)
        first, second = values(seq, 0, quarter), values(seq, 1, quarter)
        low = low_lanes(first.shape)
        target[seq * 8 + quarter] = jnp.where(low, first, swap(second)).astype(BF16)
        target[seq * 8 + 4 + quarter] = jnp.where(low, swap(first), second).astype(BF16)

    loop(8, body)


def group_rows(seq, core, quarter):
    return pl.ds(pl.multiple_of(seq * 256 + core * 128 + quarter * 32, 32), 32)


def normalize_rows(hidden, normed, inverse):
    def body(index):
        rows = rows_at(index, 32)
        values = hidden(rows)
        centred = values - jnp.mean(values, axis=1, keepdims=True)
        spread = jnp.mean(centred * centred, axis=1, keepdims=True)
        scale = lax.rsqrt(spread + EPSILON)
        normed[rows, :] = centred * scale
        inverse[rows, :] = jnp.broadcast_to(scale, (32, 128))

    loop(16, body)


def scale_rows(normed, gain, shift, target):
    def body(index):
        rows = rows_at(index, 32)
        target[rows, :] = (normed[rows, :] * gain + shift).astype(BF16)

    loop(16, body)


def project(first, weight, bias, tables, pairs, q_rows):
    whole = weight[...].reshape(D, WIN)

    def body(index):
        rows = rows_at(index, 128)
        u = jnp.dot(first[rows, :], whole, preferred_element_type=F32)
        turn = tuple(t[rows, :] for t in tables)
        q_rows[rows, :] = turned(u[:, :128] + bias[0:1, :], turn, 1.0)
        keys = turned(u[:, 128:256] + bias[1:2, :], turn, 1.0)
        values = u[:, 256:] + bias[2:3, :]
        low = low_lanes(keys.shape)
        seq = lax.div(index, 2)
        part = rows_at(lax.rem(index, 2), 128)
        pairs[seq * 2, part, :] = jnp.where(low, keys, swap(values)).astype(BF16)
        pairs[seq * 2 + 1, part, :] = jnp.where(low, swap(keys), values).astype(BF16)

    loop(4, body)


def gelu_parts(inner):
    return 0.5 * (1.0 + lax.erf(inner * (0.5**0.5)))


def expand(second, weight, bias, inner, activated):
    whole = weight[:, :, :, :, WOUT : WOUT + WFF].reshape(D, WFF)

    def body(index):
        rows = rows_at(index, 128)
        e = jnp.dot(second[rows, :], whole, preferred_element_type=F32) + bias
        inner[rows, :] = e
        activated[rows, :] = (e * gelu_parts(e)).astype(BF16)

    loop(4, body)


def first_kernel(
    win_ref, wff_ref, tok_ref, cot_ref, par_ref, trig_ref, cosine_ref, sine_ref,
    in0, ff0, in1, ff1, tok, cot, vectors, ib_ref, eb_ref, one_ref, right_ref, left_ref,
    normed, inverse, first, second, kv_out, q_out, inner, activated,
    here, send_a, recv_a, send_t, recv_t, send_p, recv_p, send_v, recv_v, send_g, recv_g, send_x, recv_x,
    column_p, joined, plane_p, column_t, pairs, q_rows, q_parts,
):
    where = y, x, z, core = place()
    seq, tp = lax.div(y, 2), lax.rem(y, 2)
    mine, chip = seq * 2 + core, x * 4 + z
    column, plane = column_partners(y, x, z, core), plane_partners(y, x, z, core)
    enter(column + plane)

    quarter = pl.ds(pl.multiple_of(core * 16, 16), 16)
    peers = [peer_at(y, x, z, core, step) for step in PEERS]
    local_copies, arriving = [], []

    def share(slot, source, target):
        copies = [
            remote(source(theirs), target, send_a.at[slot, k], recv_a.at[slot, k], device_id)
            for k, (theirs, device_id) in enumerate(peers)
        ]
        own = pltpu.make_async_copy(source(mine), target, here.at[slot])
        for copy in (*copies, own):
            copy.start()
        local_copies.append(own)
        arriving.append(copies)

    def landed(slot):
        for copy in arriving[slot]:
            copy.wait_recv()
        local_copies[slot].wait()

    share(0, lambda q: win_ref.at[0, q], in0.at[seq, x, z, quarter])
    share(1, lambda q: tok_ref, tok.at[rows_at(mine, ROWS)])
    smalls = [
        remote(par_ref, column_p.at[y * 2 + core], send_p.at[k], recv_p.at[k], peer)
        for k, peer in enumerate(column)
    ]
    for copy in smalls:
        copy.start()
    share(2, lambda q: wff_ref.at[0, q], ff0.at[seq, x, z, quarter])
    share(3, lambda q: trig_ref, column_t.at[mine])
    share(4, lambda q: win_ref.at[1, q], in1.at[seq, x, z, quarter])
    share(5, lambda q: wff_ref.at[1, q], ff1.at[seq, x, z, quarter])
    share(6, lambda q: cot_ref, cot.at[rows_at(mine, ROWS)])
    column_p[y * 2 + core] = par_ref[...]

    gathers = [
        Gather(ref, where, send_g.at[k], recv_g.at[k]) for k, ref in enumerate((in0, ff0, in1, ff1))
    ]
    landed(0)
    gathers[0].begin()
    landed(1)
    for copy in smalls:
        copy.wait_recv()
    for half in range(2):
        joined[half] = jnp.sum(column_p[half * 4 : half * 4 + 4], axis=0)
    plane_p[chip] = joined[...]
    spread = [
        remote(joined, plane_p.at[chip], send_v.at[k], recv_v.at[k], peer)
        for k, peer in enumerate(plane)
    ]
    for copy in spread:
        copy.start()
    landed(2)
    gathers[1].begin()
    gathers[0].pass_on()

    normalize_rows(lambda rows: tok[rows, :].astype(F32), normed, inverse)
    gathers[0].turn()
    gathers[1].pass_on()
    landed(3)
    for r in range(4):
        rows = pl.ds(r * ROWS, ROWS)
        cos_a, sin_a = column_t[r, 0:1, :], column_t[r, 1:2, :]
        sine = sin_a * cosine_ref[...] + cos_a * sine_ref[...]
        lane = lax.broadcasted_iota(jnp.int32, sine.shape, 1) % HEAD_DIM
        one_ref[rows, :] = cos_a * cosine_ref[...] - sin_a * sine_ref[...]
        right_ref[rows, :] = jnp.where(lane < ROT // 2, -sine, 0.0)
        left_ref[rows, :] = jnp.where(lane < ROT // 2, 0.0, sine)
    for copy in spread:
        copy.wait_recv()
    for half in range(2):
        for across in range(4):
            at = (half * 4 + across) * 128
            block = jnp.sum(plane_p[across * 4 : across * 4 + 4, half], axis=0)
            vectors[:, at : at + 128] = block
    own = [plane_p[mine * 4 + k, tp] for k in range(4)]
    ib_ref[...] = (own[0] + own[1] + own[2] + own[3])[8:16]
    for k in range(4):
        eb_ref[:, k * 128 : (k + 1) * 128] = own[k][16:24]
    scale_rows(normed, vectors[0:1, :], vectors[4:5, :], first)
    gathers[0].pass_line()
    gathers[1].turn()
    scale_rows(normed, vectors[1:2, :], vectors[5:6, :], second)
    gathers[0].end()
    project(first, in0, ib_ref[0:3, :], (one_ref, right_ref, left_ref), pairs, q_rows)
    heads_to_chips(lambda s, c, k: q_rows[group_rows(s, c, k), :], q_parts)
    gathers[1].pass_line()
    exchanged = start_exchange(where, pairs, kv_out, True, send_x.at[0], recv_x.at[0])
    exchanged += start_exchange(where, q_parts, q_out, False, send_x.at[1], recv_x.at[1])
    landed(4)
    landed(5)
    gathers[2].begin()
    gathers[3].begin()
    gathers[1].end()
    gathers[2].pass_on()
    gathers[3].pass_on()
    expand(second, ff0, eb_ref[0:1, :], inner, activated)
    for one in gathers[2:]:
        one.turn()
    for one in gathers[2:]:
        one.pass_line()
    for one in gathers[2:]:
        one.end()
    landed(6)
    for copies in arriving:
        for copy in copies:
            copy.wait_send()
    for copy in smalls + spread:
        copy.wait_send()
    for one in gathers:
        one.sent()
    for copy in exchanged:
        copy.wait()


def first_part(*operands):
    def bf(*shape):
        return jax.ShapeDtypeStruct(shape, BF16)

    def f32(*shape):
        return jax.ShapeDtypeStruct(shape, F32)

    wide = WOUT + 2 * WFF
    outs = (
        bf(2, 4, 4, 32, WIN), bf(2, 4, 4, 32, wide), bf(2, 4, 4, 32, WIN), bf(2, 4, 4, 32, wide),
        bf(GROUP, D), bf(GROUP, D), f32(24, D), f32(8, 128), f32(8, WFF),
        f32(GROUP, 128), f32(GROUP, 128), f32(GROUP, 128),
        f32(GROUP, D), f32(GROUP, 128), bf(GROUP, D), bf(GROUP, D),
        bf(16, 256, 128), bf(16, 32, 128), f32(GROUP, WFF), bf(GROUP, WFF),
    )
    scratch = [
        dma(7), dma(7, 3), dma(7, 3), dma(1), dma(1), dma(7), dma(7), dma(15), dma(15),
        dma(4, 16), dma(4, 16), dma(2, 15), dma(2, 15),
        pltpu.VMEM((8, 24, 128), F32), pltpu.VMEM((2, 24, 128), F32),
        pltpu.VMEM((16, 2, 24, 128), F32), pltpu.VMEM((4, 8, 128), F32),
        pltpu.VMEM((4, 256, 128), BF16), pltpu.VMEM((GROUP, 128), F32),
        pltpu.VMEM((16, 32, 128), BF16),
    ]
    return pl.pallas_call(
        first_kernel,
        out_shape=outs,
        in_specs=[VMEM] * len(operands),
        out_specs=(VMEM,) * len(outs),
        scratch_shapes=scratch,
        compiler_params=params(0),
        name="first_part",
    )(*operands)


def exchange_kernel(count, shared, *refs):
    sources, targets = refs[:count], refs[count : 2 * count]
    here, send, receive = refs[2 * count :]
    y, x, z, core = place()
    chip = x * 4 + z
    partners = plane_partners(y, x, z, core)
    enter(partners)
    copies = []
    steps = [(dx, dz) for dx in range(4) for dz in range(4) if dx or dz]
    for number, (source, target) in enumerate(zip(sources, targets)):
        own = pltpu.make_async_copy(
            source.at[x if shared[number] else chip], target.at[chip], here.at[number]
        )
        own.start()
        copies.append(own)
        for k, (dx, dz) in enumerate(steps):
            to_x, to_z = ring(x, dx), ring(z, dz)
            copy = remote(
                source.at[to_x if shared[number] else to_x * 4 + to_z],
                target.at[chip],
                send.at[number, k],
                receive.at[number, k],
                partners[k],
            )
            copy.start()
            copies.append(copy)
    for copy in copies:
        copy.wait()


def exchange(number, shared, *sources):
    count = len(sources)
    return pl.pallas_call(
        functools.partial(exchange_kernel, count, shared),
        out_shape=tuple(jax.ShapeDtypeStruct((16, *s.shape[1:]), s.dtype) for s in sources),
        in_specs=[HBM] * count,
        out_specs=[HBM] * count,
        scratch_shapes=[dma(count), dma(count, 15), dma(count, 15)],
        compiler_params=params(number),
        name="exchange",
    )(*sources)


def column_sum_kernel(
    everywhere, part_ref, out_ref, near, far, held, send1, recv1, send2, recv2, send3, recv3
):
    y, x, z, core = place()
    seq, tp = lax.div(y, 2), lax.rem(y, 2)
    other = lax.rem(core + 1, 2)
    sibling = device(y, x, z, other)
    partners = [device(ring(y, dy), x, z, core) for dy in (1, 2, 3)]
    enter([sibling, *partners])
    order = (2, 1, 3)
    copies = []
    nears = {}
    for dy in (*order, 0):
        to = ring(y, dy)
        nears[dy] = remote(
            part_ref.at[lax.div(to, 2), other, lax.rem(to, 2)],
            near.at[dy],
            send1.at[dy],
            recv1.at[dy],
            sibling,
        )
        nears[dy].start()
    fars = []
    for dy in order:
        to = ring(y, dy)
        nears[dy].wait_recv()
        held[dy - 1] = (
            part_ref[lax.div(to, 2), core, lax.rem(to, 2)].astype(F32) + near[dy].astype(F32)
        ).astype(BF16)
        copy = remote(
            held.at[dy - 1], far.at[dy - 1], send2.at[dy - 1], recv2.at[dy - 1], partners[dy - 1]
        )
        copy.start()
        fars.append(copy)
    nears[0].wait_recv()
    total = part_ref[seq, core, tp].astype(F32) + near[0].astype(F32)
    for copy in fars:
        copy.wait_recv()
    total = total + far[0].astype(F32) + far[1].astype(F32) + far[2].astype(F32)
    if everywhere:
        own = out_ref.at[seq, core, tp]
        out_ref[seq, core, tp] = total.astype(BF16)
        outs = []
        for dy in order:
            copy = remote(own, own, send3.at[dy - 1], recv3.at[dy - 1], partners[dy - 1])
            copy.start()
            outs.append(copy)
        copy = remote(own, own, send3.at[3], recv3.at[3], sibling)
        copy.start()
        copies.append(copy)
        for at, dy in enumerate(order):
            outs[at].wait_recv()
            source = ring(y, 4 - dy)
            block = out_ref.at[lax.div(source, 2), core, lax.rem(source, 2)]
            copy = remote(block, block, send3.at[3 + dy], recv3.at[3 + dy], sibling)
            copy.start()
            copies.append(copy)
        for copy in outs:
            copy.wait_send()
    else:
        out_ref[tp] = total.astype(BF16)
        own = out_ref.at[tp]
        copy = remote(
            own, own, send3.at[0], recv3.at[0], device(seq * 2 + lax.rem(tp + 1, 2), x, z, core)
        )
        copy.start()
        copies.append(copy)
    for copy in copies:
        copy.wait()
    for copy in [*nears.values(), *fars]:
        copy.wait_send()


def column_sum(number, part, everywhere):
    shape = (2, 2, 2, 64, D) if everywhere else (2, 64, D)
    out = pl.pallas_call(
        functools.partial(column_sum_kernel, everywhere),
        out_shape=jax.ShapeDtypeStruct(shape, BF16),
        in_specs=[VMEM],
        out_specs=VMEM,
        scratch_shapes=[
            pltpu.VMEM((4, 64, D), BF16),
            pltpu.VMEM((3, 64, D), BF16),
            pltpu.VMEM((3, 64, D), BF16),
            dma(4), dma(4), dma(3), dma(3), dma(7), dma(7),
        ],
        compiler_params=params(number),
        name="column_sum",
    )(part.reshape(2, 2, 2, 64, D))
    return out.reshape(-1, D)


def scatter_kernel(with_small, *refs):
    if with_small:
        dw_ref, small_ref, out_ref, small_out, *refs = refs
    else:
        dw_ref, out_ref, *refs = refs
    (opp1, dir1, comb1, mid, opp2, dir2, comb2, sent1, sent2, done, send, recv, here, send_f, recv_f,
     *small_scratch) = refs
    y, x, z, core = place()
    seq, tp = lax.div(y, 2), lax.rem(y, 2)
    mine = seq * 2 + core
    neighbours = {
        "x": (device(y, ring(x, 1), z, core), device(y, ring(x, 3), z, core)),
        "z": (device(y, x, ring(z, 1), core), device(y, x, ring(z, 3), core)),
    }
    column = column_partners(y, x, z, core)
    if with_small:
        plane = plane_partners(y, x, z, core)
        enter(column + plane)
    else:
        peers_now = []
        for dh, dc in ((0, 1), (1, 0), (1, 1)):
            peers_now.append(
                device(lax.rem(seq + dh, 2) * 2 + tp, x, z, lax.rem(core + dc, 2))
            )
        enter(peers_now + [*neighbours["x"], *neighbours["z"]])

    started = []

    def go(source, target, slot, partner):
        copy = remote(source, target, send.at[slot], recv.at[slot], partner)
        copy.start()
        started.append(copy)
        return copy

    two = (pl.ds(0, 2), pl.ds(2, 2))
    rows = (pl.ds(0, 16), pl.ds(16, 16))

    def part1(half, step, side):
        whole = dw_ref.at[half]
        if half == 0:
            return whole.at[two[side], ring(z, step)]
        return whole.at[ring(x, step), two[side]]

    def part2(half, step, side):
        at = ring(x, step) if half == 0 else ring(z, step)
        return mid.at[half, at].at[rows[side]]

    def begin(half, part, axis, opposite, direct, base):
        up, down = neighbours[axis]
        return (
            go(part(half, 2, 0), opposite.at[half, 0], base, up),
            go(part(half, 2, 1), opposite.at[half, 1], base + 1, down),
            go(part(half, 1, 1), direct.at[half, 0], base + 2, up),
            go(part(half, 3, 0), direct.at[half, 1], base + 3, down),
        )

    def onward(half, part, axis, opposite, combined, sent, base, copies):
        up, down = neighbours[axis]
        copies[0].wait_recv()
        sent[half, 0] = (
            part(half, 1, 0)[...].astype(F32) + opposite[half, 0].astype(F32)
        ).astype(BF16)
        first = go(sent.at[half, 0], combined.at[half, 0], base + 4, up)
        copies[1].wait_recv()
        sent[half, 1] = (
            part(half, 3, 1)[...].astype(F32) + opposite[half, 1].astype(F32)
        ).astype(BF16)
        return (*copies[2:], first, go(sent.at[half, 1], combined.at[half, 1], base + 5, down))

    def finish(half, part, direct, combined, copies):
        for copy in copies:
            copy.wait_recv()
        low = (
            part(half, 0, 0)[...].astype(F32)
            + combined[half, 0].astype(F32)
            + direct[half, 1].astype(F32)
        )
        high = (
            part(half, 0, 1)[...].astype(F32)
            + combined[half, 1].astype(F32)
            + direct[half, 0].astype(F32)
        )
        return low, high

    held = [None, None]
    for half in range(2):
        held[half] = begin(half, part1, "zx"[half], opp1, dir1, half * 12)
    if with_small:
        gathered, total, sent_s, recv_s, sent_t, recv_t, others = small_scratch
        chip = x * 4 + z
        steps = [(dx, dz) for dx in range(4) for dz in range(4) if dx or dz]
        spread = []
        for k, (dx, dz) in enumerate(steps):
            copy = remote(
                small_ref.at[ring(x, dx) * 4 + ring(z, dz)],
                gathered.at[k],
                sent_s.at[k],
                recv_s.at[k],
                plane[k],
            )
            copy.start()
            spread.append(copy)
    for half in range(2):
        held[half] = onward(half, part1, "zx"[half], opp1, comb1, sent1, half * 12, held[half])
    for half in range(2):
        low, high = finish(half, part1, dir1, comb1, held[half])
        mid[half, 0:2] = low.astype(BF16)
        mid[half, 2:4] = high.astype(BF16)
        held[half] = begin(half, part2, "xz"[half], opp2, dir2, half * 12 + 6)
    if with_small:
        for copy in spread:
            copy.wait_recv()
        total[...] = small_ref[chip] + jnp.sum(gathered[...], axis=0)
        shared = []
        for k, peer in enumerate(column):
            copy = remote(total, others.at[k], sent_t.at[k], recv_t.at[k], peer)
            copy.start()
            shared.append(copy)
    for half in range(2):
        held[half] = onward(half, part2, "xz"[half], opp2, comb2, sent2, half * 12 + 6, held[half])
    for half in range(2):
        low, high = finish(half, part2, dir2, comb2, held[half])
        done[half, 0] = low.astype(BF16)
        done[half, 1] = high.astype(BF16)
    own = pltpu.make_async_copy(done.at[seq, core], out_ref.at[mine], here)
    own.start()
    final = []
    for k, (dh, dc) in enumerate(((0, 1), (1, 0), (1, 1))):
        seq_to, core_to = lax.rem(seq + dh, 2), lax.rem(core + dc, 2)
        copy = remote(
            done.at[seq_to, core_to],
            out_ref.at[mine],
            send_f.at[k],
            recv_f.at[k],
            device(seq_to * 2 + tp, x, z, core_to),
        )
        copy.start()
        final.append(copy)
    if with_small:
        for copy in shared:
            copy.wait_recv()
        small_out[...] = total[...] + jnp.sum(others[...], axis=0)
        for copy in spread + shared:
            copy.wait_send()
    own.wait()
    for copy in final:
        copy.wait()
    for copy in started:
        copy.wait_send()


def scatter(number, grads, small=None):
    out = [jax.ShapeDtypeStruct((4, 16, COLS), BF16)]
    halves1 = pltpu.VMEM((2, 2, 2, 32, COLS), BF16)
    halves2 = pltpu.VMEM((2, 2, 16, COLS), BF16)
    scratch = [
        halves1, halves1, halves1, pltpu.VMEM((2, 4, 32, COLS), BF16),
        halves2, halves2, halves2, halves1, halves2, halves2,
        dma(24), dma(24), pltpu.SemaphoreType.DMA, dma(3), dma(3),
    ]
    args = [grads.reshape(2, 4, 4, 32, COLS)]
    if small is not None:
        args.append(small)
        out.append(jax.ShapeDtypeStruct((2, 8, 128), F32))
        scratch += [
            pltpu.VMEM((15, 2, 8, 128), F32), pltpu.VMEM((2, 8, 128), F32),
            dma(15), dma(15), dma(7), dma(7), pltpu.VMEM((7, 2, 8, 128), F32),
        ]
    return pl.pallas_call(
        functools.partial(scatter_kernel, small is not None),
        out_shape=tuple(out),
        in_specs=[VMEM] * len(args),
        out_specs=tuple([VMEM] * len(out)),
        scratch_shapes=scratch,
        compiler_params=params(number),
        name="scatter",
    )(*args)


TILE = 256
SPAN = 1024


def seen(quarter, tile):
    key = lax.broadcasted_iota(jnp.int32, (SPAN, TILE), 0)
    row = lax.broadcasted_iota(jnp.int32, (SPAN, TILE), 1)
    place_of = (row // 32) * ROWS + quarter * 32 + row % 32
    return key <= place_of


def attend_kernel(rank_ref, kv_ref, q_ref, m_ref, kvs_ref, kvt_ref, qs_ref, o_ref, lse_ref, score, rows):
    quarter = rank_ref[32]
    lane = lax.broadcasted_iota(jnp.int32, (32, 128), 1)

    def arrange(chip, carry):
        block = q_ref[chip].astype(F32) * (HEAD_DIM**-0.5)
        for core in range(2):
            rank = rank_ref[chip * 2 + core]
            keyed = kv_ref[chip * 2 + core]
            kvs_ref[pl.ds(pl.multiple_of(rank * ROWS, ROWS), ROWS), :] = keyed
            kvt_ref[rank] = keyed.astype(F32).T.astype(BF16)
            part = block if core == 0 else pltpu.roll(block, 64, 1)
            qs_ref[pl.ds(pl.multiple_of(rank * 32, 32), 32), :] = jnp.where(
                lane < 64, part, 0.0
            ).astype(BF16)
        return carry

    lax.fori_loop(0, 16, arrange, 0)

    for tile in range(4):
        queries = qs_ref[tile * TILE : (tile + 1) * TILE, :]
        highest = jnp.full((1, TILE), MASKED, F32)
        for span in range(tile + 1):
            block = lax.dot_general(
                kvs_ref[span * SPAN : (span + 1) * SPAN, :],
                queries,
                (((1,), (1,)), ((), ())),
                preferred_element_type=F32,
            )
            if span == tile:
                block = jnp.where(seen(quarter, tile), block, MASKED)
            score[span * SPAN : (span + 1) * SPAN, :] = block
            highest = jnp.maximum(highest, jnp.max(block, axis=0, keepdims=True))
        total = jnp.zeros((1, TILE), F32)
        mixed = jnp.zeros((128, TILE), F32)
        for span in range(tile + 1):
            weight = jnp.exp(score[span * SPAN : (span + 1) * SPAN, :] - highest)
            total = total + jnp.sum(weight, axis=0, keepdims=True)
            low = weight.astype(BF16)
            for part in range(8):
                mixed = mixed + jnp.dot(
                    kvt_ref[span * 8 + part],
                    low[part * ROWS : (part + 1) * ROWS],
                    preferred_element_type=F32,
                )
        mixed = mixed / total
        lse_ref[tile] = jnp.broadcast_to(highest + jnp.log(total), (8, TILE))
        o_ref[tile] = mixed
        rows[tile * TILE : (tile + 1) * TILE, :] = mixed.T

    def put_back(chip, carry):
        first = rows[pl.ds(pl.multiple_of(rank_ref[chip * 2] * 32, 32), 32), :]
        second = rows[pl.ds(pl.multiple_of(rank_ref[chip * 2 + 1] * 32, 32), 32), :]
        m_ref[chip] = jnp.where(lane < 64, pltpu.roll(first, 64, 1), second).astype(BF16)
        return carry

    lax.fori_loop(0, 16, put_back, 0)


def attend(rank, kv, q):
    return pl.pallas_call(
        attend_kernel,
        out_shape=(
            jax.ShapeDtypeStruct((16, 32, 128), BF16),
            jax.ShapeDtypeStruct((4096, 128), BF16),
            jax.ShapeDtypeStruct((32, 128, 128), BF16),
            jax.ShapeDtypeStruct((1024, 128), BF16),
            jax.ShapeDtypeStruct((4, 128, TILE), F32),
            jax.ShapeDtypeStruct((4, 8, TILE), F32),
        ),
        in_specs=[SMEM, VMEM, VMEM],
        out_specs=tuple([VMEM] * 6),
        scratch_shapes=[pltpu.VMEM((4096, TILE), F32), pltpu.VMEM((1024, 128), F32)],
        compiler_params=pltpu.CompilerParams(vmem_limit_bytes=VMEM_LIMIT),
        name="attend",
    )(rank, kv, q)


def attend_back_kernel(
    rank_ref, kvs_ref, kvt_ref, qs_ref, o_ref, lse_ref, dm_ref, dkv_ref, dq_ref, dos, acc, dqs
):
    quarter = rank_ref[32]
    lane = lax.broadcasted_iota(jnp.int32, (32, 128), 1)

    def arrange(chip, carry):
        block = dm_ref[chip].astype(F32)
        for core in range(2):
            rank = rank_ref[chip * 2 + core]
            part = pltpu.roll(block, 64, 1) if core == 0 else block
            dos[pl.ds(pl.multiple_of(rank * 32, 32), 32), :] = jnp.where(
                lane < 64, 0.0, part
            ).astype(BF16)
        return carry

    lax.fori_loop(0, 16, arrange, 0)

    for tile in range(4):
        queries = qs_ref[tile * TILE : (tile + 1) * TILE, :]
        outs = dos[tile * TILE : (tile + 1) * TILE, :]
        delta = jnp.sum(outs.astype(F32).T * o_ref[tile], axis=0, keepdims=True)
        lse = lse_ref[tile][0:1, :]
        query_grad = jnp.zeros((128, TILE), F32)
        for span in range(tile + 1):
            keyed = kvs_ref[span * SPAN : (span + 1) * SPAN, :]
            block = lax.dot_general(
                keyed, queries, (((1,), (1,)), ((), ())), preferred_element_type=F32
            )
            if span == tile:
                block = jnp.where(seen(quarter, tile), block, MASKED)
            probs = jnp.exp(block - lse)
            back = lax.dot_general(
                keyed, outs, (((1,), (1,)), ((), ())), preferred_element_type=F32
            )
            score_grad = (probs * (back - delta)).astype(BF16)
            pair = jnp.dot(score_grad, queries, preferred_element_type=F32) + jnp.dot(
                probs.astype(BF16), outs, preferred_element_type=F32
            )
            if span == tile:
                acc[span * SPAN : (span + 1) * SPAN, :] = pair
            else:
                acc[span * SPAN : (span + 1) * SPAN, :] += pair
            for part in range(8):
                query_grad = query_grad + jnp.dot(
                    kvt_ref[span * 8 + part],
                    score_grad[part * ROWS : (part + 1) * ROWS],
                    preferred_element_type=F32,
                )
        dqs[tile * TILE : (tile + 1) * TILE, :] = query_grad.T * (HEAD_DIM**-0.5)

    def put_back(chip, carry):
        first = dqs[pl.ds(pl.multiple_of(rank_ref[chip * 2] * 32, 32), 32), :]
        second = dqs[pl.ds(pl.multiple_of(rank_ref[chip * 2 + 1] * 32, 32), 32), :]
        dq_ref[chip] = jnp.where(lane < 64, first, pltpu.roll(second, 64, 1)).astype(BF16)
        for core in range(2):
            rank = rank_ref[chip * 2 + core]
            dkv_ref[chip, core] = acc[
                pl.ds(pl.multiple_of(rank * ROWS, ROWS), ROWS), :
            ].astype(BF16)
        return carry

    lax.fori_loop(0, 16, put_back, 0)


def attend_back(rank, kvs, kvt, qs, o, lse, dm):
    return pl.pallas_call(
        attend_back_kernel,
        out_shape=(
            jax.ShapeDtypeStruct((16, 2, 128, 128), BF16),
            jax.ShapeDtypeStruct((16, 32, 128), BF16),
        ),
        in_specs=[SMEM] + [VMEM] * 6,
        out_specs=tuple([VMEM] * 2),
        scratch_shapes=[
            pltpu.VMEM((1024, 128), BF16),
            pltpu.VMEM((4096, 128), F32),
            pltpu.VMEM((1024, 128), F32),
        ],
        compiler_params=pltpu.CompilerParams(vmem_limit_bytes=VMEM_LIMIT),
        name="attend_back",
    )(rank, kvs, kvt, qs, o, lse, dm)


def pack_rows(values):
    parts = values.reshape(2, 2, 4, 32, 2, HEAD_DIM)
    return parts.transpose(0, 4, 2, 3, 1, 5).reshape(16, 32, 128)


def unpack_rows(parts):
    values = parts.reshape(2, 2, 4, 32, 2, HEAD_DIM)
    return values.transpose(0, 4, 2, 3, 1, 5).reshape(GROUP, 128)


def pack_pairs(keys, values):
    pairs = jnp.concatenate(
        [keys.reshape(2, 256, 2, HEAD_DIM), values.reshape(2, 256, 2, HEAD_DIM)], axis=3
    )
    return pairs.transpose(0, 2, 1, 3).reshape(4, 256, 128)


def unpack_pairs(pairs):
    values = jnp.sum(pairs.reshape(2, 2, 4, 256, 128).astype(F32), axis=2)
    values = values.transpose(0, 2, 1, 3).reshape(GROUP, 2, 128)
    return (
        values[:, :, :HEAD_DIM].reshape(GROUP, 128),
        values[:, :, HEAD_DIM:].reshape(GROUP, 128),
    )


def rotary_parts(rank):
    half = ROT // 2
    freqs = 10000.0 ** (-(jnp.arange(half, dtype=F32) * 2.0 / ROT))
    lane = jnp.arange(128) % HEAD_DIM
    every = jnp.where(lane < ROT, jnp.tile(freqs, 128 // half), 0.0)[None, :]
    start = rank * ROWS * every
    steps = jnp.arange(ROWS, dtype=F32)[:, None] * every
    trig = jnp.concatenate([jnp.cos(start), jnp.sin(start), jnp.zeros((6, 128), F32)], axis=0)
    return trig, jnp.cos(steps), jnp.sin(steps)


def rotate(values, tables, sign):
    one, right, left = tables
    half = ROT // 2
    return (
        values * one
        + sign * jnp.roll(values, -half, axis=1) * right
        + sign * jnp.roll(values, half, axis=1) * left
    )


def normalize(values):
    centre = jnp.mean(values, axis=-1, keepdims=True)
    centred = values - centre
    spread = jnp.mean(centred * centred, axis=-1, keepdims=True)
    inverse = lax.rsqrt(spread + EPSILON)
    return centred * inverse, inverse


def matmul(left, right, dims):
    return lax.dot_general(left, right, (dims, ((), ())), preferred_element_type=F32)


def local(
    tokens, cotangent, group_order, input_weight, output_weight, expand_weight, contract_weight,
    norm_gain, norm_shift, input_bias, output_bias, expand_bias,
):
    y, x, z, core = place()
    seq, tp = lax.div(y, 2), lax.rem(y, 2)
    chip = x * 4 + z
    mine = seq * 2 + core

    def quarters(weight, width):
        shaped = weight.reshape(LAYERS, 16, -1, 4, width).transpose(0, 3, 1, 2, 4)
        return shaped.reshape(LAYERS, 4, 16, -1)

    win = quarters(input_weight, 128)
    wff = jnp.concatenate(
        [quarters(output_weight, 128), quarters(expand_weight, 512), quarters(contract_weight, 512)],
        axis=3,
    )
    lane = jnp.arange(128)[None, :]
    at = lax.rem(chip, 4) * 4 + core * 2 + tp

    def placed(values, width, place_of):
        values = values.reshape(-1, width)
        return jnp.where(lane // width == place_of, jnp.tile(values, (1, 128 // width)), 0.0)

    rank = group_order.reshape(1, 1).astype(F32)
    par = jnp.concatenate(
        [
            placed(norm_gain, 8, at),
            placed(norm_shift, 8, at),
            placed(input_bias, 8, at),
            jnp.where((lane == at * 8) & (tp == 0), rank, 0.0),
            jnp.zeros((1, 128), F32),
            placed(expand_bias, 32, core * 2 + tp),
            placed(output_bias, 8, at),
            jnp.zeros((2, 128), F32),
        ],
        axis=0,
    )
    trig, cosine, sine = rotary_parts(rank)
    (in0, ff0, in1, ff1, token_rows, grad_rows, vectors, ib, eb, one, right, left,
     normed0, inverse0, first0, second0, kv_parts0, q_parts0, inner0, activated0) = first_part(
        win, wff, tokens, cotangent, par, trig, cosine, sine
    )
    weights = []
    for full_in, full_ff in ((in0, ff0), (in1, ff1)):
        flat = full_ff.reshape(D, WOUT + 2 * WFF)
        weights.append(
            (full_in.reshape(D, WIN), flat[:, :WOUT], flat[:, WOUT : WOUT + WFF], flat[:, WOUT + WFF :])
        )
    gains, shifts = vectors[0:4].reshape(2, 2, D), vectors[4:8].reshape(2, 2, D)
    output_shifts = vectors[18:22].reshape(2, 2, D)
    ranks = vectors[14].reshape(2, 32, 16)[:, :, 0].astype(jnp.int32)
    input_at = tp * 512 + mine * 128
    expand_at = tp * 2048 + mine * 512
    tables = (one, right, left)
    task = jnp.concatenate(
        [lax.dynamic_slice_in_dim(ranks, lax.div(x, 2), 1, 0).reshape(32), z.reshape(1)]
    )

    hidden = token_rows.astype(F32)
    saved = []
    activations = None
    for layer in range(LAYERS):
        input_full, output_full, expand_full, contract_full = weights[layer]
        if layer:
            normed, inverse = normalize(hidden)
            first_in = (normed * gains[layer, 0] + shifts[layer, 0]).astype(BF16)
            second_in = (normed * gains[layer, 1] + shifts[layer, 1]).astype(BF16)
            projected = matmul(first_in, input_full, ((1,), (0,))) + ib[3:6].reshape(-1)
            queries = rotate(projected[:, :128], tables, 1.0).astype(BF16)
            keys = rotate(projected[:, 128:256], tables, 1.0).astype(BF16)
            values = projected[:, 256:].astype(BF16)
            kv_parts, q_parts = exchange(
                1, (True, False), pack_pairs(keys, values), pack_rows(queries)
            )
            inner = matmul(second_in, expand_full, ((1,), (0,))) + eb[layer]
            activated = jax.nn.gelu(inner, approximate=False).astype(BF16)
        else:
            normed, inverse, first_in, second_in = normed0, inverse0[:, :1], first0, second0
            kv_parts, q_parts, inner, activated = kv_parts0, q_parts0, inner0, activated0
        mixed_parts, kvs, kvt, qs, o, lse = attend(task, kv_parts.reshape(32, 128, 128), q_parts)
        (mixed_back,) = exchange(2, (False,), mixed_parts)
        mixed = unpack_rows(mixed_back)
        branch = matmul(mixed, output_full, ((1,), (1,))) + matmul(
            activated, contract_full, ((1,), (1,))
        )
        branch = branch.astype(BF16)
        shift = output_shifts[layer, 0] + output_shifts[layer, 1]
        if layer + 1 < LAYERS:
            hidden = hidden + column_sum(3, branch, True).astype(F32) + shift
        else:
            own = lax.dynamic_slice_in_dim(hidden, mine * ROWS, ROWS, 0)
            activations = (own + column_sum(4, branch, False).astype(F32) + shift).astype(BF16)
        saved.append(
            (normed, inverse, first_in, second_in, kvs, kvt, qs, o, lse, mixed, inner, activated)
        )

    grad = grad_rows.reshape(GROUP, D).astype(F32)
    gain_parts, shift_parts, input_shift_parts = [None] * 2, [None] * 2, [None] * 2
    output_shift_parts, expand_shift_parts = [None] * 2, [None] * 2
    weight_out = [None] * 2
    input_gradient = None
    small_out = None
    first_device = (y * 2 + core) == 0
    for layer in reversed(range(LAYERS)):
        input_full, output_full, expand_full, contract_full = weights[layer]
        normed, inverse, first_in, second_in, kvs, kvt, qs, o, lse, mixed, inner, activated = saved[
            layer
        ]
        grad_low = grad.astype(BF16)
        column = jnp.where(first_device, jnp.sum(grad, axis=0), 0.0)
        output_shift_parts[layer] = jnp.stack([column, column], axis=0)
        mixed_grad = matmul(grad_low, output_full, ((1,), (0,))).astype(BF16)
        (mixed_grad_parts,) = exchange(2, (False,), pack_rows(mixed_grad))
        pair_parts, query_parts = attend_back(task, kvs, kvt, qs, o, lse, mixed_grad_parts)
        pair_back, query_back = exchange(
            5, (False, False), pair_parts.reshape(16, 256, 128), query_parts
        )
        activated_grad = matmul(grad_low, contract_full, ((1,), (0,)))
        _, gelu_pull = jax.vjp(functools.partial(jax.nn.gelu, approximate=False), inner)
        inner_grad = gelu_pull(activated_grad)[0].astype(BF16)
        expand_shift_parts[layer] = jnp.sum(inner_grad.astype(F32), axis=0)
        second_grad = matmul(inner_grad, expand_full, ((1,), (1,)))
        key_grad, value_grad = unpack_pairs(pair_back)
        projected_grad = jnp.concatenate(
            [
                rotate(unpack_rows(query_back).astype(F32), tables, -1.0),
                rotate(key_grad, tables, -1.0),
                value_grad,
            ],
            axis=1,
        ).astype(BF16)
        input_shift_parts[layer] = jnp.sum(projected_grad.astype(F32), axis=0).reshape(3, 128)
        first_grad = matmul(projected_grad, input_full, ((1,), (1,)))
        gain_parts[layer] = jnp.stack(
            [jnp.sum(first_grad * normed, axis=0), jnp.sum(second_grad * normed, axis=0)], axis=0
        )
        shift_parts[layer] = jnp.stack(
            [jnp.sum(first_grad, axis=0), jnp.sum(second_grad, axis=0)], axis=0
        )
        scaled = (first_grad * gains[layer, 0] + second_grad * gains[layer, 1]).astype(BF16)
        if layer:
            scaled = column_sum(3, scaled, True).astype(F32)
        else:
            scaled = column_sum(4, scaled, False).astype(F32)
            normed = lax.dynamic_slice_in_dim(normed, mine * ROWS, ROWS, 0)
            inverse = lax.dynamic_slice_in_dim(inverse, mine * ROWS, ROWS, 0)
            grad = lax.dynamic_slice_in_dim(grad, mine * ROWS, ROWS, 0)
        first_mean = jnp.mean(scaled, axis=-1, keepdims=True)
        second_mean = jnp.mean(scaled * normed, axis=-1, keepdims=True)
        grad = grad + inverse * (scaled - first_mean - normed * second_mean)
        weight_grad = jnp.concatenate(
            [
                matmul(first_in, projected_grad, ((0,), (0,))).astype(BF16),
                matmul(grad_low, mixed, ((0,), (0,))).astype(BF16),
                matmul(second_in, inner_grad, ((0,), (0,))).astype(BF16),
                matmul(grad_low, activated, ((0,), (0,))).astype(BF16),
            ],
            axis=1,
        )
        if layer:
            (weight_out[layer],) = scatter(6, weight_grad)
        else:
            input_gradient = grad
            input_full_shift = lax.dynamic_update_slice_in_dim(
                jnp.zeros((2, 3, D), F32), jnp.stack(input_shift_parts, axis=0), input_at, 2
            )
            expand_full_shift = lax.dynamic_update_slice_in_dim(
                jnp.zeros((2, 4 * D), F32), jnp.stack(expand_shift_parts, axis=0), expand_at, 1
            )

            def owners(values, width):
                parts = values.reshape(-1, 128, width).transpose(1, 0, 2)
                return parts.reshape(128, -1)

            every = jnp.concatenate(
                [
                    owners(jnp.stack(gain_parts, axis=0), 8),
                    owners(jnp.stack(shift_parts, axis=0), 8),
                    owners(input_full_shift, 8),
                    owners(jnp.stack(output_shift_parts, axis=0), 8),
                    owners(expand_full_shift, 32),
                    jnp.zeros((128, 256 - PARAMS), F32),
                ],
                axis=1,
            )
            every = every.reshape(2, 16, 2, 2, 2, 128).transpose(1, 4, 0, 3, 2, 5)
            weight_out[layer], small_out = scatter(7, weight_grad, every.reshape(16, 2, 8, 128))

    def whole(layer_grads, first, width, count):
        parts = [
            g[:, :, first : first + width * count].astype(F32).reshape(4, 16, count, width)
            for g in layer_grads
        ]
        return jnp.stack(parts, axis=0).transpose(0, 2, 3, 1, 4)

    input_out = whole(weight_out, 0, 128, 3).reshape(2, 16, 3, 512)
    output_out = whole(weight_out, WIN, 128, 1).reshape(2, 16, 512)
    expand_out = whole(weight_out, WIN + WOUT, WFF, 1).reshape(2, 16, 2048)
    contract_out = whole(weight_out, WIN + WOUT + WFF, WFF, 1).reshape(2, 16, 2048)
    own = lax.dynamic_slice_in_dim(small_out, y * 2 + core, 1, 1).reshape(256)
    return (
        activations,
        input_gradient,
        input_out,
        output_out,
        expand_out,
        contract_out,
        own[0:32].reshape(2, 2, 8),
        own[32:64].reshape(2, 2, 8),
        own[64:112].reshape(2, 3, 8),
        own[112:144].reshape(2, 2, 8),
        own[144:208].reshape(2, 32),
    )


def solution(mesh):
    rows, columns = P(("seq", "ctx"), None), P(None, None, ("seq", "ctx", "tp"))
    weight, flat = P(None, ("seq", "ctx"), "tp"), P(None, ("seq", "ctx", "tp"))
    first = P(None, ("seq", "ctx"), None, "tp")
    outs = (rows, rows, first, weight, weight, weight, columns, columns, columns, columns, flat)
    return jax.shard_map(
        local,
        mesh=mesh,
        in_specs=(rows, rows, P("seq", "ctx"), *outs[2:]),
        out_specs=outs,
        check_vma=False,
    )
```

```python
import functools

import jax
import jax.numpy as jnp
from jax import lax
from jax.experimental import pallas as pl
from jax.experimental.pallas import tpu as pltpu
from jax.sharding import PartitionSpec as P

MESH = pl.DeviceIdType.MESH
F32, BF16 = jnp.float32, jnp.bfloat16
D, HEAD_DIM, ROT, LAYERS = 1024, 64, 16, 2
ROWS = 128
GROUP = 512
WIN, WOUT, WFF = 384, 128, 512
COLS = WIN + WOUT + 2 * WFF
PARAMS = 208
EPSILON = 1e-05
MASKED = -1e30
VMEM_LIMIT = 56 * 1024 * 1024


def place():
    ctx = lax.axis_index("ctx")
    chip = lax.div(ctx, 2)
    y = lax.axis_index("seq") * 2 + lax.axis_index("tp")
    return y, lax.div(chip, 4), lax.rem(chip, 4), lax.rem(ctx, 2)


def device(y, x, z, core):
    return (lax.div(y, 2), (x * 4 + z) * 2 + core, lax.rem(y, 2))


def ring(index, step):
    return lax.rem(index + step, 4)


def enter(partners):
    barrier = pltpu.get_barrier_semaphore()
    for partner in partners:
        pl.semaphore_signal(barrier, inc=1, device_id=partner, device_id_type=MESH)
    pl.semaphore_wait(barrier, len(partners))


def plane_partners(y, x, z, core):
    return [
        device(y, ring(x, dx), ring(z, dz), core)
        for dx in range(4)
        for dz in range(4)
        if dx or dz
    ]


def column_partners(y, x, z, core):
    return [
        device(ring(y, dy), x, z, lax.rem(core + dc, 2))
        for dy in range(4)
        for dc in range(2)
        if dy or dc
    ]


def remote(source, target, send, receive, partner):
    return pltpu.make_async_remote_copy(
        src_ref=source,
        dst_ref=target,
        send_sem=send,
        recv_sem=receive,
        device_id=partner,
        device_id_type=MESH,
    )


HBM = pl.BlockSpec(memory_space=pl.ANY)
VMEM = pl.BlockSpec(memory_space=pltpu.VMEM)
SMEM = pl.BlockSpec(memory_space=pltpu.SMEM)


def bf(*shape):
    return jax.ShapeDtypeStruct(shape, BF16)


def f32(*shape):
    return jax.ShapeDtypeStruct(shape, F32)


def vbf(*shape):
    return pltpu.VMEM(shape, BF16)


def vf32(*shape):
    return pltpu.VMEM(shape, F32)


def kernel(body, number, outs, scratch, name, *operands):
    return pl.pallas_call(
        body,
        out_shape=outs,
        in_specs=[VMEM] * len(operands),
        out_specs=(VMEM,) * len(outs),
        scratch_shapes=scratch,
        compiler_params=params(number),
        name=name,
    )(*operands)


def dma(*shape):
    return pltpu.SemaphoreType.DMA(shape)


def params(number):
    return pltpu.CompilerParams(
        collective_id=number, has_side_effects=True, vmem_limit_bytes=VMEM_LIMIT
    )


PEERS = ((0, 1), (1, 0), (1, 1))
STEPS = tuple((dx, dz) for dx in range(4) for dz in range(4) if dx or dz)


def peer_at(y, x, z, core, step):
    seq, tp = lax.div(y, 2), lax.rem(y, 2)
    seq_to, core_to = lax.rem(seq + step[0], 2), lax.rem(core + step[1], 2)
    return seq_to * 2 + core_to, device(seq_to * 2 + tp, x, z, core_to)


class Gather:
    def __init__(self, full, where, send, recv):
        y, x, z, core = where
        self.full, self.x, self.z, self.send, self.recv = full, x, z, send, recv
        self.near = {
            "x": (device(y, ring(x, 1), z, core), device(y, ring(x, 3), z, core)),
            "z": (device(y, x, ring(z, 1), core), device(y, x, ring(z, 3), core)),
        }
        self.held = [(), ()]
        self.started = []

    def go(self, source, slot, partner):
        copy = remote(source, source, self.send.at[slot], self.recv.at[slot], partner)
        copy.start()
        self.started.append(copy)
        return copy

    def begin(self):
        for half in range(2):
            up, down = self.near["xz"[half]]
            own = self.full.at[half, self.x, self.z]
            self.held[half] = (self.go(own, half * 8, up), self.go(own, half * 8 + 1, down))

    def arrive(self, half):
        for copy in self.held[half]:
            copy.wait_recv()

    def pass_on(self):
        x, z = self.x, self.z
        for half in range(2):
            self.arrive(half)
            up, down = self.near["xz"[half]]
            whole = self.full.at[half]
            if half == 0:
                before, after = whole.at[ring(x, 3), z], whole.at[ring(x, 1), z]
            else:
                before, after = whole.at[x, ring(z, 3)], whole.at[x, ring(z, 1)]
            self.held[half] = (
                self.go(before.at[pl.ds(0, 16)], half * 8 + 2, up),
                self.go(after.at[pl.ds(16, 16)], half * 8 + 3, down),
            )

    def turn(self):
        for half in range(2):
            self.arrive(half)
            up, down = self.near["zx"[half]]
            whole = self.full.at[half]
            line = whole.at[:, self.z] if half == 0 else whole.at[self.x]
            self.held[half] = (self.go(line, half * 8 + 4, up), self.go(line, half * 8 + 5, down))

    def pass_line(self):
        x, z = self.x, self.z
        two, more = pl.ds(0, 2), pl.ds(2, 2)
        for half in range(2):
            self.arrive(half)
            up, down = self.near["zx"[half]]
            whole = self.full.at[half]
            if half == 0:
                before, after = whole.at[two, ring(z, 3)], whole.at[more, ring(z, 1)]
            else:
                before, after = whole.at[ring(x, 3), two], whole.at[ring(x, 1), more]
            self.held[half] = (
                self.go(before, half * 8 + 6, up),
                self.go(after, half * 8 + 7, down),
            )

    def end(self):
        for half in range(2):
            self.arrive(half)

    def sent(self):
        for copy in self.started:
            copy.wait_send()


class RowShare:
    def __init__(self, source, target, where, send, recv):
        y, x, z, core = where
        self.source, self.target, self.send, self.recv = source, target, send, recv
        seq = lax.div(y, 2)
        self.own = rows_at(seq * 2 + core, ROWS)
        self.other = rows_at((1 - seq) * 2 + core, ROWS)
        self.sibling = device(y, x, z, lax.rem(core + 1, 2))
        self.facing = device(3 - y, x, z, core)
        self.copies = []

    def go(self, source, target, slot, partner):
        copy = remote(source, target, self.send.at[slot], self.recv.at[slot], partner)
        copy.start()
        self.copies.append(copy)

    def begin(self):
        self.target[self.own, :] = self.source[...]
        self.go(self.source, self.target.at[self.own], 0, self.facing)
        self.go(self.source, self.target.at[self.own], 1, self.sibling)

    def pass_on(self):
        self.copies[0].wait_recv()
        block = self.target.at[self.other]
        self.go(block, block, 2, self.sibling)

    def end(self):
        for copy in self.copies[1:]:
            copy.wait_recv()

    def sent(self):
        for copy in self.copies:
            copy.wait_send()


class ColumnSum:
    SCRATCH = [vbf(4, 64, D), vbf(3, 64, D), vbf(3, 64, D)] + [dma(4), dma(4), dma(3), dma(3), dma(7), dma(7)]
    ORDER = (2, 1, 3)

    def __init__(self, part, out, where, everywhere, scratch):
        self.part, self.out, self.where, self.everywhere = part, out, where, everywhere
        (self.near, self.far, self.held, self.send1, self.recv1, self.send2, self.recv2, self.send3, self.recv3) = scratch
        y, x, z, core = where
        self.sibling = device(y, x, z, lax.rem(core + 1, 2))
        self.chips = [device(ring(y, dy), x, z, core) for dy in (1, 2, 3)]

    def begin(self):
        y, x, z, core = self.where
        self.nears = {}
        for dy in (*self.ORDER, 0):
            to = ring(y, dy)
            source = self.part.at[lax.div(to, 2), lax.rem(core + 1, 2), lax.rem(to, 2)]
            self.nears[dy] = remote(
                source, self.near.at[dy], self.send1.at[dy], self.recv1.at[dy], self.sibling
            )
            self.nears[dy].start()

    def cross(self):
        y, x, z, core = self.where
        self.fars = []
        for dy in self.ORDER:
            to = ring(y, dy)
            self.nears[dy].wait_recv()
            own = self.part[lax.div(to, 2), core, lax.rem(to, 2)].astype(F32)
            self.held[dy - 1] = (own + self.near[dy].astype(F32)).astype(BF16)
            copy = remote(
                self.held.at[dy - 1],
                self.far.at[dy - 1],
                self.send2.at[dy - 1],
                self.recv2.at[dy - 1],
                self.chips[dy - 1],
            )
            copy.start()
            self.fars.append(copy)

    def combine(self):
        y, x, z, core = self.where
        seq, tp = lax.div(y, 2), lax.rem(y, 2)
        self.nears[0].wait_recv()
        total = self.part[seq, core, tp].astype(F32) + self.near[0].astype(F32)
        for copy in self.fars:
            copy.wait_recv()
        for k in range(3):
            total = total + self.far[k].astype(F32)
        self.outs, self.relayed = [], []
        own = self.out.at[seq, core, tp] if self.everywhere else self.out.at[tp]
        own[...] = total.astype(BF16)
        if self.everywhere:
            for dy in self.ORDER:
                self.go(self.outs, own, dy - 1, self.chips[dy - 1])
            self.go(self.relayed, own, 3, self.sibling)
        else:
            self.go(self.outs, own, 0, device(seq * 2 + lax.rem(tp + 1, 2), x, z, core))

    def go(self, kept, block, slot, partner):
        copy = remote(block, block, self.send3.at[slot], self.recv3.at[slot], partner)
        copy.start()
        kept.append(copy)

    def relay(self):
        y, x, z, core = self.where
        for at, dy in enumerate(self.ORDER):
            self.outs[at].wait_recv()
            source = ring(y, 4 - dy)
            block = self.out.at[lax.div(source, 2), core, lax.rem(source, 2)]
            self.go(self.relayed, block, 3 + dy, self.sibling)

    def end(self):
        if self.everywhere:
            for copy in self.relayed:
                copy.wait_recv()
        else:
            self.outs[0].wait_recv()

    def sent(self):
        for copy in (*self.nears.values(), *self.fars, *self.outs, *self.relayed):
            copy.wait_send()


class Scatter:
    def __init__(self, dw, out, where, scratch):
        y, x, z, core = where
        self.dw, self.out, self.where, self.x, self.z = dw, out, where, x, z
        (self.opp1, self.dir1, self.comb1, self.sent1, self.mid, self.opp2, self.dir2, self.comb2, self.sent2, self.done,
         self.send, self.recv, self.send_f, self.recv_f) = scratch
        self.near = {
            "x": (device(y, ring(x, 1), z, core), device(y, ring(x, 3), z, core)),
            "z": (device(y, x, ring(z, 1), core), device(y, x, ring(z, 3), core)),
        }
        self.started, self.held = [], [(), ()]

    @staticmethod
    def scratch(columns):
        big, small = vbf(2, 2, 2, 32, columns), vbf(2, 2, 16, columns)
        mid = vbf(2, 4, 32, columns)
        return [big] * 4 + [mid] + [small] * 5 + [dma(24), dma(24), dma(3), dma(3)]

    def go(self, source, target, slot, partner):
        copy = remote(source, target, self.send.at[slot], self.recv.at[slot], partner)
        copy.start()
        self.started.append(copy)
        return copy

    def part1(self, half, step, side):
        two = pl.ds(side * 2, 2)
        whole = self.dw.at[half]
        if half == 0:
            return whole.at[two, ring(self.z, step)]
        return whole.at[ring(self.x, step), two]

    def part2(self, half, step, side):
        at = ring(self.x, step) if half == 0 else ring(self.z, step)
        return self.mid.at[half, at].at[pl.ds(side * 16, 16)]

    def open(self, half, part, axis, opposite, direct, base):
        up, down = self.near[axis]
        self.held[half] = (
            self.go(part(half, 2, 0), opposite.at[half, 0], base, up),
            self.go(part(half, 2, 1), opposite.at[half, 1], base + 1, down),
            self.go(part(half, 1, 1), direct.at[half, 0], base + 2, up),
            self.go(part(half, 3, 0), direct.at[half, 1], base + 3, down),
        )

    def onward(self, half, part, axis, opposite, combined, sent, base):
        up, down = self.near[axis]
        copies = self.held[half]
        copies[0].wait_recv()
        sent[half, 0] = (part(half, 1, 0)[...].astype(F32) + opposite[half, 0].astype(F32)).astype(BF16)
        first = self.go(sent.at[half, 0], combined.at[half, 0], base + 4, up)
        copies[1].wait_recv()
        sent[half, 1] = (part(half, 3, 1)[...].astype(F32) + opposite[half, 1].astype(F32)).astype(BF16)
        second = self.go(sent.at[half, 1], combined.at[half, 1], base + 5, down)
        self.held[half] = (*copies[2:], first, second)

    def finish(self, half, part, direct, combined, target):
        for copy in self.held[half]:
            copy.wait_recv()
        for side in range(2):
            total = (
                part(half, 0, side)[...].astype(F32)
                + combined[half, side].astype(F32)
                + direct[half, 1 - side].astype(F32)
            )
            target(half, side)[...] = total.astype(BF16)

    def begin(self):
        for half in range(2):
            self.open(half, self.part1, "zx"[half], self.opp1, self.dir1, half * 12)

    def pass_on(self):
        for half in range(2):
            self.onward(half, self.part1, "zx"[half], self.opp1, self.comb1, self.sent1, half * 12)

    def turn(self):
        for half in range(2):
            self.finish(
                half,
                self.part1,
                self.dir1,
                self.comb1,
                lambda h, side: self.mid.at[h, pl.ds(side * 2, 2)],
            )
            self.open(half, self.part2, "xz"[half], self.opp2, self.dir2, half * 12 + 6)

    def pass_line(self):
        for half in range(2):
            self.onward(
                half, self.part2, "xz"[half], self.opp2, self.comb2, self.sent2, half * 12 + 6
            )

    def deliver(self):
        y, x, z, core = self.where
        seq = lax.div(y, 2)
        mine = seq * 2 + core
        for half in range(2):
            self.finish(
                half, self.part2, self.dir2, self.comb2, lambda h, side: self.done.at[h, side]
            )
        self.out[mine] = self.done[seq, core]
        self.final = []
        for k, step in enumerate(PEERS):
            theirs, peer = peer_at(y, x, z, core, step)
            copy = remote(
                self.done.at[lax.div(theirs, 2), lax.rem(theirs, 2)],
                self.out.at[mine],
                self.send_f.at[k],
                self.recv_f.at[k],
                peer,
            )
            copy.start()
            self.final.append(copy)

    def end(self):
        for copy in self.final:
            copy.wait()
        for copy in self.started:
            copy.wait_send()


def start_exchange(where, source, target, shared, send, recv):
    y, x, z, core = where
    chip = x * 4 + z
    target[chip] = source[x if shared else chip]
    copies = []
    for k, (dx, dz) in enumerate(STEPS):
        to_x, to_z = ring(x, dx), ring(z, dz)
        copy = remote(
            source.at[to_x if shared else to_x * 4 + to_z],
            target.at[chip],
            send.at[k],
            recv.at[k],
            device(y, to_x, to_z, core),
        )
        copy.start()
        copies.append(copy)
    return copies


def loop(count, body):
    def step(index, carry):
        body(index)
        return carry

    lax.fori_loop(0, count, step, 0)


def rows_at(index, count):
    return pl.ds(pl.multiple_of(index * count, count), count)


def turned(values, tables, sign):
    one, right, left = tables
    half = ROT // 2
    return values * one + sign * (
        pltpu.roll(values, 128 - half, 1) * right + pltpu.roll(values, half, 1) * left
    )


def low_lanes(shape):
    return lax.broadcasted_iota(jnp.int32, shape, 1) < HEAD_DIM


def swap(values):
    return pltpu.roll(values, HEAD_DIM, 1)


def heads_to_chips(values, target):
    def body(index):
        seq, quarter = lax.div(index, 4), lax.rem(index, 4)
        first, second = values(seq, 0, quarter), values(seq, 1, quarter)
        low = low_lanes(first.shape)
        target[seq * 8 + quarter] = jnp.where(low, first, swap(second)).astype(BF16)
        target[seq * 8 + 4 + quarter] = jnp.where(low, swap(first), second).astype(BF16)

    loop(8, body)


def group_rows(seq, core, quarter):
    return pl.ds(pl.multiple_of(seq * 256 + core * 128 + quarter * 32, 32), 32)


def normalize_rows(hidden, normed, inverse):
    def body(index):
        rows = rows_at(index, 32)
        values = hidden(index)
        centred = values - jnp.mean(values, axis=1, keepdims=True)
        spread = jnp.mean(centred * centred, axis=1, keepdims=True)
        scale = lax.rsqrt(spread + EPSILON)
        normed[rows, :] = centred * scale
        inverse[rows, :] = jnp.broadcast_to(scale, (32, 128))

    loop(16, body)


def scale_rows(normed, gain, shift, target):
    def body(index):
        rows = rows_at(index, 32)
        target[rows, :] = (normed[rows, :] * gain + shift).astype(BF16)

    loop(16, body)


def project(first, weight, bias, tables, pairs, q_rows):
    whole = weight[...].reshape(D, WIN)

    def body(index):
        rows = rows_at(index, 128)
        u = jnp.dot(first[rows, :], whole, preferred_element_type=F32)
        turn = tuple(t[rows, :] for t in tables)
        q_rows[rows, :] = turned(u[:, :128] + bias[0:1, :], turn, 1.0)
        keys = turned(u[:, 128:256] + bias[1:2, :], turn, 1.0)
        values = u[:, 256:] + bias[2:3, :]
        low = low_lanes(keys.shape)
        seq = lax.div(index, 2)
        part = rows_at(lax.rem(index, 2), 128)
        pairs[seq * 2, part, :] = jnp.where(low, keys, swap(values)).astype(BF16)
        pairs[seq * 2 + 1, part, :] = jnp.where(low, swap(keys), values).astype(BF16)

    loop(4, body)


def gelu_parts(inner):
    return 0.5 * (1.0 + lax.erf(inner * (0.5**0.5)))


def expand(second, weight, bias, inner, activated):
    whole = weight[:, :, :, :, WOUT : WOUT + WFF].reshape(D, WFF)

    def body(index):
        rows = rows_at(index, 128)
        e = jnp.dot(second[rows, :], whole, preferred_element_type=F32) + bias
        inner[rows, :] = e
        activated[rows, :] = (e * gelu_parts(e)).astype(BF16)

    loop(4, body)


def first_kernel(
    win_ref, wff_ref, tok_ref, par_ref, trig_ref, cosine_ref, sine_ref,
    in0, ff0, in1, ff1, tok, vectors, ib_ref, eb_ref, one_ref, right_ref, left_ref,
    normed, inverse, first, second, kv_out, q_out, inner, activated,
    here, send_a, recv_a, send_t, recv_t, send_p, recv_p, send_v, recv_v, send_g, recv_g, send_x, recv_x,
    column_p, joined, plane_p, column_t, pairs, q_rows, q_parts,
):
    where = y, x, z, core = place()
    seq, tp = lax.div(y, 2), lax.rem(y, 2)
    mine, chip = seq * 2 + core, x * 4 + z
    column, plane = column_partners(y, x, z, core), plane_partners(y, x, z, core)
    enter(column + plane)

    quarter = pl.ds(pl.multiple_of(core * 16, 16), 16)
    peers = [peer_at(y, x, z, core, step) for step in PEERS]
    local_copies, arriving = [], []

    def share(slot, source, target):
        copies = [
            remote(source(theirs), target, send_a.at[slot, k], recv_a.at[slot, k], device_id)
            for k, (theirs, device_id) in enumerate(peers)
        ]
        own = pltpu.make_async_copy(source(mine), target, here.at[slot])
        for copy in (*copies, own):
            copy.start()
        local_copies.append(own)
        arriving.append(copies)

    def landed(slot):
        for copy in arriving[slot]:
            copy.wait_recv()
        local_copies[slot].wait()

    tokens = RowShare(tok_ref, tok, where, send_t, recv_t)
    share(0, lambda q: win_ref.at[0, q], in0.at[seq, x, z, quarter])
    share(1, lambda q: wff_ref.at[0, q], ff0.at[seq, x, z, quarter])
    tokens.begin()
    smalls = [
        remote(par_ref, column_p.at[y * 2 + core], send_p.at[k], recv_p.at[k], peer)
        for k, peer in enumerate(column)
    ]
    for copy in smalls:
        copy.start()
    share(2, lambda q: trig_ref, column_t.at[mine])
    share(3, lambda q: win_ref.at[1, q], in1.at[seq, quarter])
    share(4, lambda q: wff_ref.at[1, q], ff1.at[seq, quarter])
    column_p[y * 2 + core] = par_ref[...]

    gathers = [
        Gather(ref, where, send_g.at[k], recv_g.at[k]) for k, ref in enumerate((in0, ff0))
    ]
    landed(0)
    gathers[0].begin()
    landed(1)
    gathers[1].begin()
    tokens.pass_on()
    for copy in smalls:
        copy.wait_recv()
    for half in range(2):
        joined[half] = jnp.sum(column_p[half * 4 : half * 4 + 4], axis=0)
    plane_p[chip] = joined[...]
    spread = [
        remote(joined, plane_p.at[chip], send_v.at[k], recv_v.at[k], peer)
        for k, peer in enumerate(plane)
    ]
    for copy in spread:
        copy.start()
    gathers[0].pass_on()
    tokens.end()
    normalize_rows(lambda index: tok[rows_at(index, 32), :].astype(F32), normed, inverse)
    gathers[0].turn()
    gathers[1].pass_on()
    landed(2)
    for r in range(4):
        rows = pl.ds(r * ROWS, ROWS)
        cos_a, sin_a = column_t[r, 0:1, :], column_t[r, 1:2, :]
        sine = sin_a * cosine_ref[...] + cos_a * sine_ref[...]
        lane = lax.broadcasted_iota(jnp.int32, sine.shape, 1) % HEAD_DIM
        one_ref[rows, :] = cos_a * cosine_ref[...] - sin_a * sine_ref[...]
        right_ref[rows, :] = jnp.where(lane < ROT // 2, -sine, 0.0)
        left_ref[rows, :] = jnp.where(lane < ROT // 2, 0.0, sine)
    for copy in spread:
        copy.wait_recv()
    for half in range(2):
        for across in range(4):
            at = (half * 4 + across) * 128
            block = jnp.sum(plane_p[across * 4 : across * 4 + 4, half], axis=0)
            vectors[:, at : at + 128] = block
    own = [plane_p[mine * 4 + k, tp] for k in range(4)]
    ib_ref[...] = (own[0] + own[1] + own[2] + own[3])[8:16]
    for k in range(4):
        eb_ref[:, k * 128 : (k + 1) * 128] = own[k][16:24]
    scale_rows(normed, vectors[0:1, :], vectors[4:5, :], first)
    gathers[0].pass_line()
    gathers[1].turn()
    scale_rows(normed, vectors[1:2, :], vectors[5:6, :], second)
    gathers[0].end()
    project(first, in0, ib_ref[0:3, :], (one_ref, right_ref, left_ref), pairs, q_rows)
    heads_to_chips(lambda s, c, k: q_rows[group_rows(s, c, k), :], q_parts)
    gathers[1].pass_line()
    exchanged = start_exchange(where, pairs, kv_out, True, send_x.at[0], recv_x.at[0])
    exchanged += start_exchange(where, q_parts, q_out, False, send_x.at[1], recv_x.at[1])
    gathers[1].end()
    expand(second, ff0, eb_ref[0:1, :], inner, activated)
    landed(3)
    landed(4)
    tokens.sent()
    for copies in arriving:
        for copy in copies:
            copy.wait_send()
    for copy in smalls + spread:
        copy.wait_send()
    for one in gathers:
        one.sent()
    for copy in exchanged:
        copy.wait()


def first_part(*operands):
    wide = WOUT + 2 * WFF
    outs = (
        bf(2, 4, 4, 32, WIN), bf(2, 4, 4, 32, wide), bf(2, 32, WIN), bf(2, 32, wide),
        bf(GROUP, D), f32(24, D), f32(8, 128), f32(8, WFF),
        f32(GROUP, 128), f32(GROUP, 128), f32(GROUP, 128),
        f32(GROUP, D), f32(GROUP, 128), bf(GROUP, D), bf(GROUP, D),
        bf(16, 256, 128), bf(16, 32, 128), f32(GROUP, WFF), bf(GROUP, WFF),
    )
    scratch = [
        dma(5), dma(5, 3), dma(5, 3), dma(3), dma(3), dma(7), dma(7), dma(15), dma(15),
        dma(2, 16), dma(2, 16), dma(2, 15), dma(2, 15),
        pltpu.VMEM((8, 24, 128), F32), pltpu.VMEM((2, 24, 128), F32),
        pltpu.VMEM((16, 2, 24, 128), F32), pltpu.VMEM((4, 8, 128), F32),
        pltpu.VMEM((4, 256, 128), BF16), pltpu.VMEM((GROUP, 128), F32),
        pltpu.VMEM((16, 32, 128), BF16),
    ]
    return kernel(first_kernel, 0, outs, scratch, "first_part", *operands)


def chips_to_heads(parts, target):
    def body(index):
        seq, quarter = lax.div(index, 4), lax.rem(index, 4)
        first = parts[seq * 8 + quarter].astype(F32)
        second = parts[seq * 8 + 4 + quarter].astype(F32)
        low = low_lanes(first.shape)
        target(seq, 0, quarter, jnp.where(low, first, swap(second)))
        target(seq, 1, quarter, jnp.where(low, swap(first), second))

    loop(8, body)


def block_of(index):
    return lax.div(index, 2), lax.rem(index, 2)


def contract(activated, ff, z):
    whole = ff[:, :, :, :, WOUT + WFF :].reshape(D, WFF)

    def body(index):
        rows = rows_at(index, 128)
        z[rows, :] = lax.dot_general(
            activated[rows, :], whole, (((1,), (1,)), ((), ())), preferred_element_type=F32
        )

    loop(4, body)


def add_mixed(mixed, weight, z, part):
    def body(index):
        rows = rows_at(index, 128)
        both = z[rows, :] + lax.dot_general(
            mixed[rows, :], weight, (((1,), (1,)), ((), ())), preferred_element_type=F32
        )
        seq, core = block_of(index)
        part[seq, core] = both.astype(BF16).reshape(2, 64, D)

    loop(4, body)


def rows32(summed, index):
    seq, core, tp = lax.div(index, 8), lax.rem(lax.div(index, 4), 2), lax.rem(lax.div(index, 2), 2)
    return summed[seq, core, tp, rows_at(lax.rem(index, 2), 32), :].astype(F32)


def output_weight_of(ff):
    return ff[:, :, :, :, :WOUT].reshape(D, WOUT)


def mix_back(dz, weight, rows128):
    def body(index):
        rows = rows_at(index, 128)
        dm = jnp.dot(dz(rows), weight, preferred_element_type=F32)
        rows128[rows, :] = dm.astype(BF16).astype(F32)

    loop(4, body)


def expand_back(dz, ff, inner, de, da, sums):
    up = ff[:, :, :, :, WOUT : WOUT + WFF].reshape(D, WFF)
    down = ff[:, :, :, :, WOUT + WFF :].reshape(D, WFF)
    sums[0:1, :] = jnp.zeros((1, WFF), F32)

    def body(index):
        rows = rows_at(index, 128)
        dg = jnp.dot(dz(rows), down, preferred_element_type=F32)
        e = inner[rows, :]
        slope = gelu_parts(e) + e * jnp.exp(-0.5 * e * e) * ((2.0 * jnp.pi) ** -0.5)
        low = (dg * slope).astype(BF16)
        de[rows, :] = low
        sums[0:1, :] += jnp.sum(low.astype(F32), axis=0, keepdims=True)
        da[rows, :] = lax.dot_general(
            low, up, (((1,), (1,)), ((), ())), preferred_element_type=F32
        )

    loop(4, body)


def weight_grad(left, right, dw, first, count):
    def body(index):
        block = lax.dot_general(
            left[:, rows_at(index, 256)],
            right[...],
            (((0,), (0,)), ((), ())),
            preferred_element_type=F32,
        )
        two = pl.ds(lax.rem(index, 2) * 2, 2)
        dw[lax.div(index, 2), two, :, :, first : first + count] = block.astype(BF16).reshape(
            2, 4, 32, count
        )

    loop(4, body)


def project_back(pairs, q_grad, tables, du, sums):
    sums[...] = jnp.zeros(sums.shape, F32)

    def body(index):
        seq, core = block_of(index)
        part = rows_at(core, 128)
        heads = []
        for head in range(2):
            total = pairs[seq * 8 + head * 4, part, :].astype(F32)
            for k in range(1, 4):
                total = total + pairs[seq * 8 + head * 4 + k, part, :].astype(F32)
            heads.append(total)
        low = low_lanes(heads[0].shape)
        rows = rows_at(index, 128)
        turn = tuple(t[rows, :] for t in tables)
        grads = (
            turned(q_grad[rows, :], turn, -1.0),
            turned(jnp.where(low, heads[0], swap(heads[1])), turn, -1.0),
            jnp.where(low, swap(heads[0]), heads[1]),
        )
        for k in range(3):
            rounded = grads[k].astype(BF16)
            du[rows, k * 128 : (k + 1) * 128] = rounded
            sums[k : k + 1, :] += jnp.sum(rounded.astype(F32), axis=0, keepdims=True)

    loop(4, body)


def join_back(du, weight, da2, normed, gain1, gain2, sums, part):
    whole = weight[...].reshape(D, WIN)
    sums[...] = jnp.zeros(sums.shape, F32)

    def body(index):
        rows = rows_at(index, 64)
        da = lax.dot_general(
            du[rows, :], whole, (((1,), (1,)), ((), ())), preferred_element_type=F32
        )
        db = da2[rows, :]
        n = normed[rows, :]
        for k, value in enumerate((da * n, db * n, da, db)):
            sums[k : k + 1, :] += jnp.sum(value, axis=0, keepdims=True)
        seq, core, tp = lax.div(index, 4), lax.rem(lax.div(index, 2), 2), lax.rem(index, 2)
        part[seq, core, tp] = (da * gain1 + db * gain2).astype(BF16)

    loop(8, body)


def norm_back(scaled, normed, inverse):
    first = jnp.mean(scaled, axis=1, keepdims=True)
    second = jnp.mean(scaled * normed, axis=1, keepdims=True)
    return inverse * (scaled - first - normed * second)


def second_kernel(
    m_ref, ff0, act0, tok, vectors, ib_ref, eb_ref, one_ref, right_ref, left_ref, in_own, ff_own, cot_ref,
    in1, ff1, cot, mixed, own_hidden, normed, inverse, first, second, kv_out, q_out, dm_out, inner, activated,
    m_back, z, part, summed, pairs, q_rows, q_parts, dm_rows, dm_parts,
    send_m, recv_m, send_g, recv_g, send_x, recv_x, send_c, recv_c, *column_scratch,
):
    where = y, x, z_at, core = place()
    seq = lax.div(y, 2)
    enter(column_partners(*where) + plane_partners(*where))
    returned = start_exchange(where, m_ref, m_back, False, send_m, recv_m)
    in1[0, x, z_at], in1[1, x, z_at] = in_own[0], in_own[1]
    ff1[0, x, z_at], ff1[1, x, z_at] = ff_own[0], ff_own[1]
    gathers = [Gather(ref, where, send_g.at[k], recv_g.at[k]) for k, ref in enumerate((in1, ff1))]
    gathers[0].begin()
    cots = RowShare(cot_ref, cot, where, send_c, recv_c)
    contract(act0, ff0, z)
    gathers[0].pass_on()
    gathers[1].begin()
    for copy in returned:
        copy.wait_recv()

    def keep(s, c, k, values):
        mixed[group_rows(s, c, k), :] = values.astype(BF16)

    chips_to_heads(m_back, keep)
    add_mixed(mixed, output_weight_of(ff0), z, part)
    total = ColumnSum(part, summed, where, True, column_scratch)
    total.begin()
    total.cross()
    gathers[0].turn()
    gathers[1].pass_on()
    total.combine()
    cots.begin()
    gathers[0].pass_line()
    gathers[1].turn()
    total.relay()
    cots.pass_on()
    gathers[0].end()
    gathers[1].pass_line()
    total.end()
    shift = vectors[18:19, :] + vectors[19:20, :]

    def hidden(index):
        rows = rows_at(index, 32)
        return tok[rows, :].astype(F32) + rows32(summed, index) + shift

    normalize_rows(hidden, normed, inverse)
    own = (seq * 2 + core) * 4

    def keep_own(index):
        own_hidden[rows_at(index, 32), :] = hidden(own + index)

    scale_rows(normed, vectors[2:3, :], vectors[6:7, :], first)
    project(first, in1, ib_ref[3:6, :], (one_ref, right_ref, left_ref), pairs, q_rows)
    heads_to_chips(lambda s, c, k: q_rows[group_rows(s, c, k), :], q_parts)
    exchanged = start_exchange(where, pairs, kv_out, True, send_x.at[0], recv_x.at[0])
    exchanged += start_exchange(where, q_parts, q_out, False, send_x.at[1], recv_x.at[1])
    cots.end()
    gathers[1].end()
    mix_back(lambda rows: cot[rows, :], output_weight_of(ff1), dm_rows)
    heads_to_chips(lambda s, c, k: dm_rows[group_rows(s, c, k), :], dm_parts)
    exchanged += start_exchange(where, dm_parts, dm_out, False, send_x.at[2], recv_x.at[2])
    loop(4, keep_own)
    scale_rows(normed, vectors[3:4, :], vectors[7:8, :], second)
    expand(second, ff1, eb_ref[1:2, :], inner, activated)
    total.sent()
    cots.sent()
    for copy in returned:
        copy.wait_send()
    for one in gathers:
        one.sent()
    for copy in exchanged:
        copy.wait()


def second_part(*operands):
    wide = WOUT + 2 * WFF
    outs = (
        bf(2, 4, 4, 32, WIN), bf(2, 4, 4, 32, wide), bf(GROUP, D), bf(GROUP, 128), f32(ROWS, D),
        f32(GROUP, D), f32(GROUP, 128), bf(GROUP, D), bf(GROUP, D),
        bf(16, 256, 128), bf(16, 32, 128), bf(16, 32, 128), f32(GROUP, WFF), bf(GROUP, WFF),
    )
    scratch = [
        vbf(16, 32, 128), vf32(GROUP, D), vbf(2, 2, 2, 64, D), vbf(2, 2, 2, 64, D),
        vbf(4, 256, 128), vf32(GROUP, 128), vbf(16, 32, 128), vf32(GROUP, 128), vbf(16, 32, 128),
        dma(15), dma(15), dma(2, 16), dma(2, 16), dma(3, 15), dma(3, 15), dma(3), dma(3),
        *ColumnSum.SCRATCH,
    ]
    return kernel(second_kernel, 1, outs, scratch, "second_part", *operands)


def third_kernel(
    m_ref, pair_ref, q_ref, cot, in1, ff1, wout0, vectors, one_ref, right_ref, left_ref,
    normed, inverse, first, second, inner, activated, own_hidden,
    act_out, grad, dm_out, out_in, out_ff, sums, ib_sums, eb_sums,
    m_back, pair_back, q_back, mixed, z, de, da2, du, q_grad, part, part2, summed, summed2,
    dw_in, dw_ff, dm_rows, dm_parts, dz,
    send_x, recv_x, *rest,
):
    where = y, x, z_at, core = place()
    tp = lax.rem(y, 2)
    enter(column_partners(*where) + plane_partners(*where))
    returned = [
        start_exchange(where, source, target, False, send_x.at[k], recv_x.at[k])
        for k, (source, target) in enumerate(((m_ref, m_back), (q_ref, q_back), (pair_ref, pair_back)))
    ]
    n_column = len(ColumnSum.SCRATCH)
    total1 = ColumnSum(part, summed, where, False, rest[:n_column])
    total2 = ColumnSum(part2, summed2, where, True, rest[n_column : 2 * n_column])
    rest = rest[2 * n_column :]
    scatter_ff = Scatter(dw_ff, out_ff, where, rest[: len(rest) // 2])
    scatter_in = Scatter(dw_in, out_in, where, rest[len(rest) // 2 :])

    expand_back(lambda rows: cot[rows, :], ff1, inner, de, da2, eb_sums)
    weight_grad(second, de, dw_ff, WOUT, WFF)
    for copy in returned[0]:
        copy.wait_recv()

    def keep(s, c, k, values):
        mixed[group_rows(s, c, k), :] = values.astype(BF16)

    chips_to_heads(m_back, keep)
    weight_grad(cot, mixed, dw_ff, 0, WOUT)
    weight_grad(cot, activated, dw_ff, WOUT + WFF, WFF)
    scatter_ff.begin()
    contract(activated, ff1, z)
    add_mixed(mixed, output_weight_of(ff1), z, part)
    total1.begin()
    for copies in returned[1:]:
        for copy in copies:
            copy.wait_recv()

    def keep_q(s, c, k, values):
        q_grad[group_rows(s, c, k), :] = values

    chips_to_heads(q_back, keep_q)
    project_back(pair_back, q_grad, (one_ref, right_ref, left_ref), du, ib_sums)
    join_back(du, in1, da2, normed, vectors[2:3, :], vectors[3:4, :], sums.at[pl.ds(0, 8)], part2)
    total2.begin()
    total2.cross()
    scatter_ff.pass_on()
    total1.cross()
    weight_grad(first, du, dw_in, 0, WIN)
    total2.combine()
    scatter_in.begin()
    scatter_ff.turn()
    total2.relay()
    scatter_in.pass_on()
    total1.combine()
    scatter_ff.pass_line()
    total2.end()
    sums[8:16, :] = jnp.zeros((8, D), F32)

    def put(index):
        rows = rows_at(index, 32)
        before = cot[rows, :].astype(F32)
        sums[8:9, :] += jnp.sum(before, axis=0, keepdims=True)
        after = before + norm_back(rows32(summed2, index), normed[rows, :], inverse[rows, 0:1])
        grad[rows, :] = after
        dz[rows, :] = after.astype(BF16)

    loop(16, put)
    mix_back(lambda rows: dz[rows, :], wout0[...], dm_rows)
    heads_to_chips(lambda s, c, k: dm_rows[group_rows(s, c, k), :], dm_parts)
    exchanged = start_exchange(where, dm_parts, dm_out, False, send_x.at[3], recv_x.at[3])
    scatter_in.turn()
    scatter_ff.deliver()
    total1.end()
    shift = vectors[20:21, :] + vectors[21:22, :]
    for k in range(2):
        rows = pl.ds(k * 64, 64)
        act_out[rows, :] = (own_hidden[rows, :] + summed[k].astype(F32) + shift).astype(BF16)
    scatter_in.pass_line()
    scatter_in.deliver()
    scatter_ff.end()
    scatter_in.end()
    total1.sent()
    total2.sent()
    for copies in returned:
        for copy in copies:
            copy.wait_send()
    for copy in exchanged:
        copy.wait()


def third_part(*operands):
    wide = WOUT + 2 * WFF
    outs = (
        bf(ROWS, D), f32(GROUP, D), bf(16, 32, 128), bf(4, 16, WIN), bf(4, 16, wide),
        f32(16, D), f32(8, 128), f32(8, WFF),
    )
    scratch = [
        vbf(16, 32, 128), vbf(16, 256, 128), vbf(16, 32, 128), vbf(GROUP, 128), vf32(GROUP, D),
        vbf(GROUP, WFF), vf32(GROUP, D), vbf(GROUP, WIN), vf32(GROUP, 128),
        vbf(2, 2, 2, 64, D), vbf(2, 2, 2, 64, D), vbf(2, 64, D), vbf(2, 2, 2, 64, D),
        vbf(2, 4, 4, 32, WIN), vbf(2, 4, 4, 32, wide), vf32(GROUP, 128), vbf(16, 32, 128), vbf(GROUP, D),
        dma(4, 15), dma(4, 15), *ColumnSum.SCRATCH, *ColumnSum.SCRATCH,
        *Scatter.scratch(wide), *Scatter.scratch(WIN),
    ]
    return kernel(third_kernel, 2, outs, scratch, "third_part", *operands)


def fourth_kernel(
    pair_ref, q_ref, grad, in0, ff0, vectors, one_ref, right_ref, left_ref,
    normed, inverse, first, second, inner, activated, mixed, sums1, ib_sums1, eb_sums1,
    grad_out, out_in, out_ff, small_out,
    pair_back, q_back, de, da2, du, q_grad, part, summed, dw_in, dw_ff, dz, sums, ib_sums, eb_sums,
    small, gathered, total_s, others,
    send_x, recv_x, send_s, recv_s, send_t, recv_t, *rest,
):
    where = y, x, z_at, core = place()
    seq, tp = lax.div(y, 2), lax.rem(y, 2)
    mine, chip = seq * 2 + core, x * 4 + z_at
    column, plane = column_partners(*where), plane_partners(*where)
    enter(column + plane)
    returned = [
        start_exchange(where, source, target, False, send_x.at[k], recv_x.at[k])
        for k, (source, target) in enumerate(((q_ref, q_back), (pair_ref, pair_back)))
    ]
    n_column = len(ColumnSum.SCRATCH)
    total = ColumnSum(part, summed, where, False, rest[:n_column])
    rest = rest[n_column:]
    scatter_ff = Scatter(dw_ff, out_ff, where, rest[: len(rest) // 2])
    scatter_in = Scatter(dw_in, out_in, where, rest[len(rest) // 2 :])

    sums[...] = jnp.zeros(sums.shape, F32)

    def lower(index):
        rows = rows_at(index, 32)
        values = grad[rows, :]
        sums[8:9, :] += jnp.sum(values, axis=0, keepdims=True)
        dz[rows, :] = values.astype(BF16)

    loop(16, lower)
    expand_back(lambda rows: dz[rows, :], ff0, inner, de, da2, eb_sums)
    weight_grad(second, de, dw_ff, WOUT, WFF)
    weight_grad(dz, mixed, dw_ff, 0, WOUT)
    weight_grad(dz, activated, dw_ff, WOUT + WFF, WFF)
    scatter_ff.begin()
    for copies in returned:
        for copy in copies:
            copy.wait_recv()

    def keep_q(s, c, k, values):
        q_grad[group_rows(s, c, k), :] = values

    chips_to_heads(q_back, keep_q)
    project_back(pair_back, q_grad, (one_ref, right_ref, left_ref), du, ib_sums)
    scatter_ff.pass_on()
    join_back(du, in0, da2, normed, vectors[0:1, :], vectors[1:2, :], sums.at[pl.ds(0, 8)], part)
    total.begin()
    weight_grad(first, du, dw_in, 0, WIN)
    total.cross()
    scatter_in.begin()
    scatter_ff.turn()

    once = jnp.where(y * 2 + core == 0, 1.0, 0.0)
    for half in range(2):
        for across in range(4):
            lanes = slice((half * 4 + across) * 128, (half * 4 + across + 1) * 128)
            here = jnp.where((tp == half) & (mine == across), 1.0, 0.0)
            zero = jnp.zeros((1, 128), F32)
            for chip_z in range(4):
                cut = slice(chip_z * 128, (chip_z + 1) * 128)
                at = across * 4 + chip_z
                pieces = [
                    sums[0:2, lanes], sums1[0:2, lanes], sums[2:4, lanes], sums1[2:4, lanes],
                    ib_sums[0:3, :] * here, ib_sums1[0:3, :] * here, zero, zero,
                    eb_sums[0:1, cut] * here, eb_sums1[0:1, cut] * here,
                    sums[8:9, lanes] * once, sums[8:9, lanes] * once,
                    sums1[8:9, lanes] * once, sums1[8:9, lanes] * once,
                ]
                row = 0
                for piece in pieces:
                    count = piece.shape[0]
                    small[at, half, row : row + count, :] = piece
                    row += count
                small[at, half, 22:24, :] = jnp.zeros((2, 128), F32)
    spread = []
    for k, (dx, dz_) in enumerate(STEPS):
        copy = remote(
            small.at[ring(x, dx) * 4 + ring(z_at, dz_)],
            gathered.at[k],
            send_s.at[k],
            recv_s.at[k],
            plane[k],
        )
        copy.start()
        spread.append(copy)
    total.combine()
    scatter_in.pass_on()
    scatter_ff.pass_line()
    for copy in spread:
        copy.wait_recv()
    total_s[...] = small[chip] + jnp.sum(gathered[...], axis=0)
    shared = []
    for k, peer in enumerate(column):
        copy = remote(total_s, others.at[k], send_t.at[k], recv_t.at[k], peer)
        copy.start()
        shared.append(copy)
    scatter_in.turn()
    total.end()
    own = mine * ROWS
    for k in range(4):
        rows = pl.ds(pl.multiple_of(own + k * 32, 32), 32)
        summed_rows = summed[k // 2, (k % 2) * 32 : (k % 2 + 1) * 32, :].astype(F32)
        grad_out[k * 32 : (k + 1) * 32, :] = grad[rows, :] + norm_back(
            summed_rows, normed[rows, :], inverse[rows, 0:1]
        )
    scatter_in.pass_line()
    scatter_ff.deliver()
    for copy in shared:
        copy.wait_recv()
    small_out[...] = total_s[...] + jnp.sum(others[...], axis=0)
    scatter_in.deliver()
    scatter_ff.end()
    scatter_in.end()
    total.sent()
    for copies in returned:
        for copy in copies:
            copy.wait_send()
    for copy in spread + shared:
        copy.wait_send()


def fourth_part(*operands):
    wide = WOUT + 2 * WFF
    outs = (f32(ROWS, D), bf(4, 16, WIN), bf(4, 16, wide), f32(2, 24, 128))
    scratch = [
        vbf(16, 256, 128), vbf(16, 32, 128), vbf(GROUP, WFF), vf32(GROUP, D), vbf(GROUP, WIN),
        vf32(GROUP, 128), vbf(2, 2, 2, 64, D), vbf(2, 64, D), vbf(2, 4, 4, 32, WIN), vbf(2, 4, 4, 32, wide),
        vbf(GROUP, D), vf32(16, D), vf32(8, 128), vf32(8, WFF),
        vf32(16, 2, 24, 128), vf32(15, 2, 24, 128), vf32(2, 24, 128), vf32(7, 2, 24, 128),
        dma(2, 15), dma(2, 15), dma(15), dma(15), dma(7), dma(7), *ColumnSum.SCRATCH,
        *Scatter.scratch(wide), *Scatter.scratch(WIN),
    ]
    return kernel(fourth_kernel, 3, outs, scratch, "fourth_part", *operands)


TILE = 256
SPAN = 1024


def seen(quarter, tile):
    key = lax.broadcasted_iota(jnp.int32, (SPAN, TILE), 0)
    row = lax.broadcasted_iota(jnp.int32, (SPAN, TILE), 1)
    place_of = (row // 32) * ROWS + quarter * 32 + row % 32
    return key <= place_of


def score_span(quarter, tile, span, queries, kvs):
    block = lax.dot_general(
        kvs[span * SPAN : (span + 1) * SPAN, :],
        queries,
        (((1,), (1,)), ((), ())),
        preferred_element_type=F32,
    )
    return jnp.where(seen(quarter, tile), block, MASKED) if span == tile else block


def forward_tile(quarter, tile, queries, kvs, kvt, score):
    highest = jnp.full((1, TILE), MASKED, F32)
    for span in range(tile + 1):
        block = score_span(quarter, tile, span, queries, kvs)
        score[span * SPAN : (span + 1) * SPAN, :] = block
        highest = jnp.maximum(highest, jnp.max(block, axis=0, keepdims=True))
    total = jnp.zeros((1, TILE), F32)
    mixed = jnp.zeros((128, TILE), F32)
    for span in range(tile + 1):
        weight = jnp.exp(score[span * SPAN : (span + 1) * SPAN, :] - highest)
        total = total + jnp.sum(weight, axis=0, keepdims=True)
        low = weight.astype(BF16)
        for part in range(8):
            mixed = mixed + jnp.dot(
                kvt[span * 8 + part],
                low[part * ROWS : (part + 1) * ROWS],
                preferred_element_type=F32,
            )
    return mixed / total, highest + jnp.log(total)


def backward_span(tile, span, block, lse, delta, queries, outs, kvs, kvt, acc):
    keyed = kvs[span * SPAN : (span + 1) * SPAN, :]
    probs = jnp.exp(block - lse)
    back = lax.dot_general(keyed, outs, (((1,), (1,)), ((), ())), preferred_element_type=F32)
    score_grad = (probs * (back - delta)).astype(BF16)
    pair = jnp.dot(score_grad, queries, preferred_element_type=F32) + jnp.dot(
        probs.astype(BF16), outs, preferred_element_type=F32
    )
    if span == tile:
        acc[span * SPAN : (span + 1) * SPAN, :] = pair
    else:
        acc[span * SPAN : (span + 1) * SPAN, :] += pair
    query_grad = jnp.zeros((128, TILE), F32)
    for part in range(8):
        query_grad = query_grad + jnp.dot(
            kvt[span * 8 + part],
            score_grad[part * ROWS : (part + 1) * ROWS],
            preferred_element_type=F32,
        )
    return query_grad


def put_back_rows(rank_ref, rows, target, upper):
    lane = lax.broadcasted_iota(jnp.int32, (32, 128), 1)

    def put_back(chip, carry):
        first = rows[pl.ds(pl.multiple_of(rank_ref[chip * 2] * 32, 32), 32), :]
        second = rows[pl.ds(pl.multiple_of(rank_ref[chip * 2 + 1] * 32, 32), 32), :]
        if upper:
            first = pltpu.roll(first, 64, 1)
        else:
            second = pltpu.roll(second, 64, 1)
        target[chip] = jnp.where(lane < 64, first, second).astype(BF16)
        return carry

    lax.fori_loop(0, 16, put_back, 0)


def put_back_pairs(rank_ref, acc, target):
    def put_back(chip, carry):
        for core in range(2):
            rank = rank_ref[chip * 2 + core]
            target[chip, core] = acc[pl.ds(pl.multiple_of(rank * ROWS, ROWS), ROWS), :].astype(BF16)
        return carry

    lax.fori_loop(0, 16, put_back, 0)


def attend_kernel(rank_ref, kv_ref, q_ref, m_ref, kvs_ref, kvt_ref, qs_ref, o_ref, lse_ref, score, rows):
    quarter = rank_ref[32]
    lane = lax.broadcasted_iota(jnp.int32, (32, 128), 1)

    def arrange(chip, carry):
        block = q_ref[chip].astype(F32) * (HEAD_DIM**-0.5)
        for core in range(2):
            rank = rank_ref[chip * 2 + core]
            keyed = kv_ref[chip * 2 + core]
            kvs_ref[pl.ds(pl.multiple_of(rank * ROWS, ROWS), ROWS), :] = keyed
            kvt_ref[rank] = keyed.astype(F32).T.astype(BF16)
            part = block if core == 0 else pltpu.roll(block, 64, 1)
            qs_ref[pl.ds(pl.multiple_of(rank * 32, 32), 32), :] = jnp.where(
                lane < 64, part, 0.0
            ).astype(BF16)
        return carry

    lax.fori_loop(0, 16, arrange, 0)

    for tile in range(4):
        queries = qs_ref[tile * TILE : (tile + 1) * TILE, :]
        mixed, lse = forward_tile(quarter, tile, queries, kvs_ref, kvt_ref, score)
        lse_ref[tile] = jnp.broadcast_to(lse, (8, TILE))
        o_ref[tile] = mixed
        rows[tile * TILE : (tile + 1) * TILE, :] = mixed.T

    put_back_rows(rank_ref, rows, m_ref, 1)


def attend(rank, kv, q):
    return pl.pallas_call(
        attend_kernel,
        out_shape=(
            jax.ShapeDtypeStruct((16, 32, 128), BF16),
            jax.ShapeDtypeStruct((4096, 128), BF16),
            jax.ShapeDtypeStruct((32, 128, 128), BF16),
            jax.ShapeDtypeStruct((1024, 128), BF16),
            jax.ShapeDtypeStruct((4, 128, TILE), F32),
            jax.ShapeDtypeStruct((4, 8, TILE), F32),
        ),
        in_specs=[SMEM, VMEM, VMEM],
        out_specs=tuple([VMEM] * 6),
        scratch_shapes=[pltpu.VMEM((4096, TILE), F32), pltpu.VMEM((1024, 128), F32)],
        compiler_params=pltpu.CompilerParams(vmem_limit_bytes=VMEM_LIMIT),
        name="attend",
    )(rank, kv, q)


def attend_back_kernel(
    rank_ref, kvs_ref, kvt_ref, qs_ref, o_ref, lse_ref, dm_ref, dkv_ref, dq_ref, dos, acc, dqs
):
    quarter = rank_ref[32]
    lane = lax.broadcasted_iota(jnp.int32, (32, 128), 1)

    def arrange(chip, carry):
        block = dm_ref[chip].astype(F32)
        for core in range(2):
            rank = rank_ref[chip * 2 + core]
            part = pltpu.roll(block, 64, 1) if core == 0 else block
            dos[pl.ds(pl.multiple_of(rank * 32, 32), 32), :] = jnp.where(
                lane < 64, 0.0, part
            ).astype(BF16)
        return carry

    lax.fori_loop(0, 16, arrange, 0)

    for tile in range(4):
        queries = qs_ref[tile * TILE : (tile + 1) * TILE, :]
        outs = dos[tile * TILE : (tile + 1) * TILE, :]
        delta = jnp.sum(outs.astype(F32).T * o_ref[tile], axis=0, keepdims=True)
        lse = lse_ref[tile][0:1, :]
        query_grad = jnp.zeros((128, TILE), F32)
        for span in range(tile + 1):
            block = score_span(quarter, tile, span, queries, kvs_ref)
            query_grad = query_grad + backward_span(
                tile, span, block, lse, delta, queries, outs, kvs_ref, kvt_ref, acc
            )
        dqs[tile * TILE : (tile + 1) * TILE, :] = query_grad.T * (HEAD_DIM**-0.5)

    put_back_rows(rank_ref, dqs, dq_ref, 0)
    put_back_pairs(rank_ref, acc, dkv_ref)


def attend_back(rank, kvs, kvt, qs, o, lse, dm):
    return pl.pallas_call(
        attend_back_kernel,
        out_shape=(
            jax.ShapeDtypeStruct((16, 2, 128, 128), BF16),
            jax.ShapeDtypeStruct((16, 32, 128), BF16),
        ),
        in_specs=[SMEM] + [VMEM] * 6,
        out_specs=tuple([VMEM] * 2),
        scratch_shapes=[
            pltpu.VMEM((1024, 128), BF16),
            pltpu.VMEM((4096, 128), F32),
            pltpu.VMEM((1024, 128), F32),
        ],
        compiler_params=pltpu.CompilerParams(vmem_limit_bytes=VMEM_LIMIT),
        name="attend_back",
    )(rank, kvs, kvt, qs, o, lse, dm)


def attend_both_kernel(
    rank_ref, kv_ref, q_ref, dm_ref, m_ref, dkv_ref, dq_ref, kvs, kvt, qs, dos, score, rows, acc, dqs
):
    quarter = rank_ref[32]
    lane = lax.broadcasted_iota(jnp.int32, (32, 128), 1)

    def arrange(chip, carry):
        block = q_ref[chip].astype(F32) * (HEAD_DIM**-0.5)
        back = dm_ref[chip].astype(F32)
        for core in range(2):
            rank = rank_ref[chip * 2 + core]
            keyed = kv_ref[chip * 2 + core]
            kvs[pl.ds(pl.multiple_of(rank * ROWS, ROWS), ROWS), :] = keyed
            kvt[rank] = keyed.astype(F32).T.astype(BF16)
            at = pl.ds(pl.multiple_of(rank * 32, 32), 32)
            part = block if core == 0 else pltpu.roll(block, 64, 1)
            qs[at, :] = jnp.where(lane < 64, part, 0.0).astype(BF16)
            part = pltpu.roll(back, 64, 1) if core == 0 else back
            dos[at, :] = jnp.where(lane < 64, 0.0, part).astype(BF16)
        return carry

    lax.fori_loop(0, 16, arrange, 0)

    for tile in range(4):
        queries = qs[tile * TILE : (tile + 1) * TILE, :]
        outs = dos[tile * TILE : (tile + 1) * TILE, :]
        mixed, lse = forward_tile(quarter, tile, queries, kvs, kvt, score)
        rows[tile * TILE : (tile + 1) * TILE, :] = mixed.T
        delta = jnp.sum(outs.astype(F32).T * mixed, axis=0, keepdims=True)
        query_grad = jnp.zeros((128, TILE), F32)
        for span in range(tile + 1):
            block = score[span * SPAN : (span + 1) * SPAN, :]
            query_grad = query_grad + backward_span(
                tile, span, block, lse, delta, queries, outs, kvs, kvt, acc
            )
        dqs[tile * TILE : (tile + 1) * TILE, :] = query_grad.T * (HEAD_DIM**-0.5)

    put_back_rows(rank_ref, rows, m_ref, 1)
    put_back_rows(rank_ref, dqs, dq_ref, 0)
    put_back_pairs(rank_ref, acc, dkv_ref)


def attend_both(rank, kv, q, dm):
    return pl.pallas_call(
        attend_both_kernel,
        out_shape=(bf(16, 32, 128), bf(16, 2, 128, 128), bf(16, 32, 128)),
        in_specs=[SMEM] + [VMEM] * 3,
        out_specs=(VMEM,) * 3,
        scratch_shapes=[
            vbf(4096, 128), vbf(32, 128, 128), vbf(1024, 128), vbf(1024, 128),
            vf32(4096, TILE), vf32(1024, 128), vf32(4096, 128), vf32(1024, 128),
        ],
        compiler_params=pltpu.CompilerParams(vmem_limit_bytes=VMEM_LIMIT),
        name="attend_both",
    )(rank, kv, q, dm)


def rotary_parts(rank):
    half = ROT // 2
    freqs = 10000.0 ** (-(jnp.arange(half, dtype=F32) * 2.0 / ROT))
    lane = jnp.arange(128) % HEAD_DIM
    every = jnp.where(lane < ROT, jnp.tile(freqs, 128 // half), 0.0)[None, :]
    start = rank * ROWS * every
    steps = jnp.arange(ROWS, dtype=F32)[:, None] * every
    trig = jnp.concatenate([jnp.cos(start), jnp.sin(start), jnp.zeros((6, 128), F32)], axis=0)
    return trig, jnp.cos(steps), jnp.sin(steps)


def local(
    tokens, cotangent, group_order, input_weight, output_weight, expand_weight, contract_weight,
    norm_gain, norm_shift, input_bias, output_bias, expand_bias,
):
    y, x, z, core = place()
    seq, tp = lax.div(y, 2), lax.rem(y, 2)
    chip = x * 4 + z
    mine = seq * 2 + core

    def quarters(weight, width):
        shaped = weight.reshape(LAYERS, 16, -1, 4, width).transpose(0, 3, 1, 2, 4)
        return shaped.reshape(LAYERS, 4, 16, -1)

    win = quarters(input_weight, 128)
    wff = jnp.concatenate(
        [quarters(output_weight, 128), quarters(expand_weight, 512), quarters(contract_weight, 512)],
        axis=3,
    )
    lane = jnp.arange(128)[None, :]
    at = lax.rem(chip, 4) * 4 + core * 2 + tp

    def placed(values, width, place_of):
        values = values.reshape(-1, width)
        return jnp.where(lane // width == place_of, jnp.tile(values, (1, 128 // width)), 0.0)

    rank = group_order.reshape(1, 1).astype(F32)
    par = jnp.concatenate(
        [
            placed(norm_gain, 8, at),
            placed(norm_shift, 8, at),
            placed(input_bias, 8, at),
            jnp.where((lane == at * 8) & (tp == 0), rank, 0.0),
            jnp.zeros((1, 128), F32),
            placed(expand_bias, 32, core * 2 + tp),
            placed(output_bias, 8, at),
            jnp.zeros((2, 128), F32),
        ],
        axis=0,
    )
    trig, cosine, sine = rotary_parts(rank)
    (in0, ff0, in_own, ff_own, token_rows, vectors, ib, eb, one, right, left,
     normed0, inverse0, first0, second0, kv0, q0, inner0, activated0) = first_part(
        win, wff, tokens, par, trig, cosine, sine
    )
    ranks = vectors[14].reshape(2, 32, 16)[:, :, 0].astype(jnp.int32)
    task = jnp.concatenate(
        [lax.dynamic_slice_in_dim(ranks, lax.div(x, 2), 1, 0).reshape(32), z.reshape(1)]
    )
    tables = (one, right, left)
    m0, kvs, kvt, qs, o, lse = attend(task, kv0.reshape(32, 128, 128), q0)
    (in1, ff1, cot, mixed0, own_hidden, normed1, inverse1, first1, second1, kv1, q1, dm1, inner1,
     activated1) = second_part(
        m0, ff0, activated0, token_rows, vectors, ib, eb, *tables, in_own, ff_own, cotangent
    )
    m1, pair1, query1 = attend_both(task, kv1.reshape(32, 128, 128), q1, dm1)
    wout0 = ff0.reshape(D, -1)[:, :WOUT]
    activations, grad, dm0, in1_out, ff1_out, sums1, ib1, eb1 = third_part(
        m1, pair1.reshape(16, 256, 128), query1, cot, in1, ff1, wout0, vectors, *tables,
        normed1, inverse1, first1, second1, inner1, activated1, own_hidden,
    )
    pair0, query0 = attend_back(task, kvs, kvt, qs, o, lse, dm0)
    input_gradient, in0_out, ff0_out, small = fourth_part(
        pair0.reshape(16, 256, 128), query0, grad, in0, ff0, vectors, *tables,
        normed0, inverse0, first0, second0, inner0, activated0, mixed0, sums1, ib1, eb1,
    )

    def whole(layer_grads, first, width, count):
        parts = [
            g[:, :, first : first + width * count].astype(F32).reshape(4, 16, count, width)
            for g in layer_grads
        ]
        return jnp.stack(parts, axis=0).transpose(0, 2, 3, 1, 4)

    ins, ffs = (in0_out, in1_out), (ff0_out, ff1_out)
    input_out = whole(ins, 0, 128, 3).reshape(2, 16, 3, 512)
    output_out = whole(ffs, 0, WOUT, 1).reshape(2, 16, 512)
    expand_out = whole(ffs, WOUT, WFF, 1).reshape(2, 16, 2048)
    contract_out = whole(ffs, WOUT + WFF, WFF, 1).reshape(2, 16, 2048)
    own = lax.dynamic_slice_in_dim(small, seq, 1, 0).reshape(24, 128)
    eight = lax.dynamic_slice_in_dim(own, at * 8, 8, 1)
    wide = lax.dynamic_slice_in_dim(own, (core * 2 + tp) * 32, 32, 1)
    return (
        activations,
        input_gradient,
        input_out,
        output_out,
        expand_out,
        contract_out,
        eight[0:4].reshape(2, 2, 8),
        eight[4:8].reshape(2, 2, 8),
        eight[8:14].reshape(2, 3, 8),
        eight[18:22].reshape(2, 2, 8),
        wide[16:18],
    )


def solution(mesh):
    rows, columns = P(("seq", "ctx"), None), P(None, None, ("seq", "ctx", "tp"))
    weight, flat = P(None, ("seq", "ctx"), "tp"), P(None, ("seq", "ctx", "tp"))
    first = P(None, ("seq", "ctx"), None, "tp")
    outs = (rows, rows, first, weight, weight, weight, columns, columns, columns, columns, flat)
    return jax.shard_map(
        local,
        mesh=mesh,
        in_specs=(rows, rows, P("seq", "ctx"), *outs[2:]),
        out_specs=outs,
        check_vma=False,
    )
```

```python
import jax
import jax.numpy as jnp
import numpy as np
from jax import lax
from jax.experimental import pallas as pl
from jax.experimental.pallas import tpu as pltpu
from jax.sharding import PartitionSpec as P

MESH = pl.DeviceIdType.MESH
F32, BF16 = jnp.float32, jnp.bfloat16
D, HEAD_DIM, ROT, LAYERS = 1024, 64, 16, 2
ROWS = 128
GROUP = 512
WIN, WOUT, WFF = 384, 128, 512
COLS = WIN + WOUT + 2 * WFF
PARAMS = 208
EPSILON = 1e-05
MASKED = -1e30
MIB = 1024 * 1024
LIMITS = (24, 34, 48, 42)
ATTEND_LIMIT = 20 * MIB


def place():
    ctx = lax.axis_index("ctx")
    chip = lax.div(ctx, 2)
    y = lax.axis_index("seq") * 2 + lax.axis_index("tp")
    return y, lax.div(chip, 4), lax.rem(chip, 4), lax.rem(ctx, 2)


def device(y, x, z, core):
    return (lax.div(y, 2), (x * 4 + z) * 2 + core, lax.rem(y, 2))


def ring(index, step):
    return lax.rem(index + step, 4)


def enter(partners):
    barrier = pltpu.get_barrier_semaphore()
    for partner in partners:
        pl.semaphore_signal(barrier, inc=1, device_id=partner, device_id_type=MESH)
    pl.semaphore_wait(barrier, len(partners))


def plane_partners(y, x, z, core):
    return [
        device(y, ring(x, dx), ring(z, dz), core)
        for dx in range(4)
        for dz in range(4)
        if dx or dz
    ]


def column_partners(y, x, z, core):
    return [
        device(ring(y, dy), x, z, lax.rem(core + dc, 2))
        for dy in range(4)
        for dc in range(2)
        if dy or dc
    ]


def remote(source, target, send, receive, partner):
    return pltpu.make_async_remote_copy(
        src_ref=source,
        dst_ref=target,
        send_sem=send,
        recv_sem=receive,
        device_id=partner,
        device_id_type=MESH,
    )


HBM = pl.BlockSpec(memory_space=pl.ANY)
VMEM = pl.BlockSpec(memory_space=pltpu.VMEM)
SMEM = pl.BlockSpec(memory_space=pltpu.SMEM)


def bf(*shape):
    return jax.ShapeDtypeStruct(shape, BF16)


def f32(*shape):
    return jax.ShapeDtypeStruct(shape, F32)


def vbf(*shape):
    return pltpu.VMEM(shape, BF16)


def vf32(*shape):
    return pltpu.VMEM(shape, F32)


def kernel(body, number, outs, scratch, name, *operands):
    return pl.pallas_call(
        body,
        out_shape=outs,
        in_specs=[VMEM] * len(operands),
        out_specs=(VMEM,) * len(outs),
        scratch_shapes=scratch,
        compiler_params=params(number),
        name=name,
    )(*operands)


def dma(*shape):
    return pltpu.SemaphoreType.DMA(shape)


def params(number):
    return pltpu.CompilerParams(
        collective_id=number, has_side_effects=True, vmem_limit_bytes=LIMITS[number] * MIB
    )


PEERS = ((0, 1), (1, 0), (1, 1))
STEPS = tuple((dx, dz) for dx in range(4) for dz in range(4) if dx or dz)


def peer_at(y, x, z, core, step):
    seq, tp = lax.div(y, 2), lax.rem(y, 2)
    seq_to, core_to = lax.rem(seq + step[0], 2), lax.rem(core + step[1], 2)
    return seq_to * 2 + core_to, device(seq_to * 2 + tp, x, z, core_to)


class Gather:
    def __init__(self, full, where, send, recv):
        y, x, z, core = where
        self.full, self.x, self.z, self.send, self.recv = full, x, z, send, recv
        self.near = {
            "x": (device(y, ring(x, 1), z, core), device(y, ring(x, 3), z, core)),
            "z": (device(y, x, ring(z, 1), core), device(y, x, ring(z, 3), core)),
        }
        self.held = [(), ()]
        self.started = []

    def go(self, source, slot, partner):
        copy = remote(source, source, self.send.at[slot], self.recv.at[slot], partner)
        copy.start()
        self.started.append(copy)
        return copy

    def begin(self):
        for half in range(2):
            up, down = self.near["xz"[half]]
            own = self.full.at[half, self.x, self.z]
            self.held[half] = (self.go(own, half * 8, up), self.go(own, half * 8 + 1, down))

    def arrive(self, half):
        for copy in self.held[half]:
            copy.wait_recv()

    def pass_on(self):
        x, z = self.x, self.z
        for half in range(2):
            self.arrive(half)
            up, down = self.near["xz"[half]]
            whole = self.full.at[half]
            if half == 0:
                before, after = whole.at[ring(x, 3), z], whole.at[ring(x, 1), z]
            else:
                before, after = whole.at[x, ring(z, 3)], whole.at[x, ring(z, 1)]
            self.held[half] = (
                self.go(before.at[pl.ds(0, 16)], half * 8 + 2, up),
                self.go(after.at[pl.ds(16, 16)], half * 8 + 3, down),
            )

    def turn(self):
        for half in range(2):
            self.arrive(half)
            up, down = self.near["zx"[half]]
            whole = self.full.at[half]
            line = whole.at[:, self.z] if half == 0 else whole.at[self.x]
            self.held[half] = (self.go(line, half * 8 + 4, up), self.go(line, half * 8 + 5, down))

    def pass_line(self):
        x, z = self.x, self.z
        two, more = pl.ds(0, 2), pl.ds(2, 2)
        for half in range(2):
            self.arrive(half)
            up, down = self.near["zx"[half]]
            whole = self.full.at[half]
            if half == 0:
                before, after = whole.at[two, ring(z, 3)], whole.at[more, ring(z, 1)]
            else:
                before, after = whole.at[ring(x, 3), two], whole.at[ring(x, 1), more]
            self.held[half] = (
                self.go(before, half * 8 + 6, up),
                self.go(after, half * 8 + 7, down),
            )

    def end(self):
        for half in range(2):
            self.arrive(half)

    def sent(self):
        for copy in self.started:
            copy.wait_send()


class RowShare:
    def __init__(self, source, target, where, send, recv):
        y, x, z, core = where
        self.source, self.target, self.send, self.recv = source, target, send, recv
        seq = lax.div(y, 2)
        self.own = rows_at(seq * 2 + core, ROWS)
        self.other = rows_at((1 - seq) * 2 + core, ROWS)
        self.sibling = device(y, x, z, lax.rem(core + 1, 2))
        self.facing = device(3 - y, x, z, core)
        self.copies = []

    def go(self, source, target, slot, partner):
        copy = remote(source, target, self.send.at[slot], self.recv.at[slot], partner)
        copy.start()
        self.copies.append(copy)

    def begin(self):
        self.target[self.own, :] = self.source[...]
        self.go(self.source, self.target.at[self.own], 0, self.facing)
        self.go(self.source, self.target.at[self.own], 1, self.sibling)

    def pass_on(self):
        self.copies[0].wait_recv()
        block = self.target.at[self.other]
        self.go(block, block, 2, self.sibling)

    def end(self):
        for copy in self.copies[1:]:
            copy.wait_recv()

    def sent(self):
        for copy in self.copies:
            copy.wait_send()


class ColumnSum:
    SCRATCH = [vbf(4, 64, D), vbf(3, 64, D), vbf(3, 64, D)] + [dma(4), dma(4), dma(3), dma(3), dma(7), dma(7)]
    ORDER = (2, 1, 3)

    def __init__(self, part, out, where, everywhere, scratch):
        self.part, self.out, self.where, self.everywhere = part, out, where, everywhere
        (self.near, self.far, self.held, self.send1, self.recv1, self.send2, self.recv2, self.send3, self.recv3) = scratch
        y, x, z, core = where
        self.sibling = device(y, x, z, lax.rem(core + 1, 2))
        self.chips = [device(ring(y, dy), x, z, core) for dy in (1, 2, 3)]

    def begin(self):
        y, x, z, core = self.where
        self.nears = {}
        for dy in (*self.ORDER, 0):
            to = ring(y, dy)
            source = self.part.at[lax.div(to, 2), lax.rem(core + 1, 2), lax.rem(to, 2)]
            self.nears[dy] = remote(
                source, self.near.at[dy], self.send1.at[dy], self.recv1.at[dy], self.sibling
            )
            self.nears[dy].start()

    def cross(self):
        y, x, z, core = self.where
        self.fars = []
        for dy in self.ORDER:
            to = ring(y, dy)
            self.nears[dy].wait_recv()
            own = self.part[lax.div(to, 2), core, lax.rem(to, 2)].astype(F32)
            self.held[dy - 1] = (own + self.near[dy].astype(F32)).astype(BF16)
            copy = remote(
                self.held.at[dy - 1],
                self.far.at[dy - 1],
                self.send2.at[dy - 1],
                self.recv2.at[dy - 1],
                self.chips[dy - 1],
            )
            copy.start()
            self.fars.append(copy)

    def combine(self):
        y, x, z, core = self.where
        seq, tp = lax.div(y, 2), lax.rem(y, 2)
        self.nears[0].wait_recv()
        total = self.part[seq, core, tp].astype(F32) + self.near[0].astype(F32)
        for copy in self.fars:
            copy.wait_recv()
        for k in range(3):
            total = total + self.far[k].astype(F32)
        self.outs, self.relayed = [], []
        own = self.out.at[seq, core, tp] if self.everywhere else self.out.at[tp]
        own[...] = total.astype(BF16)
        if self.everywhere:
            for dy in self.ORDER:
                self.go(self.outs, own, dy - 1, self.chips[dy - 1])
            self.go(self.relayed, own, 3, self.sibling)
        else:
            self.go(self.outs, own, 0, device(seq * 2 + lax.rem(tp + 1, 2), x, z, core))

    def go(self, kept, block, slot, partner):
        copy = remote(block, block, self.send3.at[slot], self.recv3.at[slot], partner)
        copy.start()
        kept.append(copy)

    def relay(self):
        y, x, z, core = self.where
        for at, dy in enumerate(self.ORDER):
            self.outs[at].wait_recv()
            source = ring(y, 4 - dy)
            block = self.out.at[lax.div(source, 2), core, lax.rem(source, 2)]
            self.go(self.relayed, block, 3 + dy, self.sibling)

    def end(self):
        if self.everywhere:
            for copy in self.relayed:
                copy.wait_recv()
        else:
            self.outs[0].wait_recv()

    def sent(self):
        for copy in (*self.nears.values(), *self.fars, *self.outs, *self.relayed):
            copy.wait_send()


class Scatter:
    def __init__(self, dw, out, where, scratch):
        y, x, z, core = where
        self.dw, self.out, self.where, self.x, self.z = dw, out, where, x, z
        (self.opp1, self.dir1, self.comb1, self.sent1, self.mid, self.opp2, self.dir2, self.comb2, self.sent2, self.done,
         self.send, self.recv, self.send_f, self.recv_f) = scratch
        self.near = {
            "x": (device(y, ring(x, 1), z, core), device(y, ring(x, 3), z, core)),
            "z": (device(y, x, ring(z, 1), core), device(y, x, ring(z, 3), core)),
        }
        self.started, self.held = [], [(), ()]

    @staticmethod
    def scratch(columns):
        big, small = vbf(2, 2, 2, 32, columns), vbf(2, 2, 16, columns)
        mid = vbf(2, 4, 32, columns)
        return [big] * 4 + [mid] + [small] * 5 + [dma(24), dma(24), dma(3), dma(3)]

    def go(self, source, target, slot, partner):
        copy = remote(source, target, self.send.at[slot], self.recv.at[slot], partner)
        copy.start()
        self.started.append(copy)
        return copy

    def part1(self, half, step, side):
        two = pl.ds(side * 2, 2)
        whole = self.dw.at[half]
        if half == 0:
            return whole.at[two, ring(self.z, step)]
        return whole.at[ring(self.x, step), two]

    def part2(self, half, step, side):
        at = ring(self.x, step) if half == 0 else ring(self.z, step)
        return self.mid.at[half, at].at[pl.ds(side * 16, 16)]

    def open(self, half, part, axis, opposite, direct, base):
        up, down = self.near[axis]
        self.held[half] = (
            self.go(part(half, 2, 0), opposite.at[half, 0], base, up),
            self.go(part(half, 2, 1), opposite.at[half, 1], base + 1, down),
            self.go(part(half, 1, 1), direct.at[half, 0], base + 2, up),
            self.go(part(half, 3, 0), direct.at[half, 1], base + 3, down),
        )

    def onward(self, half, part, axis, opposite, combined, sent, base):
        up, down = self.near[axis]
        copies = self.held[half]
        copies[0].wait_recv()
        sent[half, 0] = (part(half, 1, 0)[...].astype(F32) + opposite[half, 0].astype(F32)).astype(BF16)
        first = self.go(sent.at[half, 0], combined.at[half, 0], base + 4, up)
        copies[1].wait_recv()
        sent[half, 1] = (part(half, 3, 1)[...].astype(F32) + opposite[half, 1].astype(F32)).astype(BF16)
        second = self.go(sent.at[half, 1], combined.at[half, 1], base + 5, down)
        self.held[half] = (*copies[2:], first, second)

    def finish(self, half, part, direct, combined, target):
        for copy in self.held[half]:
            copy.wait_recv()
        for side in range(2):
            total = (
                part(half, 0, side)[...].astype(F32)
                + combined[half, side].astype(F32)
                + direct[half, 1 - side].astype(F32)
            )
            target(half, side)[...] = total.astype(BF16)

    def begin(self):
        for half in range(2):
            self.open(half, self.part1, "zx"[half], self.opp1, self.dir1, half * 12)

    def pass_on(self):
        for half in range(2):
            self.onward(half, self.part1, "zx"[half], self.opp1, self.comb1, self.sent1, half * 12)

    def turn(self):
        for half in range(2):
            self.finish(
                half,
                self.part1,
                self.dir1,
                self.comb1,
                lambda h, side: self.mid.at[h, pl.ds(side * 2, 2)],
            )
            self.open(half, self.part2, "xz"[half], self.opp2, self.dir2, half * 12 + 6)

    def pass_line(self):
        for half in range(2):
            self.onward(
                half, self.part2, "xz"[half], self.opp2, self.comb2, self.sent2, half * 12 + 6
            )

    def deliver(self):
        y, x, z, core = self.where
        seq = lax.div(y, 2)
        mine = seq * 2 + core
        for half in range(2):
            self.finish(
                half, self.part2, self.dir2, self.comb2, lambda h, side: self.done.at[h, side]
            )
        self.out[mine] = self.done[seq, core]
        self.final = []
        for k, step in enumerate(PEERS):
            theirs, peer = peer_at(y, x, z, core, step)
            copy = remote(
                self.done.at[lax.div(theirs, 2), lax.rem(theirs, 2)],
                self.out.at[mine],
                self.send_f.at[k],
                self.recv_f.at[k],
                peer,
            )
            copy.start()
            self.final.append(copy)

    def end(self):
        for copy in self.final:
            copy.wait()
        for copy in self.started:
            copy.wait_send()


def start_exchange(where, source, target, shared, send, recv):
    y, x, z, core = where
    chip = x * 4 + z
    target[chip] = source[x if shared else chip]
    copies = []
    for k, (dx, dz) in enumerate(STEPS):
        to_x, to_z = ring(x, dx), ring(z, dz)
        copy = remote(
            source.at[to_x if shared else to_x * 4 + to_z],
            target.at[chip],
            send.at[k],
            recv.at[k],
            device(y, to_x, to_z, core),
        )
        copy.start()
        copies.append(copy)
    return copies


def loop(count, body):
    def step(index, carry):
        body(index)
        return carry

    lax.fori_loop(0, count, step, 0)


def rows_at(index, count):
    return pl.ds(pl.multiple_of(index * count, count), count)


def turned(values, tables, sign):
    one, right, left = tables
    half = ROT // 2
    return values * one + sign * (
        pltpu.roll(values, 128 - half, 1) * right + pltpu.roll(values, half, 1) * left
    )


def low_lanes(shape):
    return lax.broadcasted_iota(jnp.int32, shape, 1) < HEAD_DIM


def swap(values):
    return pltpu.roll(values, HEAD_DIM, 1)


def heads_to_chips(values, target):
    def body(index):
        seq, quarter = lax.div(index, 4), lax.rem(index, 4)
        first, second = values(seq, 0, quarter), values(seq, 1, quarter)
        low = low_lanes(first.shape)
        target[seq * 8 + quarter] = jnp.where(low, first, swap(second)).astype(BF16)
        target[seq * 8 + 4 + quarter] = jnp.where(low, swap(first), second).astype(BF16)

    loop(8, body)


def group_rows(seq, core, quarter):
    return pl.ds(pl.multiple_of(seq * 256 + core * 128 + quarter * 32, 32), 32)


def normalize_rows(hidden, normed, inverse):
    def body(index):
        rows = rows_at(index, 32)
        values = hidden(index)
        centred = values - jnp.mean(values, axis=1, keepdims=True)
        spread = jnp.mean(centred * centred, axis=1, keepdims=True)
        scale = lax.rsqrt(spread + EPSILON)
        normed[rows, :] = centred * scale
        inverse[rows, :] = jnp.broadcast_to(scale, (32, 128))

    loop(16, body)


def scale_rows(normed, gain, shift, target):
    def body(index):
        rows = rows_at(index, 32)
        target[rows, :] = (normed[rows, :] * gain + shift).astype(BF16)

    loop(16, body)


def project(first, weight, bias, tables, pairs, q_rows):
    whole = weight[...].reshape(D, WIN)

    def body(index):
        rows = rows_at(index, 128)
        u = jnp.dot(first[rows, :], whole, preferred_element_type=F32)
        turn = tuple(t[rows, :] for t in tables)
        q_rows[rows, :] = turned(u[:, :128] + bias[0:1, :], turn, 1.0)
        keys = turned(u[:, 128:256] + bias[1:2, :], turn, 1.0)
        values = u[:, 256:] + bias[2:3, :]
        low = low_lanes(keys.shape)
        seq = lax.div(index, 2)
        part = rows_at(lax.rem(index, 2), 128)
        pairs[seq * 2, part, :] = jnp.where(low, keys, swap(values)).astype(BF16)
        pairs[seq * 2 + 1, part, :] = jnp.where(low, swap(keys), values).astype(BF16)

    loop(4, body)


def gelu_parts(inner):
    return 0.5 * (1.0 + lax.erf(inner * (0.5**0.5)))


def expand(second, weight, bias, inner, activated):
    whole = weight[:, :, :, :, WOUT : WOUT + WFF].reshape(D, WFF)

    def body(index):
        rows = rows_at(index, 128)
        e = jnp.dot(second[rows, :], whole, preferred_element_type=F32) + bias
        inner[rows, :] = e
        activated[rows, :] = (e * gelu_parts(e)).astype(BF16)

    loop(4, body)


def first_kernel(
    win_ref, wout_ref, wexp_ref, wcon_ref, tok_ref, raw_ref, starts_ref, cosine_ref, sine_ref,
    in0, ff0, in1, ff1, tok, vectors, ib_ref, eb_ref, task_ref, one_ref, right_ref, left_ref,
    normed, inverse, first, second, kv_out, q_out, inner, activated,
    here, send_a, recv_a, send_t, recv_t, send_p, recv_p, send_v, recv_v, send_g, recv_g, send_x, recv_x,
    wff_ref, par_ref, trig_ref, column_p, joined, plane_p, column_t, pairs, q_rows, q_parts,
):
    where = y, x, z, core = place()
    seq, tp = lax.div(y, 2), lax.rem(y, 2)
    mine, chip = seq * 2 + core, x * 4 + z
    column, plane = column_partners(y, x, z, core), plane_partners(y, x, z, core)
    for layer in range(LAYERS):
        for k in range(4):
            wff_ref[layer, k, :, 0:WOUT] = wout_ref[layer, :, k * WOUT : (k + 1) * WOUT]
            wff_ref[layer, k, :, WOUT : WOUT + WFF] = wexp_ref[layer, :, k * WFF : (k + 1) * WFF]
            wff_ref[layer, k, :, WOUT + WFF :] = wcon_ref[layer, :, k * WFF : (k + 1) * WFF]
    raw = raw_ref[...]
    line = lax.broadcasted_iota(jnp.int32, raw.shape, 0)
    lane = lax.broadcasted_iota(jnp.int32, raw.shape, 1)
    moved = jnp.where(
        line < 18,
        pltpu.roll(raw, (z * 4 + core * 2 + tp) * 8, 1),
        pltpu.roll(raw, (core * 2 + tp) * 32, 1),
    )
    rank = raw[20:21, 0:1]
    here_only = (lane == chip * 2 + core) & (tp == 0)
    par_ref[...] = jnp.where(line == 20, jnp.where(here_only, rank, 0.0), moved)
    trig_ref[...] = jnp.zeros((8, 128), F32)
    for k in range(2):
        starts = starts_ref[k]
        chosen = lax.broadcasted_iota(jnp.int32, starts.shape, 0).astype(F32) == rank
        trig_ref[k : k + 1, :] = jnp.sum(jnp.where(chosen, starts, 0.0), axis=0, keepdims=True)
    enter(column + plane)

    quarter = pl.ds(pl.multiple_of(core * 16, 16), 16)
    peers = [peer_at(y, x, z, core, step) for step in PEERS]
    local_copies, arriving = [], []

    def share(slot, source, target):
        copies = [
            remote(source(theirs), target, send_a.at[slot, k], recv_a.at[slot, k], device_id)
            for k, (theirs, device_id) in enumerate(peers)
        ]
        own = pltpu.make_async_copy(source(mine), target, here.at[slot])
        for copy in (*copies, own):
            copy.start()
        local_copies.append(own)
        arriving.append(copies)

    def landed(slot):
        for copy in arriving[slot]:
            copy.wait_recv()
        local_copies[slot].wait()

    tokens = RowShare(tok_ref, tok, where, send_t, recv_t)
    share(0, lambda q: win_ref.at[0, q], in0.at[seq, x, z, quarter])
    share(1, lambda q: wff_ref.at[0, q], ff0.at[seq, x, z, quarter])
    tokens.begin()
    smalls = [
        remote(par_ref, column_p.at[y * 2 + core], send_p.at[k], recv_p.at[k], peer)
        for k, peer in enumerate(column)
    ]
    for copy in smalls:
        copy.start()
    share(2, lambda q: trig_ref, column_t.at[mine])
    share(3, lambda q: win_ref.at[1, q], in1.at[seq, quarter])
    share(4, lambda q: wff_ref.at[1, q], ff1.at[seq, quarter])
    column_p[y * 2 + core] = par_ref[...]

    gathers = [
        Gather(ref, where, send_g.at[k], recv_g.at[k]) for k, ref in enumerate((in0, ff0))
    ]
    landed(0)
    gathers[0].begin()
    landed(1)
    gathers[1].begin()
    tokens.pass_on()
    for copy in smalls:
        copy.wait_recv()
    for half in range(2):
        joined[half] = jnp.sum(column_p[half * 4 : half * 4 + 4], axis=0)
    plane_p[chip] = joined[...]
    spread = [
        remote(joined, plane_p.at[chip], send_v.at[k], recv_v.at[k], peer)
        for k, peer in enumerate(plane)
    ]
    for copy in spread:
        copy.start()
    gathers[0].pass_on()
    tokens.end()
    normalize_rows(lambda index: tok[rows_at(index, 32), :].astype(F32), normed, inverse)
    gathers[0].turn()
    gathers[1].pass_on()
    landed(2)
    for r in range(4):
        rows = pl.ds(r * ROWS, ROWS)
        cos_a, sin_a = column_t[r, 0:1, :], column_t[r, 1:2, :]
        sine = sin_a * cosine_ref[...] + cos_a * sine_ref[...]
        lane = lax.broadcasted_iota(jnp.int32, sine.shape, 1) % HEAD_DIM
        one_ref[rows, :] = cos_a * cosine_ref[...] - sin_a * sine_ref[...]
        right_ref[rows, :] = jnp.where(lane < ROT // 2, -sine, 0.0)
        left_ref[rows, :] = jnp.where(lane < ROT // 2, 0.0, sine)
    for copy in spread:
        copy.wait_recv()
    for half in range(2):
        for across in range(4):
            at = (half * 4 + across) * 128
            block = jnp.sum(plane_p[across * 4 : across * 4 + 4, half], axis=0)
            vectors[:, at : at + 128] = block
    own = [plane_p[mine * 4 + k, tp] for k in range(4)]
    ib_ref[...] = (own[0] + own[1] + own[2] + own[3])[8:16]
    ranks = jnp.sum(plane_p[:, lax.div(x, 2), 16:24, :], axis=0)[4:5, :]
    spot = lax.broadcasted_iota(jnp.int32, ranks.shape, 1)
    task = jnp.where(spot == 32, z, ranks.astype(jnp.int32))
    task_ref[...] = jnp.broadcast_to(task, (8, 128))
    for k in range(4):
        eb_ref[:, k * 128 : (k + 1) * 128] = own[k][16:24]
    scale_rows(normed, vectors[0:1, :], vectors[4:5, :], first)
    gathers[0].pass_line()
    gathers[1].turn()
    scale_rows(normed, vectors[1:2, :], vectors[5:6, :], second)
    gathers[0].end()
    project(first, in0, ib_ref[0:3, :], (one_ref, right_ref, left_ref), pairs, q_rows)
    heads_to_chips(lambda s, c, k: q_rows[group_rows(s, c, k), :], q_parts)
    gathers[1].pass_line()
    exchanged = start_exchange(where, pairs, kv_out, True, send_x.at[0], recv_x.at[0])
    exchanged += start_exchange(where, q_parts, q_out, False, send_x.at[1], recv_x.at[1])
    gathers[1].end()
    expand(second, ff0, eb_ref[2:3, :], inner, activated)
    landed(3)
    landed(4)
    tokens.sent()
    for copies in arriving:
        for copy in copies:
            copy.wait_send()
    for copy in smalls + spread:
        copy.wait_send()
    for one in gathers:
        one.sent()
    for copy in exchanged:
        copy.wait()


def first_part(*operands):
    wide = WOUT + 2 * WFF
    outs = (
        bf(2, 4, 4, 32, WIN), bf(2, 4, 4, 32, wide), bf(2, 32, WIN), bf(2, 32, wide),
        bf(GROUP, D), f32(24, D), f32(8, 128), f32(8, WFF), jax.ShapeDtypeStruct((8, 128), jnp.int32),
        f32(GROUP, 128), f32(GROUP, 128), f32(GROUP, 128),
        f32(GROUP, D), f32(GROUP, 128), bf(GROUP, D), bf(GROUP, D),
        bf(16, 256, 128), bf(16, 32, 128), f32(GROUP, WFF), bf(GROUP, WFF),
    )
    scratch = [
        dma(5), dma(5, 3), dma(5, 3), dma(3), dma(3), dma(7), dma(7), dma(15), dma(15),
        dma(2, 16), dma(2, 16), dma(2, 15), dma(2, 15),
        vbf(2, 4, 16, wide), vf32(24, 128), vf32(8, 128),
        pltpu.VMEM((8, 24, 128), F32), pltpu.VMEM((2, 24, 128), F32),
        pltpu.VMEM((16, 2, 24, 128), F32), pltpu.VMEM((4, 8, 128), F32),
        pltpu.VMEM((4, 256, 128), BF16), pltpu.VMEM((GROUP, 128), F32),
        pltpu.VMEM((16, 32, 128), BF16),
    ]
    return kernel(first_kernel, 0, outs, scratch, "first_part", *operands)


def chips_to_heads(parts, target):
    def body(index):
        seq, quarter = lax.div(index, 4), lax.rem(index, 4)
        first = parts[seq * 8 + quarter].astype(F32)
        second = parts[seq * 8 + 4 + quarter].astype(F32)
        low = low_lanes(first.shape)
        target(seq, 0, quarter, jnp.where(low, first, swap(second)))
        target(seq, 1, quarter, jnp.where(low, swap(first), second))

    loop(8, body)


def block_of(index):
    return lax.div(index, 2), lax.rem(index, 2)


def contract(activated, ff, z):
    whole = ff[:, :, :, :, WOUT + WFF :].reshape(D, WFF)

    def body(index):
        rows = rows_at(index, 128)
        z[rows, :] = lax.dot_general(
            activated[rows, :], whole, (((1,), (1,)), ((), ())), preferred_element_type=F32
        )

    loop(4, body)


def add_mixed(mixed, weight, z, part):
    def body(index):
        rows = rows_at(index, 128)
        both = z[rows, :] + lax.dot_general(
            mixed[rows, :], weight, (((1,), (1,)), ((), ())), preferred_element_type=F32
        )
        seq, core = block_of(index)
        part[seq, core] = both.astype(BF16).reshape(2, 64, D)

    loop(4, body)


def rows32(summed, index):
    seq, core, tp = lax.div(index, 8), lax.rem(lax.div(index, 4), 2), lax.rem(lax.div(index, 2), 2)
    return summed[seq, core, tp, rows_at(lax.rem(index, 2), 32), :].astype(F32)


def output_weight_of(ff):
    return ff[:, :, :, :, :WOUT].reshape(D, WOUT)


def mix_back(dz, weight, rows128):
    def body(index):
        rows = rows_at(index, 128)
        dm = jnp.dot(dz(rows), weight, preferred_element_type=F32)
        rows128[rows, :] = dm.astype(BF16).astype(F32)

    loop(4, body)


def expand_back(dz, ff, inner, de, da, sums):
    up = ff[:, :, :, :, WOUT : WOUT + WFF].reshape(D, WFF)
    down = ff[:, :, :, :, WOUT + WFF :].reshape(D, WFF)
    sums[0:1, :] = jnp.zeros((1, WFF), F32)

    def body(index):
        rows = rows_at(index, 128)
        dg = jnp.dot(dz(rows), down, preferred_element_type=F32)
        e = inner[rows, :]
        slope = gelu_parts(e) + e * jnp.exp(-0.5 * e * e) * ((2.0 * jnp.pi) ** -0.5)
        low = (dg * slope).astype(BF16)
        de[rows, :] = low
        sums[0:1, :] += jnp.sum(low.astype(F32), axis=0, keepdims=True)
        da[rows, :] = lax.dot_general(
            low, up, (((1,), (1,)), ((), ())), preferred_element_type=F32
        )

    loop(4, body)


def weight_grad(left, right, dw, first, count):
    def body(index):
        block = lax.dot_general(
            left[:, rows_at(index, 256)],
            right[...],
            (((0,), (0,)), ((), ())),
            preferred_element_type=F32,
        )
        two = pl.ds(lax.rem(index, 2) * 2, 2)
        dw[lax.div(index, 2), two, :, :, first : first + count] = block.astype(BF16).reshape(
            2, 4, 32, count
        )

    loop(4, body)


def project_back(pairs, q_grad, tables, du, sums):
    sums[...] = jnp.zeros(sums.shape, F32)

    def body(index):
        seq, core = block_of(index)
        part = rows_at(core, 128)
        heads = []
        for head in range(2):
            total = pairs[seq * 8 + head * 4, part, :].astype(F32)
            for k in range(1, 4):
                total = total + pairs[seq * 8 + head * 4 + k, part, :].astype(F32)
            heads.append(total)
        low = low_lanes(heads[0].shape)
        rows = rows_at(index, 128)
        turn = tuple(t[rows, :] for t in tables)
        grads = (
            turned(q_grad[rows, :], turn, -1.0),
            turned(jnp.where(low, heads[0], swap(heads[1])), turn, -1.0),
            jnp.where(low, swap(heads[0]), heads[1]),
        )
        for k in range(3):
            rounded = grads[k].astype(BF16)
            du[rows, k * 128 : (k + 1) * 128] = rounded
            sums[k : k + 1, :] += jnp.sum(rounded.astype(F32), axis=0, keepdims=True)

    loop(4, body)


def join_back(du, weight, da2, normed, gain1, gain2, sums, part):
    whole = weight[...].reshape(D, WIN)
    sums[...] = jnp.zeros(sums.shape, F32)

    def body(index):
        rows = rows_at(index, 64)
        da = lax.dot_general(
            du[rows, :], whole, (((1,), (1,)), ((), ())), preferred_element_type=F32
        )
        db = da2[rows, :]
        n = normed[rows, :]
        for k, value in enumerate((da * n, db * n, da, db)):
            sums[k : k + 1, :] += jnp.sum(value, axis=0, keepdims=True)
        seq, core, tp = lax.div(index, 4), lax.rem(lax.div(index, 2), 2), lax.rem(index, 2)
        part[seq, core, tp] = (da * gain1 + db * gain2).astype(BF16)

    loop(8, body)


def norm_back(scaled, normed, inverse):
    first = jnp.mean(scaled, axis=1, keepdims=True)
    second = jnp.mean(scaled * normed, axis=1, keepdims=True)
    return inverse * (scaled - first - normed * second)


def second_kernel(
    m_ref, ff0, act0, tok, vectors, ib_ref, eb_ref, one_ref, right_ref, left_ref, in_own, ff_own, cot_ref,
    in1, ff1, cot, mixed, own_hidden, normed, inverse, first, second, kv_out, q_out, dm_out, inner, activated,
    m_back, z, part, summed, pairs, q_rows, q_parts, dm_rows, dm_parts,
    send_m, recv_m, send_g, recv_g, send_x, recv_x, send_c, recv_c, *column_scratch,
):
    where = y, x, z_at, core = place()
    seq = lax.div(y, 2)
    enter(column_partners(*where) + plane_partners(*where))
    returned = start_exchange(where, m_ref, m_back, False, send_m, recv_m)
    in1[0, x, z_at], in1[1, x, z_at] = in_own[0], in_own[1]
    ff1[0, x, z_at], ff1[1, x, z_at] = ff_own[0], ff_own[1]
    gathers = [Gather(ref, where, send_g.at[k], recv_g.at[k]) for k, ref in enumerate((in1, ff1))]
    gathers[0].begin()
    gathers[1].begin()
    cots = RowShare(cot_ref, cot, where, send_c, recv_c)
    cots.begin()
    contract(act0, ff0, z)
    for copy in returned:
        copy.wait_recv()
    gathers[0].pass_on()
    cots.pass_on()

    def keep(s, c, k, values):
        mixed[group_rows(s, c, k), :] = values.astype(BF16)

    chips_to_heads(m_back, keep)
    add_mixed(mixed, output_weight_of(ff0), z, part)
    total = ColumnSum(part, summed, where, True, column_scratch)
    total.begin()
    total.cross()
    gathers[0].turn()
    gathers[1].pass_on()
    total.combine()
    gathers[0].pass_line()
    gathers[1].turn()
    total.relay()
    gathers[0].end()
    gathers[1].pass_line()
    total.end()
    shift = vectors[14:15, :] + vectors[15:16, :]

    def hidden(index):
        rows = rows_at(index, 32)
        return tok[rows, :].astype(F32) + rows32(summed, index) + shift

    normalize_rows(hidden, normed, inverse)
    own = (seq * 2 + core) * 4

    def keep_own(index):
        own_hidden[rows_at(index, 32), :] = hidden(own + index)

    scale_rows(normed, vectors[2:3, :], vectors[6:7, :], first)
    project(first, in1, ib_ref[3:6, :], (one_ref, right_ref, left_ref), pairs, q_rows)
    heads_to_chips(lambda s, c, k: q_rows[group_rows(s, c, k), :], q_parts)
    exchanged = start_exchange(where, pairs, kv_out, True, send_x.at[0], recv_x.at[0])
    exchanged += start_exchange(where, q_parts, q_out, False, send_x.at[1], recv_x.at[1])
    cots.end()
    gathers[1].end()
    mix_back(lambda rows: cot[rows, :], output_weight_of(ff1), dm_rows)
    heads_to_chips(lambda s, c, k: dm_rows[group_rows(s, c, k), :], dm_parts)
    exchanged += start_exchange(where, dm_parts, dm_out, False, send_x.at[2], recv_x.at[2])
    loop(4, keep_own)
    scale_rows(normed, vectors[3:4, :], vectors[7:8, :], second)
    expand(second, ff1, eb_ref[3:4, :], inner, activated)
    total.sent()
    cots.sent()
    for copy in returned:
        copy.wait_send()
    for one in gathers:
        one.sent()
    for copy in exchanged:
        copy.wait()


def second_part(*operands):
    wide = WOUT + 2 * WFF
    outs = (
        bf(2, 4, 4, 32, WIN), bf(2, 4, 4, 32, wide), bf(GROUP, D), bf(GROUP, 128), f32(ROWS, D),
        f32(GROUP, D), f32(GROUP, 128), bf(GROUP, D), bf(GROUP, D),
        bf(16, 256, 128), bf(16, 32, 128), bf(16, 32, 128), f32(GROUP, WFF), bf(GROUP, WFF),
    )
    scratch = [
        vbf(16, 32, 128), vf32(GROUP, D), vbf(2, 2, 2, 64, D), vbf(2, 2, 2, 64, D),
        vbf(4, 256, 128), vf32(GROUP, 128), vbf(16, 32, 128), vf32(GROUP, 128), vbf(16, 32, 128),
        dma(15), dma(15), dma(2, 16), dma(2, 16), dma(3, 15), dma(3, 15), dma(3), dma(3),
        *ColumnSum.SCRATCH,
    ]
    return kernel(second_kernel, 1, outs, scratch, "second_part", *operands)


def third_kernel(
    m_ref, pair_ref, q_ref, cot, in1, ff1, wout0, vectors, one_ref, right_ref, left_ref,
    normed, inverse, first, second, inner, activated, own_hidden,
    act_out, grad, dm_out, out_in, out_ff, sums, ib_sums, eb_sums,
    m_back, pair_back, q_back, mixed, z, de, da2, du, q_grad, part, part2, summed, summed2,
    dw_in, dw_ff, dm_rows, dm_parts, dz,
    send_x, recv_x, *rest,
):
    where = y, x, z_at, core = place()
    tp = lax.rem(y, 2)
    enter(column_partners(*where) + plane_partners(*where))
    returned = [
        start_exchange(where, source, target, False, send_x.at[k], recv_x.at[k])
        for k, (source, target) in enumerate(((m_ref, m_back), (q_ref, q_back), (pair_ref, pair_back)))
    ]
    n_column = len(ColumnSum.SCRATCH)
    total1 = ColumnSum(part, summed, where, False, rest[:n_column])
    total2 = ColumnSum(part2, summed2, where, True, rest[n_column : 2 * n_column])
    rest = rest[2 * n_column :]
    scatter_ff = Scatter(dw_ff, out_ff, where, rest[: len(rest) // 2])
    scatter_in = Scatter(dw_in, out_in, where, rest[len(rest) // 2 :])

    expand_back(lambda rows: cot[rows, :], ff1, inner, de, da2, eb_sums)
    weight_grad(second, de, dw_ff, WOUT, WFF)
    for copy in returned[0]:
        copy.wait_recv()

    def keep(s, c, k, values):
        mixed[group_rows(s, c, k), :] = values.astype(BF16)

    chips_to_heads(m_back, keep)
    weight_grad(cot, mixed, dw_ff, 0, WOUT)
    weight_grad(cot, activated, dw_ff, WOUT + WFF, WFF)
    scatter_ff.begin()
    contract(activated, ff1, z)
    add_mixed(mixed, output_weight_of(ff1), z, part)
    total1.begin()
    for copies in returned[1:]:
        for copy in copies:
            copy.wait_recv()

    def keep_q(s, c, k, values):
        q_grad[group_rows(s, c, k), :] = values

    chips_to_heads(q_back, keep_q)
    project_back(pair_back, q_grad, (one_ref, right_ref, left_ref), du, ib_sums)
    join_back(du, in1, da2, normed, vectors[2:3, :], vectors[3:4, :], sums.at[pl.ds(0, 8)], part2)
    total2.begin()
    total2.cross()
    scatter_ff.pass_on()
    total1.cross()
    weight_grad(first, du, dw_in, 0, WIN)
    total2.combine()
    scatter_in.begin()
    scatter_ff.turn()
    total2.relay()
    scatter_in.pass_on()
    total1.combine()
    scatter_ff.pass_line()
    total2.end()
    sums[8:16, :] = jnp.zeros((8, D), F32)

    def put(index):
        rows = rows_at(index, 32)
        before = cot[rows, :].astype(F32)
        sums[8:9, :] += jnp.sum(before, axis=0, keepdims=True)
        after = before + norm_back(rows32(summed2, index), normed[rows, :], inverse[rows, 0:1])
        grad[rows, :] = after
        dz[rows, :] = after.astype(BF16)

    loop(16, put)
    mix_back(lambda rows: dz[rows, :], wout0[...], dm_rows)
    heads_to_chips(lambda s, c, k: dm_rows[group_rows(s, c, k), :], dm_parts)
    exchanged = start_exchange(where, dm_parts, dm_out, False, send_x.at[3], recv_x.at[3])
    scatter_in.turn()
    scatter_ff.deliver()
    total1.end()
    shift = vectors[16:17, :] + vectors[17:18, :]
    for k in range(2):
        rows = pl.ds(k * 64, 64)
        act_out[rows, :] = (own_hidden[rows, :] + summed[k].astype(F32) + shift).astype(BF16)
    scatter_in.pass_line()
    scatter_in.deliver()
    scatter_ff.end()
    scatter_in.end()
    total1.sent()
    total2.sent()
    for copies in returned:
        for copy in copies:
            copy.wait_send()
    for copy in exchanged:
        copy.wait()


def third_part(*operands):
    wide = WOUT + 2 * WFF
    outs = (
        bf(ROWS, D), f32(GROUP, D), bf(16, 32, 128), bf(4, 16, WIN), bf(4, 16, wide),
        f32(16, D), f32(8, 128), f32(8, WFF),
    )
    scratch = [
        vbf(16, 32, 128), vbf(16, 256, 128), vbf(16, 32, 128), vbf(GROUP, 128), vf32(GROUP, D),
        vbf(GROUP, WFF), vf32(GROUP, D), vbf(GROUP, WIN), vf32(GROUP, 128),
        vbf(2, 2, 2, 64, D), vbf(2, 2, 2, 64, D), vbf(2, 64, D), vbf(2, 2, 2, 64, D),
        vbf(2, 4, 4, 32, WIN), vbf(2, 4, 4, 32, wide), vf32(GROUP, 128), vbf(16, 32, 128), vbf(GROUP, D),
        dma(4, 15), dma(4, 15), *ColumnSum.SCRATCH, *ColumnSum.SCRATCH,
        *Scatter.scratch(wide), *Scatter.scratch(WIN),
    ]
    return kernel(third_kernel, 2, outs, scratch, "third_part", *operands)


def fourth_kernel(
    pair_ref, q_ref, grad, in0, ff0, vectors, one_ref, right_ref, left_ref,
    normed, inverse, first, second, inner, activated, mixed, sums1, ib_sums1, eb_sums1,
    grad_out, out_in, out_ff, small_out,
    pair_back, q_back, de, da2, du, q_grad, part, summed, dw_in, dw_ff, dz, sums, ib_sums, eb_sums,
    small, gathered, total_s, others,
    send_x, recv_x, send_s, recv_s, send_t, recv_t, *rest,
):
    where = y, x, z_at, core = place()
    seq, tp = lax.div(y, 2), lax.rem(y, 2)
    mine, chip = seq * 2 + core, x * 4 + z_at
    column, plane = column_partners(*where), plane_partners(*where)
    enter(column + plane)
    returned = [
        start_exchange(where, source, target, False, send_x.at[k], recv_x.at[k])
        for k, (source, target) in enumerate(((q_ref, q_back), (pair_ref, pair_back)))
    ]
    n_column = len(ColumnSum.SCRATCH)
    total = ColumnSum(part, summed, where, False, rest[:n_column])
    rest = rest[n_column:]
    scatter_ff = Scatter(dw_ff, out_ff, where, rest[: len(rest) // 2])
    scatter_in = Scatter(dw_in, out_in, where, rest[len(rest) // 2 :])

    sums[...] = jnp.zeros(sums.shape, F32)

    def lower(index):
        rows = rows_at(index, 32)
        values = grad[rows, :]
        sums[8:9, :] += jnp.sum(values, axis=0, keepdims=True)
        dz[rows, :] = values.astype(BF16)

    loop(16, lower)
    expand_back(lambda rows: dz[rows, :], ff0, inner, de, da2, eb_sums)
    weight_grad(second, de, dw_ff, WOUT, WFF)
    weight_grad(dz, mixed, dw_ff, 0, WOUT)
    weight_grad(dz, activated, dw_ff, WOUT + WFF, WFF)
    scatter_ff.begin()
    for copies in returned:
        for copy in copies:
            copy.wait_recv()

    def keep_q(s, c, k, values):
        q_grad[group_rows(s, c, k), :] = values

    chips_to_heads(q_back, keep_q)
    project_back(pair_back, q_grad, (one_ref, right_ref, left_ref), du, ib_sums)
    scatter_ff.pass_on()
    join_back(du, in0, da2, normed, vectors[0:1, :], vectors[1:2, :], sums.at[pl.ds(0, 8)], part)
    total.begin()
    weight_grad(first, du, dw_in, 0, WIN)
    total.cross()
    scatter_in.begin()
    scatter_ff.turn()

    once = jnp.where(y * 2 + core == 0, 1.0, 0.0)
    for half in range(2):
        for across in range(4):
            lanes = slice((half * 4 + across) * 128, (half * 4 + across + 1) * 128)
            here = jnp.where((tp == half) & (mine == across), 1.0, 0.0)
            for chip_z in range(4):
                cut = slice(chip_z * 128, (chip_z + 1) * 128)
                at = across * 4 + chip_z
                pieces = [
                    sums[0:2, lanes], sums1[0:2, lanes], sums[2:4, lanes], sums1[2:4, lanes],
                    ib_sums[0:3, :] * here, ib_sums1[0:3, :] * here,
                    sums[8:9, lanes] * once, sums[8:9, lanes] * once,
                    sums1[8:9, lanes] * once, sums1[8:9, lanes] * once,
                    eb_sums[0:1, cut] * here, eb_sums1[0:1, cut] * here,
                ]
                row = 0
                for piece in pieces:
                    count = piece.shape[0]
                    small[at, half, row : row + count, :] = piece
                    row += count
                small[at, half, 20:24, :] = jnp.zeros((4, 128), F32)
    spread = []
    for k, (dx, dz_) in enumerate(STEPS):
        copy = remote(
            small.at[ring(x, dx) * 4 + ring(z_at, dz_)],
            gathered.at[k],
            send_s.at[k],
            recv_s.at[k],
            plane[k],
        )
        copy.start()
        spread.append(copy)
    total.combine()
    scatter_in.pass_on()
    scatter_ff.pass_line()
    for copy in spread:
        copy.wait_recv()
    total_s[...] = small[chip] + jnp.sum(gathered[...], axis=0)
    shared = []
    for k, peer in enumerate(column):
        copy = remote(total_s, others.at[k], send_t.at[k], recv_t.at[k], peer)
        copy.start()
        shared.append(copy)
    scatter_in.turn()
    total.end()
    own = mine * ROWS
    for k in range(4):
        rows = pl.ds(pl.multiple_of(own + k * 32, 32), 32)
        summed_rows = summed[k // 2, (k % 2) * 32 : (k % 2 + 1) * 32, :].astype(F32)
        grad_out[k * 32 : (k + 1) * 32, :] = grad[rows, :] + norm_back(
            summed_rows, normed[rows, :], inverse[rows, 0:1]
        )
    scatter_in.pass_line()
    scatter_ff.deliver()
    for copy in shared:
        copy.wait_recv()
    sums_here = total_s[...] + jnp.sum(others[...], axis=0)
    sums_here = jnp.where(seq == 0, sums_here[0], sums_here[1])
    line = lax.broadcasted_iota(jnp.int32, sums_here.shape, 0)
    small_out[...] = jnp.where(
        line < 18,
        pltpu.roll(sums_here, 128 - (z_at * 4 + core * 2 + tp) * 8, 1),
        pltpu.roll(sums_here, 128 - (core * 2 + tp) * 32, 1),
    )
    scatter_in.deliver()
    scatter_ff.end()
    scatter_in.end()
    total.sent()
    for copies in returned:
        for copy in copies:
            copy.wait_send()
    for copy in spread + shared:
        copy.wait_send()


def fourth_part(*operands):
    wide = WOUT + 2 * WFF
    outs = (f32(ROWS, D), bf(4, 16, WIN), bf(4, 16, wide), f32(24, 128))
    scratch = [
        vbf(16, 256, 128), vbf(16, 32, 128), vbf(GROUP, WFF), vf32(GROUP, D), vbf(GROUP, WIN),
        vf32(GROUP, 128), vbf(2, 2, 2, 64, D), vbf(2, 64, D), vbf(2, 4, 4, 32, WIN), vbf(2, 4, 4, 32, wide),
        vbf(GROUP, D), vf32(16, D), vf32(8, 128), vf32(8, WFF),
        vf32(16, 2, 24, 128), vf32(15, 2, 24, 128), vf32(2, 24, 128), vf32(7, 2, 24, 128),
        dma(2, 15), dma(2, 15), dma(15), dma(15), dma(7), dma(7), *ColumnSum.SCRATCH,
        *Scatter.scratch(wide), *Scatter.scratch(WIN),
    ]
    return kernel(fourth_kernel, 3, outs, scratch, "fourth_part", *operands)


TILE = 256
SPAN = 1024


def seen(quarter, tile):
    key = lax.broadcasted_iota(jnp.int32, (SPAN, TILE), 0)
    row = lax.broadcasted_iota(jnp.int32, (SPAN, TILE), 1)
    place_of = (row // 32) * ROWS + quarter * 32 + row % 32
    return key <= place_of


def score_span(quarter, tile, span, queries, kvs):
    block = lax.dot_general(
        kvs[span * SPAN : (span + 1) * SPAN, :],
        queries,
        (((1,), (1,)), ((), ())),
        preferred_element_type=F32,
    )
    return jnp.where(seen(quarter, tile), block, MASKED) if span == tile else block


def forward_tile(quarter, tile, queries, kvs, kvt, score):
    highest = jnp.full((1, TILE), MASKED, F32)
    for span in range(tile + 1):
        block = score_span(quarter, tile, span, queries, kvs)
        score[span * SPAN : (span + 1) * SPAN, :] = block
        highest = jnp.maximum(highest, jnp.max(block, axis=0, keepdims=True))
    total = jnp.zeros((1, TILE), F32)
    mixed = jnp.zeros((128, TILE), F32)
    for span in range(tile + 1):
        weight = jnp.exp(score[span * SPAN : (span + 1) * SPAN, :] - highest)
        total = total + jnp.sum(weight, axis=0, keepdims=True)
        mixed = mixed + jnp.dot(
            kvt[:, span * SPAN : (span + 1) * SPAN],
            weight.astype(BF16),
            preferred_element_type=F32,
        )
    return mixed / total, highest + jnp.log(total)


def backward_span(tile, span, block, lse, delta, queries, outs, kvs, kvt, acc):
    keyed = kvs[span * SPAN : (span + 1) * SPAN, :]
    probs = jnp.exp(block - lse)
    back = lax.dot_general(keyed, outs, (((1,), (1,)), ((), ())), preferred_element_type=F32)
    score_grad = (probs * (back - delta)).astype(BF16)
    pair = jnp.dot(
        jnp.concatenate([score_grad, probs.astype(BF16)], axis=1),
        jnp.concatenate([queries, outs], axis=0),
        preferred_element_type=F32,
    )
    if span == tile:
        acc[span * SPAN : (span + 1) * SPAN, :] = pair
    else:
        acc[span * SPAN : (span + 1) * SPAN, :] += pair
    return jnp.dot(
        kvt[:, span * SPAN : (span + 1) * SPAN], score_grad, preferred_element_type=F32
    )


def put_back_rows(rank_ref, rows, target, upper):
    lane = lax.broadcasted_iota(jnp.int32, (32, 128), 1)

    def put_back(chip, carry):
        first = rows[pl.ds(pl.multiple_of(rank_ref[0, chip * 2] * 32, 32), 32), :]
        second = rows[pl.ds(pl.multiple_of(rank_ref[0, chip * 2 + 1] * 32, 32), 32), :]
        if upper:
            first = pltpu.roll(first, 64, 1)
        else:
            second = pltpu.roll(second, 64, 1)
        target[chip] = jnp.where(lane < 64, first, second).astype(BF16)
        return carry

    lax.fori_loop(0, 16, put_back, 0)


def put_back_pairs(rank_ref, acc, target):
    def put_back(chip, carry):
        for core in range(2):
            rank = rank_ref[0, chip * 2 + core]
            target[chip, core] = acc[pl.ds(pl.multiple_of(rank * ROWS, ROWS), ROWS), :].astype(BF16)
        return carry

    lax.fori_loop(0, 16, put_back, 0)


def attend_kernel(rank_ref, kv_ref, q_ref, m_ref, kvs_ref, kvt_ref, qs_ref, o_ref, lse_ref, score, rows):
    quarter = rank_ref[0, 32]
    lane = lax.broadcasted_iota(jnp.int32, (32, 128), 1)

    def arrange(chip, carry):
        block = q_ref[chip].astype(F32) * (HEAD_DIM**-0.5)
        for core in range(2):
            rank = rank_ref[0, chip * 2 + core]
            keyed = kv_ref[chip * 2 + core]
            kvs_ref[pl.ds(pl.multiple_of(rank * ROWS, ROWS), ROWS), :] = keyed
            kvt_ref[:, rows_at(rank, ROWS)] = keyed.astype(F32).T.astype(BF16)
            part = block if core == 0 else pltpu.roll(block, 64, 1)
            qs_ref[pl.ds(pl.multiple_of(rank * 32, 32), 32), :] = jnp.where(
                lane < 64, part, 0.0
            ).astype(BF16)
        return carry

    lax.fori_loop(0, 16, arrange, 0)

    for tile in range(4):
        queries = qs_ref[tile * TILE : (tile + 1) * TILE, :]
        mixed, lse = forward_tile(quarter, tile, queries, kvs_ref, kvt_ref, score)
        lse_ref[tile] = jnp.broadcast_to(lse, (8, TILE))
        o_ref[tile] = mixed
        rows[tile * TILE : (tile + 1) * TILE, :] = mixed.T

    put_back_rows(rank_ref, rows, m_ref, 1)


def attend(rank, kv, q):
    return pl.pallas_call(
        attend_kernel,
        out_shape=(
            jax.ShapeDtypeStruct((16, 32, 128), BF16),
            jax.ShapeDtypeStruct((4096, 128), BF16),
            jax.ShapeDtypeStruct((128, 4096), BF16),
            jax.ShapeDtypeStruct((1024, 128), BF16),
            jax.ShapeDtypeStruct((4, 128, TILE), F32),
            jax.ShapeDtypeStruct((4, 8, TILE), F32),
        ),
        in_specs=[SMEM, VMEM, VMEM],
        out_specs=tuple([VMEM] * 6),
        scratch_shapes=[pltpu.VMEM((4096, TILE), F32), pltpu.VMEM((1024, 128), F32)],
        compiler_params=pltpu.CompilerParams(vmem_limit_bytes=ATTEND_LIMIT),
        name="attend",
    )(rank, kv, q)


def attend_back_kernel(
    rank_ref, kvs_ref, kvt_ref, qs_ref, o_ref, lse_ref, dm_ref, dkv_ref, dq_ref, dos, acc, dqs
):
    quarter = rank_ref[0, 32]
    lane = lax.broadcasted_iota(jnp.int32, (32, 128), 1)

    def arrange(chip, carry):
        block = dm_ref[chip].astype(F32)
        for core in range(2):
            rank = rank_ref[0, chip * 2 + core]
            part = pltpu.roll(block, 64, 1) if core == 0 else block
            dos[pl.ds(pl.multiple_of(rank * 32, 32), 32), :] = jnp.where(
                lane < 64, 0.0, part
            ).astype(BF16)
        return carry

    lax.fori_loop(0, 16, arrange, 0)

    for tile in range(4):
        queries = qs_ref[tile * TILE : (tile + 1) * TILE, :]
        outs = dos[tile * TILE : (tile + 1) * TILE, :]
        delta = jnp.sum(outs.astype(F32).T * o_ref[tile], axis=0, keepdims=True)
        lse = lse_ref[tile][0:1, :]
        query_grad = jnp.zeros((128, TILE), F32)
        for span in range(tile + 1):
            block = score_span(quarter, tile, span, queries, kvs_ref)
            query_grad = query_grad + backward_span(
                tile, span, block, lse, delta, queries, outs, kvs_ref, kvt_ref, acc
            )
        dqs[tile * TILE : (tile + 1) * TILE, :] = query_grad.T * (HEAD_DIM**-0.5)

    put_back_rows(rank_ref, dqs, dq_ref, 0)
    put_back_pairs(rank_ref, acc, dkv_ref)


def attend_back(rank, kvs, kvt, qs, o, lse, dm):
    return pl.pallas_call(
        attend_back_kernel,
        out_shape=(
            jax.ShapeDtypeStruct((16, 2, 128, 128), BF16),
            jax.ShapeDtypeStruct((16, 32, 128), BF16),
        ),
        in_specs=[SMEM] + [VMEM] * 6,
        out_specs=tuple([VMEM] * 2),
        scratch_shapes=[
            pltpu.VMEM((1024, 128), BF16),
            pltpu.VMEM((4096, 128), F32),
            pltpu.VMEM((1024, 128), F32),
        ],
        compiler_params=pltpu.CompilerParams(vmem_limit_bytes=ATTEND_LIMIT),
        name="attend_back",
    )(rank, kvs, kvt, qs, o, lse, dm)


def attend_both_kernel(
    rank_ref, kv_ref, q_ref, dm_ref, m_ref, dkv_ref, dq_ref, kvs, kvt, qs, dos, score, rows, acc, dqs
):
    quarter = rank_ref[0, 32]
    lane = lax.broadcasted_iota(jnp.int32, (32, 128), 1)

    def arrange(chip, carry):
        block = q_ref[chip].astype(F32) * (HEAD_DIM**-0.5)
        back = dm_ref[chip].astype(F32)
        for core in range(2):
            rank = rank_ref[0, chip * 2 + core]
            keyed = kv_ref[chip * 2 + core]
            kvs[pl.ds(pl.multiple_of(rank * ROWS, ROWS), ROWS), :] = keyed
            kvt[:, rows_at(rank, ROWS)] = keyed.astype(F32).T.astype(BF16)
            at = pl.ds(pl.multiple_of(rank * 32, 32), 32)
            part = block if core == 0 else pltpu.roll(block, 64, 1)
            qs[at, :] = jnp.where(lane < 64, part, 0.0).astype(BF16)
            part = pltpu.roll(back, 64, 1) if core == 0 else back
            dos[at, :] = jnp.where(lane < 64, 0.0, part).astype(BF16)
        return carry

    lax.fori_loop(0, 16, arrange, 0)

    for tile in range(4):
        queries = qs[tile * TILE : (tile + 1) * TILE, :]
        outs = dos[tile * TILE : (tile + 1) * TILE, :]
        mixed, lse = forward_tile(quarter, tile, queries, kvs, kvt, score)
        rows[tile * TILE : (tile + 1) * TILE, :] = mixed.T
        delta = jnp.sum(outs.astype(F32).T * mixed, axis=0, keepdims=True)
        query_grad = jnp.zeros((128, TILE), F32)
        for span in range(tile + 1):
            block = score[span * SPAN : (span + 1) * SPAN, :]
            query_grad = query_grad + backward_span(
                tile, span, block, lse, delta, queries, outs, kvs, kvt, acc
            )
        dqs[tile * TILE : (tile + 1) * TILE, :] = query_grad.T * (HEAD_DIM**-0.5)

    put_back_rows(rank_ref, rows, m_ref, 1)
    put_back_rows(rank_ref, dqs, dq_ref, 0)
    put_back_pairs(rank_ref, acc, dkv_ref)


def attend_both(rank, kv, q, dm):
    return pl.pallas_call(
        attend_both_kernel,
        out_shape=(bf(16, 32, 128), bf(16, 2, 128, 128), bf(16, 32, 128)),
        in_specs=[SMEM] + [VMEM] * 3,
        out_specs=(VMEM,) * 3,
        scratch_shapes=[
            vbf(4096, 128), vbf(128, 4096), vbf(1024, 128), vbf(1024, 128),
            vf32(4096, TILE), vf32(1024, 128), vf32(4096, 128), vf32(1024, 128),
        ],
        compiler_params=pltpu.CompilerParams(vmem_limit_bytes=ATTEND_LIMIT),
        name="attend_both",
    )(rank, kv, q, dm)


def outputs_kernel(
    in0, in1, ff0, ff1, small, input_out, output_out, expand_out, contract_out,
    gain_out, shift_out, input_shift_out, output_shift_out, expand_shift_out,
):
    for layer, (ins, ffs) in enumerate(((in0, ff0), (in1, ff1))):
        for k in range(4):
            part = ins[k].astype(F32)
            for t in range(3):
                at = t * 512 + k * 128
                input_out[layer, :, at : at + 128] = part[:, t * 128 : (t + 1) * 128]
            part = ffs[k].astype(F32)
            output_out[layer, :, k * WOUT : (k + 1) * WOUT] = part[:, :WOUT]
            expand_out[layer, :, k * WFF : (k + 1) * WFF] = part[:, WOUT : WOUT + WFF]
            contract_out[layer, :, k * WFF : (k + 1) * WFF] = part[:, WOUT + WFF :]
        for k in range(2):
            row = layer * 2 + k
            gain_out[layer, k : k + 1, :] = small[row : row + 1, 0:8]
            shift_out[layer, k : k + 1, :] = small[row + 4 : row + 5, 0:8]
            output_shift_out[layer, k : k + 1, :] = small[row + 14 : row + 15, 0:8]
        input_shift_out[layer] = small[8 + layer * 3 : 11 + layer * 3, 0:8]
    expand_shift_out[...] = small[18:20, 0:32]


def outputs(*operands):
    outs = (
        f32(2, 16, 1536), f32(2, 16, 512), f32(2, 16, 2048), f32(2, 16, 2048),
        f32(2, 2, 8), f32(2, 2, 8), f32(2, 3, 8), f32(2, 2, 8), f32(2, 32),
    )
    return pl.pallas_call(
        outputs_kernel,
        out_shape=outs,
        in_specs=[VMEM] * len(operands),
        out_specs=(VMEM,) * len(outs),
        compiler_params=pltpu.CompilerParams(vmem_limit_bytes=8 * MIB),
        name="outputs",
    )(*operands)


def rotary_tables():
    half = ROT // 2
    freqs = 10000.0 ** (-(np.arange(half) * 2.0 / ROT))
    lane = np.arange(128) % HEAD_DIM
    every = np.where(lane < ROT, np.tile(freqs, 128 // half), 0.0)[None, :]
    start = np.arange(32)[:, None] * ROWS * every
    steps = np.arange(ROWS)[:, None] * every
    starts = np.stack([np.cos(start), np.sin(start)]).astype(np.float32)
    return starts, np.cos(steps).astype(np.float32), np.sin(steps).astype(np.float32)


def local(
    tokens, cotangent, group_order, input_weight, output_weight, expand_weight, contract_weight,
    norm_gain, norm_shift, input_bias, output_bias, expand_bias,
):
    win = input_weight.reshape(LAYERS, 16, 3, 4, 128).transpose(0, 3, 1, 2, 4)
    eights = [norm_gain, norm_shift, input_bias, output_bias]
    raw = jnp.concatenate(
        [
            jnp.pad(jnp.concatenate([v.reshape(-1, 8) for v in eights], axis=0), ((0, 0), (0, 120))),
            jnp.pad(expand_bias, ((0, 0), (0, 96))),
            jnp.broadcast_to(group_order.astype(F32), (4, 128)),
        ],
        axis=0,
    )
    (in0, ff0, in_own, ff_own, token_rows, vectors, ib, eb, task, one, right, left,
     normed0, inverse0, first0, second0, kv0, q0, inner0, activated0) = first_part(
        win.reshape(LAYERS, 4, 16, WIN), output_weight, expand_weight, contract_weight, tokens, raw,
        *rotary_tables(),
    )
    tables = (one, right, left)
    m0, kvs, kvt, qs, o, lse = attend(task, kv0.reshape(32, 128, 128), q0)
    (in1, ff1, cot, mixed0, own_hidden, normed1, inverse1, first1, second1, kv1, q1, dm1, inner1,
     activated1) = second_part(
        m0, ff0, activated0, token_rows, vectors, ib, eb, *tables, in_own, ff_own, cotangent
    )
    m1, pair1, query1 = attend_both(task, kv1.reshape(32, 128, 128), q1, dm1)
    wout0 = ff0.reshape(D, -1)[:, :WOUT]
    activations, grad, dm0, in1_out, ff1_out, sums1, ib1, eb1 = third_part(
        m1, pair1.reshape(16, 256, 128), query1, cot, in1, ff1, wout0, vectors, *tables,
        normed1, inverse1, first1, second1, inner1, activated1, own_hidden,
    )
    pair0, query0 = attend_back(task, kvs, kvt, qs, o, lse, dm0)
    input_gradient, in0_out, ff0_out, small = fourth_part(
        pair0.reshape(16, 256, 128), query0, grad, in0, ff0, vectors, *tables,
        normed0, inverse0, first0, second0, inner0, activated0, mixed0, sums1, ib1, eb1,
    )

    input_out, *rest = outputs(in0_out, in1_out, ff0_out, ff1_out, small)
    return (activations, input_gradient, input_out.reshape(2, 16, 3, 512), *rest)


def solution(mesh):
    rows, columns = P(("seq", "ctx"), None), P(None, None, ("seq", "ctx", "tp"))
    weight, flat = P(None, ("seq", "ctx"), "tp"), P(None, ("seq", "ctx", "tp"))
    first = P(None, ("seq", "ctx"), None, "tp")
    outs = (rows, rows, first, weight, weight, weight, columns, columns, columns, columns, flat)
    return jax.shard_map(
        local,
        mesh=mesh,
        in_specs=(rows, rows, P("seq", "ctx"), *outs[2:]),
        out_specs=outs,
        check_vma=False,
    )
```

```python
import types

import jax
import jax.numpy as jnp
import numpy as np
from jax import lax
from jax.experimental import pallas as pl
from jax.experimental.pallas import tpu as pltpu
from jax.sharding import PartitionSpec as P

MESH = pl.DeviceIdType.MESH
F32, BF16 = jnp.float32, jnp.bfloat16
D, HEAD_DIM, ROT, LAYERS = 1024, 64, 16, 2
ROWS = 128
GROUP = 512
WIN, WOUT, WFF = 384, 128, 512
COLS = WIN + WOUT + 2 * WFF
PARAMS = 208
EPSILON = 1e-05
MASKED = -1e30
MIB = 1024 * 1024
LIMIT = 62
WIDE = WOUT + 2 * WFF
MESSAGE = 320


def place():
    ctx = lax.axis_index("ctx")
    chip = lax.div(ctx, 2)
    y = lax.axis_index("seq") * 2 + lax.axis_index("tp")
    return y, lax.div(chip, 4), lax.rem(chip, 4), lax.rem(ctx, 2)


def device(y, x, z, core):
    return (lax.div(y, 2), (x * 4 + z) * 2 + core, lax.rem(y, 2))


def ring(index, step):
    return lax.rem(index + step, 4)


def enter(partners):
    barrier = pltpu.get_barrier_semaphore()
    for partner in partners:
        pl.semaphore_signal(barrier, inc=1, device_id=partner, device_id_type=MESH)
    pl.semaphore_wait(barrier, len(partners))


def plane_partners(y, x, z, core):
    return [
        device(y, ring(x, dx), ring(z, dz), core)
        for dx in range(4)
        for dz in range(4)
        if dx or dz
    ]


def column_partners(y, x, z, core):
    return [
        device(ring(y, dy), x, z, lax.rem(core + dc, 2))
        for dy in range(4)
        for dc in range(2)
        if dy or dc
    ]


def remote(source, target, send, receive, partner):
    return pltpu.make_async_remote_copy(
        src_ref=source,
        dst_ref=target,
        send_sem=send,
        recv_sem=receive,
        device_id=partner,
        device_id_type=MESH,
    )


HBM = pl.BlockSpec(memory_space=pl.ANY)
VMEM = pl.BlockSpec(memory_space=pltpu.VMEM)
SMEM = pl.BlockSpec(memory_space=pltpu.SMEM)


def bf(*shape):
    return jax.ShapeDtypeStruct(shape, BF16)


def f32(*shape):
    return jax.ShapeDtypeStruct(shape, F32)


def vbf(*shape):
    return pltpu.VMEM(shape, BF16)


def vf32(*shape):
    return pltpu.VMEM(shape, F32)


def dma(*shape):
    return pltpu.SemaphoreType.DMA(shape)


PEERS = ((0, 1), (1, 0), (1, 1))
STEPS = tuple((dx, dz) for dx in range(4) for dz in range(4) if dx or dz)


def peer_at(y, x, z, core, step):
    seq, tp = lax.div(y, 2), lax.rem(y, 2)
    seq_to, core_to = lax.rem(seq + step[0], 2), lax.rem(core + step[1], 2)
    return seq_to * 2 + core_to, device(seq_to * 2 + tp, x, z, core_to)


class Gather:
    def __init__(self, full, where, send, recv):
        y, x, z, core = where
        self.full, self.x, self.z, self.send, self.recv = full, x, z, send, recv
        self.near = {
            "x": (device(y, ring(x, 1), z, core), device(y, ring(x, 3), z, core)),
            "z": (device(y, x, ring(z, 1), core), device(y, x, ring(z, 3), core)),
        }
        self.held = [(), ()]
        self.started = []

    def go(self, source, slot, partner):
        copy = remote(source, source, self.send.at[slot], self.recv.at[slot], partner)
        copy.start()
        self.started.append(copy)
        return copy

    def begin(self):
        for half in range(2):
            up, down = self.near["xz"[half]]
            own = self.full.at[half, self.x, self.z]
            self.held[half] = (self.go(own, half * 8, up), self.go(own, half * 8 + 1, down))

    def arrive(self, half):
        for copy in self.held[half]:
            copy.wait_recv()

    def pass_on(self):
        x, z = self.x, self.z
        for half in range(2):
            self.arrive(half)
            up, down = self.near["xz"[half]]
            whole = self.full.at[half]
            if half == 0:
                before, after = whole.at[ring(x, 3), z], whole.at[ring(x, 1), z]
            else:
                before, after = whole.at[x, ring(z, 3)], whole.at[x, ring(z, 1)]
            self.held[half] = (
                self.go(before.at[pl.ds(0, 16)], half * 8 + 2, up),
                self.go(after.at[pl.ds(16, 16)], half * 8 + 3, down),
            )

    def turn(self):
        for half in range(2):
            self.arrive(half)
            up, down = self.near["zx"[half]]
            whole = self.full.at[half]
            line = whole.at[:, self.z] if half == 0 else whole.at[self.x]
            self.held[half] = (self.go(line, half * 8 + 4, up), self.go(line, half * 8 + 5, down))

    def pass_line(self):
        x, z = self.x, self.z
        two, more = pl.ds(0, 2), pl.ds(2, 2)
        for half in range(2):
            self.arrive(half)
            up, down = self.near["zx"[half]]
            whole = self.full.at[half]
            if half == 0:
                before, after = whole.at[two, ring(z, 3)], whole.at[more, ring(z, 1)]
            else:
                before, after = whole.at[ring(x, 3), two], whole.at[ring(x, 1), more]
            self.held[half] = (
                self.go(before, half * 8 + 6, up),
                self.go(after, half * 8 + 7, down),
            )

    def end(self):
        for half in range(2):
            self.arrive(half)

    def sent(self):
        for copy in self.started:
            copy.wait_send()


class RowShare:
    def __init__(self, source, target, where, send, recv):
        y, x, z, core = where
        self.source, self.target, self.send, self.recv = source, target, send, recv
        seq = lax.div(y, 2)
        self.own = rows_at(seq * 2 + core, ROWS)
        self.other = rows_at((1 - seq) * 2 + core, ROWS)
        self.sibling = device(y, x, z, lax.rem(core + 1, 2))
        self.facing = device(3 - y, x, z, core)
        self.copies = []

    def go(self, source, target, slot, partner):
        copy = remote(source, target, self.send.at[slot], self.recv.at[slot], partner)
        copy.start()
        self.copies.append(copy)

    def begin(self):
        self.target[self.own, :] = self.source[...]
        self.go(self.source, self.target.at[self.own], 0, self.facing)
        self.go(self.source, self.target.at[self.own], 1, self.sibling)

    def pass_on(self):
        self.copies[0].wait_recv()
        block = self.target.at[self.other]
        self.go(block, block, 2, self.sibling)

    def end(self):
        for copy in self.copies[1:]:
            copy.wait_recv()

    def sent(self):
        for copy in self.copies:
            copy.wait_send()


class ColumnSum:
    SCRATCH = [vbf(4, 64, D), vbf(3, 64, D), vbf(3, 64, D)] + [dma(4), dma(4), dma(3), dma(3), dma(7), dma(7)]
    ORDER = (2, 1, 3)

    def __init__(self, part, out, where, everywhere, scratch):
        self.part, self.out, self.where, self.everywhere = part, out, where, everywhere
        (self.near, self.far, self.held, self.send1, self.recv1, self.send2, self.recv2, self.send3, self.recv3) = scratch
        y, x, z, core = where
        self.sibling = device(y, x, z, lax.rem(core + 1, 2))
        self.chips = [device(ring(y, dy), x, z, core) for dy in (1, 2, 3)]

    def begin(self):
        y, x, z, core = self.where
        self.nears = {}
        for dy in (*self.ORDER, 0):
            to = ring(y, dy)
            source = self.part.at[lax.div(to, 2), lax.rem(core + 1, 2), lax.rem(to, 2)]
            self.nears[dy] = remote(
                source, self.near.at[dy], self.send1.at[dy], self.recv1.at[dy], self.sibling
            )
            self.nears[dy].start()

    def cross(self):
        y, x, z, core = self.where
        self.fars = []
        for dy in self.ORDER:
            to = ring(y, dy)
            self.nears[dy].wait_recv()
            own = self.part[lax.div(to, 2), core, lax.rem(to, 2)].astype(F32)
            self.held[dy - 1] = (own + self.near[dy].astype(F32)).astype(BF16)
            copy = remote(
                self.held.at[dy - 1],
                self.far.at[dy - 1],
                self.send2.at[dy - 1],
                self.recv2.at[dy - 1],
                self.chips[dy - 1],
            )
            copy.start()
            self.fars.append(copy)

    def combine(self):
        y, x, z, core = self.where
        seq, tp = lax.div(y, 2), lax.rem(y, 2)
        self.nears[0].wait_recv()
        total = self.part[seq, core, tp].astype(F32) + self.near[0].astype(F32)
        for copy in self.fars:
            copy.wait_recv()
        for k in range(3):
            total = total + self.far[k].astype(F32)
        self.outs, self.relayed = [], []
        own = self.out.at[seq, core, tp] if self.everywhere else self.out.at[tp]
        own[...] = total.astype(BF16)
        if self.everywhere:
            for dy in self.ORDER:
                self.go(self.outs, own, dy - 1, self.chips[dy - 1])
            self.go(self.relayed, own, 3, self.sibling)
        else:
            self.go(self.outs, own, 0, device(seq * 2 + lax.rem(tp + 1, 2), x, z, core))

    def go(self, kept, block, slot, partner):
        copy = remote(block, block, self.send3.at[slot], self.recv3.at[slot], partner)
        copy.start()
        kept.append(copy)

    def relay(self):
        y, x, z, core = self.where
        for at, dy in enumerate(self.ORDER):
            self.outs[at].wait_recv()
            source = ring(y, 4 - dy)
            block = self.out.at[lax.div(source, 2), core, lax.rem(source, 2)]
            self.go(self.relayed, block, 3 + dy, self.sibling)

    def end(self):
        if self.everywhere:
            for copy in self.relayed:
                copy.wait_recv()
        else:
            self.outs[0].wait_recv()

    def sent(self):
        for copy in (*self.nears.values(), *self.fars, *self.outs, *self.relayed):
            copy.wait_send()


class Scatter:
    def __init__(self, dw, out, where, scratch):
        y, x, z, core = where
        self.dw, self.out, self.where, self.x, self.z = dw, out, where, x, z
        (self.opp1, self.dir1, self.comb1, self.sent1, self.mid, self.opp2, self.dir2, self.comb2, self.sent2, self.done,
         self.send, self.recv, self.send_f, self.recv_f) = scratch
        self.near = {
            "x": (device(y, ring(x, 1), z, core), device(y, ring(x, 3), z, core)),
            "z": (device(y, x, ring(z, 1), core), device(y, x, ring(z, 3), core)),
        }
        self.started, self.held = [], [(), ()]

    @staticmethod
    def scratch(columns):
        big, small = vbf(2, 2, 2, 32, columns), vbf(2, 2, 16, columns)
        mid = vbf(2, 4, 32, columns)
        return [big] * 4 + [mid] + [small] * 5 + [dma(24), dma(24), dma(3), dma(3)]

    def go(self, source, target, slot, partner):
        copy = remote(source, target, self.send.at[slot], self.recv.at[slot], partner)
        copy.start()
        self.started.append(copy)
        return copy

    def part1(self, half, step, side):
        two = pl.ds(side * 2, 2)
        whole = self.dw.at[half]
        if half == 0:
            return whole.at[two, ring(self.z, step)]
        return whole.at[ring(self.x, step), two]

    def part2(self, half, step, side):
        at = ring(self.x, step) if half == 0 else ring(self.z, step)
        return self.mid.at[half, at].at[pl.ds(side * 16, 16)]

    def open(self, half, part, axis, opposite, direct, base):
        up, down = self.near[axis]
        self.held[half] = (
            self.go(part(half, 2, 0), opposite.at[half, 0], base, up),
            self.go(part(half, 2, 1), opposite.at[half, 1], base + 1, down),
            self.go(part(half, 1, 1), direct.at[half, 0], base + 2, up),
            self.go(part(half, 3, 0), direct.at[half, 1], base + 3, down),
        )

    def onward(self, half, part, axis, opposite, combined, sent, base):
        up, down = self.near[axis]
        copies = self.held[half]
        copies[0].wait_recv()
        sent[half, 0] = (part(half, 1, 0)[...].astype(F32) + opposite[half, 0].astype(F32)).astype(BF16)
        first = self.go(sent.at[half, 0], combined.at[half, 0], base + 4, up)
        copies[1].wait_recv()
        sent[half, 1] = (part(half, 3, 1)[...].astype(F32) + opposite[half, 1].astype(F32)).astype(BF16)
        second = self.go(sent.at[half, 1], combined.at[half, 1], base + 5, down)
        self.held[half] = (*copies[2:], first, second)

    def finish(self, half, part, direct, combined, target):
        for copy in self.held[half]:
            copy.wait_recv()
        for side in range(2):
            total = (
                part(half, 0, side)[...].astype(F32)
                + combined[half, side].astype(F32)
                + direct[half, 1 - side].astype(F32)
            )
            target(half, side)[...] = total.astype(BF16)

    def begin(self):
        for half in range(2):
            self.open(half, self.part1, "zx"[half], self.opp1, self.dir1, half * 12)

    def pass_on(self):
        for half in range(2):
            self.onward(half, self.part1, "zx"[half], self.opp1, self.comb1, self.sent1, half * 12)

    def turn(self):
        for half in range(2):
            self.finish(
                half,
                self.part1,
                self.dir1,
                self.comb1,
                lambda h, side: self.mid.at[h, pl.ds(side * 2, 2)],
            )
            self.open(half, self.part2, "xz"[half], self.opp2, self.dir2, half * 12 + 6)

    def pass_line(self):
        for half in range(2):
            self.onward(
                half, self.part2, "xz"[half], self.opp2, self.comb2, self.sent2, half * 12 + 6
            )

    def deliver(self):
        y, x, z, core = self.where
        seq = lax.div(y, 2)
        mine = seq * 2 + core
        for half in range(2):
            self.finish(
                half, self.part2, self.dir2, self.comb2, lambda h, side: self.done.at[h, side]
            )
        self.out[mine] = self.done[seq, core]
        self.final = []
        for k, step in enumerate(PEERS):
            theirs, peer = peer_at(y, x, z, core, step)
            copy = remote(
                self.done.at[lax.div(theirs, 2), lax.rem(theirs, 2)],
                self.out.at[mine],
                self.send_f.at[k],
                self.recv_f.at[k],
                peer,
            )
            copy.start()
            self.final.append(copy)

    def end(self):
        for copy in self.final:
            copy.wait()
        for copy in self.started:
            copy.wait_send()


class Exchange:
    def __init__(self, where, source, target, rows, send, recv):
        y, x, z, core = where
        chip = x * 4 + z
        cut = pl.ds(0, rows)
        target[chip, cut, :] = source[chip, cut, :]
        self.copies = []
        for k, (dx, dz) in enumerate(STEPS):
            to_x, to_z = ring(x, dx), ring(z, dz)
            copy = remote(
                source.at[to_x * 4 + to_z, cut],
                target.at[chip, cut],
                send.at[k],
                recv.at[k],
                device(y, to_x, to_z, core),
            )
            copy.start()
            self.copies.append(copy)

    def end(self):
        for copy in self.copies:
            copy.wait_recv()

    def sent(self):
        for copy in self.copies:
            copy.wait_send()


def loop(count, body):
    def step(index, carry):
        body(index)
        return carry

    lax.fori_loop(0, count, step, 0)


def rows_at(index, count):
    return pl.ds(pl.multiple_of(index * count, count), count)


def turned(values, tables, sign):
    one, right, left = tables
    half = ROT // 2
    return values * one + sign * (
        pltpu.roll(values, 128 - half, 1) * right + pltpu.roll(values, half, 1) * left
    )


def low_lanes(shape):
    return lax.broadcasted_iota(jnp.int32, shape, 1) < HEAD_DIM


def swap(values):
    return pltpu.roll(values, HEAD_DIM, 1)


def heads_to_chips(values, target):
    def body(index):
        seq, quarter = lax.div(index, 4), lax.rem(index, 4)
        first, second = values(seq, 0, quarter), values(seq, 1, quarter)
        low = low_lanes(first.shape)
        target(seq * 8 + quarter, jnp.where(low, first, swap(second)).astype(BF16))
        target(seq * 8 + 4 + quarter, jnp.where(low, swap(first), second).astype(BF16))

    loop(8, body)


def group_rows(seq, core, quarter):
    return pl.ds(pl.multiple_of(seq * 256 + core * 128 + quarter * 32, 32), 32)


def normalize_rows(hidden, normed, inverse):
    def body(index):
        rows = rows_at(index, 32)
        values = hidden(index)
        centred = values - jnp.mean(values, axis=1, keepdims=True)
        spread = jnp.mean(centred * centred, axis=1, keepdims=True)
        scale = lax.rsqrt(spread + EPSILON)
        normed[rows, :] = centred * scale
        inverse[rows, :] = jnp.broadcast_to(scale, (32, 128))

    loop(16, body)


def scale_rows(normed, gain, shift, target):
    def body(index):
        rows = rows_at(index, 32)
        target[rows, :] = (normed[rows, :] * gain + shift).astype(BF16)

    loop(16, body)


def project(first, weight, bias, tables, outbox, q_rows):
    whole = weight[...].reshape(D, WIN)

    def body(index):
        rows = rows_at(index, 128)
        u = jnp.dot(first[rows, :], whole, preferred_element_type=F32)
        turn = tuple(t[rows, :] for t in tables)
        q_rows[rows, :] = turned(u[:, :128] + bias[0:1, :], turn, 1.0)
        keys = turned(u[:, 128:256] + bias[1:2, :], turn, 1.0)
        values = u[:, 256:] + bias[2:3, :]
        low = low_lanes(keys.shape)
        seq = lax.div(index, 2)
        part = rows_at(lax.rem(index, 2), 128)
        for head in range(2):
            pair = (keys, swap(values)) if head == 0 else (swap(keys), values)
            pair = jnp.where(low, *pair).astype(BF16)
            for k in range(4):
                outbox[seq * 8 + head * 4 + k, part, :] = pair

    loop(4, body)


def gelu_parts(inner):
    return 0.5 * (1.0 + lax.erf(inner * (0.5**0.5)))


def expand(second, weight, bias, inner, activated):
    whole = weight[:, :, :, :, WOUT : WOUT + WFF].reshape(D, WFF)

    def body(index):
        rows = rows_at(index, 128)
        e = jnp.dot(second[rows, :], whole, preferred_element_type=F32) + bias
        inner[rows, :] = e
        activated[rows, :] = (e * gelu_parts(e)).astype(BF16)

    loop(4, body)


def chips_to_heads(parts, target):
    def body(index):
        seq, quarter = lax.div(index, 4), lax.rem(index, 4)
        first = parts(seq * 8 + quarter).astype(F32)
        second = parts(seq * 8 + 4 + quarter).astype(F32)
        low = low_lanes(first.shape)
        target(seq, 0, quarter, jnp.where(low, first, swap(second)))
        target(seq, 1, quarter, jnp.where(low, swap(first), second))

    loop(8, body)


def block_of(index):
    return lax.div(index, 2), lax.rem(index, 2)


class Wide:
    def __init__(self, buffer, base):
        self.buffer, self.base = buffer, base

    def at(self, start, count, k):
        return pl.ds(pl.multiple_of(self.base + k * GROUP + start, count), count)

    def put(self, start, count, values):
        for k in range(4):
            self.buffer[self.at(start, count, k), :] = values[:, k * 256 : (k + 1) * 256]

    def get(self, start, count):
        return jnp.concatenate([self.buffer[self.at(start, count, k), :] for k in range(4)], axis=1)


def contract(activated, ff, z):
    whole = ff[:, :, :, :, WOUT + WFF :].reshape(D, WFF)

    def body(index):
        rows = rows_at(index, 128)
        values = lax.dot_general(
            activated[rows, :], whole, (((1,), (1,)), ((), ())), preferred_element_type=F32
        )
        z.put(index * 128, 128, values)

    loop(4, body)


def add_mixed(mixed, weight, z, part):
    def body(index):
        rows = rows_at(index, 128)
        both = z.get(index * 128, 128) + lax.dot_general(
            mixed[rows, :], weight, (((1,), (1,)), ((), ())), preferred_element_type=F32
        )
        seq, core = block_of(index)
        part[seq, core] = both.astype(BF16).reshape(2, 64, D)

    loop(4, body)


def rows32(summed, index):
    seq, core, tp = lax.div(index, 8), lax.rem(lax.div(index, 4), 2), lax.rem(lax.div(index, 2), 2)
    return summed[seq, core, tp, rows_at(lax.rem(index, 2), 32), :].astype(F32)


def output_weight_of(ff):
    return ff[:, :, :, :, :WOUT].reshape(D, WOUT)


def mix_back(dz, weight, rows128):
    def body(index):
        rows = rows_at(index, 128)
        dm = jnp.dot(dz(rows), weight, preferred_element_type=F32)
        rows128[rows, :] = dm.astype(BF16).astype(F32)

    loop(4, body)


def expand_back(dz, ff, inner, de, da, sums):
    up = ff[:, :, :, :, WOUT : WOUT + WFF].reshape(D, WFF)
    down = ff[:, :, :, :, WOUT + WFF :].reshape(D, WFF)
    sums[0:1, :] = jnp.zeros((1, WFF), F32)

    def body(index):
        rows = rows_at(index, 128)
        dg = jnp.dot(dz(rows), down, preferred_element_type=F32)
        e = inner[rows, :]
        slope = gelu_parts(e) + e * jnp.exp(-0.5 * e * e) * ((2.0 * jnp.pi) ** -0.5)
        low = (dg * slope).astype(BF16)
        de[rows, :] = low
        sums[0:1, :] += jnp.sum(low.astype(F32), axis=0, keepdims=True)
        values = lax.dot_general(low, up, (((1,), (1,)), ((), ())), preferred_element_type=F32)
        da.put(index * 128, 128, values)

    loop(4, body)


def weight_grad(left, right, dw, first, count):
    def body(index):
        block = lax.dot_general(
            left[:, rows_at(index, 256)],
            right[...],
            (((0,), (0,)), ((), ())),
            preferred_element_type=F32,
        )
        two = pl.ds(lax.rem(index, 2) * 2, 2)
        dw[lax.div(index, 2), two, :, :, first : first + count] = block.astype(BF16).reshape(
            2, 4, 32, count
        )

    loop(4, body)


def project_back(pairs, q_grad, tables, du, sums):
    sums[...] = jnp.zeros(sums.shape, F32)

    def body(index):
        seq, core = block_of(index)
        part = rows_at(core, 128)
        heads = []
        for head in range(2):
            total = pairs[seq * 8 + head * 4, part, :].astype(F32)
            for k in range(1, 4):
                total = total + pairs[seq * 8 + head * 4 + k, part, :].astype(F32)
            heads.append(total)
        low = low_lanes(heads[0].shape)
        rows = rows_at(index, 128)
        turn = tuple(t[rows, :] for t in tables)
        grads = (
            turned(q_grad[rows, :], turn, -1.0),
            turned(jnp.where(low, heads[0], swap(heads[1])), turn, -1.0),
            jnp.where(low, swap(heads[0]), heads[1]),
        )
        for k in range(3):
            rounded = grads[k].astype(BF16)
            du[rows, k * 128 : (k + 1) * 128] = rounded
            sums[k : k + 1, :] += jnp.sum(rounded.astype(F32), axis=0, keepdims=True)

    loop(4, body)


def join_back(du, weight, da2, normed, gain1, gain2, sums, part):
    whole = weight[...].reshape(D, WIN)
    sums[...] = jnp.zeros(sums.shape, F32)

    def body(index):
        rows = rows_at(index, 64)
        da = lax.dot_general(
            du[rows, :], whole, (((1,), (1,)), ((), ())), preferred_element_type=F32
        )
        db = da2.get(index * 64, 64)
        n = normed[rows, :]
        for k, value in enumerate((da * n, db * n, da, db)):
            sums[k : k + 1, :] += jnp.sum(value, axis=0, keepdims=True)
        seq, core, tp = lax.div(index, 4), lax.rem(lax.div(index, 2), 2), lax.rem(index, 2)
        part[seq, core, tp] = (da * gain1 + db * gain2).astype(BF16)

    loop(8, body)


def norm_back(scaled, normed, inverse):
    first = jnp.mean(scaled, axis=1, keepdims=True)
    second = jnp.mean(scaled * normed, axis=1, keepdims=True)
    return inverse * (scaled - first - normed * second)


TILE = 256
SPAN = 1024


def seen(quarter, tile):
    key = lax.broadcasted_iota(jnp.int32, (SPAN, TILE), 0)
    row = lax.broadcasted_iota(jnp.int32, (SPAN, TILE), 1)
    place_of = (row // 32) * ROWS + quarter * 32 + row % 32
    return key <= place_of


def score_span(quarter, tile, span, queries, kvs):
    block = lax.dot_general(
        kvs[span * SPAN : (span + 1) * SPAN, :],
        queries,
        (((1,), (1,)), ((), ())),
        preferred_element_type=F32,
    )
    return jnp.where(seen(quarter, tile), block, MASKED) if span == tile else block


def forward_tile(quarter, tile, queries, kvs, kvt, score):
    highest = jnp.full((1, TILE), MASKED, F32)
    for span in range(tile + 1):
        block = score_span(quarter, tile, span, queries, kvs)
        score[span * SPAN : (span + 1) * SPAN, :] = block
        highest = jnp.maximum(highest, jnp.max(block, axis=0, keepdims=True))
    total = jnp.zeros((1, TILE), F32)
    mixed = jnp.zeros((128, TILE), F32)
    for span in range(tile + 1):
        weight = jnp.exp(score[span * SPAN : (span + 1) * SPAN, :] - highest)
        total = total + jnp.sum(weight, axis=0, keepdims=True)
        mixed = mixed + jnp.dot(
            kvt[:, span * SPAN : (span + 1) * SPAN],
            weight.astype(BF16),
            preferred_element_type=F32,
        )
    return mixed / total, highest + jnp.log(total)


def backward_span(tile, span, block, lse, delta, queries, outs, kvs, kvt, acc):
    keyed = kvs[span * SPAN : (span + 1) * SPAN, :]
    probs = jnp.exp(block - lse)
    back = lax.dot_general(keyed, outs, (((1,), (1,)), ((), ())), preferred_element_type=F32)
    score_grad = (probs * (back - delta)).astype(BF16)
    pair = jnp.dot(
        jnp.concatenate([score_grad, probs.astype(BF16)], axis=1),
        jnp.concatenate([queries, outs], axis=0),
        preferred_element_type=F32,
    )
    pair = pair.reshape(8, ROWS, 128)
    if span == tile:
        acc[span * 8 : (span + 1) * 8] = pair
    else:
        acc[span * 8 : (span + 1) * 8] += pair
    return jnp.dot(
        kvt[:, span * SPAN : (span + 1) * SPAN], score_grad, preferred_element_type=F32
    )


def put_back_rows(ranks, rows, target, upper):
    def body(chip):
        first = rows[ranks[0, chip * 2]]
        second = rows[ranks[0, chip * 2 + 1]]
        if upper:
            first = swap(first)
        else:
            second = swap(second)
        target(chip, jnp.where(low_lanes(first.shape), first, second).astype(BF16))

    loop(16, body)


def put_back_pairs(ranks, acc, outbox):
    def body(chip):
        for core in range(2):
            rank = ranks[0, chip * 2 + core]
            outbox[chip, core * ROWS : (core + 1) * ROWS, :] = acc[rank].astype(BF16)

    loop(16, body)


def owner(order, rank):
    return order[rank, 0], order[rank, 1]


def sort_rows(order, source, target, upper, scale):
    def body(rank):
        chip, core = owner(order, rank)
        block = source(chip).astype(F32) * scale
        other = swap(block)
        low = low_lanes(block.shape)
        if upper:
            part = jnp.where(low, 0.0, jnp.where(core == 0, other, block))
        else:
            part = jnp.where(low, jnp.where(core == 0, block, other), 0.0)
        target[rows_at(rank, 32), :] = part.astype(BF16)

    loop(32, body)


def sort_pairs(order, inbox, kvs, kvt):
    def body(rank):
        chip, core = owner(order, rank)
        keyed = jnp.where(core == 0, inbox[chip, 0:ROWS, :], inbox[chip, ROWS : 2 * ROWS, :])
        kvs[rows_at(rank, ROWS), :] = keyed
        kvt[:, rows_at(rank, ROWS)] = keyed.astype(F32).T.astype(BF16)

    loop(32, body)


def tile_rows(tile):
    return slice(tile * TILE, (tile + 1) * TILE)


NAMES = {
    "win": None, "wout": None, "wexp": None, "wcon": None, "tok_in": None, "cot_in": None, "raw": None, "rank": None,
    "starts": None, "cosine": None, "sine": None,
    "act_out": bf(ROWS, D), "grad_out": f32(ROWS, D), "in0_out": bf(4, 16, WIN), "in1_out": bf(4, 16, WIN),
    "ff0_out": bf(4, 16, WIDE), "ff1_out": bf(4, 16, WIDE), "small_out": f32(24, 128),
}
I32 = jnp.int32
SCRATCH = {
    "in0": vbf(2, 4, 4, 32, WIN), "in1": vbf(2, 4, 4, 32, WIN),
    "ff0": vbf(2, 4, 4, 32, WIDE), "ff1": vbf(2, 4, 4, 32, WIDE), "wff": vbf(2, 4, 16, WIDE),
    "tok": vbf(GROUP, D), "cot": vbf(GROUP, D),
    "par": vf32(24, 128), "trig": vf32(8, 128), "column_p": vf32(8, 24, 128), "joined": vf32(2, 24, 128),
    "plane_p": vf32(16, 2, 24, 128), "column_t": vf32(4, 8, 128), "vectors": vf32(24, D),
    "ib": vf32(8, 128), "eb": vf32(8, WFF),
    "par_i": pltpu.VMEM((8, 128), I32), "column_i": pltpu.VMEM((8, 8, 128), I32),
    "joined_i": pltpu.VMEM((2, 8, 128), I32), "plane_i": pltpu.VMEM((16, 2, 8, 128), I32),
    "ranks_v": pltpu.VMEM((8, 128), I32), "order_v": pltpu.VMEM((32, 128), I32),
    "ranks": pltpu.SMEM((8, 128), I32), "order": pltpu.SMEM((32, 128), I32),
    "one": vf32(GROUP, 128), "right": vf32(GROUP, 128), "left": vf32(GROUP, 128),
    "normed0": vf32(GROUP, D), "normed1": vf32(GROUP, D), "inverse0": vf32(GROUP, 128), "inverse1": vf32(GROUP, 128),
    "first": vbf(GROUP, D), "second": vbf(GROUP, D),
    "inner0": vf32(GROUP, WFF), "inner1": vf32(GROUP, WFF), "act0": vbf(GROUP, WFF), "act1": vbf(GROUP, WFF),
    "mixed0": vbf(GROUP, 128), "mixed1": vbf(GROUP, 128), "q_rows": vf32(GROUP, 128),
    "outbox": vbf(16, MESSAGE, 128), "inbox0": vbf(16, MESSAGE, 128), "inbox1": vbf(16, MESSAGE, 128),
    "m_out": vbf(16, 32, 128), "m_in": vbf(16, 32, 128), "dm_out": vbf(16, 32, 128), "dm_in": vbf(16, 32, 128),
    "kvs0": vbf(4096, 128), "kvs1": vbf(4096, 128), "kvt0": vbf(128, 4096), "kvt1": vbf(128, 4096),
    "qs0": vbf(1024, 128), "qs1": vbf(1024, 128), "dos": vbf(1024, 128), "o0": vf32(4, 128, TILE), "lse0": vf32(4, 8, TILE),
    "wide": vf32(4096, TILE), "rows": vf32(32, 32, 128), "o1": vf32(32, 32, 128), "acc": vf32(32, 128, 128),
    "de": vbf(GROUP, WFF), "du": vbf(GROUP, WIN), "own_grad": vf32(ROWS, D), "own_hidden": vf32(ROWS, D),
    "part": vbf(2, 2, 2, 64, D), "part2": vbf(2, 2, 2, 64, D), "summed": vbf(2, 2, 2, 64, D),
    "summed2": vbf(2, 64, D), "summed3": vbf(2, 64, D),
    "dw_in": vbf(2, 4, 4, 32, WIN), "dw_ff": vbf(2, 4, 4, 32, WIDE),
    "sums0": vf32(16, D), "sums1": vf32(16, D), "ib_sums0": vf32(8, 128), "ib_sums1": vf32(8, 128),
    "eb_sums0": vf32(8, WFF), "eb_sums1": vf32(8, WFF),
    "small": vf32(16, 2, 24, 128), "gathered": vf32(15, 2, 24, 128), "total_s": vf32(2, 24, 128), "others": vf32(7, 2, 24, 128),
    "here": dma(7), "send_a": dma(5, 3), "recv_a": dma(5, 3), "send_t": dma(2, 3), "recv_t": dma(2, 3),
    "send_p": dma(2, 7), "recv_p": dma(2, 7), "send_v": dma(2, 15), "recv_v": dma(2, 15),
    "send_g": dma(4, 16), "recv_g": dma(4, 16), "send_x": dma(6, 15), "recv_x": dma(6, 15),
    "send_s": dma(15), "recv_s": dma(15), "send_d": dma(7), "recv_d": dma(7),
}
COLUMN = len(ColumnSum.SCRATCH)
LINES = len(Scatter.scratch(WIN))


def whole_kernel(*refs):
    names = [*NAMES, *SCRATCH]
    r = types.SimpleNamespace(**dict(zip(names, refs)))
    rest = refs[len(names) :]
    column_sets = [rest[k * COLUMN : (k + 1) * COLUMN] for k in range(2)]
    rest = rest[2 * COLUMN :]
    lines_in, lines_ff = rest[:LINES], rest[LINES:]
    where = y, x, z, core = place()
    seq, tp = lax.div(y, 2), lax.rem(y, 2)
    mine, chip = seq * 2 + core, x * 4 + z
    column, plane = column_partners(*where), plane_partners(*where)
    tables = (r.one, r.right, r.left)
    dz_rows = r.tok
    z_sum, da2 = Wide(r.wide, 0), Wide(r.wide, 4 * GROUP)

    def exchange(number, source, target, rows):
        return Exchange(where, source, target, rows, r.send_x.at[number], r.recv_x.at[number])

    for layer in range(LAYERS):
        for k in range(4):
            r.wff[layer, k, :, 0:WOUT] = r.wout[layer, :, k * WOUT : (k + 1) * WOUT]
            r.wff[layer, k, :, WOUT : WOUT + WFF] = r.wexp[layer, :, k * WFF : (k + 1) * WFF]
            r.wff[layer, k, :, WOUT + WFF :] = r.wcon[layer, :, k * WFF : (k + 1) * WFF]
    raw = r.raw[...]
    line = lax.broadcasted_iota(I32, raw.shape, 0)
    r.par[...] = jnp.where(
        line < 18,
        pltpu.roll(raw, (z * 4 + core * 2 + tp) * 8, 1),
        pltpu.roll(raw, (core * 2 + tp) * 32, 1),
    )
    lane = lax.broadcasted_iota(I32, (8, 128), 1)
    r.par_i[...] = jnp.where((lane == chip * 2 + core) & (tp == 0), r.rank[...], 0)
    r.trig[...] = jnp.zeros((8, 128), F32)
    for k in range(2):
        starts = r.starts[k]
        chosen = lax.broadcasted_iota(I32, starts.shape, 0) == r.rank[0:1, :]
        r.trig[k : k + 1, :] = jnp.sum(jnp.where(chosen, starts, 0.0), axis=0, keepdims=True)
    enter(column + plane)

    quarter = pl.ds(pl.multiple_of(core * 16, 16), 16)
    peers = [peer_at(*where, step) for step in PEERS]
    local_copies, arriving = [], []

    def share(slot, source, target):
        copies = [
            remote(source(theirs), target, r.send_a.at[slot, k], r.recv_a.at[slot, k], device_id)
            for k, (theirs, device_id) in enumerate(peers)
        ]
        own = pltpu.make_async_copy(source(mine), target, r.here.at[slot])
        for copy in (*copies, own):
            copy.start()
        local_copies.append(own)
        arriving.append(copies)

    def landed(slot):
        for copy in arriving[slot]:
            copy.wait_recv()
        local_copies[slot].wait()

    def to_all(number, source, target, partners, send, recv):
        copies = [
            remote(source, target, send.at[number, k], recv.at[number, k], peer)
            for k, peer in enumerate(partners)
        ]
        for copy in copies:
            copy.start()
        return copies

    share(0, lambda q: r.win.at[0, q], r.in0.at[seq, x, z, quarter])
    share(1, lambda q: r.wff.at[0, q], r.ff0.at[seq, x, z, quarter])
    tokens = RowShare(r.tok_in, r.tok, where, r.send_t.at[0], r.recv_t.at[0])
    tokens.begin()
    place_in_column = y * 2 + core
    smalls = to_all(0, r.par, r.column_p.at[place_in_column], column, r.send_p, r.recv_p)
    smalls += to_all(1, r.par_i, r.column_i.at[place_in_column], column, r.send_p, r.recv_p)
    share(2, lambda q: r.trig, r.column_t.at[mine])
    share(3, lambda q: r.win.at[1, q], r.in1.at[seq, x, z, quarter])
    share(4, lambda q: r.wff.at[1, q], r.ff1.at[seq, x, z, quarter])
    cots = RowShare(r.cot_in, r.cot, where, r.send_t.at[1], r.recv_t.at[1])
    cots.begin()
    r.column_p[place_in_column] = r.par[...]
    r.column_i[place_in_column] = r.par_i[...]

    in0, ff0, in1, ff1 = (
        Gather(ref, where, r.send_g.at[k], r.recv_g.at[k])
        for k, ref in enumerate((r.in0, r.ff0, r.in1, r.ff1))
    )
    landed(0)
    in0.begin()
    landed(1)
    ff0.begin()
    tokens.pass_on()
    for copy in smalls:
        copy.wait_recv()
    for half in range(2):
        r.joined[half] = jnp.sum(r.column_p[half * 4 : half * 4 + 4], axis=0)
        cut = r.column_i
        r.joined_i[half] = cut[half * 4] + cut[half * 4 + 1] + cut[half * 4 + 2] + cut[half * 4 + 3]
    r.plane_p[chip] = r.joined[...]
    r.plane_i[chip] = r.joined_i[...]
    spread = to_all(0, r.joined, r.plane_p.at[chip], plane, r.send_v, r.recv_v)
    spread += to_all(1, r.joined_i, r.plane_i.at[chip], plane, r.send_v, r.recv_v)
    in0.pass_on()
    tokens.end()
    normalize_rows(lambda index: r.tok[rows_at(index, 32), :].astype(F32), r.normed0, r.inverse0)
    in0.turn()
    ff0.pass_on()
    landed(2)
    for k in range(4):
        rows = pl.ds(k * ROWS, ROWS)
        cos_a, sin_a = r.column_t[k, 0:1, :], r.column_t[k, 1:2, :]
        sine = sin_a * r.cosine[...] + cos_a * r.sine[...]
        spot = lax.broadcasted_iota(I32, sine.shape, 1) % HEAD_DIM
        r.one[rows, :] = cos_a * r.cosine[...] - sin_a * r.sine[...]
        r.right[rows, :] = jnp.where(spot < ROT // 2, -sine, 0.0)
        r.left[rows, :] = jnp.where(spot < ROT // 2, 0.0, sine)
    for copy in spread:
        copy.wait_recv()
    for half in range(2):
        for across in range(4):
            at = (half * 4 + across) * 128
            block = jnp.sum(r.plane_p[across * 4 : across * 4 + 4, half], axis=0)
            r.vectors[:, at : at + 128] = block
    own = [r.plane_p[mine * 4 + k, tp] for k in range(4)]
    r.ib[...] = (own[0] + own[1] + own[2] + own[3])[8:16]
    for k in range(4):
        r.eb[:, k * 128 : (k + 1) * 128] = own[k][16:24]
    in0.pass_line()
    ff0.turn()
    scale_rows(r.normed0, r.vectors[0:1, :], r.vectors[4:5, :], r.first)
    in0.end()

    def put_message(first):
        def put(at, values):
            r.outbox[at, first : first + 32, :] = values

        return put

    project(r.first, r.in0, r.ib[0:3, :], tables, r.outbox, r.q_rows)
    heads_to_chips(lambda s, c, k: r.q_rows[group_rows(s, c, k), :], put_message(256))
    sent = exchange(0, r.outbox, r.inbox0, 288)
    ff0.pass_line()
    cots.pass_on()
    landed(3)
    in1.begin()
    landed(4)
    ff1.begin()
    ranks = r.plane_i[0, lax.div(x, 2)]
    for k in range(1, 16):
        ranks = ranks + r.plane_i[k, lax.div(x, 2)]
    r.ranks_v[...] = jnp.minimum(ranks, 31)
    spot = lax.broadcasted_iota(I32, (32, 128), 1)
    match = (ranks[0:1, :] == lax.broadcasted_iota(I32, (32, 128), 0)) & (spot < 32)
    found = [jnp.where(match, value, 0) for value in (lax.div(spot, 2), lax.rem(spot, 2))]
    for k in range(7):
        found = [value + pltpu.roll(value, 1 << k, 1) for value in found]
    r.order_v[...] = jnp.where(spot == 0, jnp.minimum(found[0], 15), jnp.minimum(found[1], 1))
    scalars = [
        pltpu.make_async_copy(r.ranks_v, r.ranks, r.here.at[5]),
        pltpu.make_async_copy(r.order_v, r.order, r.here.at[6]),
    ]
    for copy in scalars:
        copy.start()
    scale_rows(r.normed0, r.vectors[1:2, :], r.vectors[5:6, :], r.second)
    ff0.end()
    expand(r.second, r.ff0, r.eb[2:3, :], r.inner0, r.act0)
    in1.pass_on()
    tokens.sent()
    for copy in scalars:
        copy.wait()
    sent.end()

    sort_pairs(r.order, r.inbox0, r.kvs0, r.kvt0)
    sort_rows(r.order, lambda at: r.inbox0[at, 256:288, :], r.qs0, False, HEAD_DIM**-0.5)
    steps = {0: (ff1.pass_on,), 1: (in1.turn,), 2: (ff1.turn,), 3: (in1.pass_line,)}
    for tile in range(4):
        mixed, lse = forward_tile(z, tile, r.qs0[tile_rows(tile), :], r.kvs0, r.kvt0, r.wide)
        r.lse0[tile] = jnp.broadcast_to(lse, (8, TILE))
        r.o0[tile] = mixed
        r.rows[tile * 8 : tile * 8 + 8] = mixed.T.reshape(8, 32, 128)
        for step in steps[tile]:
            step()

    def put_to(ref):
        def put(at, values):
            ref[at] = values

        return put

    put_back_rows(r.ranks, r.rows, put_to(r.m_out), 1)
    returned = exchange(1, r.m_out, r.m_in, 32)
    ff1.pass_line()
    sent.sent()
    contract(r.act0, r.ff0, z_sum)
    cots.end()
    in1.end()
    ff1.end()
    mix_back(lambda rows: r.cot[rows, :], output_weight_of(r.ff1), r.q_rows)
    heads_to_chips(lambda s, c, k: r.q_rows[group_rows(s, c, k), :], put_message(288))

    def keep(ref):
        def put(s, c, k, values):
            ref[group_rows(s, c, k), :] = values.astype(ref.dtype)

        return put

    returned.end()
    chips_to_heads(lambda at: r.m_in[at], keep(r.mixed0))
    add_mixed(r.mixed0, output_weight_of(r.ff0), z_sum, r.part)
    total = ColumnSum(r.part, r.summed, where, True, column_sets[0])
    total.begin()
    total.cross()
    total.combine()
    total.relay()
    total.end()
    shift = r.vectors[14:15, :] + r.vectors[15:16, :]

    def hidden(index):
        return r.tok[rows_at(index, 32), :].astype(F32) + rows32(r.summed, index) + shift

    normalize_rows(hidden, r.normed1, r.inverse1)
    scale_rows(r.normed1, r.vectors[2:3, :], r.vectors[6:7, :], r.first)
    project(r.first, r.in1, r.ib[3:6, :], tables, r.outbox, r.q_rows)
    heads_to_chips(lambda s, c, k: r.q_rows[group_rows(s, c, k), :], put_message(256))
    sent = exchange(2, r.outbox, r.inbox1, 320)

    def keep_own(index):
        r.own_hidden[rows_at(index, 32), :] = hidden(mine * 4 + index)

    loop(4, keep_own)
    scale_rows(r.normed1, r.vectors[3:4, :], r.vectors[7:8, :], r.second)
    expand(r.second, r.ff1, r.eb[3:4, :], r.inner1, r.act1)
    total.sent()
    sent.end()

    sort_pairs(r.order, r.inbox1, r.kvs1, r.kvt1)
    sort_rows(r.order, lambda at: r.inbox1[at, 256:288, :], r.qs1, False, HEAD_DIM**-0.5)
    sort_rows(r.order, lambda at: r.inbox1[at, 288:320, :], r.dos, True, 1.0)
    sent.sent()
    for tile in range(4):
        queries, outs = r.qs1[tile_rows(tile), :], r.dos[tile_rows(tile), :]
        mixed, lse = forward_tile(z, tile, queries, r.kvs1, r.kvt1, r.wide)
        r.rows[tile * 8 : tile * 8 + 8] = mixed.T.reshape(8, 32, 128)
        delta = jnp.sum(outs.astype(F32).T * mixed, axis=0, keepdims=True)
        query_grad = jnp.zeros((128, TILE), F32)
        for span in range(tile + 1):
            block = r.wide[span * SPAN : (span + 1) * SPAN, :]
            query_grad = query_grad + backward_span(
                tile, span, block, lse, delta, queries, outs, r.kvs1, r.kvt1, r.acc
            )
        r.o1[tile * 8 : tile * 8 + 8] = (query_grad.T * (HEAD_DIM**-0.5)).reshape(8, 32, 128)
    put_back_rows(r.ranks, r.rows, put_message(288), 1)
    put_back_rows(r.ranks, r.o1, put_message(256), 0)
    put_back_pairs(r.ranks, r.acc, r.outbox)
    sent = exchange(3, r.outbox, r.inbox0, 320)

    total1 = ColumnSum(r.part, r.summed2, where, False, column_sets[1])
    total2 = ColumnSum(r.part2, r.summed, where, True, column_sets[0])
    scatter_ff = Scatter(r.dw_ff, r.ff1_out, where, lines_ff)
    scatter_in = Scatter(r.dw_in, r.in1_out, where, lines_in)
    expand_back(lambda rows: r.cot[rows, :], r.ff1, r.inner1, r.de, da2, r.eb_sums1)
    contract(r.act1, r.ff1, z_sum)
    weight_grad(r.second, r.de, r.dw_ff, WOUT, WFF)
    weight_grad(r.cot, r.act1, r.dw_ff, WOUT + WFF, WFF)
    sent.end()
    chips_to_heads(lambda at: r.inbox0[at, 256:288, :], keep(r.q_rows))
    project_back(r.inbox0, r.q_rows, tables, r.du, r.ib_sums1)
    join_back(
        r.du, r.in1, da2, r.normed1, r.vectors[2:3, :], r.vectors[3:4, :], r.sums1.at[pl.ds(0, 8)], r.part2
    )
    total2.begin()
    chips_to_heads(lambda at: r.inbox0[at, 288:320, :], keep(r.mixed1))
    total2.cross()
    weight_grad(r.cot, r.mixed1, r.dw_ff, 0, WOUT)
    scatter_ff.begin()
    add_mixed(r.mixed1, output_weight_of(r.ff1), z_sum, r.part)
    total1.begin()
    total2.combine()
    weight_grad(r.first, r.du, r.dw_in, 0, WIN)
    scatter_in.begin()
    total1.cross()
    total2.relay()
    scatter_ff.pass_on()
    total2.end()
    r.sums1[8:16, :] = jnp.zeros((8, D), F32)
    r.sums0[8:16, :] = jnp.zeros((8, D), F32)

    def after(index):
        rows = rows_at(index, 32)
        before = r.cot[rows, :].astype(F32)
        return before, before + norm_back(
            rows32(r.summed, index), r.normed1[rows, :], r.inverse1[rows, 0:1]
        )

    def put_grad(index):
        before, values = after(index)
        r.sums1[8:9, :] += jnp.sum(before, axis=0, keepdims=True)
        r.sums0[8:9, :] += jnp.sum(values, axis=0, keepdims=True)
        dz_rows[rows_at(index, 32), :] = values.astype(BF16)

    loop(16, put_grad)
    mix_back(lambda rows: dz_rows[rows, :], output_weight_of(r.ff0), r.q_rows)
    heads_to_chips(lambda s, c, k: r.q_rows[group_rows(s, c, k), :], put_to(r.dm_out))
    back = exchange(4, r.dm_out, r.dm_in, 32)
    sent.sent()
    scatter_in.pass_on()
    scatter_ff.turn()
    total1.combine()

    def keep_grad(index):
        r.own_grad[rows_at(index, 32), :] = after(mine * 4 + index)[1]

    loop(4, keep_grad)
    back.end()

    sort_rows(r.order, lambda at: r.dm_in[at], r.dos, True, 1.0)
    steps = {
        0: (scatter_in.turn, scatter_ff.pass_line),
        1: (scatter_in.pass_line,),
        2: (scatter_ff.deliver,),
        3: (scatter_in.deliver,),
    }
    for tile in range(4):
        queries, outs = r.qs0[tile_rows(tile), :], r.dos[tile_rows(tile), :]
        delta = jnp.sum(outs.astype(F32).T * r.o0[tile], axis=0, keepdims=True)
        lse = r.lse0[tile][0:1, :]
        query_grad = jnp.zeros((128, TILE), F32)
        for span in range(tile + 1):
            block = score_span(z, tile, span, queries, r.kvs0)
            query_grad = query_grad + backward_span(
                tile, span, block, lse, delta, queries, outs, r.kvs0, r.kvt0, r.acc
            )
        r.o1[tile * 8 : tile * 8 + 8] = (query_grad.T * (HEAD_DIM**-0.5)).reshape(8, 32, 128)
        for step in steps[tile]:
            step()
    scatter_ff.end()
    scatter_in.end()
    put_back_rows(r.ranks, r.o1, put_message(256), 0)
    put_back_pairs(r.ranks, r.acc, r.outbox)
    sent = exchange(5, r.outbox, r.inbox1, 288)
    total1.end()
    shift = r.vectors[16:17, :] + r.vectors[17:18, :]
    for k in range(2):
        rows = pl.ds(k * 64, 64)
        r.act_out[rows, :] = (r.own_hidden[rows, :] + r.summed2[k].astype(F32) + shift).astype(BF16)
    total1.sent()
    total2.sent()

    total3 = ColumnSum(r.part, r.summed3, where, False, column_sets[0])
    scatter_ff = Scatter(r.dw_ff, r.ff0_out, where, lines_ff)
    scatter_in = Scatter(r.dw_in, r.in0_out, where, lines_in)
    scale_rows(r.normed0, r.vectors[1:2, :], r.vectors[5:6, :], r.second)
    expand_back(lambda rows: dz_rows[rows, :], r.ff0, r.inner0, r.de, da2, r.eb_sums0)
    weight_grad(r.second, r.de, r.dw_ff, WOUT, WFF)
    weight_grad(dz_rows, r.mixed0, r.dw_ff, 0, WOUT)
    weight_grad(dz_rows, r.act0, r.dw_ff, WOUT + WFF, WFF)
    scatter_ff.begin()
    scale_rows(r.normed0, r.vectors[0:1, :], r.vectors[4:5, :], r.first)
    sent.end()
    chips_to_heads(lambda at: r.inbox1[at, 256:288, :], keep(r.q_rows))
    project_back(r.inbox1, r.q_rows, tables, r.du, r.ib_sums0)
    weight_grad(r.first, r.du, r.dw_in, 0, WIN)
    scatter_in.begin()
    scatter_ff.pass_on()
    join_back(
        r.du, r.in0, da2, r.normed0, r.vectors[0:1, :], r.vectors[1:2, :], r.sums0.at[pl.ds(0, 8)], r.part
    )
    total3.begin()
    scatter_in.pass_on()
    total3.cross()

    once = jnp.where(place_in_column == 0, 1.0, 0.0)
    for half in range(2):
        for across in range(4):
            lanes = slice((half * 4 + across) * 128, (half * 4 + across + 1) * 128)
            at_home = jnp.where((tp == half) & (mine == across), 1.0, 0.0)
            for chip_z in range(4):
                cut = slice(chip_z * 128, (chip_z + 1) * 128)
                at = across * 4 + chip_z
                pieces = [
                    r.sums0[0:2, lanes], r.sums1[0:2, lanes], r.sums0[2:4, lanes], r.sums1[2:4, lanes],
                    r.ib_sums0[0:3, :] * at_home, r.ib_sums1[0:3, :] * at_home,
                    r.sums0[8:9, lanes] * once, r.sums0[8:9, lanes] * once,
                    r.sums1[8:9, lanes] * once, r.sums1[8:9, lanes] * once,
                    r.eb_sums0[0:1, cut] * at_home, r.eb_sums1[0:1, cut] * at_home,
                ]
                row = 0
                for piece in pieces:
                    count = piece.shape[0]
                    r.small[at, half, row : row + count, :] = piece
                    row += count
                r.small[at, half, 20:24, :] = jnp.zeros((4, 128), F32)
    around = []
    for k, (dx, dz) in enumerate(STEPS):
        copy = remote(
            r.small.at[ring(x, dx) * 4 + ring(z, dz)],
            r.gathered.at[k],
            r.send_s.at[k],
            r.recv_s.at[k],
            plane[k],
        )
        copy.start()
        around.append(copy)
    scatter_ff.turn()
    scatter_in.turn()
    total3.combine()
    for copy in around:
        copy.wait_recv()
    r.total_s[...] = r.small[chip] + jnp.sum(r.gathered[...], axis=0)
    shared = []
    for k, peer in enumerate(column):
        copy = remote(r.total_s, r.others.at[k], r.send_d.at[k], r.recv_d.at[k], peer)
        copy.start()
        shared.append(copy)
    scatter_ff.pass_line()
    scatter_in.pass_line()
    total3.end()
    own = mine * ROWS
    for k in range(4):
        rows = pl.ds(pl.multiple_of(own + k * 32, 32), 32)
        summed = r.summed3[k // 2, (k % 2) * 32 : (k % 2 + 1) * 32, :].astype(F32)
        r.grad_out[k * 32 : (k + 1) * 32, :] = r.own_grad[k * 32 : (k + 1) * 32, :] + norm_back(
            summed, r.normed0[rows, :], r.inverse0[rows, 0:1]
        )
    scatter_ff.deliver()
    scatter_in.deliver()
    for copy in shared:
        copy.wait_recv()
    sums_here = r.total_s[...] + jnp.sum(r.others[...], axis=0)
    sums_here = jnp.where(seq == 0, sums_here[0], sums_here[1])
    line = lax.broadcasted_iota(I32, sums_here.shape, 0)
    r.small_out[...] = jnp.where(
        line < 18,
        pltpu.roll(sums_here, 128 - (z * 4 + core * 2 + tp) * 8, 1),
        pltpu.roll(sums_here, 128 - (core * 2 + tp) * 32, 1),
    )
    scatter_ff.end()
    scatter_in.end()
    for copies in arriving:
        for copy in copies:
            copy.wait_send()
    for copy in smalls + spread + around + shared:
        copy.wait_send()
    for one in (cots, in0, ff0, in1, ff1, returned, back, sent, total3):
        one.sent()


def whole(*operands):
    outs = tuple(v for v in NAMES.values() if v is not None)
    scratch = [*SCRATCH.values(), *ColumnSum.SCRATCH * 2, *Scatter.scratch(WIN), *Scatter.scratch(WIDE)]
    return pl.pallas_call(
        whole_kernel,
        out_shape=outs,
        in_specs=[VMEM] * len(operands),
        out_specs=(VMEM,) * len(outs),
        scratch_shapes=scratch,
        compiler_params=pltpu.CompilerParams(
            collective_id=0, has_side_effects=True, vmem_limit_bytes=LIMIT * MIB
        ),
        name="whole",
    )(*operands)


def outputs_kernel(
    in0, in1, ff0, ff1, small, input_out, output_out, expand_out, contract_out,
    gain_out, shift_out, input_shift_out, output_shift_out, expand_shift_out,
):
    for layer, (ins, ffs) in enumerate(((in0, ff0), (in1, ff1))):
        for k in range(4):
            part = ins[k].astype(F32)
            for t in range(3):
                at = t * 512 + k * 128
                input_out[layer, :, at : at + 128] = part[:, t * 128 : (t + 1) * 128]
            part = ffs[k].astype(F32)
            output_out[layer, :, k * WOUT : (k + 1) * WOUT] = part[:, :WOUT]
            expand_out[layer, :, k * WFF : (k + 1) * WFF] = part[:, WOUT : WOUT + WFF]
            contract_out[layer, :, k * WFF : (k + 1) * WFF] = part[:, WOUT + WFF :]
        for k in range(2):
            row = layer * 2 + k
            gain_out[layer, k : k + 1, :] = small[row : row + 1, 0:8]
            shift_out[layer, k : k + 1, :] = small[row + 4 : row + 5, 0:8]
            output_shift_out[layer, k : k + 1, :] = small[row + 14 : row + 15, 0:8]
        input_shift_out[layer] = small[8 + layer * 3 : 11 + layer * 3, 0:8]
    expand_shift_out[...] = small[18:20, 0:32]


def outputs(*operands):
    outs = (
        f32(2, 16, 1536), f32(2, 16, 512), f32(2, 16, 2048), f32(2, 16, 2048),
        f32(2, 2, 8), f32(2, 2, 8), f32(2, 3, 8), f32(2, 2, 8), f32(2, 32),
    )
    return pl.pallas_call(
        outputs_kernel,
        out_shape=outs,
        in_specs=[VMEM] * len(operands),
        out_specs=(VMEM,) * len(outs),
        compiler_params=pltpu.CompilerParams(vmem_limit_bytes=8 * MIB),
        name="outputs",
    )(*operands)


def rotary_tables():
    half = ROT // 2
    freqs = 10000.0 ** (-(np.arange(half) * 2.0 / ROT))
    lane = np.arange(128) % HEAD_DIM
    every = np.where(lane < ROT, np.tile(freqs, 128 // half), 0.0)[None, :]
    start = np.arange(32)[:, None] * ROWS * every
    steps = np.arange(ROWS)[:, None] * every
    starts = np.stack([np.cos(start), np.sin(start)]).astype(np.float32)
    return starts, np.cos(steps).astype(np.float32), np.sin(steps).astype(np.float32)


def local(
    tokens, cotangent, group_order, input_weight, output_weight, expand_weight, contract_weight,
    norm_gain, norm_shift, input_bias, output_bias, expand_bias,
):
    win = input_weight.reshape(LAYERS, 16, 3, 4, 128).transpose(0, 3, 1, 2, 4)
    eights = [norm_gain, norm_shift, input_bias, output_bias]
    raw = jnp.concatenate(
        [
            jnp.pad(jnp.concatenate([v.reshape(-1, 8) for v in eights], axis=0), ((0, 0), (0, 120))),
            jnp.pad(expand_bias, ((0, 4), (0, 96))),
        ],
        axis=0,
    )
    activations, input_gradient, in0_out, in1_out, ff0_out, ff1_out, small = whole(
        win.reshape(LAYERS, 4, 16, WIN), output_weight, expand_weight, contract_weight, tokens, cotangent, raw,
        jnp.broadcast_to(group_order, (8, 128)), *rotary_tables(),
    )
    input_out, *rest = outputs(in0_out, in1_out, ff0_out, ff1_out, small)
    return (activations, input_gradient, input_out.reshape(2, 16, 3, 512), *rest)


def solution(mesh):
    rows, columns = P(("seq", "ctx"), None), P(None, None, ("seq", "ctx", "tp"))
    weight, flat = P(None, ("seq", "ctx"), "tp"), P(None, ("seq", "ctx", "tp"))
    first = P(None, ("seq", "ctx"), None, "tp")
    outs = (rows, rows, first, weight, weight, weight, columns, columns, columns, columns, flat)
    return jax.shard_map(
        local,
        mesh=mesh,
        in_specs=(rows, rows, P("seq", "ctx"), *outs[2:]),
        out_specs=outs,
        check_vma=False,
    )
```

```python
import types

import jax
import jax.numpy as jnp
import numpy as np
from jax import lax
from jax.experimental import pallas as pl
from jax.experimental.pallas import tpu as pltpu
from jax.sharding import PartitionSpec as P

MESH = pl.DeviceIdType.MESH
F32, BF16 = jnp.float32, jnp.bfloat16
D, HEAD_DIM, ROT, LAYERS = 1024, 64, 16, 2
ROWS = 128
GROUP = 512
WIN, WOUT, WFF = 384, 128, 512
COLS = WIN + WOUT + 2 * WFF
PARAMS = 208
EPSILON = 1e-05
MASKED = -1e30
MIB = 1024 * 1024
LIMIT = 62
WIDE = WOUT + 2 * WFF
PAIR, TWICE = WIN + WOUT, 2 * WFF
MESSAGE = 320


def place():
    ctx = lax.axis_index("ctx")
    chip = lax.div(ctx, 2)
    y = lax.axis_index("seq") * 2 + lax.axis_index("tp")
    return y, lax.div(chip, 4), lax.rem(chip, 4), lax.rem(ctx, 2)


def device(y, x, z, core):
    return (lax.div(y, 2), (x * 4 + z) * 2 + core, lax.rem(y, 2))


def ring(index, step):
    return lax.rem(index + step, 4)


def enter(partners):
    barrier = pltpu.get_barrier_semaphore()
    for partner in partners:
        pl.semaphore_signal(barrier, inc=1, device_id=partner, device_id_type=MESH)
    pl.semaphore_wait(barrier, len(partners))


def plane_partners(y, x, z, core):
    return [
        device(y, ring(x, dx), ring(z, dz), core)
        for dx in range(4)
        for dz in range(4)
        if dx or dz
    ]


def column_partners(y, x, z, core):
    return [
        device(ring(y, dy), x, z, lax.rem(core + dc, 2))
        for dy in range(4)
        for dc in range(2)
        if dy or dc
    ]


def remote(source, target, send, receive, partner):
    return pltpu.make_async_remote_copy(
        src_ref=source,
        dst_ref=target,
        send_sem=send,
        recv_sem=receive,
        device_id=partner,
        device_id_type=MESH,
    )


HBM = pl.BlockSpec(memory_space=pl.ANY)
VMEM = pl.BlockSpec(memory_space=pltpu.VMEM)
SMEM = pl.BlockSpec(memory_space=pltpu.SMEM)


def bf(*shape):
    return jax.ShapeDtypeStruct(shape, BF16)


def f32(*shape):
    return jax.ShapeDtypeStruct(shape, F32)


def vbf(*shape):
    return pltpu.VMEM(shape, BF16)


def vf32(*shape):
    return pltpu.VMEM(shape, F32)


def dma(*shape):
    return pltpu.SemaphoreType.DMA(shape)


PEERS = ((0, 1), (1, 0), (1, 1))
STEPS = tuple((dx, dz) for dx in range(4) for dz in range(4) if dx or dz)


def peer_at(y, x, z, core, step):
    seq, tp = lax.div(y, 2), lax.rem(y, 2)
    seq_to, core_to = lax.rem(seq + step[0], 2), lax.rem(core + step[1], 2)
    return seq_to * 2 + core_to, device(seq_to * 2 + tp, x, z, core_to)


class Gather:
    def __init__(self, full, where, send, recv):
        y, x, z, core = where
        self.full, self.x, self.z, self.send, self.recv = full, x, z, send, recv
        self.near = {
            "x": (device(y, ring(x, 1), z, core), device(y, ring(x, 3), z, core)),
            "z": (device(y, x, ring(z, 1), core), device(y, x, ring(z, 3), core)),
        }
        self.held = [(), ()]
        self.started = []

    def go(self, source, slot, partner):
        copy = remote(source, source, self.send.at[slot], self.recv.at[slot], partner)
        copy.start()
        self.started.append(copy)
        return copy

    def begin(self):
        for half in range(2):
            up, down = self.near["xz"[half]]
            own = self.full.at[half, self.x, self.z]
            self.held[half] = (self.go(own, half * 8, up), self.go(own, half * 8 + 1, down))

    def arrive(self, half):
        for copy in self.held[half]:
            copy.wait_recv()

    def pass_on(self):
        x, z = self.x, self.z
        for half in range(2):
            self.arrive(half)
            up, down = self.near["xz"[half]]
            whole = self.full.at[half]
            if half == 0:
                before, after = whole.at[ring(x, 3), z], whole.at[ring(x, 1), z]
            else:
                before, after = whole.at[x, ring(z, 3)], whole.at[x, ring(z, 1)]
            self.held[half] = (
                self.go(before.at[pl.ds(0, 16)], half * 8 + 2, up),
                self.go(after.at[pl.ds(16, 16)], half * 8 + 3, down),
            )

    def turn(self):
        for half in range(2):
            self.arrive(half)
            up, down = self.near["zx"[half]]
            whole = self.full.at[half]
            line = whole.at[:, self.z] if half == 0 else whole.at[self.x]
            self.held[half] = (self.go(line, half * 8 + 4, up), self.go(line, half * 8 + 5, down))

    def pass_line(self):
        x, z = self.x, self.z
        two, more = pl.ds(0, 2), pl.ds(2, 2)
        for half in range(2):
            self.arrive(half)
            up, down = self.near["zx"[half]]
            whole = self.full.at[half]
            if half == 0:
                before, after = whole.at[two, ring(z, 3)], whole.at[more, ring(z, 1)]
            else:
                before, after = whole.at[ring(x, 3), two], whole.at[ring(x, 1), more]
            self.held[half] = (
                self.go(before, half * 8 + 6, up),
                self.go(after, half * 8 + 7, down),
            )

    def end(self):
        for half in range(2):
            self.arrive(half)

    def sent(self):
        for copy in self.started:
            copy.wait_send()


class RowShare:
    def __init__(self, source, target, where, send, recv):
        y, x, z, core = where
        self.source, self.target, self.send, self.recv = source, target, send, recv
        seq = lax.div(y, 2)
        self.own = rows_at(seq * 2 + core, ROWS)
        self.other = rows_at((1 - seq) * 2 + core, ROWS)
        self.sibling = device(y, x, z, lax.rem(core + 1, 2))
        self.facing = device(3 - y, x, z, core)
        self.copies = []

    def go(self, source, target, slot, partner):
        copy = remote(source, target, self.send.at[slot], self.recv.at[slot], partner)
        copy.start()
        self.copies.append(copy)

    def begin(self):
        self.target[self.own, :] = self.source[...]
        self.go(self.source, self.target.at[self.own], 0, self.facing)
        self.go(self.source, self.target.at[self.own], 1, self.sibling)

    def pass_on(self):
        self.copies[0].wait_recv()
        block = self.target.at[self.other]
        self.go(block, block, 2, self.sibling)

    def end(self):
        for copy in self.copies[1:]:
            copy.wait_recv()

    def sent(self):
        for copy in self.copies:
            copy.wait_send()


class ColumnSum:
    SCRATCH = [vbf(4, 64, D), vbf(3, 64, D), vbf(3, 64, D)] + [dma(4), dma(4), dma(3), dma(3), dma(7), dma(7)]
    ORDER = (2, 1, 3)

    def __init__(self, part, out, where, everywhere, scratch):
        self.part, self.out, self.where, self.everywhere = part, out, where, everywhere
        (self.near, self.far, self.held, self.send1, self.recv1, self.send2, self.recv2, self.send3, self.recv3) = scratch
        y, x, z, core = where
        self.sibling = device(y, x, z, lax.rem(core + 1, 2))
        self.chips = [device(ring(y, dy), x, z, core) for dy in (1, 2, 3)]

    def begin(self):
        y, x, z, core = self.where
        self.nears = {}
        for dy in (*self.ORDER, 0):
            to = ring(y, dy)
            source = self.part.at[lax.div(to, 2), lax.rem(core + 1, 2), lax.rem(to, 2)]
            self.nears[dy] = remote(
                source, self.near.at[dy], self.send1.at[dy], self.recv1.at[dy], self.sibling
            )
            self.nears[dy].start()

    def cross(self):
        y, x, z, core = self.where
        self.fars = []
        for dy in self.ORDER:
            to = ring(y, dy)
            self.nears[dy].wait_recv()
            own = self.part[lax.div(to, 2), core, lax.rem(to, 2)].astype(F32)
            self.held[dy - 1] = (own + self.near[dy].astype(F32)).astype(BF16)
            copy = remote(
                self.held.at[dy - 1],
                self.far.at[dy - 1],
                self.send2.at[dy - 1],
                self.recv2.at[dy - 1],
                self.chips[dy - 1],
            )
            copy.start()
            self.fars.append(copy)

    def combine(self):
        y, x, z, core = self.where
        seq, tp = lax.div(y, 2), lax.rem(y, 2)
        self.nears[0].wait_recv()
        total = self.part[seq, core, tp].astype(F32) + self.near[0].astype(F32)
        for copy in self.fars:
            copy.wait_recv()
        for k in range(3):
            total = total + self.far[k].astype(F32)
        self.outs, self.relayed = [], []
        own = self.out.at[seq, core, tp] if self.everywhere else self.out.at[tp]
        own[...] = total.astype(BF16)
        if self.everywhere:
            for dy in self.ORDER:
                self.go(self.outs, own, dy - 1, self.chips[dy - 1])
            self.go(self.relayed, own, 3, self.sibling)
        else:
            self.go(self.outs, own, 0, device(seq * 2 + lax.rem(tp + 1, 2), x, z, core))

    def go(self, kept, block, slot, partner):
        copy = remote(block, block, self.send3.at[slot], self.recv3.at[slot], partner)
        copy.start()
        kept.append(copy)

    def relay(self):
        y, x, z, core = self.where
        for at, dy in enumerate(self.ORDER):
            self.outs[at].wait_recv()
            source = ring(y, 4 - dy)
            block = self.out.at[lax.div(source, 2), core, lax.rem(source, 2)]
            self.go(self.relayed, block, 3 + dy, self.sibling)

    def end(self):
        if self.everywhere:
            for copy in self.relayed:
                copy.wait_recv()
        else:
            self.outs[0].wait_recv()

    def sent(self):
        for copy in (*self.nears.values(), *self.fars, *self.outs, *self.relayed):
            copy.wait_send()


class Scatter:
    def __init__(self, dw, out, where, final, scratch):
        y, x, z, core = where
        self.dw, self.out, self.where, self.x, self.z = dw, out, where, x, z
        (self.opp1, self.dir1, self.comb1, self.sent1, self.mid, self.opp2, self.dir2, self.comb2, self.sent2, self.done,
         self.send, self.recv) = scratch
        self.send_f, self.recv_f = final
        self.near = {
            "x": (device(y, ring(x, 1), z, core), device(y, ring(x, 3), z, core)),
            "z": (device(y, x, ring(z, 1), core), device(y, x, ring(z, 3), core)),
        }
        self.started, self.held = [], [(), ()]

    @staticmethod
    def scratch(columns):
        big, small = vbf(2, 2, 2, 32, columns), vbf(2, 2, 16, columns)
        mid = vbf(2, 4, 32, columns)
        return [big] * 4 + [mid] + [small] * 5 + [dma(24), dma(24)]

    def go(self, source, target, slot, partner):
        copy = remote(source, target, self.send.at[slot], self.recv.at[slot], partner)
        copy.start()
        self.started.append(copy)
        return copy

    def part1(self, half, step, side):
        two = pl.ds(side * 2, 2)
        whole = self.dw.at[half]
        if half == 0:
            return whole.at[two, ring(self.z, step)]
        return whole.at[ring(self.x, step), two]

    def part2(self, half, step, side):
        at = ring(self.x, step) if half == 0 else ring(self.z, step)
        return self.mid.at[half, at].at[pl.ds(side * 16, 16)]

    def open(self, half, part, axis, opposite, direct, base):
        up, down = self.near[axis]
        self.held[half] = (
            self.go(part(half, 2, 0), opposite.at[half, 0], base, up),
            self.go(part(half, 2, 1), opposite.at[half, 1], base + 1, down),
            self.go(part(half, 1, 1), direct.at[half, 0], base + 2, up),
            self.go(part(half, 3, 0), direct.at[half, 1], base + 3, down),
        )

    def onward(self, half, part, axis, opposite, combined, sent, base):
        up, down = self.near[axis]
        copies = self.held[half]
        copies[0].wait_recv()
        sent[half, 0] = (part(half, 1, 0)[...].astype(F32) + opposite[half, 0].astype(F32)).astype(BF16)
        first = self.go(sent.at[half, 0], combined.at[half, 0], base + 4, up)
        copies[1].wait_recv()
        sent[half, 1] = (part(half, 3, 1)[...].astype(F32) + opposite[half, 1].astype(F32)).astype(BF16)
        second = self.go(sent.at[half, 1], combined.at[half, 1], base + 5, down)
        self.held[half] = (*copies[2:], first, second)

    def finish(self, half, part, direct, combined, target):
        for copy in self.held[half]:
            copy.wait_recv()
        for side in range(2):
            total = (
                part(half, 0, side)[...].astype(F32)
                + combined[half, side].astype(F32)
                + direct[half, 1 - side].astype(F32)
            )
            target(half, side)[...] = total.astype(BF16)

    def begin(self):
        for half in range(2):
            self.open(half, self.part1, "zx"[half], self.opp1, self.dir1, half * 12)

    def pass_on(self):
        for half in range(2):
            self.onward(half, self.part1, "zx"[half], self.opp1, self.comb1, self.sent1, half * 12)

    def turn(self):
        for half in range(2):
            self.finish(
                half,
                self.part1,
                self.dir1,
                self.comb1,
                lambda h, side: self.mid.at[h, pl.ds(side * 2, 2)],
            )
            self.open(half, self.part2, "xz"[half], self.opp2, self.dir2, half * 12 + 6)

    def pass_line(self):
        for half in range(2):
            self.onward(
                half, self.part2, "xz"[half], self.opp2, self.comb2, self.sent2, half * 12 + 6
            )

    def deliver(self):
        y, x, z, core = self.where
        seq = lax.div(y, 2)
        mine = seq * 2 + core
        for half in range(2):
            self.finish(
                half, self.part2, self.dir2, self.comb2, lambda h, side: self.done.at[h, side]
            )
        self.out[mine] = self.done[seq, core]
        self.final = []
        for k, step in enumerate(PEERS):
            theirs, peer = peer_at(y, x, z, core, step)
            copy = remote(
                self.done.at[lax.div(theirs, 2), lax.rem(theirs, 2)],
                self.out.at[mine],
                self.send_f.at[k],
                self.recv_f.at[k],
                peer,
            )
            copy.start()
            self.final.append(copy)

    def end(self):
        for copy in self.final:
            copy.wait()
        for copy in self.started:
            copy.wait_send()


class Exchange:
    def __init__(self, where, source, target, rows, send, recv):
        y, x, z, core = where
        chip = x * 4 + z
        cut = pl.ds(0, rows)
        target[chip, cut, :] = source[chip, cut, :]
        self.copies = []
        for k, (dx, dz) in enumerate(STEPS):
            to_x, to_z = ring(x, dx), ring(z, dz)
            copy = remote(
                source.at[to_x * 4 + to_z, cut],
                target.at[chip, cut],
                send.at[k],
                recv.at[k],
                device(y, to_x, to_z, core),
            )
            copy.start()
            self.copies.append(copy)

    def end(self):
        for copy in self.copies:
            copy.wait_recv()

    def sent(self):
        for copy in self.copies:
            copy.wait_send()


def loop(count, body, together=1):
    def step(index, carry):
        for k in range(together):
            body(index * together + k)
        return carry

    lax.fori_loop(0, count // together, step, 0)


def rows_at(index, count):
    return pl.ds(pl.multiple_of(index * count, count), count)


def turned(values, tables, sign):
    one, right, left = tables
    half = ROT // 2
    return values * one + sign * (
        pltpu.roll(values, 128 - half, 1) * right + pltpu.roll(values, half, 1) * left
    )


def low_lanes(shape):
    return lax.broadcasted_iota(jnp.int32, shape, 1) < HEAD_DIM


def swap(values):
    return pltpu.roll(values, HEAD_DIM, 1)


def heads_to_chips(values, target):
    def body(index):
        seq, quarter = lax.div(index, 4), lax.rem(index, 4)
        first, second = values(seq, 0, quarter), values(seq, 1, quarter)
        low = low_lanes(first.shape)
        target(seq * 8 + quarter, jnp.where(low, first, swap(second)).astype(BF16))
        target(seq * 8 + 4 + quarter, jnp.where(low, swap(first), second).astype(BF16))

    loop(8, body, 4)


def group_rows(seq, core, quarter):
    return pl.ds(pl.multiple_of(seq * 256 + core * 128 + quarter * 32, 32), 32)


def normalize_rows(hidden, normed, inverse, first=0, count=16):
    def body(step):
        index = step + first
        rows = rows_at(index, 32)
        values = hidden(index)
        centred = values - jnp.mean(values, axis=1, keepdims=True)
        spread = jnp.mean(centred * centred, axis=1, keepdims=True)
        scale = lax.rsqrt(spread + EPSILON)
        normed[rows, :] = centred * scale
        inverse[rows, :] = jnp.broadcast_to(scale, (32, 128))

    loop(count, body, 2)


def scale_rows(normed, gain, shift, target):
    def body(index):
        rows = rows_at(index, 32)
        target[rows, :] = (normed[rows, :] * gain + shift).astype(BF16)

    loop(16, body)


def project(first, weight, bias, tables, outbox, q_rows):
    whole = columns_of(weight, 0, WIN)

    def body(index):
        rows = rows_at(index, 128)
        u = jnp.dot(first[rows, :], whole, preferred_element_type=F32)
        turn = tuple(t[rows, :] for t in tables)
        q_rows[rows, :] = turned(u[:, :128] + bias[0:1, :], turn, 1.0)
        keys = turned(u[:, 128:256] + bias[1:2, :], turn, 1.0)
        values = u[:, 256:] + bias[2:3, :]
        low = low_lanes(keys.shape)
        seq = lax.div(index, 2)
        part = rows_at(lax.rem(index, 2), 128)
        for head in range(2):
            pair = (keys, swap(values)) if head == 0 else (swap(keys), values)
            pair = jnp.where(low, *pair).astype(BF16)
            for k in range(4):
                outbox[seq * 8 + head * 4 + k, part, :] = pair

    loop(4, body)


def gelu_parts(inner):
    return 0.5 * (1.0 + lax.erf(inner * (0.5**0.5)))


def columns_of(weight, first, count):
    return weight[:, :, :, :, first : first + count].reshape(D, count)


def expand(second, whole, bias, inner, activated):

    def body(index):
        rows = rows_at(index, 128)
        e = jnp.dot(second[rows, :], whole, preferred_element_type=F32) + bias
        inner[rows, :] = e
        activated[rows, :] = (e * gelu_parts(e)).astype(BF16)

    loop(4, body)


def chips_to_heads(parts, target):
    def body(index):
        seq, quarter = lax.div(index, 4), lax.rem(index, 4)
        first = parts(seq * 8 + quarter).astype(F32)
        second = parts(seq * 8 + 4 + quarter).astype(F32)
        low = low_lanes(first.shape)
        target(seq, 0, quarter, jnp.where(low, first, swap(second)))
        target(seq, 1, quarter, jnp.where(low, swap(first), second))

    loop(8, body, 4)


def block_of(index):
    return lax.div(index, 2), lax.rem(index, 2)


class Wide:
    def __init__(self, buffer, base):
        self.buffer, self.base = buffer, base

    def at(self, start, count, k):
        return pl.ds(pl.multiple_of(self.base + k * GROUP + start, count), count)

    def put(self, start, count, values):
        for k in range(4):
            self.buffer[self.at(start, count, k), :] = values[:, k * 256 : (k + 1) * 256]

    def get(self, start, count):
        return jnp.concatenate([self.buffer[self.at(start, count, k), :] for k in range(4)], axis=1)


def contract(activated, whole, z):

    def body(index):
        rows = rows_at(index, 128)
        values = lax.dot_general(
            activated[rows, :], whole, (((1,), (1,)), ((), ())), preferred_element_type=F32
        )
        z.put(index * 128, 128, values)

    loop(4, body)


def add_mixed(mixed, weight, z, part):
    def body(index):
        rows = rows_at(index, 128)
        both = z.get(index * 128, 128) + lax.dot_general(
            mixed[rows, :], weight, (((1,), (1,)), ((), ())), preferred_element_type=F32
        )
        seq, core = block_of(index)
        part[seq, core] = both.astype(BF16).reshape(2, 64, D)

    loop(4, body)


def rows32(summed, index):
    seq, core, tp = lax.div(index, 8), lax.rem(lax.div(index, 4), 2), lax.rem(lax.div(index, 2), 2)
    return summed[seq, core, tp, rows_at(lax.rem(index, 2), 32), :].astype(F32)


def mix_back(dz, weight, rows128):
    def body(index):
        rows = rows_at(index, 128)
        dm = jnp.dot(dz(rows), weight, preferred_element_type=F32)
        rows128[rows, :] = dm.astype(BF16).astype(F32)

    loop(4, body)


def expand_back(dz, up, down, inner, de, da, sums):
    sums[0:1, :] = jnp.zeros((1, WFF), F32)

    def body(index):
        rows = rows_at(index, 128)
        dg = jnp.dot(dz(rows), down, preferred_element_type=F32)
        e = inner[rows, :]
        slope = gelu_parts(e) + e * jnp.exp(-0.5 * e * e) * ((2.0 * jnp.pi) ** -0.5)
        low = (dg * slope).astype(BF16)
        de[rows, :] = low
        sums[0:1, :] += jnp.sum(low.astype(F32), axis=0, keepdims=True)
        values = lax.dot_general(low, up, (((1,), (1,)), ((), ())), preferred_element_type=F32)
        da.put(index * 128, 128, values)

    loop(4, body)


def weight_grad(left, right, dw, first, count):
    def body(index):
        block = lax.dot_general(
            left[:, rows_at(index, 256)],
            right[...],
            (((0,), (0,)), ((), ())),
            preferred_element_type=F32,
        )
        two = pl.ds(lax.rem(index, 2) * 2, 2)
        dw[lax.div(index, 2), two, :, :, first : first + count] = block.astype(BF16).reshape(
            2, 4, 32, count
        )

    loop(4, body)


def project_back(pairs, q_grad, tables, du, sums):
    sums[...] = jnp.zeros(sums.shape, F32)

    def body(index):
        seq, core = block_of(index)
        part = rows_at(core, 128)
        heads = []
        for head in range(2):
            total = pairs[seq * 8 + head * 4, part, :].astype(F32)
            for k in range(1, 4):
                total = total + pairs[seq * 8 + head * 4 + k, part, :].astype(F32)
            heads.append(total)
        low = low_lanes(heads[0].shape)
        rows = rows_at(index, 128)
        turn = tuple(t[rows, :] for t in tables)
        grads = (
            turned(q_grad[rows, :], turn, -1.0),
            turned(jnp.where(low, heads[0], swap(heads[1])), turn, -1.0),
            jnp.where(low, swap(heads[0]), heads[1]),
        )
        for k in range(3):
            rounded = grads[k].astype(BF16)
            du[rows, k * 128 : (k + 1) * 128] = rounded
            sums[k : k + 1, :] += jnp.sum(rounded.astype(F32), axis=0, keepdims=True)

    loop(4, body)


def join_back(du, weight, da2, normed, gain1, gain2, sums, part):
    whole = columns_of(weight, 0, WIN)
    sums[...] = jnp.zeros(sums.shape, F32)

    def body(index):
        rows = rows_at(index, 64)
        da = lax.dot_general(
            du[rows, :], whole, (((1,), (1,)), ((), ())), preferred_element_type=F32
        )
        db = da2.get(index * 64, 64)
        n = normed[rows, :]
        for k, value in enumerate((da * n, db * n, da, db)):
            sums[k : k + 1, :] += jnp.sum(value, axis=0, keepdims=True)
        seq, core, tp = lax.div(index, 4), lax.rem(lax.div(index, 2), 2), lax.rem(index, 2)
        part[seq, core, tp] = (da * gain1 + db * gain2).astype(BF16)

    loop(8, body)


def norm_back(scaled, normed, inverse):
    first = jnp.mean(scaled, axis=1, keepdims=True)
    second = jnp.mean(scaled * normed, axis=1, keepdims=True)
    return inverse * (scaled - first - normed * second)


TILE = 256
SPAN = 1024


def seen(quarter, tile):
    key = lax.broadcasted_iota(jnp.int32, (SPAN, TILE), 0)
    row = lax.broadcasted_iota(jnp.int32, (SPAN, TILE), 1)
    place_of = (row // 32) * ROWS + quarter * 32 + row % 32
    return key <= place_of


def score_span(quarter, tile, span, queries, kvs):
    block = lax.dot_general(
        kvs[span * SPAN : (span + 1) * SPAN, :],
        queries,
        (((1,), (1,)), ((), ())),
        preferred_element_type=F32,
    )
    return jnp.where(seen(quarter, tile), block, MASKED) if span == tile else block


def forward_tile(quarter, tile, queries, kvs, kvt, score):
    highest = jnp.full((1, TILE), MASKED, F32)
    for span in range(tile + 1):
        block = score_span(quarter, tile, span, queries, kvs)
        score[span * SPAN : (span + 1) * SPAN, :] = block
        highest = jnp.maximum(highest, jnp.max(block, axis=0, keepdims=True))
    total = jnp.zeros((1, TILE), F32)
    mixed = jnp.zeros((128, TILE), F32)
    for span in range(tile + 1):
        weight = jnp.exp(score[span * SPAN : (span + 1) * SPAN, :] - highest)
        total = total + jnp.sum(weight, axis=0, keepdims=True)
        mixed = mixed + jnp.dot(
            kvt[:, span * SPAN : (span + 1) * SPAN],
            weight.astype(BF16),
            preferred_element_type=F32,
        )
    return mixed / total, highest + jnp.log(total)


def backward_span(tile, span, block, lse, delta, queries, outs, kvs, kvt, acc):
    keyed = kvs[span * SPAN : (span + 1) * SPAN, :]
    probs = jnp.exp(block - lse)
    back = lax.dot_general(keyed, outs, (((1,), (1,)), ((), ())), preferred_element_type=F32)
    score_grad = (probs * (back - delta)).astype(BF16)
    pair = jnp.dot(
        jnp.concatenate([score_grad, probs.astype(BF16)], axis=1),
        jnp.concatenate([queries, outs], axis=0),
        preferred_element_type=F32,
    )
    pair = pair.reshape(8, ROWS, 128)
    if tile == 3:
        acc[span * 8 : (span + 1) * 8] = pair
    else:
        acc[span * 8 : (span + 1) * 8] += pair
    return jnp.dot(
        kvt[:, span * SPAN : (span + 1) * SPAN], score_grad, preferred_element_type=F32
    )


def put_back_rows(ranks, rows, target, upper):
    def body(chip):
        first = rows[ranks[0, chip * 2]]
        second = rows[ranks[0, chip * 2 + 1]]
        if upper:
            first = swap(first)
        else:
            second = swap(second)
        target(chip, jnp.where(low_lanes(first.shape), first, second).astype(BF16))

    loop(16, body, 8)


def put_back_pairs(ranks, acc, outbox):
    def body(chip):
        for core in range(2):
            rank = ranks[0, chip * 2 + core]
            outbox[chip, core * ROWS : (core + 1) * ROWS, :] = acc[rank].astype(BF16)

    loop(16, body, 2)


def owner(order, rank):
    return order[rank, 0], order[rank, 1]


def sort_rows(order, source, target, upper, scale):
    def body(rank):
        chip, core = owner(order, rank)
        block = source(chip).astype(F32) * scale
        other = swap(block)
        low = low_lanes(block.shape)
        if upper:
            part = jnp.where(low, 0.0, jnp.where(core == 0, other, block))
        else:
            part = jnp.where(low, jnp.where(core == 0, block, other), 0.0)
        target[rows_at(rank, 32), :] = part.astype(BF16)

    loop(32, body, 8)


def sort_pairs(order, inbox, kvs, kvt):
    def body(rank):
        chip, core = owner(order, rank)
        keyed = jnp.where(core == 0, inbox[chip, 0:ROWS, :], inbox[chip, ROWS : 2 * ROWS, :])
        kvs[rows_at(rank, ROWS), :] = keyed
        kvt[:, rows_at(rank, ROWS)] = keyed.astype(F32).T.astype(BF16)

    loop(32, body, 4)


def tile_rows(tile):
    return slice(tile * TILE, (tile + 1) * TILE)


NAMES = {
    "win": None, "wout": None, "wexp": None, "wcon": None, "tok_in": None, "cot_in": None, "raw": None, "rank": None,
    "starts": None, "cosine": None, "sine": None,
    "act_out": bf(ROWS, D), "grad_out": f32(ROWS, D), "in0_out": bf(4, 16, PAIR), "in1_out": bf(4, 16, PAIR),
    "ff0_out": bf(4, 16, TWICE), "ff1_out": bf(4, 16, TWICE), "small_out": f32(24, 128),
}
I32 = jnp.int32
SCRATCH = {
    "in0": vbf(2, 4, 4, 32, WIN), "in1": vbf(2, 4, 4, 32, PAIR),
    "ff0": vbf(2, 4, 4, 32, WIDE), "ff1": vbf(2, 4, 4, 32, TWICE),
    "wff0": vbf(4, 16, WIDE), "win1": vbf(4, 16, PAIR), "wff1": vbf(4, 16, TWICE),
    "tok": vbf(GROUP, D), "cot": vbf(GROUP, D),
    "par": vf32(24, 128), "trig": vf32(8, 128), "column_p": vf32(8, 24, 128), "joined": vf32(2, 24, 128),
    "plane_p": vf32(16, 2, 24, 128), "column_t": vf32(4, 8, 128), "vectors": vf32(24, D),
    "ib": vf32(8, 128), "eb": vf32(8, WFF),
    "par_i": pltpu.VMEM((8, 128), I32), "column_i": pltpu.VMEM((8, 8, 128), I32),
    "joined_i": pltpu.VMEM((2, 8, 128), I32), "plane_i": pltpu.VMEM((16, 2, 8, 128), I32),
    "ranks_v": pltpu.VMEM((8, 128), I32), "order_v": pltpu.VMEM((32, 128), I32),
    "ranks": pltpu.SMEM((8, 128), I32), "order": pltpu.SMEM((32, 128), I32),
    "one": vf32(GROUP, 128), "right": vf32(GROUP, 128), "left": vf32(GROUP, 128),
    "normed0": vf32(GROUP, D), "normed1": vf32(GROUP, D), "inverse0": vf32(GROUP, 128), "inverse1": vf32(GROUP, 128),
    "first": vbf(GROUP, D), "second": vbf(GROUP, D),
    "inner0": vf32(GROUP, WFF), "inner1": vf32(GROUP, WFF), "act0": vbf(GROUP, WFF), "act1": vbf(GROUP, WFF),
    "mixed0": vbf(GROUP, 128), "mixed1": vbf(GROUP, 128), "q_rows": vf32(GROUP, 128),
    "outbox": vbf(16, MESSAGE, 128), "inbox0": vbf(16, MESSAGE, 128), "inbox1": vbf(16, MESSAGE, 128),
    "m_out": vbf(16, 32, 128), "m_in": vbf(16, 32, 128), "dm_out": vbf(16, 32, 128), "dm_in": vbf(16, 32, 128),
    "kvs0": vbf(4096, 128), "kvs1": vbf(4096, 128), "kvt0": vbf(128, 4096), "kvt1": vbf(128, 4096),
    "qs0": vbf(1024, 128), "qs1": vbf(1024, 128), "dos": vbf(1024, 128), "o0": vf32(4, 128, TILE), "lse0": vf32(4, 8, TILE),
    "wide": vf32(4096, TILE), "rows": vf32(32, 32, 128), "o1": vf32(32, 32, 128), "acc": vf32(32, 128, 128),
    "de": vbf(GROUP, WFF), "du": vbf(GROUP, WIN), "own_grad": vf32(ROWS, D), "own_hidden": vf32(ROWS, D),
    "part": vbf(2, 2, 2, 64, D), "part2": vbf(2, 2, 2, 64, D), "summed": vbf(2, 2, 2, 64, D),
    "summed2": vbf(2, 64, D), "summed3": vbf(2, 64, D),
    "dw_in": vbf(2, 4, 4, 32, PAIR), "dw_ff": vbf(2, 4, 4, 32, TWICE),
    "sums0": vf32(16, D), "sums1": vf32(16, D), "ib_sums0": vf32(8, 128), "ib_sums1": vf32(8, 128),
    "eb_sums0": vf32(8, WFF), "eb_sums1": vf32(8, WFF),
    "small": vf32(16, 2, 24, 128), "gathered": vf32(15, 2, 24, 128), "total_s": vf32(2, 24, 128), "others": vf32(7, 2, 24, 128),
    "here": dma(7), "send_a": dma(5, 3), "recv_a": dma(5, 3), "send_t": dma(2, 3), "recv_t": dma(2, 3),
    "send_p": dma(2, 7), "recv_p": dma(2, 7), "send_v": dma(2, 15), "recv_v": dma(2, 15),
    "send_g": dma(4, 16), "recv_g": dma(4, 16), "send_x": dma(6, 15), "recv_x": dma(6, 15),
    "send_f": dma(4, 3), "recv_f": dma(4, 3), "send_s": dma(15), "recv_s": dma(15), "send_d": dma(7), "recv_d": dma(7),
}
COLUMN = len(ColumnSum.SCRATCH)
LINES = len(Scatter.scratch(WIN))


def whole_kernel(*refs):
    names = [*NAMES, *SCRATCH]
    r = types.SimpleNamespace(**dict(zip(names, refs)))
    rest = refs[len(names) :]
    column_sets = [rest[k * COLUMN : (k + 1) * COLUMN] for k in range(2)]
    rest = rest[2 * COLUMN :]
    lines_in, lines_ff = rest[:LINES], rest[LINES:]
    where = y, x, z, core = place()
    seq, tp = lax.div(y, 2), lax.rem(y, 2)
    mine, chip = seq * 2 + core, x * 4 + z
    column, plane = column_partners(*where), plane_partners(*where)
    tables = (r.one, r.right, r.left)
    dz_rows = r.tok
    z_sum, da2 = Wide(r.wide, 0), Wide(r.wide, 4 * GROUP)

    def exchange(number, source, target, rows):
        return Exchange(where, source, target, rows, r.send_x.at[number], r.recv_x.at[number])

    def final(number):
        return r.send_f.at[number], r.recv_f.at[number]

    raw = r.raw[...]
    line = lax.broadcasted_iota(I32, raw.shape, 0)
    r.par[...] = jnp.where(
        line < 18,
        pltpu.roll(raw, (z * 4 + core * 2 + tp) * 8, 1),
        pltpu.roll(raw, (core * 2 + tp) * 32, 1),
    )
    lane = lax.broadcasted_iota(I32, (8, 128), 1)
    r.par_i[...] = jnp.where((lane == chip * 2 + core) & (tp == 0), r.rank[...], 0)
    r.trig[...] = jnp.zeros((8, 128), F32)
    for k in range(2):
        starts = r.starts[k]
        chosen = lax.broadcasted_iota(I32, starts.shape, 0) == r.rank[0:1, :]
        r.trig[k : k + 1, :] = jnp.sum(jnp.where(chosen, starts, 0.0), axis=0, keepdims=True)
    enter(column + plane)

    quarter = pl.ds(pl.multiple_of(core * 16, 16), 16)
    peers = [peer_at(*where, step) for step in PEERS]
    local_copies, arriving = [], []

    def share(slot, source, target):
        copies = [
            remote(source(theirs), target, r.send_a.at[slot, k], r.recv_a.at[slot, k], device_id)
            for k, (theirs, device_id) in enumerate(peers)
        ]
        own = pltpu.make_async_copy(source(mine), target, r.here.at[slot])
        for copy in (*copies, own):
            copy.start()
        local_copies.append(own)
        arriving.append(copies)

    def landed(slot):
        for copy in arriving[slot]:
            copy.wait_recv()
        local_copies[slot].wait()

    def to_all(number, source, target, partners, send, recv):
        copies = [
            remote(source, target, send.at[number, k], recv.at[number, k], peer)
            for k, peer in enumerate(partners)
        ]
        for copy in copies:
            copy.start()
        return copies

    share(0, lambda q: r.win.at[0, q], r.in0.at[seq, x, z, quarter])
    place_in_column = y * 2 + core
    smalls = to_all(0, r.par, r.column_p.at[place_in_column], column, r.send_p, r.recv_p)
    tokens = RowShare(r.tok_in, r.tok, where, r.send_t.at[0], r.recv_t.at[0])
    tokens.begin()
    share(1, lambda q: r.trig, r.column_t.at[mine])
    ranks_here = to_all(1, r.par_i, r.column_i.at[place_in_column], column, r.send_p, r.recv_p)
    r.column_p[place_in_column] = r.par[...]
    r.column_i[place_in_column] = r.par_i[...]

    in0, ff0, in1, ff1 = (
        Gather(ref, where, r.send_g.at[k], r.recv_g.at[k])
        for k, ref in enumerate((r.in0, r.ff0, r.in1, r.ff1))
    )
    landed(0)
    in0.begin()
    for copy in smalls:
        copy.wait_recv()
    for half in range(2):
        r.joined[half] = jnp.sum(r.column_p[half * 4 : half * 4 + 4], axis=0)
    r.plane_p[chip] = r.joined[...]
    spread = to_all(0, r.joined, r.plane_p.at[chip], plane, r.send_v, r.recv_v)
    in0.pass_on()
    tokens.pass_on()
    for k in range(4):
        r.wff0[k, :, 0:WOUT] = r.wout[0, :, k * WOUT : (k + 1) * WOUT]
        r.wff0[k, :, WOUT : WOUT + WFF] = r.wexp[0, :, k * WFF : (k + 1) * WFF]
        r.wff0[k, :, WOUT + WFF :] = r.wcon[0, :, k * WFF : (k + 1) * WFF]
    share(2, lambda q: r.wff0.at[q], r.ff0.at[seq, x, z, quarter])
    in0.turn()
    tokens.end()

    def token_rows(index):
        return r.tok[rows_at(index, 32), :].astype(F32)

    normalize_rows(token_rows, r.normed0, r.inverse0, 0, 6)
    in0.pass_line()
    normalize_rows(token_rows, r.normed0, r.inverse0, 6, 10)
    landed(1)
    for k in range(4):
        rows = pl.ds(k * ROWS, ROWS)
        cos_a, sin_a = r.column_t[k, 0:1, :], r.column_t[k, 1:2, :]
        sine = sin_a * r.cosine[...] + cos_a * r.sine[...]
        spot = lax.broadcasted_iota(I32, sine.shape, 1) % HEAD_DIM
        r.one[rows, :] = cos_a * r.cosine[...] - sin_a * r.sine[...]
        r.right[rows, :] = jnp.where(spot < ROT // 2, -sine, 0.0)
        r.left[rows, :] = jnp.where(spot < ROT // 2, 0.0, sine)
    for copy in spread:
        copy.wait_recv()
    for half in range(2):
        for across in range(4):
            at = (half * 4 + across) * 128
            block = jnp.sum(r.plane_p[across * 4 : across * 4 + 4, half], axis=0)
            r.vectors[:, at : at + 128] = block
    own = [r.plane_p[mine * 4 + k, tp] for k in range(4)]
    r.ib[...] = (own[0] + own[1] + own[2] + own[3])[8:16]
    for k in range(4):
        r.eb[:, k * 128 : (k + 1) * 128] = own[k][16:24]
    scale_rows(r.normed0, r.vectors[0:1, :], r.vectors[4:5, :], r.first)
    in0.end()

    def put_message(first):
        def put(at, values):
            r.outbox[at, first : first + 32, :] = values

        return put

    project(r.first, r.in0, r.ib[0:3, :], tables, r.outbox, r.q_rows)
    heads_to_chips(lambda s, c, k: r.q_rows[group_rows(s, c, k), :], put_message(256))
    sent = exchange(0, r.outbox, r.inbox0, 288)
    for copy in ranks_here:
        copy.wait_recv()
    for half in range(2):
        cut = r.column_i
        r.joined_i[half] = cut[half * 4] + cut[half * 4 + 1] + cut[half * 4 + 2] + cut[half * 4 + 3]
    r.plane_i[chip] = r.joined_i[...]
    ranks_there = to_all(1, r.joined_i, r.plane_i.at[chip], plane, r.send_v, r.recv_v)
    for k in range(4):
        r.win1[k, :, :WIN] = r.win[1, k]
        r.win1[k, :, WIN:] = r.wout[1, :, k * WOUT : (k + 1) * WOUT]
        r.wff1[k, :, :WFF] = r.wexp[1, :, k * WFF : (k + 1) * WFF]
        r.wff1[k, :, WFF:] = r.wcon[1, :, k * WFF : (k + 1) * WFF]
    landed(2)
    ff0.begin()
    share(3, lambda q: r.win1.at[q], r.in1.at[seq, x, z, quarter])
    share(4, lambda q: r.wff1.at[q], r.ff1.at[seq, x, z, quarter])
    cots = RowShare(r.cot_in, r.cot, where, r.send_t.at[1], r.recv_t.at[1])
    cots.begin()
    scale_rows(r.normed0, r.vectors[1:2, :], r.vectors[5:6, :], r.second)
    ff0.pass_on()
    for copy in ranks_there:
        copy.wait_recv()
    ranks = r.plane_i[0, lax.div(x, 2)]
    for k in range(1, 16):
        ranks = ranks + r.plane_i[k, lax.div(x, 2)]
    r.ranks_v[...] = jnp.minimum(ranks, 31)
    spot = lax.broadcasted_iota(I32, (32, 128), 1)
    match = (ranks[0:1, :] == lax.broadcasted_iota(I32, (32, 128), 0)) & (spot < 32)
    found = [jnp.where(match, value, 0) for value in (lax.div(spot, 2), lax.rem(spot, 2))]
    for k in range(7):
        found = [value + pltpu.roll(value, 1 << k, 1) for value in found]
    r.order_v[...] = jnp.where(spot == 0, jnp.minimum(found[0], 15), jnp.minimum(found[1], 1))
    scalars = [
        pltpu.make_async_copy(r.ranks_v, r.ranks, r.here.at[5]),
        pltpu.make_async_copy(r.order_v, r.order, r.here.at[6]),
    ]
    for copy in scalars:
        copy.start()
    tokens.sent()
    for copy in scalars:
        copy.wait()
    sent.end()
    landed(3)
    ff0.turn()
    in1.begin()

    sort_pairs(r.order, r.inbox0, r.kvs0, r.kvt0)
    sort_rows(r.order, lambda at: r.inbox0[at, 256:288, :], r.qs0, False, HEAD_DIM**-0.5)
    steps = {
        3: (in1.pass_on, cots.pass_on),
        2: (ff0.pass_line, in1.turn),
        1: (),
        0: (in1.pass_line, lambda: landed(4), ff1.begin),
    }
    for tile in (3, 2, 1, 0):
        mixed, lse = forward_tile(z, tile, r.qs0[tile_rows(tile), :], r.kvs0, r.kvt0, r.wide)
        r.lse0[tile] = jnp.broadcast_to(lse, (8, TILE))
        r.o0[tile] = mixed
        r.rows[tile * 8 : tile * 8 + 8] = mixed.T.reshape(8, 32, 128)
        for step in steps[tile]:
            step()

    def put_to(ref):
        def put(at, values):
            ref[at] = values

        return put

    put_back_rows(r.ranks, r.rows, put_to(r.m_out), 1)
    returned = exchange(1, r.m_out, r.m_in, 32)
    sent.sent()
    ff0.end()
    expand(r.second, columns_of(r.ff0, WOUT, WFF), r.eb[2:3, :], r.inner0, r.act0)
    ff1.pass_on()
    contract(r.act0, columns_of(r.ff0, WOUT + WFF, WFF), z_sum)

    def keep(ref):
        def put(s, c, k, values):
            ref[group_rows(s, c, k), :] = values.astype(ref.dtype)

        return put

    returned.end()
    chips_to_heads(lambda at: r.m_in[at], keep(r.mixed0))
    add_mixed(r.mixed0, columns_of(r.ff0, 0, WOUT), z_sum, r.part)
    total = ColumnSum(r.part, r.summed, where, True, column_sets[0])
    total.begin()
    total.cross()
    ff1.turn()
    cots.end()
    in1.end()
    mix_back(lambda rows: r.cot[rows, :], columns_of(r.in1, WIN, WOUT), r.q_rows)
    heads_to_chips(lambda s, c, k: r.q_rows[group_rows(s, c, k), :], put_message(288))
    total.combine()
    ff1.pass_line()
    total.relay()
    total.end()
    shift = r.vectors[14:15, :] + r.vectors[15:16, :]

    def hidden(index):
        return r.tok[rows_at(index, 32), :].astype(F32) + rows32(r.summed, index) + shift

    normalize_rows(hidden, r.normed1, r.inverse1)
    scale_rows(r.normed1, r.vectors[2:3, :], r.vectors[6:7, :], r.first)
    project(r.first, r.in1, r.ib[3:6, :], tables, r.outbox, r.q_rows)
    heads_to_chips(lambda s, c, k: r.q_rows[group_rows(s, c, k), :], put_message(256))
    sent = exchange(2, r.outbox, r.inbox1, 320)

    def keep_own(index):
        r.own_hidden[rows_at(index, 32), :] = hidden(mine * 4 + index)

    loop(4, keep_own)
    scale_rows(r.normed1, r.vectors[3:4, :], r.vectors[7:8, :], r.second)
    ff1.end()
    expand(r.second, columns_of(r.ff1, 0, WFF), r.eb[3:4, :], r.inner1, r.act1)
    total.sent()
    sent.end()

    sort_pairs(r.order, r.inbox1, r.kvs1, r.kvt1)
    sort_rows(r.order, lambda at: r.inbox1[at, 256:288, :], r.qs1, False, HEAD_DIM**-0.5)
    sort_rows(r.order, lambda at: r.inbox1[at, 288:320, :], r.dos, True, 1.0)
    sent.sent()
    for tile in (3, 2, 1, 0):
        queries, outs = r.qs1[tile_rows(tile), :], r.dos[tile_rows(tile), :]
        mixed, lse = forward_tile(z, tile, queries, r.kvs1, r.kvt1, r.wide)
        r.rows[tile * 8 : tile * 8 + 8] = mixed.T.reshape(8, 32, 128)
        delta = jnp.sum(outs.astype(F32).T * mixed, axis=0, keepdims=True)
        query_grad = jnp.zeros((128, TILE), F32)
        for span in range(tile + 1):
            block = r.wide[span * SPAN : (span + 1) * SPAN, :]
            query_grad = query_grad + backward_span(
                tile, span, block, lse, delta, queries, outs, r.kvs1, r.kvt1, r.acc
            )
        r.o1[tile * 8 : tile * 8 + 8] = (query_grad.T * (HEAD_DIM**-0.5)).reshape(8, 32, 128)
    put_back_rows(r.ranks, r.rows, put_message(288), 1)
    put_back_rows(r.ranks, r.o1, put_message(256), 0)
    put_back_pairs(r.ranks, r.acc, r.outbox)
    sent = exchange(3, r.outbox, r.inbox0, 320)

    total1 = ColumnSum(r.part, r.summed2, where, False, column_sets[1])
    total2 = ColumnSum(r.part2, r.summed, where, True, column_sets[0])
    scatter_ff = Scatter(r.dw_ff, r.ff1_out, where, final(0), lines_ff)
    scatter_in = Scatter(r.dw_in, r.in1_out, where, final(1), lines_in)
    up, down = columns_of(r.ff1, 0, WFF), columns_of(r.ff1, WFF, WFF)
    expand_back(lambda rows: r.cot[rows, :], up, down, r.inner1, r.de, da2, r.eb_sums1)
    weight_grad(r.second, r.de, r.dw_ff, 0, WFF)
    weight_grad(r.cot, r.act1, r.dw_ff, WFF, WFF)
    sent.end()
    chips_to_heads(lambda at: r.inbox0[at, 256:288, :], keep(r.q_rows))
    project_back(r.inbox0, r.q_rows, tables, r.du, r.ib_sums1)
    join_back(
        r.du, r.in1, da2, r.normed1, r.vectors[2:3, :], r.vectors[3:4, :], r.sums1.at[pl.ds(0, 8)], r.part2
    )
    total2.begin()
    scatter_ff.begin()
    total2.cross()
    chips_to_heads(lambda at: r.inbox0[at, 288:320, :], keep(r.mixed1))
    weight_grad(r.cot, r.mixed1, r.dw_in, WIN, WOUT)
    weight_grad(r.first, r.du, r.dw_in, 0, WIN)
    total2.combine()
    scatter_ff.pass_on()
    scatter_in.begin()
    total2.relay()
    total2.end()
    r.sums1[8:16, :] = jnp.zeros((8, D), F32)
    r.sums0[8:16, :] = jnp.zeros((8, D), F32)

    def after(index):
        rows = rows_at(index, 32)
        before = r.cot[rows, :].astype(F32)
        return before, before + norm_back(
            rows32(r.summed, index), r.normed1[rows, :], r.inverse1[rows, 0:1]
        )

    def put_grad(index):
        before, values = after(index)
        r.sums1[8:9, :] += jnp.sum(before, axis=0, keepdims=True)
        r.sums0[8:9, :] += jnp.sum(values, axis=0, keepdims=True)
        dz_rows[rows_at(index, 32), :] = values.astype(BF16)

    loop(16, put_grad, 2)
    mix_back(lambda rows: dz_rows[rows, :], columns_of(r.ff0, 0, WOUT), r.q_rows)
    heads_to_chips(lambda s, c, k: r.q_rows[group_rows(s, c, k), :], put_to(r.dm_out))
    back = exchange(4, r.dm_out, r.dm_in, 32)
    sent.sent()
    scatter_ff.turn()
    scatter_in.pass_on()
    contract(r.act1, columns_of(r.ff1, WFF, WFF), z_sum)
    add_mixed(r.mixed1, columns_of(r.in1, WIN, WOUT), z_sum, r.part)
    total1.begin()
    scatter_ff.pass_line()
    scatter_in.turn()
    scale_rows(r.normed0, r.vectors[1:2, :], r.vectors[5:6, :], r.second)
    total1.cross()
    up, down = columns_of(r.ff0, WOUT, WFF), columns_of(r.ff0, WOUT + WFF, WFF)
    expand_back(lambda rows: dz_rows[rows, :], up, down, r.inner0, r.de, da2, r.eb_sums0)

    def keep_grad(index):
        r.own_grad[rows_at(index, 32), :] = after(mine * 4 + index)[1]

    back.end()

    sort_rows(r.order, lambda at: r.dm_in[at], r.dos, True, 1.0)
    scatter_ff0 = Scatter(r.dw_ff, r.ff0_out, where, final(2), lines_ff)
    scatter_in0 = Scatter(r.dw_in, r.in0_out, where, final(3), lines_in)

    def next_scatter():
        scatter_ff.end()
        weight_grad(r.second, r.de, r.dw_ff, 0, WFF)
        weight_grad(dz_rows, r.act0, r.dw_ff, WFF, WFF)
        scatter_ff0.begin()

    steps = {
        3: (scatter_ff.deliver, scatter_in.pass_line, total1.combine),
        2: (next_scatter,),
        1: (scatter_in.deliver,),
        0: (scatter_ff0.pass_on,),
    }
    for tile in (3, 2, 1, 0):
        queries, outs = r.qs0[tile_rows(tile), :], r.dos[tile_rows(tile), :]
        delta = jnp.sum(outs.astype(F32).T * r.o0[tile], axis=0, keepdims=True)
        lse = r.lse0[tile][0:1, :]
        query_grad = jnp.zeros((128, TILE), F32)
        for span in range(tile + 1):
            block = score_span(z, tile, span, queries, r.kvs0)
            query_grad = query_grad + backward_span(
                tile, span, block, lse, delta, queries, outs, r.kvs0, r.kvt0, r.acc
            )
        r.o1[tile * 8 : tile * 8 + 8] = (query_grad.T * (HEAD_DIM**-0.5)).reshape(8, 32, 128)
        for step in steps[tile]:
            step()
    put_back_rows(r.ranks, r.o1, put_message(256), 0)
    put_back_pairs(r.ranks, r.acc, r.outbox)
    sent = exchange(5, r.outbox, r.inbox1, 288)
    total1.end()
    shift = r.vectors[16:17, :] + r.vectors[17:18, :]
    for k in range(2):
        rows = pl.ds(k * 64, 64)
        r.act_out[rows, :] = (r.own_hidden[rows, :] + r.summed2[k].astype(F32) + shift).astype(BF16)
    total1.sent()
    total2.sent()

    total3 = ColumnSum(r.part, r.summed3, where, False, column_sets[0])
    loop(4, keep_grad)
    scatter_in.end()
    scatter_ff0.turn()
    weight_grad(dz_rows, r.mixed0, r.dw_in, WIN, WOUT)
    scatter_ff0.pass_line()
    scale_rows(r.normed0, r.vectors[0:1, :], r.vectors[4:5, :], r.first)
    scatter_ff0.deliver()
    sent.end()
    chips_to_heads(lambda at: r.inbox1[at, 256:288, :], keep(r.q_rows))
    project_back(r.inbox1, r.q_rows, tables, r.du, r.ib_sums0)
    weight_grad(r.first, r.du, r.dw_in, 0, WIN)
    scatter_in0.begin()
    join_back(
        r.du, r.in0, da2, r.normed0, r.vectors[0:1, :], r.vectors[1:2, :], r.sums0.at[pl.ds(0, 8)], r.part
    )
    total3.begin()
    scatter_in0.pass_on()
    total3.cross()

    once = jnp.where(place_in_column == 0, 1.0, 0.0)
    for half in range(2):
        for across in range(4):
            lanes = slice((half * 4 + across) * 128, (half * 4 + across + 1) * 128)
            at_home = jnp.where((tp == half) & (mine == across), 1.0, 0.0)
            for chip_z in range(4):
                cut = slice(chip_z * 128, (chip_z + 1) * 128)
                at = across * 4 + chip_z
                pieces = [
                    r.sums0[0:2, lanes], r.sums1[0:2, lanes], r.sums0[2:4, lanes], r.sums1[2:4, lanes],
                    r.ib_sums0[0:3, :] * at_home, r.ib_sums1[0:3, :] * at_home,
                    r.sums0[8:9, lanes] * once, r.sums0[8:9, lanes] * once,
                    r.sums1[8:9, lanes] * once, r.sums1[8:9, lanes] * once,
                    r.eb_sums0[0:1, cut] * at_home, r.eb_sums1[0:1, cut] * at_home,
                ]
                row = 0
                for piece in pieces:
                    count = piece.shape[0]
                    r.small[at, half, row : row + count, :] = piece
                    row += count
                r.small[at, half, 20:24, :] = jnp.zeros((4, 128), F32)
    around = []
    for k, (dx, dz) in enumerate(STEPS):
        copy = remote(
            r.small.at[ring(x, dx) * 4 + ring(z, dz)],
            r.gathered.at[k],
            r.send_s.at[k],
            r.recv_s.at[k],
            plane[k],
        )
        copy.start()
        around.append(copy)
    scatter_in0.turn()
    total3.combine()
    for copy in around:
        copy.wait_recv()
    r.total_s[...] = r.small[chip] + jnp.sum(r.gathered[...], axis=0)
    shared = []
    for k, peer in enumerate(column):
        copy = remote(r.total_s, r.others.at[k], r.send_d.at[k], r.recv_d.at[k], peer)
        copy.start()
        shared.append(copy)
    scatter_in0.pass_line()
    total3.end()
    own = mine * ROWS
    for k in range(4):
        rows = pl.ds(pl.multiple_of(own + k * 32, 32), 32)
        summed = r.summed3[k // 2, (k % 2) * 32 : (k % 2 + 1) * 32, :].astype(F32)
        r.grad_out[k * 32 : (k + 1) * 32, :] = r.own_grad[k * 32 : (k + 1) * 32, :] + norm_back(
            summed, r.normed0[rows, :], r.inverse0[rows, 0:1]
        )
    scatter_in0.deliver()
    for copy in shared:
        copy.wait_recv()
    sums_here = r.total_s[...] + jnp.sum(r.others[...], axis=0)
    sums_here = jnp.where(seq == 0, sums_here[0], sums_here[1])
    line = lax.broadcasted_iota(I32, sums_here.shape, 0)
    r.small_out[...] = jnp.where(
        line < 18,
        pltpu.roll(sums_here, 128 - (z * 4 + core * 2 + tp) * 8, 1),
        pltpu.roll(sums_here, 128 - (core * 2 + tp) * 32, 1),
    )
    scatter_ff0.end()
    scatter_in0.end()
    for copies in arriving:
        for copy in copies:
            copy.wait_send()
    for copy in smalls + spread + ranks_here + ranks_there + around + shared:
        copy.wait_send()
    for one in (cots, in0, ff0, in1, ff1, returned, back, sent, total3):
        one.sent()


def whole(*operands):
    outs = tuple(v for v in NAMES.values() if v is not None)
    scratch = [*SCRATCH.values(), *ColumnSum.SCRATCH * 2, *Scatter.scratch(PAIR), *Scatter.scratch(TWICE)]
    return pl.pallas_call(
        whole_kernel,
        out_shape=outs,
        in_specs=[VMEM] * len(operands),
        out_specs=(VMEM,) * len(outs),
        scratch_shapes=scratch,
        compiler_params=pltpu.CompilerParams(
            collective_id=0, has_side_effects=True, vmem_limit_bytes=LIMIT * MIB
        ),
        name="whole",
    )(*operands)


def outputs_kernel(
    in0, in1, ff0, ff1, small, input_out, output_out, expand_out, contract_out,
    gain_out, shift_out, input_shift_out, output_shift_out, expand_shift_out,
):
    for layer, (ins, ffs) in enumerate(((in0, ff0), (in1, ff1))):
        for k in range(4):
            part = ins[k].astype(F32)
            for t in range(3):
                at = t * 512 + k * 128
                input_out[layer, :, at : at + 128] = part[:, t * 128 : (t + 1) * 128]
            output_out[layer, :, k * WOUT : (k + 1) * WOUT] = part[:, WIN:]
            part = ffs[k].astype(F32)
            expand_out[layer, :, k * WFF : (k + 1) * WFF] = part[:, :WFF]
            contract_out[layer, :, k * WFF : (k + 1) * WFF] = part[:, WFF:]
        for k in range(2):
            row = layer * 2 + k
            gain_out[layer, k : k + 1, :] = small[row : row + 1, 0:8]
            shift_out[layer, k : k + 1, :] = small[row + 4 : row + 5, 0:8]
            output_shift_out[layer, k : k + 1, :] = small[row + 14 : row + 15, 0:8]
        input_shift_out[layer] = small[8 + layer * 3 : 11 + layer * 3, 0:8]
    expand_shift_out[...] = small[18:20, 0:32]


def outputs(*operands):
    outs = (
        f32(2, 16, 1536), f32(2, 16, 512), f32(2, 16, 2048), f32(2, 16, 2048),
        f32(2, 2, 8), f32(2, 2, 8), f32(2, 3, 8), f32(2, 2, 8), f32(2, 32),
    )
    return pl.pallas_call(
        outputs_kernel,
        out_shape=outs,
        in_specs=[VMEM] * len(operands),
        out_specs=(VMEM,) * len(outs),
        compiler_params=pltpu.CompilerParams(vmem_limit_bytes=8 * MIB),
        name="outputs",
    )(*operands)


def rotary_tables():
    half = ROT // 2
    freqs = 10000.0 ** (-(np.arange(half) * 2.0 / ROT))
    lane = np.arange(128) % HEAD_DIM
    every = np.where(lane < ROT, np.tile(freqs, 128 // half), 0.0)[None, :]
    start = np.arange(32)[:, None] * ROWS * every
    steps = np.arange(ROWS)[:, None] * every
    starts = np.stack([np.cos(start), np.sin(start)]).astype(np.float32)
    return starts, np.cos(steps).astype(np.float32), np.sin(steps).astype(np.float32)


def local(
    tokens, cotangent, group_order, input_weight, output_weight, expand_weight, contract_weight,
    norm_gain, norm_shift, input_bias, output_bias, expand_bias,
):
    win = input_weight.reshape(LAYERS, 16, 3, 4, 128).transpose(0, 3, 1, 2, 4)
    eights = [norm_gain, norm_shift, input_bias, output_bias]
    raw = jnp.concatenate(
        [
            jnp.pad(jnp.concatenate([v.reshape(-1, 8) for v in eights], axis=0), ((0, 0), (0, 120))),
            jnp.pad(expand_bias, ((0, 4), (0, 96))),
        ],
        axis=0,
    )
    activations, input_gradient, in0_out, in1_out, ff0_out, ff1_out, small = whole(
        win.reshape(LAYERS, 4, 16, WIN), output_weight, expand_weight, contract_weight, tokens, cotangent, raw,
        jnp.broadcast_to(group_order, (8, 128)), *rotary_tables(),
    )
    input_out, *rest = outputs(in0_out, in1_out, ff0_out, ff1_out, small)
    return (activations, input_gradient, input_out.reshape(2, 16, 3, 512), *rest)


def solution(mesh):
    rows, columns = P(("seq", "ctx"), None), P(None, None, ("seq", "ctx", "tp"))
    weight, flat = P(None, ("seq", "ctx"), "tp"), P(None, ("seq", "ctx", "tp"))
    first = P(None, ("seq", "ctx"), None, "tp")
    outs = (rows, rows, first, weight, weight, weight, columns, columns, columns, columns, flat)
    return jax.shard_map(
        local,
        mesh=mesh,
        in_specs=(rows, rows, P("seq", "ctx"), *outs[2:]),
        out_specs=outs,
        check_vma=False,
    )
```

```python
import types

import jax
import jax.numpy as jnp
import numpy as np
from jax import lax
from jax.experimental import pallas as pl
from jax.experimental.pallas import tpu as pltpu
from jax.sharding import PartitionSpec as P

MESH = pl.DeviceIdType.MESH
F32, BF16 = jnp.float32, jnp.bfloat16
D, HEAD_DIM, ROT, LAYERS = 1024, 64, 16, 2
ROWS = 128
GROUP = 512
WIN, WOUT, WFF = 384, 128, 512
COLS = WIN + WOUT + 2 * WFF
PARAMS = 208
EPSILON = 1e-05
MASKED = -1e30
MIB = 1024 * 1024
LIMIT = 62
WIDE = WOUT + 2 * WFF
PAIR, TWICE = WIN + WOUT, 2 * WFF
MESSAGE = 320


def place():
    ctx = lax.axis_index("ctx")
    chip = lax.div(ctx, 2)
    y = lax.axis_index("seq") * 2 + lax.axis_index("tp")
    return y, lax.div(chip, 4), lax.rem(chip, 4), lax.rem(ctx, 2)


def device(y, x, z, core):
    return (lax.div(y, 2), (x * 4 + z) * 2 + core, lax.rem(y, 2))


def ring(index, step):
    return lax.rem(index + step, 4)


def enter(partners):
    barrier = pltpu.get_barrier_semaphore()
    for partner in partners:
        pl.semaphore_signal(barrier, inc=1, device_id=partner, device_id_type=MESH)
    pl.semaphore_wait(barrier, len(partners))


STEPS = (
    (2, 2), (2, 1), (1, 2), (2, 3), (3, 2), (1, 1), (3, 3), (1, 3), (3, 1), (2, 0), (0, 2), (0, 1), (1, 0), (0, 3), (3, 0)
)


def plane_partners(y, x, z, core):
    return [device(y, ring(x, dx), ring(z, dz), core) for dx, dz in STEPS]


def column_partners(y, x, z, core):
    return [
        device(ring(y, dy), x, z, lax.rem(core + dc, 2))
        for dy in range(4)
        for dc in range(2)
        if dy or dc
    ]


def remote(source, target, send, receive, partner):
    return pltpu.make_async_remote_copy(
        src_ref=source,
        dst_ref=target,
        send_sem=send,
        recv_sem=receive,
        device_id=partner,
        device_id_type=MESH,
    )


HBM = pl.BlockSpec(memory_space=pl.ANY)
VMEM = pl.BlockSpec(memory_space=pltpu.VMEM)
SMEM = pl.BlockSpec(memory_space=pltpu.SMEM)


def bf(*shape):
    return jax.ShapeDtypeStruct(shape, BF16)


def f32(*shape):
    return jax.ShapeDtypeStruct(shape, F32)


def vbf(*shape):
    return pltpu.VMEM(shape, BF16)


def vf32(*shape):
    return pltpu.VMEM(shape, F32)


def dma(*shape):
    return pltpu.SemaphoreType.DMA(shape)


PEERS = ((0, 1), (1, 0), (1, 1))


def peer_at(y, x, z, core, step):
    seq, tp = lax.div(y, 2), lax.rem(y, 2)
    seq_to, core_to = lax.rem(seq + step[0], 2), lax.rem(core + step[1], 2)
    return seq_to * 2 + core_to, device(seq_to * 2 + tp, x, z, core_to)


class Gather:
    def __init__(self, full, where, send, recv):
        y, x, z, core = where
        self.full, self.x, self.z, self.send, self.recv = full, x, z, send, recv
        self.near = {
            "x": (device(y, ring(x, 1), z, core), device(y, ring(x, 3), z, core)),
            "z": (device(y, x, ring(z, 1), core), device(y, x, ring(z, 3), core)),
        }
        self.held = [(), ()]
        self.started = []

    def go(self, source, slot, partner):
        copy = remote(source, source, self.send.at[slot], self.recv.at[slot], partner)
        copy.start()
        self.started.append(copy)
        return copy

    def begin(self):
        for half in range(2):
            up, down = self.near["xz"[half]]
            own = self.full.at[half, self.x, self.z]
            self.held[half] = (self.go(own, half * 8, up), self.go(own, half * 8 + 1, down))

    def arrive(self, half):
        for copy in self.held[half]:
            copy.wait_recv()

    def pass_on(self):
        x, z = self.x, self.z
        for half in range(2):
            self.arrive(half)
            up, down = self.near["xz"[half]]
            whole = self.full.at[half]
            if half == 0:
                before, after = whole.at[ring(x, 3), z], whole.at[ring(x, 1), z]
            else:
                before, after = whole.at[x, ring(z, 3)], whole.at[x, ring(z, 1)]
            self.held[half] = (
                self.go(before.at[pl.ds(0, 16)], half * 8 + 2, up),
                self.go(after.at[pl.ds(16, 16)], half * 8 + 3, down),
            )

    def turn(self):
        for half in range(2):
            self.arrive(half)
            up, down = self.near["zx"[half]]
            whole = self.full.at[half]
            line = whole.at[:, self.z] if half == 0 else whole.at[self.x]
            self.held[half] = (self.go(line, half * 8 + 4, up), self.go(line, half * 8 + 5, down))

    def pass_line(self):
        x, z = self.x, self.z
        two, more = pl.ds(0, 2), pl.ds(2, 2)
        for half in range(2):
            self.arrive(half)
            up, down = self.near["zx"[half]]
            whole = self.full.at[half]
            if half == 0:
                before, after = whole.at[two, ring(z, 3)], whole.at[more, ring(z, 1)]
            else:
                before, after = whole.at[ring(x, 3), two], whole.at[ring(x, 1), more]
            self.held[half] = (
                self.go(before, half * 8 + 6, up),
                self.go(after, half * 8 + 7, down),
            )

    def end(self):
        for half in range(2):
            self.arrive(half)

    def sent(self):
        for copy in self.started:
            copy.wait_send()


class RowShare:
    def __init__(self, source, target, where, send, recv):
        y, x, z, core = where
        self.source, self.target, self.send, self.recv = source, target, send, recv
        seq = lax.div(y, 2)
        self.own = rows_at(seq * 2 + core, ROWS)
        self.other = rows_at((1 - seq) * 2 + core, ROWS)
        self.sibling = device(y, x, z, lax.rem(core + 1, 2))
        self.facing = device(3 - y, x, z, core)
        self.copies = []

    def go(self, source, target, slot, partner):
        copy = remote(source, target, self.send.at[slot], self.recv.at[slot], partner)
        copy.start()
        self.copies.append(copy)

    def begin(self):
        self.target[self.own, :] = self.source[...]
        self.go(self.source, self.target.at[self.own], 0, self.facing)
        self.go(self.source, self.target.at[self.own], 1, self.sibling)

    def pass_on(self):
        self.copies[0].wait_recv()
        block = self.target.at[self.other]
        self.go(block, block, 2, self.sibling)

    def end(self):
        for copy in self.copies[1:]:
            copy.wait_recv()

    def sent(self):
        for copy in self.copies:
            copy.wait_send()


class ColumnSum:
    SCRATCH = [vbf(4, 64, D), vbf(3, 64, D), vbf(3, 64, D)] + [dma(4), dma(4), dma(3), dma(3), dma(7), dma(7)]
    ORDER = (2, 1, 3)

    def __init__(self, part, out, where, everywhere, scratch):
        self.part, self.out, self.where, self.everywhere = part, out, where, everywhere
        (self.near, self.far, self.held, self.send1, self.recv1, self.send2, self.recv2, self.send3, self.recv3) = scratch
        y, x, z, core = where
        self.sibling = device(y, x, z, lax.rem(core + 1, 2))
        self.chips = [device(ring(y, dy), x, z, core) for dy in (1, 2, 3)]

    def begin(self):
        y, x, z, core = self.where
        self.nears = {}
        for dy in (*self.ORDER, 0):
            to = ring(y, dy)
            source = self.part.at[lax.div(to, 2), lax.rem(core + 1, 2), lax.rem(to, 2)]
            self.nears[dy] = remote(
                source, self.near.at[dy], self.send1.at[dy], self.recv1.at[dy], self.sibling
            )
            self.nears[dy].start()

    def cross(self):
        y, x, z, core = self.where
        self.fars = []
        for dy in self.ORDER:
            to = ring(y, dy)
            self.nears[dy].wait_recv()
            own = self.part[lax.div(to, 2), core, lax.rem(to, 2)].astype(F32)
            self.held[dy - 1] = (own + self.near[dy].astype(F32)).astype(BF16)
            copy = remote(
                self.held.at[dy - 1],
                self.far.at[dy - 1],
                self.send2.at[dy - 1],
                self.recv2.at[dy - 1],
                self.chips[dy - 1],
            )
            copy.start()
            self.fars.append(copy)

    def combine(self):
        y, x, z, core = self.where
        seq, tp = lax.div(y, 2), lax.rem(y, 2)
        self.nears[0].wait_recv()
        total = self.part[seq, core, tp].astype(F32) + self.near[0].astype(F32)
        for copy in self.fars:
            copy.wait_recv()
        for k in range(3):
            total = total + self.far[k].astype(F32)
        self.outs, self.relayed = [], []
        own = self.out.at[seq, core, tp] if self.everywhere else self.out.at[tp]
        own[...] = total.astype(BF16)
        if self.everywhere:
            for dy in self.ORDER:
                self.go(self.outs, own, dy - 1, self.chips[dy - 1])
            self.go(self.relayed, own, 3, self.sibling)
        else:
            self.go(self.outs, own, 0, device(seq * 2 + lax.rem(tp + 1, 2), x, z, core))

    def go(self, kept, block, slot, partner):
        copy = remote(block, block, self.send3.at[slot], self.recv3.at[slot], partner)
        copy.start()
        kept.append(copy)

    def relay(self):
        y, x, z, core = self.where
        for at, dy in enumerate(self.ORDER):
            self.outs[at].wait_recv()
            source = ring(y, 4 - dy)
            block = self.out.at[lax.div(source, 2), core, lax.rem(source, 2)]
            self.go(self.relayed, block, 3 + dy, self.sibling)

    def end(self):
        if self.everywhere:
            for copy in self.relayed:
                copy.wait_recv()
        else:
            self.outs[0].wait_recv()

    def sent(self):
        for copy in (*self.nears.values(), *self.fars, *self.outs, *self.relayed):
            copy.wait_send()


class Scatter:
    def __init__(self, dw, out, where, final, scratch):
        y, x, z, core = where
        self.dw, self.out, self.where, self.x, self.z = dw, out, where, x, z
        (self.opp1, self.dir1, self.comb1, self.sent1, self.mid, self.opp2, self.dir2, self.comb2, self.sent2, self.done,
         self.send, self.recv) = scratch
        self.send_f, self.recv_f = final
        self.near = {
            "x": (device(y, ring(x, 1), z, core), device(y, ring(x, 3), z, core)),
            "z": (device(y, x, ring(z, 1), core), device(y, x, ring(z, 3), core)),
        }
        self.started, self.held = [], [(), ()]

    @staticmethod
    def scratch(columns):
        big, small = vbf(2, 2, 2, 32, columns), vbf(2, 2, 16, columns)
        mid = vbf(2, 4, 32, columns)
        return [big] * 4 + [mid] + [small] * 5 + [dma(24), dma(24)]

    def go(self, source, target, slot, partner):
        copy = remote(source, target, self.send.at[slot], self.recv.at[slot], partner)
        copy.start()
        self.started.append(copy)
        return copy

    def part1(self, half, step, side):
        two = pl.ds(side * 2, 2)
        whole = self.dw.at[half]
        if half == 0:
            return whole.at[two, ring(self.z, step)]
        return whole.at[ring(self.x, step), two]

    def part2(self, half, step, side):
        at = ring(self.x, step) if half == 0 else ring(self.z, step)
        return self.mid.at[half, at].at[pl.ds(side * 16, 16)]

    def open(self, half, part, axis, opposite, direct, base):
        up, down = self.near[axis]
        self.held[half] = (
            self.go(part(half, 2, 0), opposite.at[half, 0], base, up),
            self.go(part(half, 2, 1), opposite.at[half, 1], base + 1, down),
            self.go(part(half, 1, 1), direct.at[half, 0], base + 2, up),
            self.go(part(half, 3, 0), direct.at[half, 1], base + 3, down),
        )

    def onward(self, half, part, axis, opposite, combined, sent, base):
        up, down = self.near[axis]
        copies = self.held[half]
        copies[0].wait_recv()
        sent[half, 0] = (part(half, 1, 0)[...].astype(F32) + opposite[half, 0].astype(F32)).astype(BF16)
        first = self.go(sent.at[half, 0], combined.at[half, 0], base + 4, up)
        copies[1].wait_recv()
        sent[half, 1] = (part(half, 3, 1)[...].astype(F32) + opposite[half, 1].astype(F32)).astype(BF16)
        second = self.go(sent.at[half, 1], combined.at[half, 1], base + 5, down)
        self.held[half] = (*copies[2:], first, second)

    def finish(self, half, part, direct, combined, target):
        for copy in self.held[half]:
            copy.wait_recv()
        for side in range(2):
            total = (
                part(half, 0, side)[...].astype(F32)
                + combined[half, side].astype(F32)
                + direct[half, 1 - side].astype(F32)
            )
            target(half, side)[...] = total.astype(BF16)

    def begin(self):
        for half in range(2):
            self.open(half, self.part1, "zx"[half], self.opp1, self.dir1, half * 12)

    def pass_on(self):
        for half in range(2):
            self.onward(half, self.part1, "zx"[half], self.opp1, self.comb1, self.sent1, half * 12)

    def turn(self):
        for half in range(2):
            self.finish(
                half,
                self.part1,
                self.dir1,
                self.comb1,
                lambda h, side: self.mid.at[h, pl.ds(side * 2, 2)],
            )
            self.open(half, self.part2, "xz"[half], self.opp2, self.dir2, half * 12 + 6)

    def pass_line(self):
        for half in range(2):
            self.onward(
                half, self.part2, "xz"[half], self.opp2, self.comb2, self.sent2, half * 12 + 6
            )

    def deliver(self):
        y, x, z, core = self.where
        seq = lax.div(y, 2)
        mine = seq * 2 + core
        for half in range(2):
            self.finish(
                half, self.part2, self.dir2, self.comb2, lambda h, side: self.done.at[h, side]
            )
        self.out[mine] = self.done[seq, core]
        self.final = []
        for k, step in enumerate(PEERS):
            theirs, peer = peer_at(y, x, z, core, step)
            copy = remote(
                self.done.at[lax.div(theirs, 2), lax.rem(theirs, 2)],
                self.out.at[mine],
                self.send_f.at[k],
                self.recv_f.at[k],
                peer,
            )
            copy.start()
            self.final.append(copy)

    def end(self):
        for copy in self.final:
            copy.wait()
        for copy in self.started:
            copy.wait_send()


class Exchange:
    def __init__(self, where, source, target, rows, send, recv):
        y, x, z, core = where
        chip = x * 4 + z
        cut = pl.ds(0, rows)
        target[chip, cut, :] = source[chip, cut, :]
        self.copies = []
        for k, (dx, dz) in enumerate(STEPS):
            to_x, to_z = ring(x, dx), ring(z, dz)
            copy = remote(
                source.at[to_x * 4 + to_z, cut],
                target.at[chip, cut],
                send.at[k],
                recv.at[k],
                device(y, to_x, to_z, core),
            )
            copy.start()
            self.copies.append(copy)

    def end(self):
        for copy in self.copies:
            copy.wait_recv()

    def sent(self):
        for copy in self.copies:
            copy.wait_send()


def loop(count, body, together=1):
    def step(index, carry):
        for k in range(together):
            body(index * together + k)
        return carry

    lax.fori_loop(0, count // together, step, 0)


def rows_at(index, count):
    return pl.ds(pl.multiple_of(index * count, count), count)


def turned(values, tables, sign):
    one, right, left = tables
    half = ROT // 2
    return values * one + sign * (
        pltpu.roll(values, 128 - half, 1) * right + pltpu.roll(values, half, 1) * left
    )


def low_lanes(shape):
    return lax.broadcasted_iota(jnp.int32, shape, 1) < HEAD_DIM


def swap(values):
    return pltpu.roll(values, HEAD_DIM, 1)


def heads_to_chips(values, target):
    def body(index):
        seq, quarter = lax.div(index, 4), lax.rem(index, 4)
        first, second = values(seq, 0, quarter), values(seq, 1, quarter)
        low = low_lanes(first.shape)
        target(seq * 8 + quarter, jnp.where(low, first, swap(second)).astype(BF16))
        target(seq * 8 + 4 + quarter, jnp.where(low, swap(first), second).astype(BF16))

    loop(8, body, 4)


def group_rows(seq, core, quarter):
    return pl.ds(pl.multiple_of(seq * 256 + core * 128 + quarter * 32, 32), 32)


def normalize_rows(hidden, normed, inverse, first=0, count=16):
    def body(step):
        index = step + first
        rows = rows_at(index, 32)
        values = hidden(index)
        centred = values - jnp.mean(values, axis=1, keepdims=True)
        spread = jnp.mean(centred * centred, axis=1, keepdims=True)
        scale = lax.rsqrt(spread + EPSILON)
        normed[rows, :] = centred * scale
        inverse[rows, :] = jnp.broadcast_to(scale, (32, 128))

    loop(count, body, 2)


def scale_rows(normed, gain, shift, target):
    def body(index):
        rows = rows_at(index, 32)
        target[rows, :] = (normed[rows, :] * gain + shift).astype(BF16)

    loop(16, body)


def project(first, weight, bias, tables, outbox, q_rows):
    whole = columns_of(weight, 0, WIN)

    def body(index):
        rows = rows_at(index, 128)
        u = jnp.dot(first[rows, :], whole, preferred_element_type=F32)
        turn = tuple(t[rows, :] for t in tables)
        q_rows[rows, :] = turned(u[:, :128] + bias[0:1, :], turn, 1.0)
        keys = turned(u[:, 128:256] + bias[1:2, :], turn, 1.0)
        values = u[:, 256:] + bias[2:3, :]
        low = low_lanes(keys.shape)
        seq = lax.div(index, 2)
        part = rows_at(lax.rem(index, 2), 128)
        for head in range(2):
            pair = (keys, swap(values)) if head == 0 else (swap(keys), values)
            pair = jnp.where(low, *pair).astype(BF16)
            for k in range(4):
                outbox[seq * 8 + head * 4 + k, part, :] = pair

    loop(4, body)


def gelu_parts(inner):
    return 0.5 * (1.0 + lax.erf(inner * (0.5**0.5)))


def columns_of(weight, first, count):
    return weight[:, :, :, :, first : first + count].reshape(D, count)


def expand(second, whole, bias, inner, activated):

    def body(index):
        rows = rows_at(index, 128)
        e = jnp.dot(second[rows, :], whole, preferred_element_type=F32) + bias
        inner[rows, :] = e
        activated[rows, :] = (e * gelu_parts(e)).astype(BF16)

    loop(4, body)


def chips_to_heads(parts, target):
    def body(index):
        seq, quarter = lax.div(index, 4), lax.rem(index, 4)
        first = parts(seq * 8 + quarter).astype(F32)
        second = parts(seq * 8 + 4 + quarter).astype(F32)
        low = low_lanes(first.shape)
        target(seq, 0, quarter, jnp.where(low, first, swap(second)))
        target(seq, 1, quarter, jnp.where(low, swap(first), second))

    loop(8, body, 4)


def block_of(index):
    return lax.div(index, 2), lax.rem(index, 2)


class Wide:
    def __init__(self, buffer, base):
        self.buffer, self.base = buffer, base

    def at(self, start, count, k):
        return pl.ds(pl.multiple_of(self.base + k * GROUP + start, count), count)

    def put(self, start, count, values):
        for k in range(4):
            self.buffer[self.at(start, count, k), :] = values[:, k * 256 : (k + 1) * 256]

    def get(self, start, count):
        return jnp.concatenate([self.buffer[self.at(start, count, k), :] for k in range(4)], axis=1)


def contract(activated, whole, z):

    def body(index):
        rows = rows_at(index, 128)
        values = lax.dot_general(
            activated[rows, :], whole, (((1,), (1,)), ((), ())), preferred_element_type=F32
        )
        z.put(index * 128, 128, values)

    loop(4, body)


def add_mixed(mixed, weight, z, part, core, between):
    def one(seq, core):
        index = seq * 2 + core
        rows = rows_at(index, 128)
        both = z.get(index * 128, 128) + lax.dot_general(
            mixed[rows, :], weight, (((1,), (1,)), ((), ())), preferred_element_type=F32
        )
        part[seq, core] = both.astype(BF16).reshape(2, 64, D)

    loop(2, lambda seq: one(seq, 1 - core))
    between()
    loop(2, lambda seq: one(seq, core))


def rows32(summed, index):
    seq, core, tp = lax.div(index, 8), lax.rem(lax.div(index, 4), 2), lax.rem(lax.div(index, 2), 2)
    return summed[seq, core, tp, rows_at(lax.rem(index, 2), 32), :].astype(F32)


def mix_back(dz, weight, rows128):
    def body(index):
        rows = rows_at(index, 128)
        dm = jnp.dot(dz(rows), weight, preferred_element_type=F32)
        rows128[rows, :] = dm.astype(BF16).astype(F32)

    loop(4, body)


def expand_back(dz, up, down, inner, de, da, sums):
    sums[0:1, :] = jnp.zeros((1, WFF), F32)

    def body(index):
        rows = rows_at(index, 128)
        dg = jnp.dot(dz(rows), down, preferred_element_type=F32)
        e = inner[rows, :]
        slope = gelu_parts(e) + e * jnp.exp(-0.5 * e * e) * ((2.0 * jnp.pi) ** -0.5)
        low = (dg * slope).astype(BF16)
        de[rows, :] = low
        sums[0:1, :] += jnp.sum(low.astype(F32), axis=0, keepdims=True)
        values = lax.dot_general(low, up, (((1,), (1,)), ((), ())), preferred_element_type=F32)
        da.put(index * 128, 128, values)

    loop(4, body)


def weight_grad(left, right, dw, first, count):
    def body(index):
        block = lax.dot_general(
            left[:, rows_at(index, 256)],
            right[...],
            (((0,), (0,)), ((), ())),
            preferred_element_type=F32,
        )
        two = pl.ds(lax.rem(index, 2) * 2, 2)
        dw[lax.div(index, 2), two, :, :, first : first + count] = block.astype(BF16).reshape(
            2, 4, 32, count
        )

    loop(4, body)


def project_back(pairs, q_grad, tables, du, sums):
    sums[...] = jnp.zeros(sums.shape, F32)

    def body(index):
        seq, core = block_of(index)
        part = rows_at(core, 128)
        heads = []
        for head in range(2):
            total = pairs[seq * 8 + head * 4, part, :].astype(F32)
            for k in range(1, 4):
                total = total + pairs[seq * 8 + head * 4 + k, part, :].astype(F32)
            heads.append(total)
        low = low_lanes(heads[0].shape)
        rows = rows_at(index, 128)
        turn = tuple(t[rows, :] for t in tables)
        grads = (
            turned(q_grad[rows, :], turn, -1.0),
            turned(jnp.where(low, heads[0], swap(heads[1])), turn, -1.0),
            jnp.where(low, swap(heads[0]), heads[1]),
        )
        for k in range(3):
            rounded = grads[k].astype(BF16)
            du[rows, k * 128 : (k + 1) * 128] = rounded
            sums[k : k + 1, :] += jnp.sum(rounded.astype(F32), axis=0, keepdims=True)

    loop(4, body)


def join_back(du, weight, da2, normed, gain1, gain2, sums, part, core, between):
    whole = columns_of(weight, 0, WIN)
    sums[...] = jnp.zeros(sums.shape, F32)

    def one(step, core):
        seq, tp = lax.div(step, 2), lax.rem(step, 2)
        index = seq * 4 + core * 2 + tp
        rows = rows_at(index, 64)
        da = lax.dot_general(
            du[rows, :], whole, (((1,), (1,)), ((), ())), preferred_element_type=F32
        )
        db = da2.get(index * 64, 64)
        n = normed[rows, :]
        for k, value in enumerate((da * n, db * n, da, db)):
            sums[k : k + 1, :] += jnp.sum(value, axis=0, keepdims=True)
        part[seq, core, tp] = (da * gain1 + db * gain2).astype(BF16)

    loop(4, lambda step: one(step, 1 - core), 2)
    between()
    loop(4, lambda step: one(step, core), 2)


def norm_back(scaled, normed, inverse):
    first = jnp.mean(scaled, axis=1, keepdims=True)
    second = jnp.mean(scaled * normed, axis=1, keepdims=True)
    return inverse * (scaled - first - normed * second)


TILE = 256
SPAN = 1024


def seen(quarter, tile):
    key = lax.broadcasted_iota(jnp.int32, (SPAN, TILE), 0)
    row = lax.broadcasted_iota(jnp.int32, (SPAN, TILE), 1)
    place_of = (row // 32) * ROWS + quarter * 32 + row % 32
    return key <= place_of


def score_span(quarter, tile, span, queries, kvs):
    block = lax.dot_general(
        kvs[span * SPAN : (span + 1) * SPAN, :],
        queries,
        (((1,), (1,)), ((), ())),
        preferred_element_type=F32,
    )
    return jnp.where(seen(quarter, tile), block, MASKED) if span == tile else block


def forward_tile(quarter, tile, queries, kvs, kvt, score):
    highest = jnp.full((1, TILE), MASKED, F32)
    for span in range(tile + 1):
        block = score_span(quarter, tile, span, queries, kvs)
        score[span * SPAN : (span + 1) * SPAN, :] = block
        highest = jnp.maximum(highest, jnp.max(block, axis=0, keepdims=True))
    total = jnp.zeros((1, TILE), F32)
    mixed = jnp.zeros((128, TILE), F32)
    for span in range(tile + 1):
        weight = jnp.exp(score[span * SPAN : (span + 1) * SPAN, :] - highest)
        total = total + jnp.sum(weight, axis=0, keepdims=True)
        mixed = mixed + jnp.dot(
            kvt[:, span * SPAN : (span + 1) * SPAN],
            weight.astype(BF16),
            preferred_element_type=F32,
        )
    return mixed / total, highest + jnp.log(total)


def backward_span(tile, span, block, lse, delta, queries, outs, kvs, kvt, acc):
    keyed = kvs[span * SPAN : (span + 1) * SPAN, :]
    probs = jnp.exp(block - lse)
    back = lax.dot_general(keyed, outs, (((1,), (1,)), ((), ())), preferred_element_type=F32)
    score_grad = (probs * (back - delta)).astype(BF16)
    pair = jnp.dot(
        jnp.concatenate([score_grad, probs.astype(BF16)], axis=1),
        jnp.concatenate([queries, outs], axis=0),
        preferred_element_type=F32,
    )
    pair = pair.reshape(8, ROWS, 128)
    if tile == 3:
        acc[span * 8 : (span + 1) * 8] = pair
    else:
        acc[span * 8 : (span + 1) * 8] += pair
    return jnp.dot(
        kvt[:, span * SPAN : (span + 1) * SPAN], score_grad, preferred_element_type=F32
    )


def put_back_rows(ranks, rows, target, upper):
    def body(chip):
        first = rows[ranks[0, chip * 2]]
        second = rows[ranks[0, chip * 2 + 1]]
        if upper:
            first = swap(first)
        else:
            second = swap(second)
        target(chip, jnp.where(low_lanes(first.shape), first, second).astype(BF16))

    loop(16, body, 8)


def put_back_pairs(ranks, acc, outbox):
    def body(chip):
        for core in range(2):
            rank = ranks[0, chip * 2 + core]
            outbox[chip, core * ROWS : (core + 1) * ROWS, :] = acc[rank].astype(BF16)

    loop(16, body, 2)


def owner(order, rank):
    return order[rank, 0], order[rank, 1]


def sort_rows(order, source, target, upper, scale):
    def body(rank):
        chip, core = owner(order, rank)
        block = source(chip).astype(F32) * scale
        other = swap(block)
        low = low_lanes(block.shape)
        if upper:
            part = jnp.where(low, 0.0, jnp.where(core == 0, other, block))
        else:
            part = jnp.where(low, jnp.where(core == 0, block, other), 0.0)
        target[rows_at(rank, 32), :] = part.astype(BF16)

    loop(32, body, 8)


def sort_pairs(order, inbox, kvs, kvt):
    def body(rank):
        chip, core = owner(order, rank)
        keyed = jnp.where(core == 0, inbox[chip, 0:ROWS, :], inbox[chip, ROWS : 2 * ROWS, :])
        kvs[rows_at(rank, ROWS), :] = keyed
        kvt[:, rows_at(rank, ROWS)] = keyed.astype(F32).T.astype(BF16)

    loop(32, body, 4)


def tile_rows(tile):
    return slice(tile * TILE, (tile + 1) * TILE)


NAMES = {
    "win": None, "wout": None, "wexp": None, "wcon": None, "tok_in": None, "cot_in": None, "raw": None, "rank": None,
    "angles": None,
    "act_out": bf(ROWS, D), "grad_out": f32(ROWS, D), "weights_out": bf(2, 4, 16, PAIR + TWICE), "small_out": f32(24, 128),
}
I32 = jnp.int32
SCRATCH = {
    "in0": vbf(2, 4, 4, 32, WIN), "in1": vbf(2, 4, 4, 32, PAIR),
    "ff0": vbf(2, 4, 4, 32, WIDE), "ff1": vbf(2, 4, 4, 32, TWICE),
    "wff0": vbf(4, 16, WIDE), "win1": vbf(4, 16, PAIR), "wff1": vbf(4, 16, TWICE),
    "tok": vbf(GROUP, D), "cot": vbf(GROUP, D),
    "par": vf32(24, 128), "trig": vf32(8, 128), "column_p": vf32(8, 24, 128), "joined": vf32(2, 24, 128),
    "plane_p": vf32(16, 2, 24, 128), "column_t": vf32(4, 8, 128), "vectors": vf32(24, D),
    "ib": vf32(8, 128), "eb": vf32(8, WFF),
    "par_i": pltpu.VMEM((8, 128), I32), "column_i": pltpu.VMEM((8, 8, 128), I32),
    "joined_i": pltpu.VMEM((2, 8, 128), I32), "plane_i": pltpu.VMEM((16, 2, 8, 128), I32),
    "ranks_v": pltpu.VMEM((8, 128), I32), "order_v": pltpu.VMEM((32, 128), I32),
    "ranks": pltpu.SMEM((8, 128), I32), "order": pltpu.SMEM((32, 128), I32),
    "one": vf32(GROUP, 128), "right": vf32(GROUP, 128), "left": vf32(GROUP, 128),
    "normed0": vf32(GROUP, D), "normed1": vf32(GROUP, D), "inverse0": vf32(GROUP, 128), "inverse1": vf32(GROUP, 128),
    "first": vbf(GROUP, D), "second": vbf(GROUP, D),
    "inner0": vf32(GROUP, WFF), "inner1": vf32(GROUP, WFF), "act0": vbf(GROUP, WFF), "act1": vbf(GROUP, WFF),
    "mixed0": vbf(GROUP, 128), "mixed1": vbf(GROUP, 128), "q_rows": vf32(GROUP, 128),
    "outbox": vbf(16, MESSAGE, 128), "inbox0": vbf(16, MESSAGE, 128), "inbox1": vbf(16, MESSAGE, 128),
    "m_out": vbf(16, 32, 128), "m_in": vbf(16, 32, 128), "dm_out": vbf(16, 32, 128), "dm_in": vbf(16, 32, 128),
    "kvs0": vbf(4096, 128), "kvs1": vbf(4096, 128), "kvt0": vbf(128, 4096), "kvt1": vbf(128, 4096),
    "qs0": vbf(1024, 128), "qs1": vbf(1024, 128), "dos": vbf(1024, 128), "o0": vf32(4, 128, TILE), "lse0": vf32(4, 8, TILE),
    "wide": vf32(4096, TILE), "rows": vf32(32, 32, 128), "o1": vf32(32, 32, 128), "acc": vf32(32, 128, 128),
    "de": vbf(GROUP, WFF), "du": vbf(GROUP, WIN), "own_grad": vf32(ROWS, D), "own_hidden": vf32(ROWS, D),
    "part": vbf(2, 2, 2, 64, D), "part2": vbf(2, 2, 2, 64, D), "summed": vbf(2, 2, 2, 64, D),
    "summed2": vbf(2, 64, D), "summed3": vbf(2, 64, D),
    "dw_in": vbf(2, 4, 4, 32, PAIR), "dw_ff": vbf(2, 4, 4, 32, TWICE),
    "sums0": vf32(16, D), "sums1": vf32(16, D), "ib_sums0": vf32(8, 128), "ib_sums1": vf32(8, 128),
    "eb_sums0": vf32(8, WFF), "eb_sums1": vf32(8, WFF),
    "small": vf32(16, 2, 24, 128), "gathered": vf32(15, 2, 24, 128), "total_s": vf32(2, 24, 128), "others": vf32(7, 2, 24, 128),
    "here": dma(7), "send_a": dma(5, 3), "recv_a": dma(5, 3), "send_t": dma(2, 3), "recv_t": dma(2, 3),
    "send_p": dma(2, 7), "recv_p": dma(2, 7), "send_v": dma(2, 15), "recv_v": dma(2, 15),
    "send_g": dma(4, 16), "recv_g": dma(4, 16), "send_x": dma(6, 15), "recv_x": dma(6, 15),
    "send_f": dma(4, 3), "recv_f": dma(4, 3), "send_s": dma(15), "recv_s": dma(15), "send_d": dma(7), "recv_d": dma(7),
}
COLUMN = len(ColumnSum.SCRATCH)
LINES = len(Scatter.scratch(WIN))


def whole_kernel(*refs):
    names = [*NAMES, *SCRATCH]
    r = types.SimpleNamespace(**dict(zip(names, refs)))
    rest = refs[len(names) :]
    column_sets = [rest[k * COLUMN : (k + 1) * COLUMN] for k in range(2)]
    rest = rest[2 * COLUMN :]
    lines_in, lines_ff = rest[:LINES], rest[LINES:]
    where = y, x, z, core = place()
    seq, tp = lax.div(y, 2), lax.rem(y, 2)
    mine, chip = seq * 2 + core, x * 4 + z
    column, plane = column_partners(*where), plane_partners(*where)
    tables = (r.one, r.right, r.left)
    dz_rows = r.tok
    z_sum, da2 = Wide(r.wide, 0), Wide(r.wide, 4 * GROUP)

    def exchange(number, source, target, rows):
        return Exchange(where, source, target, rows, r.send_x.at[number], r.recv_x.at[number])

    def final(number):
        return r.send_f.at[number], r.recv_f.at[number]

    raw = r.raw[...]
    line = lax.broadcasted_iota(I32, raw.shape, 0)
    r.par[...] = jnp.where(
        line < 18,
        pltpu.roll(raw, (z * 4 + core * 2 + tp) * 8, 1),
        pltpu.roll(raw, (core * 2 + tp) * 32, 1),
    )
    lane = lax.broadcasted_iota(I32, (8, 128), 1)
    r.par_i[...] = jnp.where((lane == chip * 2 + core) & (tp == 0), r.rank[...], 0)
    r.trig[...] = jnp.zeros((8, 128), F32)
    for k in range(2):
        starts = r.angles[k * 32 : (k + 1) * 32, :]
        chosen = lax.broadcasted_iota(I32, starts.shape, 0) == r.rank[...]
        r.trig[k : k + 1, :] = jnp.sum(jnp.where(chosen, starts, 0.0), axis=0, keepdims=True)
    enter(column + plane)

    quarter = pl.ds(pl.multiple_of(core * 16, 16), 16)
    peers = [peer_at(*where, step) for step in PEERS]
    local_copies, arriving = [], []

    def share(slot, source, target):
        copies = [
            remote(source(theirs), target, r.send_a.at[slot, k], r.recv_a.at[slot, k], device_id)
            for k, (theirs, device_id) in enumerate(peers)
        ]
        own = pltpu.make_async_copy(source(mine), target, r.here.at[slot])
        for copy in (*copies, own):
            copy.start()
        local_copies.append(own)
        arriving.append(copies)

    def landed(slot):
        for copy in arriving[slot]:
            copy.wait_recv()
        local_copies[slot].wait()

    def to_all(number, source, target, partners, send, recv):
        copies = [
            remote(source, target, send.at[number, k], recv.at[number, k], peer)
            for k, peer in enumerate(partners)
        ]
        for copy in copies:
            copy.start()
        return copies

    share(0, lambda q: r.win.at[0, q], r.in0.at[seq, x, z, quarter])
    place_in_column = y * 2 + core
    smalls = to_all(0, r.par, r.column_p.at[place_in_column], column, r.send_p, r.recv_p)
    tokens = RowShare(r.tok_in, r.tok, where, r.send_t.at[0], r.recv_t.at[0])
    tokens.begin()
    share(1, lambda q: r.trig, r.column_t.at[mine])
    ranks_here = to_all(1, r.par_i, r.column_i.at[place_in_column], column, r.send_p, r.recv_p)
    r.column_p[place_in_column] = r.par[...]
    r.column_i[place_in_column] = r.par_i[...]

    in0, ff0, in1, ff1 = (
        Gather(ref, where, r.send_g.at[k], r.recv_g.at[k])
        for k, ref in enumerate((r.in0, r.ff0, r.in1, r.ff1))
    )
    landed(0)
    in0.begin()
    for copy in smalls:
        copy.wait_recv()
    for half in range(2):
        r.joined[half] = jnp.sum(r.column_p[half * 4 : half * 4 + 4], axis=0)
    r.plane_p[chip] = r.joined[...]
    spread = to_all(0, r.joined, r.plane_p.at[chip], plane, r.send_v, r.recv_v)
    in0.pass_on()
    tokens.pass_on()
    for k in range(4):
        r.wff0[k, :, 0:WOUT] = r.wout[0, :, k * WOUT : (k + 1) * WOUT]
        r.wff0[k, :, WOUT : WOUT + WFF] = r.wexp[0, :, k * WFF : (k + 1) * WFF]
        r.wff0[k, :, WOUT + WFF :] = r.wcon[0, :, k * WFF : (k + 1) * WFF]
    share(2, lambda q: r.wff0.at[q], r.ff0.at[seq, x, z, quarter])
    in0.turn()
    tokens.end()

    def token_rows(index):
        return r.tok[rows_at(index, 32), :].astype(F32)

    normalize_rows(token_rows, r.normed0, r.inverse0, 0, 6)
    in0.pass_line()
    normalize_rows(token_rows, r.normed0, r.inverse0, 6, 10)
    landed(1)
    for k in range(4):
        rows = pl.ds(k * ROWS, ROWS)
        cos_a, sin_a = r.column_t[k, 0:1, :], r.column_t[k, 1:2, :]
        cos_b, sin_b = r.angles[64:192, :], r.angles[192:320, :]
        sine = sin_a * cos_b + cos_a * sin_b
        spot = lax.broadcasted_iota(I32, sine.shape, 1) % HEAD_DIM
        r.one[rows, :] = cos_a * cos_b - sin_a * sin_b
        r.right[rows, :] = jnp.where(spot < ROT // 2, -sine, 0.0)
        r.left[rows, :] = jnp.where(spot < ROT // 2, 0.0, sine)
    for copy in spread:
        copy.wait_recv()
    for half in range(2):
        for across in range(4):
            at = (half * 4 + across) * 128
            block = jnp.sum(r.plane_p[across * 4 : across * 4 + 4, half], axis=0)
            r.vectors[:, at : at + 128] = block
    own = [r.plane_p[mine * 4 + k, tp] for k in range(4)]
    r.ib[...] = (own[0] + own[1] + own[2] + own[3])[8:16]
    for k in range(4):
        r.eb[:, k * 128 : (k + 1) * 128] = own[k][16:24]
    scale_rows(r.normed0, r.vectors[0:1, :], r.vectors[4:5, :], r.first)
    in0.end()

    def put_message(first):
        def put(at, values):
            r.outbox[at, first : first + 32, :] = values

        return put

    project(r.first, r.in0, r.ib[0:3, :], tables, r.outbox, r.q_rows)
    heads_to_chips(lambda s, c, k: r.q_rows[group_rows(s, c, k), :], put_message(256))
    sent = exchange(0, r.outbox, r.inbox0, 288)
    for copy in ranks_here:
        copy.wait_recv()
    for half in range(2):
        cut = r.column_i
        r.joined_i[half] = cut[half * 4] + cut[half * 4 + 1] + cut[half * 4 + 2] + cut[half * 4 + 3]
    r.plane_i[chip] = r.joined_i[...]
    ranks_there = to_all(1, r.joined_i, r.plane_i.at[chip], plane, r.send_v, r.recv_v)
    for k in range(4):
        r.win1[k, :, :WIN] = r.win[1, k]
        r.win1[k, :, WIN:] = r.wout[1, :, k * WOUT : (k + 1) * WOUT]
        r.wff1[k, :, :WFF] = r.wexp[1, :, k * WFF : (k + 1) * WFF]
        r.wff1[k, :, WFF:] = r.wcon[1, :, k * WFF : (k + 1) * WFF]
    landed(2)
    ff0.begin()
    share(3, lambda q: r.win1.at[q], r.in1.at[seq, x, z, quarter])
    share(4, lambda q: r.wff1.at[q], r.ff1.at[seq, x, z, quarter])
    cots = RowShare(r.cot_in, r.cot, where, r.send_t.at[1], r.recv_t.at[1])
    cots.begin()
    scale_rows(r.normed0, r.vectors[1:2, :], r.vectors[5:6, :], r.second)
    ff0.pass_on()
    for copy in ranks_there:
        copy.wait_recv()
    ranks = r.plane_i[0, lax.div(x, 2)]
    for k in range(1, 16):
        ranks = ranks + r.plane_i[k, lax.div(x, 2)]
    r.ranks_v[...] = jnp.minimum(ranks, 31)
    spot = lax.broadcasted_iota(I32, (32, 128), 1)
    match = (ranks[0:1, :] == lax.broadcasted_iota(I32, (32, 128), 0)) & (spot < 32)
    found = [jnp.where(match, value, 0) for value in (lax.div(spot, 2), lax.rem(spot, 2))]
    for k in range(7):
        found = [value + pltpu.roll(value, 1 << k, 1) for value in found]
    r.order_v[...] = jnp.where(spot == 0, jnp.minimum(found[0], 15), jnp.minimum(found[1], 1))
    scalars = [
        pltpu.make_async_copy(r.ranks_v, r.ranks, r.here.at[5]),
        pltpu.make_async_copy(r.order_v, r.order, r.here.at[6]),
    ]
    for copy in scalars:
        copy.start()
    tokens.sent()
    for copy in scalars:
        copy.wait()
    sent.end()
    landed(3)
    ff0.turn()
    in1.begin()

    sort_pairs(r.order, r.inbox0, r.kvs0, r.kvt0)
    sort_rows(r.order, lambda at: r.inbox0[at, 256:288, :], r.qs0, False, HEAD_DIM**-0.5)
    steps = {
        3: (in1.pass_on, cots.pass_on),
        2: (ff0.pass_line, in1.turn),
        1: (),
        0: (in1.pass_line, lambda: landed(4), ff1.begin),
    }
    for tile in (3, 2, 1, 0):
        mixed, lse = forward_tile(z, tile, r.qs0[tile_rows(tile), :], r.kvs0, r.kvt0, r.wide)
        r.lse0[tile] = jnp.broadcast_to(lse, (8, TILE))
        r.o0[tile] = mixed
        r.rows[tile * 8 : tile * 8 + 8] = mixed.T.reshape(8, 32, 128)
        for step in steps[tile]:
            step()

    def put_to(ref):
        def put(at, values):
            ref[at] = values

        return put

    put_back_rows(r.ranks, r.rows, put_to(r.m_out), 1)
    returned = exchange(1, r.m_out, r.m_in, 32)
    sent.sent()
    ff0.end()
    expand(r.second, columns_of(r.ff0, WOUT, WFF), r.eb[2:3, :], r.inner0, r.act0)
    ff1.pass_on()
    contract(r.act0, columns_of(r.ff0, WOUT + WFF, WFF), z_sum)

    def keep(ref):
        def put(s, c, k, values):
            ref[group_rows(s, c, k), :] = values.astype(ref.dtype)

        return put

    returned.end()
    chips_to_heads(lambda at: r.m_in[at], keep(r.mixed0))
    total = ColumnSum(r.part, r.summed, where, True, column_sets[0])
    add_mixed(r.mixed0, columns_of(r.ff0, 0, WOUT), z_sum, r.part, core, total.begin)
    total.cross()
    ff1.turn()
    cots.end()
    in1.end()
    mix_back(lambda rows: r.cot[rows, :], columns_of(r.in1, WIN, WOUT), r.q_rows)
    heads_to_chips(lambda s, c, k: r.q_rows[group_rows(s, c, k), :], put_message(288))
    total.combine()
    ff1.pass_line()
    total.relay()
    total.end()
    shift = r.vectors[14:15, :] + r.vectors[15:16, :]

    def hidden(index):
        return r.tok[rows_at(index, 32), :].astype(F32) + rows32(r.summed, index) + shift

    normalize_rows(hidden, r.normed1, r.inverse1)
    scale_rows(r.normed1, r.vectors[2:3, :], r.vectors[6:7, :], r.first)
    project(r.first, r.in1, r.ib[3:6, :], tables, r.outbox, r.q_rows)
    heads_to_chips(lambda s, c, k: r.q_rows[group_rows(s, c, k), :], put_message(256))
    sent = exchange(2, r.outbox, r.inbox1, 320)

    def keep_own(index):
        r.own_hidden[rows_at(index, 32), :] = hidden(mine * 4 + index)

    loop(4, keep_own)
    scale_rows(r.normed1, r.vectors[3:4, :], r.vectors[7:8, :], r.second)
    ff1.end()
    expand(r.second, columns_of(r.ff1, 0, WFF), r.eb[3:4, :], r.inner1, r.act1)
    total.sent()
    sent.end()

    sort_pairs(r.order, r.inbox1, r.kvs1, r.kvt1)
    sort_rows(r.order, lambda at: r.inbox1[at, 256:288, :], r.qs1, False, HEAD_DIM**-0.5)
    sort_rows(r.order, lambda at: r.inbox1[at, 288:320, :], r.dos, True, 1.0)
    sent.sent()
    for tile in (3, 2, 1, 0):
        queries, outs = r.qs1[tile_rows(tile), :], r.dos[tile_rows(tile), :]
        mixed, lse = forward_tile(z, tile, queries, r.kvs1, r.kvt1, r.wide)
        r.rows[tile * 8 : tile * 8 + 8] = mixed.T.reshape(8, 32, 128)
        delta = jnp.sum(outs.astype(F32).T * mixed, axis=0, keepdims=True)
        query_grad = jnp.zeros((128, TILE), F32)
        for span in range(tile + 1):
            block = r.wide[span * SPAN : (span + 1) * SPAN, :]
            query_grad = query_grad + backward_span(
                tile, span, block, lse, delta, queries, outs, r.kvs1, r.kvt1, r.acc
            )
        r.o1[tile * 8 : tile * 8 + 8] = (query_grad.T * (HEAD_DIM**-0.5)).reshape(8, 32, 128)
    put_back_rows(r.ranks, r.rows, put_message(288), 1)
    put_back_rows(r.ranks, r.o1, put_message(256), 0)
    put_back_pairs(r.ranks, r.acc, r.outbox)
    sent = exchange(3, r.outbox, r.inbox0, 320)

    total1 = ColumnSum(r.part, r.summed2, where, False, column_sets[1])
    total2 = ColumnSum(r.part2, r.summed, where, True, column_sets[0])
    scatter_ff = Scatter(r.dw_ff, r.weights_out.at[1, :, :, pl.ds(PAIR, TWICE)], where, final(0), lines_ff)
    scatter_in = Scatter(r.dw_in, r.weights_out.at[1, :, :, pl.ds(0, PAIR)], where, final(1), lines_in)
    up, down = columns_of(r.ff1, 0, WFF), columns_of(r.ff1, WFF, WFF)
    expand_back(lambda rows: r.cot[rows, :], up, down, r.inner1, r.de, da2, r.eb_sums1)
    weight_grad(r.second, r.de, r.dw_ff, 0, WFF)
    weight_grad(r.cot, r.act1, r.dw_ff, WFF, WFF)
    sent.end()
    chips_to_heads(lambda at: r.inbox0[at, 256:288, :], keep(r.q_rows))
    project_back(r.inbox0, r.q_rows, tables, r.du, r.ib_sums1)
    join_back(
        r.du, r.in1, da2, r.normed1, r.vectors[2:3, :], r.vectors[3:4, :], r.sums1.at[pl.ds(0, 8)], r.part2,
        core, total2.begin,
    )
    scatter_ff.begin()
    total2.cross()
    chips_to_heads(lambda at: r.inbox0[at, 288:320, :], keep(r.mixed1))
    weight_grad(r.cot, r.mixed1, r.dw_in, WIN, WOUT)
    weight_grad(r.first, r.du, r.dw_in, 0, WIN)
    total2.combine()
    scatter_ff.pass_on()
    scatter_in.begin()
    total2.relay()
    total2.end()
    r.sums1[8:16, :] = jnp.zeros((8, D), F32)
    r.sums0[8:16, :] = jnp.zeros((8, D), F32)

    def after(index):
        rows = rows_at(index, 32)
        before = r.cot[rows, :].astype(F32)
        return before, before + norm_back(
            rows32(r.summed, index), r.normed1[rows, :], r.inverse1[rows, 0:1]
        )

    def put_grad(index):
        before, values = after(index)
        r.sums1[8:9, :] += jnp.sum(before, axis=0, keepdims=True)
        r.sums0[8:9, :] += jnp.sum(values, axis=0, keepdims=True)
        dz_rows[rows_at(index, 32), :] = values.astype(BF16)

    loop(16, put_grad, 2)
    mix_back(lambda rows: dz_rows[rows, :], columns_of(r.ff0, 0, WOUT), r.q_rows)
    heads_to_chips(lambda s, c, k: r.q_rows[group_rows(s, c, k), :], put_to(r.dm_out))
    back = exchange(4, r.dm_out, r.dm_in, 32)
    sent.sent()
    scatter_ff.turn()
    scatter_in.pass_on()
    contract(r.act1, columns_of(r.ff1, WFF, WFF), z_sum)
    add_mixed(r.mixed1, columns_of(r.in1, WIN, WOUT), z_sum, r.part, core, total1.begin)
    scatter_ff.pass_line()
    scatter_in.turn()
    scale_rows(r.normed0, r.vectors[1:2, :], r.vectors[5:6, :], r.second)
    total1.cross()
    up, down = columns_of(r.ff0, WOUT, WFF), columns_of(r.ff0, WOUT + WFF, WFF)
    expand_back(lambda rows: dz_rows[rows, :], up, down, r.inner0, r.de, da2, r.eb_sums0)

    def keep_grad(index):
        r.own_grad[rows_at(index, 32), :] = after(mine * 4 + index)[1]

    back.end()

    sort_rows(r.order, lambda at: r.dm_in[at], r.dos, True, 1.0)
    scatter_ff0 = Scatter(r.dw_ff, r.weights_out.at[0, :, :, pl.ds(PAIR, TWICE)], where, final(2), lines_ff)
    scatter_in0 = Scatter(r.dw_in, r.weights_out.at[0, :, :, pl.ds(0, PAIR)], where, final(3), lines_in)

    def next_scatter():
        scatter_ff.end()
        weight_grad(r.second, r.de, r.dw_ff, 0, WFF)
        weight_grad(dz_rows, r.act0, r.dw_ff, WFF, WFF)
        scatter_ff0.begin()

    steps = {
        3: (scatter_ff.deliver, scatter_in.pass_line, total1.combine),
        2: (next_scatter,),
        1: (scatter_in.deliver,),
        0: (scatter_ff0.pass_on,),
    }
    for tile in (3, 2, 1, 0):
        queries, outs = r.qs0[tile_rows(tile), :], r.dos[tile_rows(tile), :]
        delta = jnp.sum(outs.astype(F32).T * r.o0[tile], axis=0, keepdims=True)
        lse = r.lse0[tile][0:1, :]
        query_grad = jnp.zeros((128, TILE), F32)
        for span in range(tile + 1):
            block = score_span(z, tile, span, queries, r.kvs0)
            query_grad = query_grad + backward_span(
                tile, span, block, lse, delta, queries, outs, r.kvs0, r.kvt0, r.acc
            )
        r.o1[tile * 8 : tile * 8 + 8] = (query_grad.T * (HEAD_DIM**-0.5)).reshape(8, 32, 128)
        for step in steps[tile]:
            step()
    put_back_rows(r.ranks, r.o1, put_message(256), 0)
    put_back_pairs(r.ranks, r.acc, r.outbox)
    sent = exchange(5, r.outbox, r.inbox1, 288)
    total1.end()
    shift = r.vectors[16:17, :] + r.vectors[17:18, :]
    for k in range(2):
        rows = pl.ds(k * 64, 64)
        r.act_out[rows, :] = (r.own_hidden[rows, :] + r.summed2[k].astype(F32) + shift).astype(BF16)
    total1.sent()
    total2.sent()

    total3 = ColumnSum(r.part, r.summed3, where, False, column_sets[0])
    loop(4, keep_grad)
    scatter_in.end()
    scatter_ff0.turn()
    weight_grad(dz_rows, r.mixed0, r.dw_in, WIN, WOUT)
    scatter_ff0.pass_line()
    scale_rows(r.normed0, r.vectors[0:1, :], r.vectors[4:5, :], r.first)
    scatter_ff0.deliver()
    sent.end()
    chips_to_heads(lambda at: r.inbox1[at, 256:288, :], keep(r.q_rows))
    project_back(r.inbox1, r.q_rows, tables, r.du, r.ib_sums0)
    weight_grad(r.first, r.du, r.dw_in, 0, WIN)
    scatter_in0.begin()
    join_back(
        r.du, r.in0, da2, r.normed0, r.vectors[0:1, :], r.vectors[1:2, :], r.sums0.at[pl.ds(0, 8)], r.part,
        core, total3.begin,
    )
    scatter_in0.pass_on()
    total3.cross()

    once = jnp.where(place_in_column == 0, 1.0, 0.0)
    for half in range(2):
        for across in range(4):
            lanes = slice((half * 4 + across) * 128, (half * 4 + across + 1) * 128)
            at_home = jnp.where((tp == half) & (mine == across), 1.0, 0.0)
            for chip_z in range(4):
                cut = slice(chip_z * 128, (chip_z + 1) * 128)
                at = across * 4 + chip_z
                pieces = [
                    r.sums0[0:2, lanes], r.sums1[0:2, lanes], r.sums0[2:4, lanes], r.sums1[2:4, lanes],
                    r.ib_sums0[0:3, :] * at_home, r.ib_sums1[0:3, :] * at_home,
                    r.sums0[8:9, lanes] * once, r.sums0[8:9, lanes] * once,
                    r.sums1[8:9, lanes] * once, r.sums1[8:9, lanes] * once,
                    r.eb_sums0[0:1, cut] * at_home, r.eb_sums1[0:1, cut] * at_home,
                ]
                row = 0
                for piece in pieces:
                    count = piece.shape[0]
                    r.small[at, half, row : row + count, :] = piece
                    row += count
                r.small[at, half, 20:24, :] = jnp.zeros((4, 128), F32)
    around = []
    for k, (dx, dz) in enumerate(STEPS):
        copy = remote(
            r.small.at[ring(x, dx) * 4 + ring(z, dz)],
            r.gathered.at[k],
            r.send_s.at[k],
            r.recv_s.at[k],
            plane[k],
        )
        copy.start()
        around.append(copy)
    scatter_in0.turn()
    total3.combine()
    for copy in around:
        copy.wait_recv()
    r.total_s[...] = r.small[chip] + jnp.sum(r.gathered[...], axis=0)
    shared = []
    for k, peer in enumerate(column):
        copy = remote(r.total_s, r.others.at[k], r.send_d.at[k], r.recv_d.at[k], peer)
        copy.start()
        shared.append(copy)
    scatter_in0.pass_line()
    total3.end()
    own = mine * ROWS
    for k in range(4):
        rows = pl.ds(pl.multiple_of(own + k * 32, 32), 32)
        summed = r.summed3[k // 2, (k % 2) * 32 : (k % 2 + 1) * 32, :].astype(F32)
        r.grad_out[k * 32 : (k + 1) * 32, :] = r.own_grad[k * 32 : (k + 1) * 32, :] + norm_back(
            summed, r.normed0[rows, :], r.inverse0[rows, 0:1]
        )
    scatter_in0.deliver()
    for copy in shared:
        copy.wait_recv()
    sums_here = r.total_s[...] + jnp.sum(r.others[...], axis=0)
    sums_here = jnp.where(seq == 0, sums_here[0], sums_here[1])
    line = lax.broadcasted_iota(I32, sums_here.shape, 0)
    r.small_out[...] = jnp.where(
        line < 18,
        pltpu.roll(sums_here, 128 - (z * 4 + core * 2 + tp) * 8, 1),
        pltpu.roll(sums_here, 128 - (core * 2 + tp) * 32, 1),
    )
    scatter_ff0.end()
    scatter_in0.end()
    for copies in arriving:
        for copy in copies:
            copy.wait_send()
    for copy in smalls + spread + ranks_here + ranks_there + around + shared:
        copy.wait_send()
    for one in (cots, in0, ff0, in1, ff1, returned, back, sent, total3):
        one.sent()


def whole(*operands):
    outs = tuple(v for v in NAMES.values() if v is not None)
    scratch = [*SCRATCH.values(), *ColumnSum.SCRATCH * 2, *Scatter.scratch(PAIR), *Scatter.scratch(TWICE)]
    return pl.pallas_call(
        whole_kernel,
        out_shape=outs,
        in_specs=[VMEM] * len(operands),
        out_specs=(VMEM,) * len(outs),
        scratch_shapes=scratch,
        compiler_params=pltpu.CompilerParams(
            collective_id=0, has_side_effects=True, vmem_limit_bytes=LIMIT * MIB
        ),
        name="whole",
    )(*operands)


def outputs_kernel(
    weights, small, input_out, output_out, expand_out, contract_out,
    gain_out, shift_out, input_shift_out, output_shift_out, expand_shift_out,
):
    for layer in range(LAYERS):
        for k in range(4):
            part = weights[layer, k].astype(F32)
            for t in range(3):
                at = t * 512 + k * 128
                input_out[layer, :, at : at + 128] = part[:, t * 128 : (t + 1) * 128]
            output_out[layer, :, k * WOUT : (k + 1) * WOUT] = part[:, WIN:PAIR]
            expand_out[layer, :, k * WFF : (k + 1) * WFF] = part[:, PAIR : PAIR + WFF]
            contract_out[layer, :, k * WFF : (k + 1) * WFF] = part[:, PAIR + WFF :]
        for k in range(2):
            row = layer * 2 + k
            gain_out[layer, k : k + 1, :] = small[row : row + 1, 0:8]
            shift_out[layer, k : k + 1, :] = small[row + 4 : row + 5, 0:8]
            output_shift_out[layer, k : k + 1, :] = small[row + 14 : row + 15, 0:8]
        input_shift_out[layer] = small[8 + layer * 3 : 11 + layer * 3, 0:8]
    expand_shift_out[...] = small[18:20, 0:32]


def outputs(*operands):
    outs = (
        f32(2, 16, 1536), f32(2, 16, 512), f32(2, 16, 2048), f32(2, 16, 2048),
        f32(2, 2, 8), f32(2, 2, 8), f32(2, 3, 8), f32(2, 2, 8), f32(2, 32),
    )
    return pl.pallas_call(
        outputs_kernel,
        out_shape=outs,
        in_specs=[VMEM] * len(operands),
        out_specs=(VMEM,) * len(outs),
        compiler_params=pltpu.CompilerParams(vmem_limit_bytes=8 * MIB),
        name="outputs",
    )(*operands)


def rotary_tables():
    half = ROT // 2
    freqs = 10000.0 ** (-(np.arange(half) * 2.0 / ROT))
    lane = np.arange(128) % HEAD_DIM
    every = np.where(lane < ROT, np.tile(freqs, 128 // half), 0.0)[None, :]
    start = np.arange(32)[:, None] * ROWS * every
    steps = np.arange(ROWS)[:, None] * every
    return np.concatenate([np.cos(start), np.sin(start), np.cos(steps), np.sin(steps)]).astype(np.float32)


def local(
    tokens, cotangent, group_order, input_weight, output_weight, expand_weight, contract_weight,
    norm_gain, norm_shift, input_bias, output_bias, expand_bias,
):
    win = input_weight.reshape(LAYERS, 16, 3, 4, 128).transpose(0, 3, 1, 2, 4)
    eights = [norm_gain, norm_shift, input_bias, output_bias]
    raw = jnp.concatenate(
        [
            jnp.pad(jnp.concatenate([v.reshape(-1, 8) for v in eights], axis=0), ((0, 0), (0, 120))),
            jnp.pad(expand_bias, ((0, 4), (0, 96))),
        ],
        axis=0,
    )
    activations, input_gradient, weights_out, small = whole(
        win.reshape(LAYERS, 4, 16, WIN), output_weight, expand_weight, contract_weight, tokens, cotangent, raw,
        group_order, rotary_tables(),
    )
    input_out, *rest = outputs(weights_out, small)
    return (activations, input_gradient, input_out.reshape(2, 16, 3, 512), *rest)


def solution(mesh):
    rows, columns = P(("seq", "ctx"), None), P(None, None, ("seq", "ctx", "tp"))
    weight, flat = P(None, ("seq", "ctx"), "tp"), P(None, ("seq", "ctx", "tp"))
    first = P(None, ("seq", "ctx"), None, "tp")
    outs = (rows, rows, first, weight, weight, weight, columns, columns, columns, columns, flat)
    return jax.shard_map(
        local,
        mesh=mesh,
        in_specs=(rows, rows, P("seq", "ctx"), *outs[2:]),
        out_specs=outs,
        check_vma=False,
    )
```

```python
import types

import jax
import jax.numpy as jnp
import numpy as np
from jax import lax
from jax.experimental import pallas as pl
from jax.experimental.pallas import tpu as pltpu
from jax.sharding import PartitionSpec as P

MESH = pl.DeviceIdType.MESH
F32, BF16 = jnp.float32, jnp.bfloat16
D, HEAD_DIM, ROT, LAYERS = 1024, 64, 16, 2
ROWS = 128
GROUP = 512
WIN, WOUT, WFF = 384, 128, 512
COLS = WIN + WOUT + 2 * WFF
PARAMS = 208
EPSILON = 1e-05
MASKED = -1e30
MIB = 1024 * 1024
LIMIT = 62
WIDE = WOUT + 2 * WFF
PAIR, TWICE = WIN + WOUT, 2 * WFF
MESSAGE = 320


def place():
    ctx = lax.axis_index("ctx")
    chip = lax.div(ctx, 2)
    y = lax.axis_index("seq") * 2 + lax.axis_index("tp")
    return y, lax.div(chip, 4), lax.rem(chip, 4), lax.rem(ctx, 2)


def device(y, x, z, core):
    return (lax.div(y, 2), (x * 4 + z) * 2 + core, lax.rem(y, 2))


def ring(index, step):
    return lax.rem(index + step, 4)


def enter(partners):
    barrier = pltpu.get_barrier_semaphore()
    for partner in partners:
        pl.semaphore_signal(barrier, inc=1, device_id=partner, device_id_type=MESH)
    pl.semaphore_wait(barrier, len(partners))


STEPS = (
    (2, 2), (2, 1), (1, 2), (2, 3), (3, 2), (1, 1), (3, 3), (1, 3), (3, 1), (2, 0), (0, 2), (0, 1), (1, 0), (0, 3), (3, 0)
)


def plane_partners(y, x, z, core):
    return [device(y, ring(x, dx), ring(z, dz), core) for dx, dz in STEPS]


def column_partners(y, x, z, core):
    return [
        device(ring(y, dy), x, z, lax.rem(core + dc, 2))
        for dy in range(4)
        for dc in range(2)
        if dy or dc
    ]


def remote(source, target, send, receive, partner):
    return pltpu.make_async_remote_copy(
        src_ref=source,
        dst_ref=target,
        send_sem=send,
        recv_sem=receive,
        device_id=partner,
        device_id_type=MESH,
    )


HBM = pl.BlockSpec(memory_space=pl.ANY)
VMEM = pl.BlockSpec(memory_space=pltpu.VMEM)
SMEM = pl.BlockSpec(memory_space=pltpu.SMEM)


def bf(*shape):
    return jax.ShapeDtypeStruct(shape, BF16)


def f32(*shape):
    return jax.ShapeDtypeStruct(shape, F32)


def vbf(*shape):
    return pltpu.VMEM(shape, BF16)


def vf32(*shape):
    return pltpu.VMEM(shape, F32)


def dma(*shape):
    return pltpu.SemaphoreType.DMA(shape)


PEERS = ((0, 1), (1, 0), (1, 1))


def peer_at(y, x, z, core, step):
    seq, tp = lax.div(y, 2), lax.rem(y, 2)
    seq_to, core_to = lax.rem(seq + step[0], 2), lax.rem(core + step[1], 2)
    return seq_to * 2 + core_to, device(seq_to * 2 + tp, x, z, core_to)


class Gather:
    def __init__(self, full, where, send, recv):
        y, x, z, core = where
        self.full, self.x, self.z, self.send, self.recv = full, x, z, send, recv
        self.near = {
            "x": (device(y, ring(x, 1), z, core), device(y, ring(x, 3), z, core)),
            "z": (device(y, x, ring(z, 1), core), device(y, x, ring(z, 3), core)),
        }
        self.held = [(), ()]
        self.started = []

    def go(self, source, slot, partner):
        copy = remote(source, source, self.send.at[slot], self.recv.at[slot], partner)
        copy.start()
        self.started.append(copy)
        return copy

    def begin(self):
        for half in range(2):
            up, down = self.near["xz"[half]]
            own = self.full.at[half, self.x, self.z]
            self.held[half] = (self.go(own, half * 8, up), self.go(own, half * 8 + 1, down))

    def arrive(self, half):
        for copy in self.held[half]:
            copy.wait_recv()

    def pass_on(self):
        x, z = self.x, self.z
        for half in range(2):
            self.arrive(half)
            up, down = self.near["xz"[half]]
            whole = self.full.at[half]
            if half == 0:
                before, after = whole.at[ring(x, 3), z], whole.at[ring(x, 1), z]
            else:
                before, after = whole.at[x, ring(z, 3)], whole.at[x, ring(z, 1)]
            self.held[half] = (
                self.go(before.at[pl.ds(0, 16)], half * 8 + 2, up),
                self.go(after.at[pl.ds(16, 16)], half * 8 + 3, down),
            )

    def turn(self):
        for half in range(2):
            self.arrive(half)
            up, down = self.near["zx"[half]]
            whole = self.full.at[half]
            line = whole.at[:, self.z] if half == 0 else whole.at[self.x]
            self.held[half] = (self.go(line, half * 8 + 4, up), self.go(line, half * 8 + 5, down))

    def pass_line(self):
        x, z = self.x, self.z
        two, more = pl.ds(0, 2), pl.ds(2, 2)
        for half in range(2):
            self.arrive(half)
            up, down = self.near["zx"[half]]
            whole = self.full.at[half]
            if half == 0:
                before, after = whole.at[two, ring(z, 3)], whole.at[more, ring(z, 1)]
            else:
                before, after = whole.at[ring(x, 3), two], whole.at[ring(x, 1), more]
            self.held[half] = (
                self.go(before, half * 8 + 6, up),
                self.go(after, half * 8 + 7, down),
            )

    def end(self):
        for half in range(2):
            self.arrive(half)

    def sent(self):
        for copy in self.started:
            copy.wait_send()


class RowShare:
    def __init__(self, source, target, where, send, recv):
        y, x, z, core = where
        self.source, self.target, self.send, self.recv = source, target, send, recv
        seq = lax.div(y, 2)
        self.own = rows_at(seq * 2 + core, ROWS)
        self.other = rows_at((1 - seq) * 2 + core, ROWS)
        self.sibling = device(y, x, z, lax.rem(core + 1, 2))
        self.facing = device(3 - y, x, z, core)
        self.copies = []

    def go(self, source, target, slot, partner):
        copy = remote(source, target, self.send.at[slot], self.recv.at[slot], partner)
        copy.start()
        self.copies.append(copy)

    def begin(self):
        self.target[self.own, :] = self.source[...]
        self.go(self.source, self.target.at[self.own], 0, self.facing)
        self.go(self.source, self.target.at[self.own], 1, self.sibling)

    def pass_on(self):
        self.copies[0].wait_recv()
        block = self.target.at[self.other]
        self.go(block, block, 2, self.sibling)

    def end(self):
        for copy in self.copies[1:]:
            copy.wait_recv()

    def sent(self):
        for copy in self.copies:
            copy.wait_send()


class ColumnSum:
    SCRATCH = [vbf(4, 64, D), vbf(3, 64, D), vbf(3, 64, D)] + [dma(4), dma(4), dma(3), dma(3), dma(7), dma(7)]
    ORDER = (2, 1, 3)

    def __init__(self, part, out, where, everywhere, scratch):
        self.part, self.out, self.where, self.everywhere = part, out, where, everywhere
        (self.near, self.far, self.held, self.send1, self.recv1, self.send2, self.recv2, self.send3, self.recv3) = scratch
        y, x, z, core = where
        self.sibling = device(y, x, z, lax.rem(core + 1, 2))
        self.chips = [device(ring(y, dy), x, z, core) for dy in (1, 2, 3)]

    def begin(self):
        y, x, z, core = self.where
        self.nears = {}
        for dy in (*self.ORDER, 0):
            to = ring(y, dy)
            source = self.part.at[lax.div(to, 2), lax.rem(core + 1, 2), lax.rem(to, 2)]
            self.nears[dy] = remote(
                source, self.near.at[dy], self.send1.at[dy], self.recv1.at[dy], self.sibling
            )
            self.nears[dy].start()

    def cross(self):
        y, x, z, core = self.where
        self.fars = []
        for dy in self.ORDER:
            to = ring(y, dy)
            self.nears[dy].wait_recv()
            own = self.part[lax.div(to, 2), core, lax.rem(to, 2)].astype(F32)
            self.held[dy - 1] = (own + self.near[dy].astype(F32)).astype(BF16)
            copy = remote(
                self.held.at[dy - 1],
                self.far.at[dy - 1],
                self.send2.at[dy - 1],
                self.recv2.at[dy - 1],
                self.chips[dy - 1],
            )
            copy.start()
            self.fars.append(copy)

    def combine(self):
        y, x, z, core = self.where
        seq, tp = lax.div(y, 2), lax.rem(y, 2)
        self.nears[0].wait_recv()
        total = self.part[seq, core, tp].astype(F32) + self.near[0].astype(F32)
        for copy in self.fars:
            copy.wait_recv()
        for k in range(3):
            total = total + self.far[k].astype(F32)
        self.outs, self.relayed = [], []
        own = self.out.at[seq, core, tp] if self.everywhere else self.out.at[tp]
        own[...] = total.astype(BF16)
        if self.everywhere:
            for dy in self.ORDER:
                self.go(self.outs, own, dy - 1, self.chips[dy - 1])
            self.go(self.relayed, own, 3, self.sibling)
        else:
            self.go(self.outs, own, 0, device(seq * 2 + lax.rem(tp + 1, 2), x, z, core))

    def go(self, kept, block, slot, partner):
        copy = remote(block, block, self.send3.at[slot], self.recv3.at[slot], partner)
        copy.start()
        kept.append(copy)

    def relay(self):
        y, x, z, core = self.where
        for at, dy in enumerate(self.ORDER):
            self.outs[at].wait_recv()
            source = ring(y, 4 - dy)
            block = self.out.at[lax.div(source, 2), core, lax.rem(source, 2)]
            self.go(self.relayed, block, 3 + dy, self.sibling)

    def end(self):
        if self.everywhere:
            for copy in self.relayed:
                copy.wait_recv()
        else:
            self.outs[0].wait_recv()

    def sent(self):
        for copy in (*self.nears.values(), *self.fars, *self.outs, *self.relayed):
            copy.wait_send()


class Scatter:
    def __init__(self, dw, out, where, final, scratch):
        y, x, z, core = where
        self.dw, self.out, self.where, self.x, self.z = dw, out, where, x, z
        (self.opp1, self.dir1, self.comb1, self.sent1, self.mid, self.opp2, self.dir2, self.comb2, self.sent2, self.done,
         self.send, self.recv) = scratch
        self.send_f, self.recv_f = final
        self.near = {
            "x": (device(y, ring(x, 1), z, core), device(y, ring(x, 3), z, core)),
            "z": (device(y, x, ring(z, 1), core), device(y, x, ring(z, 3), core)),
        }
        self.started, self.held = [], [(), ()]

    @staticmethod
    def scratch(columns):
        big, small = vbf(2, 2, 2, 32, columns), vbf(2, 2, 16, columns)
        mid = vbf(2, 4, 32, columns)
        return [big] * 4 + [mid] + [small] * 5 + [dma(24), dma(24)]

    def go(self, source, target, slot, partner):
        copy = remote(source, target, self.send.at[slot], self.recv.at[slot], partner)
        copy.start()
        self.started.append(copy)
        return copy

    def part1(self, half, step, side):
        two = pl.ds(side * 2, 2)
        whole = self.dw.at[half]
        if half == 0:
            return whole.at[two, ring(self.z, step)]
        return whole.at[ring(self.x, step), two]

    def part2(self, half, step, side):
        at = ring(self.x, step) if half == 0 else ring(self.z, step)
        return self.mid.at[half, at].at[pl.ds(side * 16, 16)]

    def open(self, half, part, axis, opposite, direct, base):
        up, down = self.near[axis]
        self.held[half] = (
            self.go(part(half, 2, 0), opposite.at[half, 0], base, up),
            self.go(part(half, 2, 1), opposite.at[half, 1], base + 1, down),
            self.go(part(half, 1, 1), direct.at[half, 0], base + 2, up),
            self.go(part(half, 3, 0), direct.at[half, 1], base + 3, down),
        )

    def onward(self, half, part, axis, opposite, combined, sent, base):
        up, down = self.near[axis]
        copies = self.held[half]
        copies[0].wait_recv()
        sent[half, 0] = (part(half, 1, 0)[...].astype(F32) + opposite[half, 0].astype(F32)).astype(BF16)
        first = self.go(sent.at[half, 0], combined.at[half, 0], base + 4, up)
        copies[1].wait_recv()
        sent[half, 1] = (part(half, 3, 1)[...].astype(F32) + opposite[half, 1].astype(F32)).astype(BF16)
        second = self.go(sent.at[half, 1], combined.at[half, 1], base + 5, down)
        self.held[half] = (*copies[2:], first, second)

    def finish(self, half, part, direct, combined, target):
        for copy in self.held[half]:
            copy.wait_recv()
        for side in range(2):
            total = (
                part(half, 0, side)[...].astype(F32)
                + combined[half, side].astype(F32)
                + direct[half, 1 - side].astype(F32)
            )
            target(half, side)[...] = total.astype(BF16)

    def begin(self):
        for half in range(2):
            self.open(half, self.part1, "zx"[half], self.opp1, self.dir1, half * 12)

    def pass_on(self):
        for half in range(2):
            self.onward(half, self.part1, "zx"[half], self.opp1, self.comb1, self.sent1, half * 12)

    def turn(self):
        for half in range(2):
            self.finish(
                half,
                self.part1,
                self.dir1,
                self.comb1,
                lambda h, side: self.mid.at[h, pl.ds(side * 2, 2)],
            )
            self.open(half, self.part2, "xz"[half], self.opp2, self.dir2, half * 12 + 6)

    def pass_line(self):
        for half in range(2):
            self.onward(
                half, self.part2, "xz"[half], self.opp2, self.comb2, self.sent2, half * 12 + 6
            )

    def deliver(self):
        y, x, z, core = self.where
        seq = lax.div(y, 2)
        mine = seq * 2 + core
        for half in range(2):
            self.finish(
                half, self.part2, self.dir2, self.comb2, lambda h, side: self.done.at[h, side]
            )
        self.out[mine] = self.done[seq, core]
        self.final = []
        for k, step in enumerate(PEERS):
            theirs, peer = peer_at(y, x, z, core, step)
            copy = remote(
                self.done.at[lax.div(theirs, 2), lax.rem(theirs, 2)],
                self.out.at[mine],
                self.send_f.at[k],
                self.recv_f.at[k],
                peer,
            )
            copy.start()
            self.final.append(copy)

    def end(self):
        for copy in self.final:
            copy.wait()
        for copy in self.started:
            copy.wait_send()


class Exchange:
    def __init__(self, where, source, target, rows, send, recv):
        y, x, z, core = where
        chip = x * 4 + z
        cut = pl.ds(0, rows)
        target[chip, cut, :] = source[chip, cut, :]
        self.copies = []
        for k, (dx, dz) in enumerate(STEPS):
            to_x, to_z = ring(x, dx), ring(z, dz)
            copy = remote(
                source.at[to_x * 4 + to_z, cut],
                target.at[chip, cut],
                send.at[k],
                recv.at[k],
                device(y, to_x, to_z, core),
            )
            copy.start()
            self.copies.append(copy)

    def end(self):
        for copy in self.copies:
            copy.wait_recv()

    def sent(self):
        for copy in self.copies:
            copy.wait_send()


def loop(count, body, together=1):
    def step(index, carry):
        for k in range(together):
            body(index * together + k)
        return carry

    lax.fori_loop(0, count // together, step, 0)


def rows_at(index, count):
    return pl.ds(pl.multiple_of(index * count, count), count)


def turned(values, tables, sign):
    one, right, left = tables
    half = ROT // 2
    return values * one + sign * (
        pltpu.roll(values, 128 - half, 1) * right + pltpu.roll(values, half, 1) * left
    )


def low_lanes(shape):
    return lax.broadcasted_iota(jnp.int32, shape, 1) < HEAD_DIM


def swap(values):
    return pltpu.roll(values, HEAD_DIM, 1)


def heads_to_chips(values, target):
    def body(index):
        seq, quarter = lax.div(index, 4), lax.rem(index, 4)
        first, second = values(seq, 0, quarter), values(seq, 1, quarter)
        low = low_lanes(first.shape)
        target(seq * 8 + quarter, jnp.where(low, first, swap(second)).astype(BF16))
        target(seq * 8 + 4 + quarter, jnp.where(low, swap(first), second).astype(BF16))

    loop(8, body, 4)


def group_rows(seq, core, quarter):
    return pl.ds(pl.multiple_of(seq * 256 + core * 128 + quarter * 32, 32), 32)


def core_rows(step, core):
    return lax.div(step, 4) * 8 + core * 4 + lax.rem(step, 4)


def normalize_rows(hidden, normed, inverse, count, index_of):
    def body(step):
        index = index_of(step)
        rows = rows_at(index, 32)
        values = hidden(index)
        centred = values - jnp.mean(values, axis=1, keepdims=True)
        spread = jnp.mean(centred * centred, axis=1, keepdims=True)
        scale = lax.rsqrt(spread + EPSILON)
        normed[rows, :] = centred * scale
        inverse[rows, :] = jnp.broadcast_to(scale, (32, 128))

    loop(count, body, 2)


def scale_rows(normed, gain, shift, target):
    def body(index):
        rows = rows_at(index, 32)
        target[rows, :] = (normed[rows, :] * gain + shift).astype(BF16)

    loop(16, body)


def project(first, weight, bias, tables, outbox, q_rows):
    whole = columns_of(weight, 0, WIN)

    def body(index):
        rows = rows_at(index, 128)
        u = jnp.dot(first[rows, :], whole, preferred_element_type=F32)
        turn = tuple(t[rows, :] for t in tables)
        q_rows[rows, :] = turned(u[:, :128] + bias[0:1, :], turn, 1.0)
        keys = turned(u[:, 128:256] + bias[1:2, :], turn, 1.0)
        values = u[:, 256:] + bias[2:3, :]
        low = low_lanes(keys.shape)
        seq = lax.div(index, 2)
        part = rows_at(lax.rem(index, 2), 128)
        for head in range(2):
            pair = (keys, swap(values)) if head == 0 else (swap(keys), values)
            pair = jnp.where(low, *pair).astype(BF16)
            for k in range(4):
                outbox[seq * 8 + head * 4 + k, part, :] = pair

    loop(4, body)


def gelu_parts(inner):
    return 0.5 * (1.0 + lax.erf(inner * (0.5**0.5)))


def columns_of(weight, first, count):
    return weight[:, :, :, :, first : first + count].reshape(D, count)


def expand(second, whole, bias, inner, activated):

    def body(index):
        rows = rows_at(index, 128)
        e = jnp.dot(second[rows, :], whole, preferred_element_type=F32) + bias
        inner[rows, :] = e
        activated[rows, :] = (e * gelu_parts(e)).astype(BF16)

    loop(4, body)


def chips_to_heads(parts, target):
    def body(index):
        seq, quarter = lax.div(index, 4), lax.rem(index, 4)
        first = parts(seq * 8 + quarter).astype(F32)
        second = parts(seq * 8 + 4 + quarter).astype(F32)
        low = low_lanes(first.shape)
        target(seq, 0, quarter, jnp.where(low, first, swap(second)))
        target(seq, 1, quarter, jnp.where(low, swap(first), second))

    loop(8, body, 4)


def block_of(index):
    return lax.div(index, 2), lax.rem(index, 2)


class Wide:
    def __init__(self, buffer, base):
        self.buffer, self.base = buffer, base

    def at(self, start, count, k):
        return pl.ds(pl.multiple_of(self.base + k * GROUP + start, count), count)

    def put(self, start, count, values):
        for k in range(4):
            self.buffer[self.at(start, count, k), :] = values[:, k * 256 : (k + 1) * 256]

    def get(self, start, count):
        return jnp.concatenate([self.buffer[self.at(start, count, k), :] for k in range(4)], axis=1)


def contract(activated, whole, z):

    def body(index):
        rows = rows_at(index, 128)
        values = lax.dot_general(
            activated[rows, :], whole, (((1,), (1,)), ((), ())), preferred_element_type=F32
        )
        z.put(index * 128, 128, values)

    loop(4, body)


def add_mixed(mixed, weight, z, part, core, between):
    def one(seq, core):
        index = seq * 2 + core
        rows = rows_at(index, 128)
        both = z.get(index * 128, 128) + lax.dot_general(
            mixed[rows, :], weight, (((1,), (1,)), ((), ())), preferred_element_type=F32
        )
        part[seq, core] = both.astype(BF16).reshape(2, 64, D)

    loop(2, lambda seq: one(seq, 1 - core))
    between()
    loop(2, lambda seq: one(seq, core))


def rows32(summed, index):
    seq, core, tp = lax.div(index, 8), lax.rem(lax.div(index, 4), 2), lax.rem(lax.div(index, 2), 2)
    return summed[seq, core, tp, rows_at(lax.rem(index, 2), 32), :].astype(F32)


def mix_back(dz, weight, rows128):
    def body(index):
        rows = rows_at(index, 128)
        dm = jnp.dot(dz(rows), weight, preferred_element_type=F32)
        rows128[rows, :] = dm.astype(BF16).astype(F32)

    loop(4, body)


def expand_back(dz, up, down, inner, de, da, sums):
    sums[0:1, :] = jnp.zeros((1, WFF), F32)

    def body(index):
        rows = rows_at(index, 128)
        dg = jnp.dot(dz(rows), down, preferred_element_type=F32)
        e = inner[rows, :]
        slope = gelu_parts(e) + e * jnp.exp(-0.5 * e * e) * ((2.0 * jnp.pi) ** -0.5)
        low = (dg * slope).astype(BF16)
        de[rows, :] = low
        sums[0:1, :] += jnp.sum(low.astype(F32), axis=0, keepdims=True)
        values = lax.dot_general(low, up, (((1,), (1,)), ((), ())), preferred_element_type=F32)
        da.put(index * 128, 128, values)

    loop(4, body)


def weight_grad(left, right, dw, first, count):
    def body(index):
        block = lax.dot_general(
            left[:, rows_at(index, 256)],
            right[...],
            (((0,), (0,)), ((), ())),
            preferred_element_type=F32,
        )
        two = pl.ds(lax.rem(index, 2) * 2, 2)
        dw[lax.div(index, 2), two, :, :, first : first + count] = block.astype(BF16).reshape(
            2, 4, 32, count
        )

    loop(4, body)


def project_back(pairs, q_grad, tables, du, sums):
    sums[...] = jnp.zeros(sums.shape, F32)

    def body(index):
        seq, core = block_of(index)
        part = rows_at(core, 128)
        heads = []
        for head in range(2):
            total = pairs[seq * 8 + head * 4, part, :].astype(F32)
            for k in range(1, 4):
                total = total + pairs[seq * 8 + head * 4 + k, part, :].astype(F32)
            heads.append(total)
        low = low_lanes(heads[0].shape)
        rows = rows_at(index, 128)
        turn = tuple(t[rows, :] for t in tables)
        grads = (
            turned(q_grad[rows, :], turn, -1.0),
            turned(jnp.where(low, heads[0], swap(heads[1])), turn, -1.0),
            jnp.where(low, swap(heads[0]), heads[1]),
        )
        for k in range(3):
            rounded = grads[k].astype(BF16)
            du[rows, k * 128 : (k + 1) * 128] = rounded
            sums[k : k + 1, :] += jnp.sum(rounded.astype(F32), axis=0, keepdims=True)

    loop(4, body)


def join_back(du, weight, da2, normed, gain1, gain2, sums, part, core, between):
    whole = columns_of(weight, 0, WIN)
    sums[...] = jnp.zeros(sums.shape, F32)

    def one(step, core):
        seq, tp = lax.div(step, 2), lax.rem(step, 2)
        index = seq * 4 + core * 2 + tp
        rows = rows_at(index, 64)
        da = lax.dot_general(
            du[rows, :], whole, (((1,), (1,)), ((), ())), preferred_element_type=F32
        )
        db = da2.get(index * 64, 64)
        n = normed[rows, :]
        for k, value in enumerate((da * n, db * n, da, db)):
            sums[k : k + 1, :] += jnp.sum(value, axis=0, keepdims=True)
        part[seq, core, tp] = (da * gain1 + db * gain2).astype(BF16)

    loop(4, lambda step: one(step, 1 - core), 2)
    between()
    loop(4, lambda step: one(step, core), 2)


def norm_back(scaled, normed, inverse):
    first = jnp.mean(scaled, axis=1, keepdims=True)
    second = jnp.mean(scaled * normed, axis=1, keepdims=True)
    return inverse * (scaled - first - normed * second)


TILE = 256
SPAN = 1024


def seen(quarter, tile):
    key = lax.broadcasted_iota(jnp.int32, (SPAN, TILE), 0)
    row = lax.broadcasted_iota(jnp.int32, (SPAN, TILE), 1)
    place_of = (row // 32) * ROWS + quarter * 32 + row % 32
    return key <= place_of


def score_span(quarter, tile, span, queries, kvs):
    block = lax.dot_general(
        kvs[span * SPAN : (span + 1) * SPAN, :],
        queries,
        (((1,), (1,)), ((), ())),
        preferred_element_type=F32,
    )
    return jnp.where(seen(quarter, tile), block, MASKED) if span == tile else block


def forward_tile(quarter, tile, queries, kvs, kvt, score):
    highest = jnp.full((1, TILE), MASKED, F32)
    for span in range(tile + 1):
        block = score_span(quarter, tile, span, queries, kvs)
        score[span * SPAN : (span + 1) * SPAN, :] = block
        highest = jnp.maximum(highest, jnp.max(block, axis=0, keepdims=True))
    total = jnp.zeros((1, TILE), F32)
    mixed = jnp.zeros((128, TILE), F32)
    for span in range(tile + 1):
        weight = jnp.exp(score[span * SPAN : (span + 1) * SPAN, :] - highest)
        total = total + jnp.sum(weight, axis=0, keepdims=True)
        mixed = mixed + jnp.dot(
            kvt[:, span * SPAN : (span + 1) * SPAN],
            weight.astype(BF16),
            preferred_element_type=F32,
        )
    return mixed / total, highest + jnp.log(total)


def backward_span(tile, span, block, lse, delta, queries, outs, kvs, kvt, acc):
    keyed = kvs[span * SPAN : (span + 1) * SPAN, :]
    probs = jnp.exp(block - lse)
    back = lax.dot_general(keyed, outs, (((1,), (1,)), ((), ())), preferred_element_type=F32)
    score_grad = (probs * (back - delta)).astype(BF16)
    pair = jnp.dot(
        jnp.concatenate([score_grad, probs.astype(BF16)], axis=1),
        jnp.concatenate([queries, outs], axis=0),
        preferred_element_type=F32,
    )
    pair = pair.reshape(8, ROWS, 128)
    if tile == 3:
        acc[span * 8 : (span + 1) * 8] = pair
    else:
        acc[span * 8 : (span + 1) * 8] += pair
    return jnp.dot(
        kvt[:, span * SPAN : (span + 1) * SPAN], score_grad, preferred_element_type=F32
    )


def put_back_rows(ranks, rows, target, upper):
    def body(chip):
        first = rows[ranks[0, chip * 2]]
        second = rows[ranks[0, chip * 2 + 1]]
        if upper:
            first = swap(first)
        else:
            second = swap(second)
        target(chip, jnp.where(low_lanes(first.shape), first, second).astype(BF16))

    loop(16, body, 8)


def put_back_pairs(ranks, acc, outbox):
    def body(chip):
        for core in range(2):
            rank = ranks[0, chip * 2 + core]
            outbox[chip, core * ROWS : (core + 1) * ROWS, :] = acc[rank].astype(BF16)

    loop(16, body, 2)


def owner(order, rank):
    return order[rank, 0], order[rank, 1]


def sort_rows(order, source, target, upper, scale):
    def body(rank):
        chip, core = owner(order, rank)
        block = source(chip).astype(F32) * scale
        other = swap(block)
        low = low_lanes(block.shape)
        if upper:
            part = jnp.where(low, 0.0, jnp.where(core == 0, other, block))
        else:
            part = jnp.where(low, jnp.where(core == 0, block, other), 0.0)
        target[rows_at(rank, 32), :] = part.astype(BF16)

    loop(32, body, 8)


def sort_pairs(order, inbox, kvs, kvt):
    def body(rank):
        chip, core = owner(order, rank)
        keyed = jnp.where(core == 0, inbox[chip, 0:ROWS, :], inbox[chip, ROWS : 2 * ROWS, :])
        kvs[rows_at(rank, ROWS), :] = keyed
        kvt[:, rows_at(rank, ROWS)] = keyed.astype(F32).T.astype(BF16)

    loop(32, body, 4)


def tile_rows(tile):
    return slice(tile * TILE, (tile + 1) * TILE)


NAMES = {
    "win": None, "wout": None, "wexp": None, "wcon": None, "tok_in": None, "cot_in": None, "raw": None, "rank": None,
    "angles": None,
    "act_out": bf(ROWS, D), "grad_out": f32(ROWS, D), "weights_out": bf(2, 4, 16, PAIR + TWICE), "small_out": f32(24, 128),
}
I32 = jnp.int32
SCRATCH = {
    "in0": vbf(2, 4, 4, 32, WIN), "in1": vbf(2, 4, 4, 32, PAIR),
    "ff0": vbf(2, 4, 4, 32, WIDE), "ff1": vbf(2, 4, 4, 32, TWICE),
    "wff0": vbf(4, 16, WIDE), "win1": vbf(4, 16, PAIR), "wff1": vbf(4, 16, TWICE),
    "tok": vbf(GROUP, D), "cot": vbf(GROUP, D),
    "par": vf32(24, 128), "trig": vf32(8, 128), "column_p": vf32(8, 24, 128), "joined": vf32(2, 24, 128),
    "plane_p": vf32(16, 2, 24, 128), "column_t": vf32(4, 8, 128), "vectors": vf32(24, D),
    "ib": vf32(8, 128), "eb": vf32(8, WFF),
    "par_i": pltpu.VMEM((8, 128), I32), "column_i": pltpu.VMEM((8, 8, 128), I32),
    "joined_i": pltpu.VMEM((2, 8, 128), I32), "plane_i": pltpu.VMEM((16, 2, 8, 128), I32),
    "ranks_v": pltpu.VMEM((8, 128), I32), "order_v": pltpu.VMEM((32, 128), I32),
    "ranks": pltpu.SMEM((8, 128), I32), "order": pltpu.SMEM((32, 128), I32),
    "one": vf32(GROUP, 128), "right": vf32(GROUP, 128), "left": vf32(GROUP, 128),
    "normed0": vf32(GROUP, D), "normed1": vf32(GROUP, D), "inverse0": vf32(GROUP, 128), "inverse1": vf32(GROUP, 128),
    "first": vbf(GROUP, D), "second": vbf(GROUP, D),
    "inner0": vf32(GROUP, WFF), "inner1": vf32(GROUP, WFF), "act0": vbf(GROUP, WFF), "act1": vbf(GROUP, WFF),
    "mixed0": vbf(GROUP, 128), "mixed1": vbf(GROUP, 128), "q_rows": vf32(GROUP, 128),
    "outbox": vbf(16, MESSAGE, 128), "inbox0": vbf(16, MESSAGE, 128), "inbox1": vbf(16, MESSAGE, 128),
    "m_out": vbf(16, 32, 128), "m_in": vbf(16, 32, 128), "dm_out": vbf(16, 32, 128), "dm_in": vbf(16, 32, 128),
    "kvs0": vbf(4096, 128), "kvs1": vbf(4096, 128), "kvt0": vbf(128, 4096), "kvt1": vbf(128, 4096),
    "qs0": vbf(1024, 128), "qs1": vbf(1024, 128), "dos": vbf(1024, 128), "o0": vf32(4, 128, TILE), "lse0": vf32(4, 8, TILE),
    "wide": vf32(4096, TILE), "rows": vf32(32, 32, 128), "o1": vf32(32, 32, 128), "acc": vf32(32, 128, 128),
    "de": vbf(GROUP, WFF), "du": vbf(GROUP, WIN), "own_grad": vf32(ROWS, D), "own_hidden": vf32(ROWS, D),
    "part": vbf(2, 2, 2, 64, D), "part2": vbf(2, 2, 2, 64, D), "summed": vbf(2, 2, 2, 64, D),
    "summed2": vbf(2, 64, D), "summed3": vbf(2, 64, D),
    "dw_in": vbf(2, 4, 4, 32, PAIR), "dw_ff": vbf(2, 4, 4, 32, TWICE),
    "sums0": vf32(16, D), "sums1": vf32(16, D), "ib_sums0": vf32(8, 128), "ib_sums1": vf32(8, 128),
    "eb_sums0": vf32(8, WFF), "eb_sums1": vf32(8, WFF),
    "small": vf32(16, 2, 24, 128), "gathered": vf32(15, 2, 24, 128), "total_s": vf32(2, 24, 128), "others": vf32(7, 2, 24, 128),
    "here": dma(7), "send_a": dma(5, 3), "recv_a": dma(5, 3), "send_t": dma(2, 3), "recv_t": dma(2, 3),
    "send_p": dma(2, 7), "recv_p": dma(2, 7), "send_v": dma(2, 15), "recv_v": dma(2, 15),
    "send_g": dma(4, 16), "recv_g": dma(4, 16), "send_x": dma(6, 15), "recv_x": dma(6, 15),
    "send_f": dma(4, 3), "recv_f": dma(4, 3), "send_s": dma(15), "recv_s": dma(15), "send_d": dma(7), "recv_d": dma(7),
}
COLUMN = len(ColumnSum.SCRATCH)
LINES = len(Scatter.scratch(WIN))


def whole_kernel(*refs):
    names = [*NAMES, *SCRATCH]
    r = types.SimpleNamespace(**dict(zip(names, refs)))
    rest = refs[len(names) :]
    column_sets = [rest[k * COLUMN : (k + 1) * COLUMN] for k in range(2)]
    rest = rest[2 * COLUMN :]
    lines_in, lines_ff = rest[:LINES], rest[LINES:]
    where = y, x, z, core = place()
    seq, tp = lax.div(y, 2), lax.rem(y, 2)
    mine, chip = seq * 2 + core, x * 4 + z
    column, plane = column_partners(*where), plane_partners(*where)
    tables = (r.one, r.right, r.left)
    dz_rows = r.tok
    z_sum, da2 = Wide(r.wide, 0), Wide(r.wide, 4 * GROUP)

    def exchange(number, source, target, rows):
        return Exchange(where, source, target, rows, r.send_x.at[number], r.recv_x.at[number])

    def final(number):
        return r.send_f.at[number], r.recv_f.at[number]

    raw = r.raw[...]
    line = lax.broadcasted_iota(I32, raw.shape, 0)
    r.par[...] = jnp.where(
        line < 18,
        pltpu.roll(raw, (z * 4 + core * 2 + tp) * 8, 1),
        pltpu.roll(raw, (core * 2 + tp) * 32, 1),
    )
    lane = lax.broadcasted_iota(I32, (8, 128), 1)
    r.par_i[...] = jnp.where((lane == chip * 2 + core) & (tp == 0), r.rank[...], 0)
    r.trig[...] = jnp.zeros((8, 128), F32)
    for k in range(2):
        starts = r.angles[k * 32 : (k + 1) * 32, :]
        chosen = lax.broadcasted_iota(I32, starts.shape, 0) == r.rank[...]
        r.trig[k : k + 1, :] = jnp.sum(jnp.where(chosen, starts, 0.0), axis=0, keepdims=True)
    enter(column + plane)

    quarter = pl.ds(pl.multiple_of(core * 16, 16), 16)
    peers = [peer_at(*where, step) for step in PEERS]
    local_copies, arriving = [], []

    def share(slot, source, target):
        copies = [
            remote(source(theirs), target, r.send_a.at[slot, k], r.recv_a.at[slot, k], device_id)
            for k, (theirs, device_id) in enumerate(peers)
        ]
        own = pltpu.make_async_copy(source(mine), target, r.here.at[slot])
        for copy in (*copies, own):
            copy.start()
        local_copies.append(own)
        arriving.append(copies)

    def landed(slot):
        for copy in arriving[slot]:
            copy.wait_recv()
        local_copies[slot].wait()

    def to_all(number, source, target, partners, send, recv):
        copies = [
            remote(source, target, send.at[number, k], recv.at[number, k], peer)
            for k, peer in enumerate(partners)
        ]
        for copy in copies:
            copy.start()
        return copies

    share(0, lambda q: r.win.at[0, q], r.in0.at[seq, x, z, quarter])
    place_in_column = y * 2 + core
    smalls = to_all(0, r.par, r.column_p.at[place_in_column], column, r.send_p, r.recv_p)
    tokens = RowShare(r.tok_in, r.tok, where, r.send_t.at[0], r.recv_t.at[0])
    tokens.begin()
    share(1, lambda q: r.trig, r.column_t.at[mine])
    ranks_here = to_all(1, r.par_i, r.column_i.at[place_in_column], column, r.send_p, r.recv_p)
    r.column_p[place_in_column] = r.par[...]
    r.column_i[place_in_column] = r.par_i[...]

    in0, ff0, in1, ff1 = (
        Gather(ref, where, r.send_g.at[k], r.recv_g.at[k])
        for k, ref in enumerate((r.in0, r.ff0, r.in1, r.ff1))
    )
    landed(0)
    in0.begin()
    for copy in smalls:
        copy.wait_recv()
    for half in range(2):
        r.joined[half] = jnp.sum(r.column_p[half * 4 : half * 4 + 4], axis=0)
    r.plane_p[chip] = r.joined[...]
    in0.pass_on()
    spread = to_all(0, r.joined, r.plane_p.at[chip], plane, r.send_v, r.recv_v)
    tokens.pass_on()
    for k in range(4):
        r.wff0[k, :, 0:WOUT] = r.wout[0, :, k * WOUT : (k + 1) * WOUT]
        r.wff0[k, :, WOUT : WOUT + WFF] = r.wexp[0, :, k * WFF : (k + 1) * WFF]
        r.wff0[k, :, WOUT + WFF :] = r.wcon[0, :, k * WFF : (k + 1) * WFF]
    share(2, lambda q: r.wff0.at[q], r.ff0.at[seq, x, z, quarter])
    in0.turn()
    tokens.end()

    def token_rows(index):
        return r.tok[rows_at(index, 32), :].astype(F32)

    normalize_rows(token_rows, r.normed0, r.inverse0, 6, lambda step: step)
    in0.pass_line()
    normalize_rows(token_rows, r.normed0, r.inverse0, 10, lambda step: step + 6)
    landed(1)
    for k in range(4):
        rows = pl.ds(k * ROWS, ROWS)
        cos_a, sin_a = r.column_t[k, 0:1, :], r.column_t[k, 1:2, :]
        cos_b, sin_b = r.angles[64:192, :], r.angles[192:320, :]
        sine = sin_a * cos_b + cos_a * sin_b
        spot = lax.broadcasted_iota(I32, sine.shape, 1) % HEAD_DIM
        r.one[rows, :] = cos_a * cos_b - sin_a * sin_b
        r.right[rows, :] = jnp.where(spot < ROT // 2, -sine, 0.0)
        r.left[rows, :] = jnp.where(spot < ROT // 2, 0.0, sine)
    for copy in spread:
        copy.wait_recv()
    for half in range(2):
        for across in range(4):
            at = (half * 4 + across) * 128
            block = jnp.sum(r.plane_p[across * 4 : across * 4 + 4, half], axis=0)
            r.vectors[:, at : at + 128] = block
    own = [r.plane_p[mine * 4 + k, tp] for k in range(4)]
    r.ib[...] = (own[0] + own[1] + own[2] + own[3])[8:16]
    for k in range(4):
        r.eb[:, k * 128 : (k + 1) * 128] = own[k][16:24]
    scale_rows(r.normed0, r.vectors[0:1, :], r.vectors[4:5, :], r.first)
    in0.end()

    def put_message(first):
        def put(at, values):
            r.outbox[at, first : first + 32, :] = values

        return put

    project(r.first, r.in0, r.ib[0:3, :], tables, r.outbox, r.q_rows)
    heads_to_chips(lambda s, c, k: r.q_rows[group_rows(s, c, k), :], put_message(256))
    sent = exchange(0, r.outbox, r.inbox0, 288)
    for copy in ranks_here:
        copy.wait_recv()
    for half in range(2):
        cut = r.column_i
        r.joined_i[half] = cut[half * 4] + cut[half * 4 + 1] + cut[half * 4 + 2] + cut[half * 4 + 3]
    r.plane_i[chip] = r.joined_i[...]
    ranks_there = to_all(1, r.joined_i, r.plane_i.at[chip], plane, r.send_v, r.recv_v)
    for k in range(4):
        r.win1[k, :, :WIN] = r.win[1, k]
        r.win1[k, :, WIN:] = r.wout[1, :, k * WOUT : (k + 1) * WOUT]
        r.wff1[k, :, :WFF] = r.wexp[1, :, k * WFF : (k + 1) * WFF]
        r.wff1[k, :, WFF:] = r.wcon[1, :, k * WFF : (k + 1) * WFF]
    landed(2)
    ff0.begin()
    share(3, lambda q: r.win1.at[q], r.in1.at[seq, x, z, quarter])
    share(4, lambda q: r.wff1.at[q], r.ff1.at[seq, x, z, quarter])
    cots = RowShare(r.cot_in, r.cot, where, r.send_t.at[1], r.recv_t.at[1])
    cots.begin()
    scale_rows(r.normed0, r.vectors[1:2, :], r.vectors[5:6, :], r.second)
    ff0.pass_on()
    for copy in ranks_there:
        copy.wait_recv()
    ranks = r.plane_i[0, lax.div(x, 2)]
    for k in range(1, 16):
        ranks = ranks + r.plane_i[k, lax.div(x, 2)]
    r.ranks_v[...] = jnp.minimum(ranks, 31)
    spot = lax.broadcasted_iota(I32, (32, 128), 1)
    match = (ranks[0:1, :] == lax.broadcasted_iota(I32, (32, 128), 0)) & (spot < 32)
    found = [jnp.where(match, value, 0) for value in (lax.div(spot, 2), lax.rem(spot, 2))]
    for k in range(7):
        found = [value + pltpu.roll(value, 1 << k, 1) for value in found]
    r.order_v[...] = jnp.where(spot == 0, jnp.minimum(found[0], 15), jnp.minimum(found[1], 1))
    scalars = [
        pltpu.make_async_copy(r.ranks_v, r.ranks, r.here.at[5]),
        pltpu.make_async_copy(r.order_v, r.order, r.here.at[6]),
    ]
    for copy in scalars:
        copy.start()
    tokens.sent()
    for copy in scalars:
        copy.wait()
    sent.end()
    ff0.turn()

    sort_pairs(r.order, r.inbox0, r.kvs0, r.kvt0)
    sort_rows(r.order, lambda at: r.inbox0[at, 256:288, :], r.qs0, False, HEAD_DIM**-0.5)
    steps = {3: (), 2: (cots.pass_on,), 1: (), 0: (ff0.pass_line,)}
    for tile in (3, 2, 1, 0):
        mixed, lse = forward_tile(z, tile, r.qs0[tile_rows(tile), :], r.kvs0, r.kvt0, r.wide)
        r.lse0[tile] = jnp.broadcast_to(lse, (8, TILE))
        r.o0[tile] = mixed
        r.rows[tile * 8 : tile * 8 + 8] = mixed.T.reshape(8, 32, 128)
        for step in steps[tile]:
            step()

    def put_to(ref):
        def put(at, values):
            ref[at] = values

        return put

    put_back_rows(r.ranks, r.rows, put_to(r.m_out), 1)
    returned = exchange(1, r.m_out, r.m_in, 32)
    landed(3)
    in1.begin()
    landed(4)
    ff1.begin()
    sent.sent()
    ff0.end()
    expand(r.second, columns_of(r.ff0, WOUT, WFF), r.eb[2:3, :], r.inner0, r.act0)
    in1.pass_on()
    contract(r.act0, columns_of(r.ff0, WOUT + WFF, WFF), z_sum)

    def keep(ref):
        def put(s, c, k, values):
            ref[group_rows(s, c, k), :] = values.astype(ref.dtype)

        return put

    ff1.pass_on()
    returned.end()
    chips_to_heads(lambda at: r.m_in[at], keep(r.mixed0))
    total = ColumnSum(r.part, r.summed, where, True, column_sets[0])
    add_mixed(r.mixed0, columns_of(r.ff0, 0, WOUT), z_sum, r.part, core, total.begin)
    total.cross()
    in1.turn()
    ff1.turn()
    total.combine()
    in1.pass_line()
    total.relay()
    ff1.pass_line()
    shift = r.vectors[14:15, :] + r.vectors[15:16, :]

    def hidden(index):
        return r.tok[rows_at(index, 32), :].astype(F32) + rows32(r.summed, index) + shift

    normalize_rows(hidden, r.normed1, r.inverse1, 8, lambda step: core_rows(step, core))
    total.end()
    normalize_rows(hidden, r.normed1, r.inverse1, 8, lambda step: core_rows(step, 1 - core))
    scale_rows(r.normed1, r.vectors[2:3, :], r.vectors[6:7, :], r.first)
    cots.end()
    in1.end()
    mix_back(lambda rows: r.cot[rows, :], columns_of(r.in1, WIN, WOUT), r.q_rows)
    heads_to_chips(lambda s, c, k: r.q_rows[group_rows(s, c, k), :], put_message(288))
    project(r.first, r.in1, r.ib[3:6, :], tables, r.outbox, r.q_rows)
    heads_to_chips(lambda s, c, k: r.q_rows[group_rows(s, c, k), :], put_message(256))
    sent = exchange(2, r.outbox, r.inbox1, 320)

    def keep_own(index):
        r.own_hidden[rows_at(index, 32), :] = hidden(mine * 4 + index)

    loop(4, keep_own)
    scale_rows(r.normed1, r.vectors[3:4, :], r.vectors[7:8, :], r.second)
    ff1.end()
    expand(r.second, columns_of(r.ff1, 0, WFF), r.eb[3:4, :], r.inner1, r.act1)
    weight_grad(r.cot, r.act1, r.dw_ff, WFF, WFF)
    total.sent()
    sent.end()

    sort_pairs(r.order, r.inbox1, r.kvs1, r.kvt1)
    sort_rows(r.order, lambda at: r.inbox1[at, 256:288, :], r.qs1, False, HEAD_DIM**-0.5)
    sort_rows(r.order, lambda at: r.inbox1[at, 288:320, :], r.dos, True, 1.0)
    sent.sent()
    for tile in (3, 2, 1, 0):
        queries, outs = r.qs1[tile_rows(tile), :], r.dos[tile_rows(tile), :]
        mixed, lse = forward_tile(z, tile, queries, r.kvs1, r.kvt1, r.wide)
        r.rows[tile * 8 : tile * 8 + 8] = mixed.T.reshape(8, 32, 128)
        delta = jnp.sum(outs.astype(F32).T * mixed, axis=0, keepdims=True)
        query_grad = jnp.zeros((128, TILE), F32)
        for span in range(tile + 1):
            block = r.wide[span * SPAN : (span + 1) * SPAN, :]
            query_grad = query_grad + backward_span(
                tile, span, block, lse, delta, queries, outs, r.kvs1, r.kvt1, r.acc
            )
        r.o1[tile * 8 : tile * 8 + 8] = (query_grad.T * (HEAD_DIM**-0.5)).reshape(8, 32, 128)
    put_back_rows(r.ranks, r.rows, put_message(288), 1)
    put_back_rows(r.ranks, r.o1, put_message(256), 0)
    put_back_pairs(r.ranks, r.acc, r.outbox)
    sent = exchange(3, r.outbox, r.inbox0, 320)

    total1 = ColumnSum(r.part, r.summed2, where, False, column_sets[1])
    total2 = ColumnSum(r.part2, r.summed, where, True, column_sets[0])
    scatter_ff = Scatter(r.dw_ff, r.weights_out.at[1, :, :, pl.ds(PAIR, TWICE)], where, final(0), lines_ff)
    scatter_in = Scatter(r.dw_in, r.weights_out.at[1, :, :, pl.ds(0, PAIR)], where, final(1), lines_in)
    up, down = columns_of(r.ff1, 0, WFF), columns_of(r.ff1, WFF, WFF)
    expand_back(lambda rows: r.cot[rows, :], up, down, r.inner1, r.de, da2, r.eb_sums1)
    weight_grad(r.second, r.de, r.dw_ff, 0, WFF)
    contract(r.act1, columns_of(r.ff1, WFF, WFF), z_sum)
    sent.end()
    chips_to_heads(lambda at: r.inbox0[at, 256:288, :], keep(r.q_rows))
    project_back(r.inbox0, r.q_rows, tables, r.du, r.ib_sums1)
    join_back(
        r.du, r.in1, da2, r.normed1, r.vectors[2:3, :], r.vectors[3:4, :], r.sums1.at[pl.ds(0, 8)], r.part2,
        core, total2.begin,
    )
    total2.cross()
    scatter_ff.begin()
    chips_to_heads(lambda at: r.inbox0[at, 288:320, :], keep(r.mixed1))
    weight_grad(r.cot, r.mixed1, r.dw_in, WIN, WOUT)
    weight_grad(r.first, r.du, r.dw_in, 0, WIN)
    total2.combine()
    scatter_ff.pass_on()
    scatter_in.begin()
    total2.relay()
    r.sums1[8:16, :] = jnp.zeros((8, D), F32)
    r.sums0[8:16, :] = jnp.zeros((8, D), F32)

    def after(index):
        rows = rows_at(index, 32)
        before = r.cot[rows, :].astype(F32)
        return before, before + norm_back(
            rows32(r.summed, index), r.normed1[rows, :], r.inverse1[rows, 0:1]
        )

    def put_grad(index):
        before, values = after(index)
        r.sums1[8:9, :] += jnp.sum(before, axis=0, keepdims=True)
        r.sums0[8:9, :] += jnp.sum(values, axis=0, keepdims=True)
        dz_rows[rows_at(index, 32), :] = values.astype(BF16)

    loop(8, lambda step: put_grad(core_rows(step, core)), 2)
    total2.end()
    loop(8, lambda step: put_grad(core_rows(step, 1 - core)), 2)
    mix_back(lambda rows: dz_rows[rows, :], columns_of(r.ff0, 0, WOUT), r.q_rows)
    heads_to_chips(lambda s, c, k: r.q_rows[group_rows(s, c, k), :], put_to(r.dm_out))
    back = exchange(4, r.dm_out, r.dm_in, 32)
    sent.sent()
    scatter_ff.turn()
    scatter_in.pass_on()
    up, down = columns_of(r.ff0, WOUT, WFF), columns_of(r.ff0, WOUT + WFF, WFF)
    expand_back(lambda rows: dz_rows[rows, :], up, down, r.inner0, r.de, da2, r.eb_sums0)
    scatter_ff.pass_line()
    scatter_in.turn()
    scale_rows(r.normed0, r.vectors[1:2, :], r.vectors[5:6, :], r.second)

    def keep_grad(index):
        r.own_grad[rows_at(index, 32), :] = after(mine * 4 + index)[1]

    back.end()

    sort_rows(r.order, lambda at: r.dm_in[at], r.dos, True, 1.0)
    scatter_ff.deliver()
    scatter_ff0 = Scatter(r.dw_ff, r.weights_out.at[0, :, :, pl.ds(PAIR, TWICE)], where, final(2), lines_ff)
    scatter_in0 = Scatter(r.dw_in, r.weights_out.at[0, :, :, pl.ds(0, PAIR)], where, final(3), lines_in)

    def next_scatter():
        scatter_ff.end()
        weight_grad(r.second, r.de, r.dw_ff, 0, WFF)
        weight_grad(dz_rows, r.act0, r.dw_ff, WFF, WFF)
        scatter_ff0.begin()

    steps = {
        3: (scatter_in.pass_line, next_scatter),
        2: (scatter_in.deliver,),
        1: (),
        0: (scatter_ff0.pass_on,),
    }
    for tile in (3, 2, 1, 0):
        queries, outs = r.qs0[tile_rows(tile), :], r.dos[tile_rows(tile), :]
        delta = jnp.sum(outs.astype(F32).T * r.o0[tile], axis=0, keepdims=True)
        lse = r.lse0[tile][0:1, :]
        query_grad = jnp.zeros((128, TILE), F32)
        for span in range(tile + 1):
            block = score_span(z, tile, span, queries, r.kvs0)
            query_grad = query_grad + backward_span(
                tile, span, block, lse, delta, queries, outs, r.kvs0, r.kvt0, r.acc
            )
        r.o1[tile * 8 : tile * 8 + 8] = (query_grad.T * (HEAD_DIM**-0.5)).reshape(8, 32, 128)
        for step in steps[tile]:
            step()
    put_back_rows(r.ranks, r.o1, put_message(256), 0)
    put_back_pairs(r.ranks, r.acc, r.outbox)
    sent = exchange(5, r.outbox, r.inbox1, 288)
    total3 = ColumnSum(r.part, r.summed3, where, False, column_sets[0])
    add_mixed(r.mixed1, columns_of(r.in1, WIN, WOUT), z_sum, r.part, core, total1.begin)
    loop(4, keep_grad)
    scatter_in.end()
    total1.cross()
    weight_grad(dz_rows, r.mixed0, r.dw_in, WIN, WOUT)
    scatter_ff0.turn()
    scale_rows(r.normed0, r.vectors[0:1, :], r.vectors[4:5, :], r.first)
    total1.combine()
    scatter_ff0.pass_line()
    total1.sent()
    total2.sent()
    sent.end()
    chips_to_heads(lambda at: r.inbox1[at, 256:288, :], keep(r.q_rows))
    project_back(r.inbox1, r.q_rows, tables, r.du, r.ib_sums0)
    weight_grad(r.first, r.du, r.dw_in, 0, WIN)
    scatter_in0.begin()
    join_back(
        r.du, r.in0, da2, r.normed0, r.vectors[0:1, :], r.vectors[1:2, :], r.sums0.at[pl.ds(0, 8)], r.part,
        core, total3.begin,
    )
    scatter_in0.pass_on()
    total3.cross()
    scatter_ff0.deliver()

    once = jnp.where(place_in_column == 0, 1.0, 0.0)
    for half in range(2):
        for across in range(4):
            lanes = slice((half * 4 + across) * 128, (half * 4 + across + 1) * 128)
            at_home = jnp.where((tp == half) & (mine == across), 1.0, 0.0)
            for chip_z in range(4):
                cut = slice(chip_z * 128, (chip_z + 1) * 128)
                at = across * 4 + chip_z
                pieces = [
                    r.sums0[0:2, lanes], r.sums1[0:2, lanes], r.sums0[2:4, lanes], r.sums1[2:4, lanes],
                    r.ib_sums0[0:3, :] * at_home, r.ib_sums1[0:3, :] * at_home,
                    r.sums0[8:9, lanes] * once, r.sums0[8:9, lanes] * once,
                    r.sums1[8:9, lanes] * once, r.sums1[8:9, lanes] * once,
                    r.eb_sums0[0:1, cut] * at_home, r.eb_sums1[0:1, cut] * at_home,
                ]
                row = 0
                for piece in pieces:
                    count = piece.shape[0]
                    r.small[at, half, row : row + count, :] = piece
                    row += count
                r.small[at, half, 20:24, :] = jnp.zeros((4, 128), F32)
    around = []
    for k, (dx, dz) in enumerate(STEPS):
        copy = remote(
            r.small.at[ring(x, dx) * 4 + ring(z, dz)],
            r.gathered.at[k],
            r.send_s.at[k],
            r.recv_s.at[k],
            plane[k],
        )
        copy.start()
        around.append(copy)
    scatter_in0.turn()
    total3.combine()
    for copy in around:
        copy.wait_recv()
    r.total_s[...] = r.small[chip] + jnp.sum(r.gathered[...], axis=0)
    shared = []
    for k, peer in enumerate(column):
        copy = remote(r.total_s, r.others.at[k], r.send_d.at[k], r.recv_d.at[k], peer)
        copy.start()
        shared.append(copy)
    scatter_in0.pass_line()
    total1.end()
    shift = r.vectors[16:17, :] + r.vectors[17:18, :]
    for k in range(2):
        rows = pl.ds(k * 64, 64)
        r.act_out[rows, :] = (r.own_hidden[rows, :] + r.summed2[k].astype(F32) + shift).astype(BF16)

    total3.end()
    own = mine * ROWS
    for k in range(4):
        rows = pl.ds(pl.multiple_of(own + k * 32, 32), 32)
        summed = r.summed3[k // 2, (k % 2) * 32 : (k % 2 + 1) * 32, :].astype(F32)
        r.grad_out[k * 32 : (k + 1) * 32, :] = r.own_grad[k * 32 : (k + 1) * 32, :] + norm_back(
            summed, r.normed0[rows, :], r.inverse0[rows, 0:1]
        )
    scatter_in0.deliver()
    for copy in shared:
        copy.wait_recv()
    sums_here = r.total_s[...] + jnp.sum(r.others[...], axis=0)
    sums_here = jnp.where(seq == 0, sums_here[0], sums_here[1])
    line = lax.broadcasted_iota(I32, sums_here.shape, 0)
    r.small_out[...] = jnp.where(
        line < 18,
        pltpu.roll(sums_here, 128 - (z * 4 + core * 2 + tp) * 8, 1),
        pltpu.roll(sums_here, 128 - (core * 2 + tp) * 32, 1),
    )
    scatter_ff0.end()
    scatter_in0.end()
    for copies in arriving:
        for copy in copies:
            copy.wait_send()
    for copy in smalls + spread + ranks_here + ranks_there + around + shared:
        copy.wait_send()
    for one in (cots, in0, ff0, in1, ff1, returned, back, sent, total3):
        one.sent()


def whole(*operands):
    outs = tuple(v for v in NAMES.values() if v is not None)
    scratch = [*SCRATCH.values(), *ColumnSum.SCRATCH * 2, *Scatter.scratch(PAIR), *Scatter.scratch(TWICE)]
    return pl.pallas_call(
        whole_kernel,
        out_shape=outs,
        in_specs=[VMEM] * len(operands),
        out_specs=(VMEM,) * len(outs),
        scratch_shapes=scratch,
        compiler_params=pltpu.CompilerParams(
            collective_id=0, has_side_effects=True, vmem_limit_bytes=LIMIT * MIB
        ),
        name="whole",
    )(*operands)


def outputs_kernel(
    weights, small, input_out, output_out, expand_out, contract_out,
    gain_out, shift_out, input_shift_out, output_shift_out, expand_shift_out,
):
    for layer in range(LAYERS):
        for k in range(4):
            part = weights[layer, k].astype(F32)
            for t in range(3):
                at = t * 512 + k * 128
                input_out[layer, :, at : at + 128] = part[:, t * 128 : (t + 1) * 128]
            output_out[layer, :, k * WOUT : (k + 1) * WOUT] = part[:, WIN:PAIR]
            expand_out[layer, :, k * WFF : (k + 1) * WFF] = part[:, PAIR : PAIR + WFF]
            contract_out[layer, :, k * WFF : (k + 1) * WFF] = part[:, PAIR + WFF :]
        for k in range(2):
            row = layer * 2 + k
            gain_out[layer, k : k + 1, :] = small[row : row + 1, 0:8]
            shift_out[layer, k : k + 1, :] = small[row + 4 : row + 5, 0:8]
            output_shift_out[layer, k : k + 1, :] = small[row + 14 : row + 15, 0:8]
        input_shift_out[layer] = small[8 + layer * 3 : 11 + layer * 3, 0:8]
    expand_shift_out[...] = small[18:20, 0:32]


def outputs(*operands):
    outs = (
        f32(2, 16, 1536), f32(2, 16, 512), f32(2, 16, 2048), f32(2, 16, 2048),
        f32(2, 2, 8), f32(2, 2, 8), f32(2, 3, 8), f32(2, 2, 8), f32(2, 32),
    )
    return pl.pallas_call(
        outputs_kernel,
        out_shape=outs,
        in_specs=[VMEM] * len(operands),
        out_specs=(VMEM,) * len(outs),
        compiler_params=pltpu.CompilerParams(vmem_limit_bytes=8 * MIB),
        name="outputs",
    )(*operands)


def rotary_tables():
    half = ROT // 2
    freqs = 10000.0 ** (-(np.arange(half) * 2.0 / ROT))
    lane = np.arange(128) % HEAD_DIM
    every = np.where(lane < ROT, np.tile(freqs, 128 // half), 0.0)[None, :]
    start = np.arange(32)[:, None] * ROWS * every
    steps = np.arange(ROWS)[:, None] * every
    return np.concatenate([np.cos(start), np.sin(start), np.cos(steps), np.sin(steps)]).astype(np.float32)


def local(
    tokens, cotangent, group_order, input_weight, output_weight, expand_weight, contract_weight,
    norm_gain, norm_shift, input_bias, output_bias, expand_bias,
):
    win = input_weight.reshape(LAYERS, 16, 3, 4, 128).transpose(0, 3, 1, 2, 4)
    eights = [norm_gain, norm_shift, input_bias, output_bias]
    raw = jnp.concatenate(
        [
            jnp.pad(jnp.concatenate([v.reshape(-1, 8) for v in eights], axis=0), ((0, 0), (0, 120))),
            jnp.pad(expand_bias, ((0, 4), (0, 96))),
        ],
        axis=0,
    )
    activations, input_gradient, weights_out, small = whole(
        win.reshape(LAYERS, 4, 16, WIN), output_weight, expand_weight, contract_weight, tokens, cotangent, raw,
        group_order, rotary_tables(),
    )
    input_out, *rest = outputs(weights_out, small)
    return (activations, input_gradient, input_out.reshape(2, 16, 3, 512), *rest)


def solution(mesh):
    rows, columns = P(("seq", "ctx"), None), P(None, None, ("seq", "ctx", "tp"))
    weight, flat = P(None, ("seq", "ctx"), "tp"), P(None, ("seq", "ctx", "tp"))
    first = P(None, ("seq", "ctx"), None, "tp")
    outs = (rows, rows, first, weight, weight, weight, columns, columns, columns, columns, flat)
    return jax.shard_map(
        local,
        mesh=mesh,
        in_specs=(rows, rows, P("seq", "ctx"), *outs[2:]),
        out_specs=outs,
        check_vma=False,
    )
```

```python
import types

import jax
import jax.numpy as jnp
import numpy as np
from jax import lax
from jax.experimental import pallas as pl
from jax.experimental.pallas import tpu as pltpu
from jax.sharding import PartitionSpec as P

MESH = pl.DeviceIdType.MESH
F32, BF16 = jnp.float32, jnp.bfloat16
D, HEAD_DIM, ROT, LAYERS = 1024, 64, 16, 2
ROWS = 128
GROUP = 512
WIN, WOUT, WFF = 384, 128, 512
COLS = WIN + WOUT + 2 * WFF
PARAMS = 208
EPSILON = 1e-05
MASKED = -1e30
MIB = 1024 * 1024
LIMIT = 62
WIDE = WOUT + 2 * WFF
PAIR, TWICE = WIN + WOUT, 2 * WFF
MESSAGE = 320


def place():
    ctx = lax.axis_index("ctx")
    chip = lax.div(ctx, 2)
    y = lax.axis_index("seq") * 2 + lax.axis_index("tp")
    return y, lax.div(chip, 4), lax.rem(chip, 4), lax.rem(ctx, 2)


def device(y, x, z, core):
    return (lax.div(y, 2), (x * 4 + z) * 2 + core, lax.rem(y, 2))


def ring(index, step):
    return lax.rem(index + step, 4)


def enter(partners):
    barrier = pltpu.get_barrier_semaphore()
    for partner in partners:
        pl.semaphore_signal(barrier, inc=1, device_id=partner, device_id_type=MESH)
    pl.semaphore_wait(barrier, len(partners))


STEPS = (
    (2, 2), (2, 1), (1, 2), (2, 3), (3, 2), (1, 1), (3, 3), (1, 3), (3, 1), (2, 0), (0, 2), (0, 1), (1, 0), (0, 3), (3, 0)
)


def plane_partners(y, x, z, core):
    return [device(y, ring(x, dx), ring(z, dz), core) for dx, dz in STEPS]


def column_partners(y, x, z, core):
    return [
        device(ring(y, dy), x, z, lax.rem(core + dc, 2))
        for dy in range(4)
        for dc in range(2)
        if dy or dc
    ]


def remote(source, target, send, receive, partner):
    return pltpu.make_async_remote_copy(
        src_ref=source,
        dst_ref=target,
        send_sem=send,
        recv_sem=receive,
        device_id=partner,
        device_id_type=MESH,
    )


HBM = pl.BlockSpec(memory_space=pl.ANY)
VMEM = pl.BlockSpec(memory_space=pltpu.VMEM)
SMEM = pl.BlockSpec(memory_space=pltpu.SMEM)


def bf(*shape):
    return jax.ShapeDtypeStruct(shape, BF16)


def f32(*shape):
    return jax.ShapeDtypeStruct(shape, F32)


def vbf(*shape):
    return pltpu.VMEM(shape, BF16)


def vf32(*shape):
    return pltpu.VMEM(shape, F32)


def dma(*shape):
    return pltpu.SemaphoreType.DMA(shape)


PEERS = ((0, 1), (1, 0), (1, 1))


def peer_at(y, x, z, core, step):
    seq, tp = lax.div(y, 2), lax.rem(y, 2)
    seq_to, core_to = lax.rem(seq + step[0], 2), lax.rem(core + step[1], 2)
    return seq_to * 2 + core_to, device(seq_to * 2 + tp, x, z, core_to)


class Gather:
    def __init__(self, full, where, send, recv):
        y, x, z, core = where
        self.full, self.x, self.z, self.send, self.recv = full, x, z, send, recv
        self.near = {
            "x": (device(y, ring(x, 1), z, core), device(y, ring(x, 3), z, core)),
            "z": (device(y, x, ring(z, 1), core), device(y, x, ring(z, 3), core)),
        }
        self.held = [(), ()]
        self.started = []

    def go(self, source, slot, partner):
        copy = remote(source, source, self.send.at[slot], self.recv.at[slot], partner)
        copy.start()
        self.started.append(copy)
        return copy

    def begin(self):
        for half in range(2):
            up, down = self.near["xz"[half]]
            own = self.full.at[half, self.x, self.z]
            self.held[half] = (self.go(own, half * 8, up), self.go(own, half * 8 + 1, down))

    def arrive(self, half):
        for copy in self.held[half]:
            copy.wait_recv()

    def pass_on(self):
        x, z = self.x, self.z
        for half in range(2):
            self.arrive(half)
            up, down = self.near["xz"[half]]
            whole = self.full.at[half]
            if half == 0:
                before, after = whole.at[ring(x, 3), z], whole.at[ring(x, 1), z]
            else:
                before, after = whole.at[x, ring(z, 3)], whole.at[x, ring(z, 1)]
            self.held[half] = (
                self.go(before.at[pl.ds(0, 16)], half * 8 + 2, up),
                self.go(after.at[pl.ds(16, 16)], half * 8 + 3, down),
            )

    def turn(self):
        for half in range(2):
            self.arrive(half)
            up, down = self.near["zx"[half]]
            whole = self.full.at[half]
            line = whole.at[:, self.z] if half == 0 else whole.at[self.x]
            self.held[half] = (self.go(line, half * 8 + 4, up), self.go(line, half * 8 + 5, down))

    def pass_line(self):
        x, z = self.x, self.z
        two, more = pl.ds(0, 2), pl.ds(2, 2)
        for half in range(2):
            self.arrive(half)
            up, down = self.near["zx"[half]]
            whole = self.full.at[half]
            if half == 0:
                before, after = whole.at[two, ring(z, 3)], whole.at[more, ring(z, 1)]
            else:
                before, after = whole.at[ring(x, 3), two], whole.at[ring(x, 1), more]
            self.held[half] = (
                self.go(before, half * 8 + 6, up),
                self.go(after, half * 8 + 7, down),
            )

    def end(self):
        for half in range(2):
            self.arrive(half)

    def sent(self):
        for copy in self.started:
            copy.wait_send()


class RowShare:
    def __init__(self, source, target, where, send, recv):
        y, x, z, core = where
        self.source, self.target, self.send, self.recv = source, target, send, recv
        seq = lax.div(y, 2)
        self.own = rows_at(seq * 2 + core, ROWS)
        self.other = rows_at((1 - seq) * 2 + core, ROWS)
        self.sibling = device(y, x, z, lax.rem(core + 1, 2))
        self.facing = device(3 - y, x, z, core)
        self.copies = []

    def go(self, source, target, slot, partner):
        copy = remote(source, target, self.send.at[slot], self.recv.at[slot], partner)
        copy.start()
        self.copies.append(copy)

    def begin(self):
        self.target[self.own, :] = self.source[...]
        self.go(self.source, self.target.at[self.own], 0, self.facing)
        self.go(self.source, self.target.at[self.own], 1, self.sibling)

    def pass_on(self):
        self.copies[0].wait_recv()
        block = self.target.at[self.other]
        self.go(block, block, 2, self.sibling)

    def end(self):
        for copy in self.copies[1:]:
            copy.wait_recv()

    def sent(self):
        for copy in self.copies:
            copy.wait_send()


class ColumnSum:
    SCRATCH = [vbf(4, 64, D), vbf(3, 64, D), vbf(3, 64, D)] + [dma(4), dma(4), dma(3), dma(3), dma(7), dma(7)]
    ORDER = (2, 1, 3)

    def __init__(self, part, out, where, everywhere, scratch):
        self.part, self.out, self.where, self.everywhere = part, out, where, everywhere
        (self.near, self.far, self.held, self.send1, self.recv1, self.send2, self.recv2, self.send3, self.recv3) = scratch
        y, x, z, core = where
        self.sibling = device(y, x, z, lax.rem(core + 1, 2))
        self.chips = [device(ring(y, dy), x, z, core) for dy in (1, 2, 3)]

    def begin(self):
        y, x, z, core = self.where
        self.nears = {}
        for dy in (*self.ORDER, 0):
            to = ring(y, dy)
            source = self.part.at[lax.div(to, 2), lax.rem(core + 1, 2), lax.rem(to, 2)]
            self.nears[dy] = remote(
                source, self.near.at[dy], self.send1.at[dy], self.recv1.at[dy], self.sibling
            )
            self.nears[dy].start()

    def cross(self):
        y, x, z, core = self.where
        self.fars = []
        for dy in self.ORDER:
            to = ring(y, dy)
            self.nears[dy].wait_recv()
            own = self.part[lax.div(to, 2), core, lax.rem(to, 2)].astype(F32)
            self.held[dy - 1] = (own + self.near[dy].astype(F32)).astype(BF16)
            copy = remote(
                self.held.at[dy - 1],
                self.far.at[dy - 1],
                self.send2.at[dy - 1],
                self.recv2.at[dy - 1],
                self.chips[dy - 1],
            )
            copy.start()
            self.fars.append(copy)

    def combine(self):
        y, x, z, core = self.where
        seq, tp = lax.div(y, 2), lax.rem(y, 2)
        self.nears[0].wait_recv()
        total = self.part[seq, core, tp].astype(F32) + self.near[0].astype(F32)
        for copy in self.fars:
            copy.wait_recv()
        for k in range(3):
            total = total + self.far[k].astype(F32)
        self.outs, self.relayed = [], []
        own = self.out.at[seq, core, tp] if self.everywhere else self.out.at[tp]
        own[...] = total.astype(BF16)
        if self.everywhere:
            for dy in self.ORDER:
                self.go(self.outs, own, dy - 1, self.chips[dy - 1])
            self.go(self.relayed, own, 3, self.sibling)
        else:
            self.go(self.outs, own, 0, device(seq * 2 + lax.rem(tp + 1, 2), x, z, core))

    def go(self, kept, block, slot, partner):
        copy = remote(block, block, self.send3.at[slot], self.recv3.at[slot], partner)
        copy.start()
        kept.append(copy)

    def relay(self):
        y, x, z, core = self.where
        for at, dy in enumerate(self.ORDER):
            self.outs[at].wait_recv()
            source = ring(y, 4 - dy)
            block = self.out.at[lax.div(source, 2), core, lax.rem(source, 2)]
            self.go(self.relayed, block, 3 + dy, self.sibling)

    def end(self):
        if self.everywhere:
            for copy in self.relayed:
                copy.wait_recv()
        else:
            self.outs[0].wait_recv()

    def sent(self):
        for copy in (*self.nears.values(), *self.fars, *self.outs, *self.relayed):
            copy.wait_send()


class Scatter:
    def __init__(self, dw, out, where, final, scratch):
        y, x, z, core = where
        self.dw, self.out, self.where, self.x, self.z = dw, out, where, x, z
        (self.opp1, self.dir1, self.comb1, self.sent1, self.mid, self.opp2, self.dir2, self.comb2, self.sent2, self.done,
         self.send, self.recv) = scratch
        self.send_f, self.recv_f = final
        self.near = {
            "x": (device(y, ring(x, 1), z, core), device(y, ring(x, 3), z, core)),
            "z": (device(y, x, ring(z, 1), core), device(y, x, ring(z, 3), core)),
        }
        self.started, self.held = [], [(), ()]

    @staticmethod
    def scratch(columns):
        big, small = vbf(2, 2, 2, 32, columns), vbf(2, 2, 16, columns)
        mid = vbf(2, 4, 32, columns)
        return [big] * 4 + [mid] + [small] * 5 + [dma(24), dma(24)]

    def go(self, source, target, slot, partner):
        copy = remote(source, target, self.send.at[slot], self.recv.at[slot], partner)
        copy.start()
        self.started.append(copy)
        return copy

    def part1(self, half, step, side):
        two = pl.ds(side * 2, 2)
        whole = self.dw.at[half]
        if half == 0:
            return whole.at[two, ring(self.z, step)]
        return whole.at[ring(self.x, step), two]

    def part2(self, half, step, side):
        at = ring(self.x, step) if half == 0 else ring(self.z, step)
        return self.mid.at[half, at].at[pl.ds(side * 16, 16)]

    def open(self, half, part, axis, opposite, direct, base):
        up, down = self.near[axis]
        self.held[half] = (
            self.go(part(half, 2, 0), opposite.at[half, 0], base, up),
            self.go(part(half, 2, 1), opposite.at[half, 1], base + 1, down),
            self.go(part(half, 1, 1), direct.at[half, 0], base + 2, up),
            self.go(part(half, 3, 0), direct.at[half, 1], base + 3, down),
        )

    def onward(self, half, part, axis, opposite, combined, sent, base):
        up, down = self.near[axis]
        copies = self.held[half]
        copies[0].wait_recv()
        sent[half, 0] = (part(half, 1, 0)[...].astype(F32) + opposite[half, 0].astype(F32)).astype(BF16)
        first = self.go(sent.at[half, 0], combined.at[half, 0], base + 4, up)
        copies[1].wait_recv()
        sent[half, 1] = (part(half, 3, 1)[...].astype(F32) + opposite[half, 1].astype(F32)).astype(BF16)
        second = self.go(sent.at[half, 1], combined.at[half, 1], base + 5, down)
        self.held[half] = (*copies[2:], first, second)

    def finish(self, half, part, direct, combined, target):
        for copy in self.held[half]:
            copy.wait_recv()
        for side in range(2):
            total = (
                part(half, 0, side)[...].astype(F32)
                + combined[half, side].astype(F32)
                + direct[half, 1 - side].astype(F32)
            )
            target(half, side)[...] = total.astype(BF16)

    def begin(self):
        for half in range(2):
            self.open(half, self.part1, "zx"[half], self.opp1, self.dir1, half * 12)

    def pass_on(self):
        for half in range(2):
            self.onward(half, self.part1, "zx"[half], self.opp1, self.comb1, self.sent1, half * 12)

    def turn(self):
        for half in range(2):
            self.finish(
                half,
                self.part1,
                self.dir1,
                self.comb1,
                lambda h, side: self.mid.at[h, pl.ds(side * 2, 2)],
            )
            self.open(half, self.part2, "xz"[half], self.opp2, self.dir2, half * 12 + 6)

    def pass_line(self):
        for half in range(2):
            self.onward(
                half, self.part2, "xz"[half], self.opp2, self.comb2, self.sent2, half * 12 + 6
            )

    def deliver(self):
        y, x, z, core = self.where
        seq = lax.div(y, 2)
        mine = seq * 2 + core
        for half in range(2):
            self.finish(
                half, self.part2, self.dir2, self.comb2, lambda h, side: self.done.at[h, side]
            )
        self.out[mine] = self.done[seq, core]
        self.final = []
        for k, step in enumerate(PEERS):
            theirs, peer = peer_at(y, x, z, core, step)
            copy = remote(
                self.done.at[lax.div(theirs, 2), lax.rem(theirs, 2)],
                self.out.at[mine],
                self.send_f.at[k],
                self.recv_f.at[k],
                peer,
            )
            copy.start()
            self.final.append(copy)

    def end(self):
        for copy in self.final:
            copy.wait()
        for copy in self.started:
            copy.wait_send()


class Exchange:
    def __init__(self, where, source, target, rows, send, recv):
        y, x, z, core = where
        chip = x * 4 + z
        cut = pl.ds(0, rows)
        target[chip, cut, :] = source[chip, cut, :]
        self.copies = []
        for k, (dx, dz) in enumerate(STEPS):
            to_x, to_z = ring(x, dx), ring(z, dz)
            copy = remote(
                source.at[to_x * 4 + to_z, cut],
                target.at[chip, cut],
                send.at[k],
                recv.at[k],
                device(y, to_x, to_z, core),
            )
            copy.start()
            self.copies.append(copy)

    def end(self):
        for copy in self.copies:
            copy.wait_recv()

    def sent(self):
        for copy in self.copies:
            copy.wait_send()


def loop(count, body, together=1):
    def step(index, carry):
        for k in range(together):
            body(index * together + k)
        return carry

    lax.fori_loop(0, count // together, step, 0)


def rows_at(index, count):
    return pl.ds(pl.multiple_of(index * count, count), count)


def turned(values, tables, sign):
    one, right, left = tables
    half = ROT // 2
    return values * one + sign * (
        pltpu.roll(values, 128 - half, 1) * right + pltpu.roll(values, half, 1) * left
    )


def low_lanes(shape):
    return lax.broadcasted_iota(jnp.int32, shape, 1) < HEAD_DIM


def swap(values):
    return pltpu.roll(values, HEAD_DIM, 1)


def heads_to_chips(values, target):
    def body(index):
        seq, quarter = lax.div(index, 4), lax.rem(index, 4)
        first, second = values(seq, 0, quarter), values(seq, 1, quarter)
        low = low_lanes(first.shape)
        target(seq * 8 + quarter, jnp.where(low, first, swap(second)).astype(BF16))
        target(seq * 8 + 4 + quarter, jnp.where(low, swap(first), second).astype(BF16))

    loop(8, body, 4)


def group_rows(seq, core, quarter):
    return pl.ds(pl.multiple_of(seq * 256 + core * 128 + quarter * 32, 32), 32)


def core_rows(step, core):
    return lax.div(step, 4) * 8 + core * 4 + lax.rem(step, 4)


def normalize_rows(hidden, normed, inverse, count, index_of):
    def body(step):
        index = index_of(step)
        rows = rows_at(index, 32)
        values = hidden(index)
        centred = values - jnp.mean(values, axis=1, keepdims=True)
        spread = jnp.mean(centred * centred, axis=1, keepdims=True)
        scale = lax.rsqrt(spread + EPSILON)
        normed[rows, :] = centred * scale
        inverse[rows, :] = jnp.broadcast_to(scale, (32, 128))

    loop(count, body, 2)


def scale_rows(normed, gain, shift, target):
    def body(index):
        rows = rows_at(index, 32)
        target[rows, :] = (normed[rows, :] * gain + shift).astype(BF16)

    loop(16, body)


def project(first, weight, bias, tables, outbox, q_rows):
    whole = columns_of(weight, 0, WIN)

    def body(index):
        rows = rows_at(index, 128)
        u = jnp.dot(first[rows, :], whole, preferred_element_type=F32)
        turn = tuple(t[rows, :] for t in tables)
        q_rows[rows, :] = turned(u[:, :128] + bias[0:1, :], turn, 1.0)
        keys = turned(u[:, 128:256] + bias[1:2, :], turn, 1.0)
        values = u[:, 256:] + bias[2:3, :]
        low = low_lanes(keys.shape)
        seq = lax.div(index, 2)
        part = rows_at(lax.rem(index, 2), 128)
        for head in range(2):
            pair = (keys, swap(values)) if head == 0 else (swap(keys), values)
            pair = jnp.where(low, *pair).astype(BF16)
            for k in range(4):
                outbox[seq * 8 + head * 4 + k, part, :] = pair

    loop(4, body)


def gelu_parts(inner):
    return 0.5 * (1.0 + lax.erf(inner * (0.5**0.5)))


def columns_of(weight, first, count):
    return weight[:, :, :, :, first : first + count].reshape(D, count)


def expand(second, whole, bias, inner, activated):

    def body(index):
        rows = rows_at(index, 128)
        e = jnp.dot(second[rows, :], whole, preferred_element_type=F32) + bias
        inner[rows, :] = e
        activated[rows, :] = (e * gelu_parts(e)).astype(BF16)

    loop(4, body)


def chips_to_heads(parts, target):
    def body(index):
        seq, quarter = lax.div(index, 4), lax.rem(index, 4)
        first = parts(seq * 8 + quarter).astype(F32)
        second = parts(seq * 8 + 4 + quarter).astype(F32)
        low = low_lanes(first.shape)
        target(seq, 0, quarter, jnp.where(low, first, swap(second)))
        target(seq, 1, quarter, jnp.where(low, swap(first), second))

    loop(8, body, 4)


def block_of(index):
    return lax.div(index, 2), lax.rem(index, 2)


class Wide:
    def __init__(self, buffer, base):
        self.buffer, self.base = buffer, base

    def at(self, start, count, k):
        return pl.ds(pl.multiple_of(self.base + k * GROUP + start, count), count)

    def put(self, start, count, values):
        for k in range(4):
            self.buffer[self.at(start, count, k), :] = values[:, k * 256 : (k + 1) * 256]

    def get(self, start, count):
        return jnp.concatenate([self.buffer[self.at(start, count, k), :] for k in range(4)], axis=1)


def contract(activated, whole, z):

    def body(index):
        rows = rows_at(index, 128)
        values = lax.dot_general(
            activated[rows, :], whole, (((1,), (1,)), ((), ())), preferred_element_type=F32
        )
        z.put(index * 128, 128, values)

    loop(4, body)


def add_mixed(mixed, weight, z, part, core, between):
    def one(seq, core):
        index = seq * 2 + core
        rows = rows_at(index, 128)
        both = z.get(index * 128, 128) + lax.dot_general(
            mixed[rows, :], weight, (((1,), (1,)), ((), ())), preferred_element_type=F32
        )
        part[seq, core] = both.astype(BF16).reshape(2, 64, D)

    loop(2, lambda seq: one(seq, 1 - core))
    between()
    loop(2, lambda seq: one(seq, core))


def rows32(summed, index):
    seq, core, tp = lax.div(index, 8), lax.rem(lax.div(index, 4), 2), lax.rem(lax.div(index, 2), 2)
    return summed[seq, core, tp, rows_at(lax.rem(index, 2), 32), :].astype(F32)


def mix_back(dz, weight, rows128):
    def body(index):
        rows = rows_at(index, 128)
        dm = jnp.dot(dz(rows), weight, preferred_element_type=F32)
        rows128[rows, :] = dm.astype(BF16).astype(F32)

    loop(4, body)


def expand_back(dz, up, down, inner, de, da, sums):
    sums[0:1, :] = jnp.zeros((1, WFF), F32)

    def body(index):
        rows = rows_at(index, 128)
        dg = jnp.dot(dz(rows), down, preferred_element_type=F32)
        e = inner[rows, :]
        slope = gelu_parts(e) + e * jnp.exp(-0.5 * e * e) * ((2.0 * jnp.pi) ** -0.5)
        low = (dg * slope).astype(BF16)
        de[rows, :] = low
        sums[0:1, :] += jnp.sum(low.astype(F32), axis=0, keepdims=True)
        values = lax.dot_general(low, up, (((1,), (1,)), ((), ())), preferred_element_type=F32)
        da.put(index * 128, 128, values)

    loop(4, body)


def weight_grad(left, right, dw, first, count):
    def body(index):
        block = lax.dot_general(
            left[:, rows_at(index, 256)],
            right[...],
            (((0,), (0,)), ((), ())),
            preferred_element_type=F32,
        )
        two = pl.ds(lax.rem(index, 2) * 2, 2)
        dw[lax.div(index, 2), two, :, :, first : first + count] = block.astype(BF16).reshape(
            2, 4, 32, count
        )

    loop(4, body)


def project_back(pairs, q_grad, tables, du, sums):
    sums[...] = jnp.zeros(sums.shape, F32)

    def body(index):
        seq, core = block_of(index)
        part = rows_at(core, 128)
        heads = []
        for head in range(2):
            total = pairs[seq * 8 + head * 4, part, :].astype(F32)
            for k in range(1, 4):
                total = total + pairs[seq * 8 + head * 4 + k, part, :].astype(F32)
            heads.append(total)
        low = low_lanes(heads[0].shape)
        rows = rows_at(index, 128)
        turn = tuple(t[rows, :] for t in tables)
        grads = (
            turned(q_grad[rows, :], turn, -1.0),
            turned(jnp.where(low, heads[0], swap(heads[1])), turn, -1.0),
            jnp.where(low, swap(heads[0]), heads[1]),
        )
        for k in range(3):
            rounded = grads[k].astype(BF16)
            du[rows, k * 128 : (k + 1) * 128] = rounded
            sums[k : k + 1, :] += jnp.sum(rounded.astype(F32), axis=0, keepdims=True)

    loop(4, body)


def join_back(du, weight, da2, normed, gain1, gain2, sums, part, core, between):
    whole = columns_of(weight, 0, WIN)
    sums[...] = jnp.zeros(sums.shape, F32)

    def one(step, core):
        seq, tp = lax.div(step, 2), lax.rem(step, 2)
        index = seq * 4 + core * 2 + tp
        rows = rows_at(index, 64)
        da = lax.dot_general(
            du[rows, :], whole, (((1,), (1,)), ((), ())), preferred_element_type=F32
        )
        db = da2.get(index * 64, 64)
        n = normed[rows, :]
        for k, value in enumerate((da * n, db * n, da, db)):
            sums[k : k + 1, :] += jnp.sum(value, axis=0, keepdims=True)
        part[seq, core, tp] = (da * gain1 + db * gain2).astype(BF16)

    loop(4, lambda step: one(step, 1 - core), 2)
    between()
    loop(4, lambda step: one(step, core), 2)


def norm_back(scaled, normed, inverse):
    first = jnp.mean(scaled, axis=1, keepdims=True)
    second = jnp.mean(scaled * normed, axis=1, keepdims=True)
    return inverse * (scaled - first - normed * second)


TILE = 256
SPAN = 1024


def seen(quarter, tile):
    key = lax.broadcasted_iota(jnp.int32, (SPAN, TILE), 0)
    row = lax.broadcasted_iota(jnp.int32, (SPAN, TILE), 1)
    place_of = (row // 32) * ROWS + quarter * 32 + row % 32
    return key <= place_of


def score_span(quarter, tile, span, queries, kvs):
    block = lax.dot_general(
        kvs[span * SPAN : (span + 1) * SPAN, :],
        queries,
        (((1,), (1,)), ((), ())),
        preferred_element_type=F32,
    )
    return jnp.where(seen(quarter, tile), block, MASKED) if span == tile else block


def forward_tile(quarter, tile, queries, kvs, kvt, score):
    highest = jnp.full((1, TILE), MASKED, F32)
    for span in range(tile + 1):
        block = score_span(quarter, tile, span, queries, kvs)
        score[span * SPAN : (span + 1) * SPAN, :] = block
        highest = jnp.maximum(highest, jnp.max(block, axis=0, keepdims=True))
    total = jnp.zeros((1, TILE), F32)
    mixed = jnp.zeros((128, TILE), F32)
    for span in range(tile + 1):
        weight = jnp.exp(score[span * SPAN : (span + 1) * SPAN, :] - highest)
        total = total + jnp.sum(weight, axis=0, keepdims=True)
        mixed = mixed + jnp.dot(
            kvt[:, span * SPAN : (span + 1) * SPAN],
            weight.astype(BF16),
            preferred_element_type=F32,
        )
    return mixed / total, highest + jnp.log(total)


def backward_span(tile, span, block, lse, delta, queries, outs, kvs, kvt, acc):
    keyed = kvs[span * SPAN : (span + 1) * SPAN, :]
    probs = jnp.exp(block - lse)
    back = lax.dot_general(keyed, outs, (((1,), (1,)), ((), ())), preferred_element_type=F32)
    score_grad = (probs * (back - delta)).astype(BF16)
    pair = jnp.dot(
        jnp.concatenate([score_grad, probs.astype(BF16)], axis=1),
        jnp.concatenate([queries, outs], axis=0),
        preferred_element_type=F32,
    )
    pair = pair.reshape(8, ROWS, 128)
    if tile == 3:
        acc[span * 8 : (span + 1) * 8] = pair
    else:
        acc[span * 8 : (span + 1) * 8] += pair
    return jnp.dot(
        kvt[:, span * SPAN : (span + 1) * SPAN], score_grad, preferred_element_type=F32
    )


def put_back_rows(ranks, rows, target, upper):
    def body(chip):
        first = rows[ranks[0, chip * 2]]
        second = rows[ranks[0, chip * 2 + 1]]
        if upper:
            first = swap(first)
        else:
            second = swap(second)
        target(chip, jnp.where(low_lanes(first.shape), first, second).astype(BF16))

    loop(16, body, 8)


def put_back_pairs(ranks, acc, outbox):
    def body(chip):
        for core in range(2):
            rank = ranks[0, chip * 2 + core]
            outbox[chip, core * ROWS : (core + 1) * ROWS, :] = acc[rank].astype(BF16)

    loop(16, body, 2)


def owner(order, rank):
    return order[rank, 0], order[rank, 1]


def sort_rows(order, source, target, upper, scale):
    def body(rank):
        chip, core = owner(order, rank)
        block = source(chip).astype(F32) * scale
        other = swap(block)
        low = low_lanes(block.shape)
        if upper:
            part = jnp.where(low, 0.0, jnp.where(core == 0, other, block))
        else:
            part = jnp.where(low, jnp.where(core == 0, block, other), 0.0)
        target[rows_at(rank, 32), :] = part.astype(BF16)

    loop(32, body, 8)


def sort_pairs(order, inbox, kvs, kvt):
    def body(rank):
        chip, core = owner(order, rank)
        keyed = jnp.where(core == 0, inbox[chip, 0:ROWS, :], inbox[chip, ROWS : 2 * ROWS, :])
        kvs[rows_at(rank, ROWS), :] = keyed
        kvt[:, rows_at(rank, ROWS)] = keyed.astype(F32).T.astype(BF16)

    loop(32, body, 4)


def tile_rows(tile):
    return slice(tile * TILE, (tile + 1) * TILE)


NAMES = {
    "win": None, "wout": None, "wexp": None, "wcon": None, "tok_in": None, "cot_in": None, "raw": None, "rank": None,
    "angles": None,
    "act_out": bf(ROWS, D), "grad_out": f32(ROWS, D), "weights_out": bf(2, 4, 16, PAIR + TWICE), "small_out": f32(24, 128),
}
I32 = jnp.int32
SCRATCH = {
    "in0": vbf(2, 4, 4, 32, WIN), "in1": vbf(2, 4, 4, 32, PAIR),
    "ff0": vbf(2, 4, 4, 32, WIDE), "ff1": vbf(2, 4, 4, 32, TWICE),
    "win0": vbf(4, 16, WIN), "wff0": vbf(4, 16, WIDE), "win1": vbf(4, 16, PAIR), "wff1": vbf(4, 16, TWICE),
    "tok": vbf(GROUP, D), "cot": vbf(GROUP, D),
    "par": vf32(24, 128), "trig": vf32(8, 128), "column_p": vf32(8, 24, 128), "joined": vf32(2, 24, 128),
    "plane_p": vf32(16, 2, 24, 128), "column_t": vf32(4, 8, 128), "vectors": vf32(24, D),
    "ib": vf32(8, 128), "eb": vf32(8, WFF),
    "par_i": pltpu.VMEM((8, 128), I32), "column_i": pltpu.VMEM((8, 8, 128), I32),
    "joined_i": pltpu.VMEM((2, 8, 128), I32), "plane_i": pltpu.VMEM((16, 2, 8, 128), I32),
    "ranks_v": pltpu.VMEM((8, 128), I32), "order_v": pltpu.VMEM((32, 128), I32),
    "ranks": pltpu.SMEM((8, 128), I32), "order": pltpu.SMEM((32, 128), I32),
    "one": vf32(GROUP, 128), "right": vf32(GROUP, 128), "left": vf32(GROUP, 128),
    "normed0": vf32(GROUP, D), "normed1": vf32(GROUP, D), "inverse0": vf32(GROUP, 128), "inverse1": vf32(GROUP, 128),
    "first": vbf(GROUP, D), "second": vbf(GROUP, D),
    "inner0": vf32(GROUP, WFF), "inner1": vf32(GROUP, WFF), "act0": vbf(GROUP, WFF), "act1": vbf(GROUP, WFF),
    "mixed0": vbf(GROUP, 128), "mixed1": vbf(GROUP, 128), "q_rows": vf32(GROUP, 128),
    "outbox": vbf(16, MESSAGE, 128), "inbox0": vbf(16, MESSAGE, 128), "inbox1": vbf(16, MESSAGE, 128),
    "m_out": vbf(16, 32, 128), "m_in": vbf(16, 32, 128), "dm_out": vbf(16, 32, 128), "dm_in": vbf(16, 32, 128),
    "kvs0": vbf(4096, 128), "kvs1": vbf(4096, 128), "kvt0": vbf(128, 4096), "kvt1": vbf(128, 4096),
    "qs0": vbf(1024, 128), "qs1": vbf(1024, 128), "dos": vbf(1024, 128), "o0": vf32(4, 128, TILE), "lse0": vf32(4, 8, TILE),
    "wide": vf32(4096, TILE), "rows": vf32(32, 32, 128), "o1": vf32(32, 32, 128), "acc": vf32(32, 128, 128),
    "de": vbf(GROUP, WFF), "du": vbf(GROUP, WIN), "own_grad": vf32(ROWS, D), "own_hidden": vf32(ROWS, D),
    "part": vbf(2, 2, 2, 64, D), "part2": vbf(2, 2, 2, 64, D), "summed": vbf(2, 2, 2, 64, D),
    "summed2": vbf(2, 64, D), "summed3": vbf(2, 64, D),
    "dw_in": vbf(2, 4, 4, 32, PAIR), "dw_ff": vbf(2, 4, 4, 32, TWICE),
    "sums0": vf32(16, D), "sums1": vf32(16, D), "ib_sums0": vf32(8, 128), "ib_sums1": vf32(8, 128),
    "eb_sums0": vf32(8, WFF), "eb_sums1": vf32(8, WFF),
    "small": vf32(16, 2, 24, 128), "gathered": vf32(15, 2, 24, 128), "total_s": vf32(2, 24, 128), "others": vf32(7, 2, 24, 128),
    "here": dma(7), "send_a": dma(5, 3), "recv_a": dma(5, 3), "send_t": dma(2, 3), "recv_t": dma(2, 3),
    "send_p": dma(2, 7), "recv_p": dma(2, 7), "send_v": dma(2, 15), "recv_v": dma(2, 15),
    "send_g": dma(4, 16), "recv_g": dma(4, 16), "send_x": dma(6, 15), "recv_x": dma(6, 15),
    "send_f": dma(4, 3), "recv_f": dma(4, 3), "send_s": dma(15), "recv_s": dma(15), "send_d": dma(7), "recv_d": dma(7),
}
COLUMN = len(ColumnSum.SCRATCH)
LINES = len(Scatter.scratch(WIN))


def whole_kernel(*refs):
    names = [*NAMES, *SCRATCH]
    r = types.SimpleNamespace(**dict(zip(names, refs)))
    rest = refs[len(names) :]
    column_sets = [rest[k * COLUMN : (k + 1) * COLUMN] for k in range(2)]
    rest = rest[2 * COLUMN :]
    lines_in, lines_ff = rest[:LINES], rest[LINES:]
    where = y, x, z, core = place()
    seq, tp = lax.div(y, 2), lax.rem(y, 2)
    mine, chip = seq * 2 + core, x * 4 + z
    column, plane = column_partners(*where), plane_partners(*where)
    tables = (r.one, r.right, r.left)
    dz_rows = r.tok
    z_sum, da2 = Wide(r.wide, 0), Wide(r.wide, 4 * GROUP)

    def exchange(number, source, target, rows):
        return Exchange(where, source, target, rows, r.send_x.at[number], r.recv_x.at[number])

    def final(number):
        return r.send_f.at[number], r.recv_f.at[number]

    raw = r.raw[...]
    line = lax.broadcasted_iota(I32, raw.shape, 0)
    r.par[...] = jnp.where(
        line < 18,
        pltpu.roll(raw, (z * 4 + core * 2 + tp) * 8, 1),
        pltpu.roll(raw, (core * 2 + tp) * 32, 1),
    )
    lane = lax.broadcasted_iota(I32, (8, 128), 1)
    r.par_i[...] = jnp.where((lane == chip * 2 + core) & (tp == 0), r.rank[...], 0)
    r.trig[...] = jnp.zeros((8, 128), F32)
    for k in range(2):
        starts = r.angles[k * 32 : (k + 1) * 32, :]
        chosen = lax.broadcasted_iota(I32, starts.shape, 0) == r.rank[...]
        r.trig[k : k + 1, :] = jnp.sum(jnp.where(chosen, starts, 0.0), axis=0, keepdims=True)

    def share(slot, source, target):
        copies = [
            remote(source(theirs), target, r.send_a.at[slot, k], r.recv_a.at[slot, k], device_id)
            for k, (theirs, device_id) in enumerate(peers)
        ]
        own = pltpu.make_async_copy(source(mine), target, r.here.at[slot])
        for copy in (*copies, own):
            copy.start()
        local_copies.append(own)
        arriving.append(copies)

    def landed(slot):
        for copy in arriving[slot]:
            copy.wait_recv()
        local_copies[slot].wait()

    def to_all(number, source, target, partners, send, recv):
        copies = [
            remote(source, target, send.at[number, k], recv.at[number, k], peer)
            for k, peer in enumerate(partners)
        ]
        for copy in copies:
            copy.start()
        return copies

    for k in range(4):
        for t in range(3):
            r.win0[k, :, t * 128 : (t + 1) * 128] = r.win[0, :, t * 512 + k * 128 : t * 512 + (k + 1) * 128]
    enter(column + plane)

    quarter = pl.ds(pl.multiple_of(core * 16, 16), 16)
    peers = [peer_at(*where, step) for step in PEERS]
    local_copies, arriving = [], []
    share(0, lambda q: r.win0.at[q], r.in0.at[seq, x, z, quarter])
    place_in_column = y * 2 + core
    smalls = to_all(0, r.par, r.column_p.at[place_in_column], column, r.send_p, r.recv_p)
    tokens = RowShare(r.tok_in, r.tok, where, r.send_t.at[0], r.recv_t.at[0])
    tokens.begin()
    share(1, lambda q: r.trig, r.column_t.at[mine])
    ranks_here = to_all(1, r.par_i, r.column_i.at[place_in_column], column, r.send_p, r.recv_p)
    r.column_p[place_in_column] = r.par[...]
    r.column_i[place_in_column] = r.par_i[...]

    in0, ff0, in1, ff1 = (
        Gather(ref, where, r.send_g.at[k], r.recv_g.at[k])
        for k, ref in enumerate((r.in0, r.ff0, r.in1, r.ff1))
    )
    landed(0)
    in0.begin()
    for copy in smalls:
        copy.wait_recv()
    for half in range(2):
        r.joined[half] = jnp.sum(r.column_p[half * 4 : half * 4 + 4], axis=0)
    r.plane_p[chip] = r.joined[...]
    in0.pass_on()
    spread = to_all(0, r.joined, r.plane_p.at[chip], plane, r.send_v, r.recv_v)
    tokens.pass_on()
    for k in range(4):
        r.wff0[k, :, 0:WOUT] = r.wout[0, :, k * WOUT : (k + 1) * WOUT]
        r.wff0[k, :, WOUT : WOUT + WFF] = r.wexp[0, :, k * WFF : (k + 1) * WFF]
        r.wff0[k, :, WOUT + WFF :] = r.wcon[0, :, k * WFF : (k + 1) * WFF]
    share(2, lambda q: r.wff0.at[q], r.ff0.at[seq, x, z, quarter])
    in0.turn()
    tokens.end()

    def token_rows(index):
        return r.tok[rows_at(index, 32), :].astype(F32)

    normalize_rows(token_rows, r.normed0, r.inverse0, 6, lambda step: step)
    in0.pass_line()
    normalize_rows(token_rows, r.normed0, r.inverse0, 10, lambda step: step + 6)
    landed(1)
    for k in range(4):
        rows = pl.ds(k * ROWS, ROWS)
        cos_a, sin_a = r.column_t[k, 0:1, :], r.column_t[k, 1:2, :]
        cos_b, sin_b = r.angles[64:192, :], r.angles[192:320, :]
        sine = sin_a * cos_b + cos_a * sin_b
        spot = lax.broadcasted_iota(I32, sine.shape, 1) % HEAD_DIM
        r.one[rows, :] = cos_a * cos_b - sin_a * sin_b
        r.right[rows, :] = jnp.where(spot < ROT // 2, -sine, 0.0)
        r.left[rows, :] = jnp.where(spot < ROT // 2, 0.0, sine)
    for copy in spread:
        copy.wait_recv()
    for half in range(2):
        for across in range(4):
            at = (half * 4 + across) * 128
            block = jnp.sum(r.plane_p[across * 4 : across * 4 + 4, half], axis=0)
            r.vectors[:, at : at + 128] = block
    own = [r.plane_p[mine * 4 + k, tp] for k in range(4)]
    r.ib[...] = (own[0] + own[1] + own[2] + own[3])[8:16]
    for k in range(4):
        r.eb[:, k * 128 : (k + 1) * 128] = own[k][16:24]
    scale_rows(r.normed0, r.vectors[0:1, :], r.vectors[4:5, :], r.first)
    in0.end()

    def put_message(first):
        def put(at, values):
            r.outbox[at, first : first + 32, :] = values

        return put

    project(r.first, r.in0, r.ib[0:3, :], tables, r.outbox, r.q_rows)
    heads_to_chips(lambda s, c, k: r.q_rows[group_rows(s, c, k), :], put_message(256))
    sent = exchange(0, r.outbox, r.inbox0, 288)
    for copy in ranks_here:
        copy.wait_recv()
    for half in range(2):
        cut = r.column_i
        r.joined_i[half] = cut[half * 4] + cut[half * 4 + 1] + cut[half * 4 + 2] + cut[half * 4 + 3]
    r.plane_i[chip] = r.joined_i[...]
    ranks_there = to_all(1, r.joined_i, r.plane_i.at[chip], plane, r.send_v, r.recv_v)
    for k in range(4):
        for t in range(3):
            r.win1[k, :, t * 128 : (t + 1) * 128] = r.win[1, :, t * 512 + k * 128 : t * 512 + (k + 1) * 128]
        r.win1[k, :, WIN:] = r.wout[1, :, k * WOUT : (k + 1) * WOUT]
        r.wff1[k, :, :WFF] = r.wexp[1, :, k * WFF : (k + 1) * WFF]
        r.wff1[k, :, WFF:] = r.wcon[1, :, k * WFF : (k + 1) * WFF]
    landed(2)
    ff0.begin()
    share(3, lambda q: r.win1.at[q], r.in1.at[seq, x, z, quarter])
    share(4, lambda q: r.wff1.at[q], r.ff1.at[seq, x, z, quarter])
    cots = RowShare(r.cot_in, r.cot, where, r.send_t.at[1], r.recv_t.at[1])
    cots.begin()
    scale_rows(r.normed0, r.vectors[1:2, :], r.vectors[5:6, :], r.second)
    ff0.pass_on()
    for copy in ranks_there:
        copy.wait_recv()
    ranks = r.plane_i[0, lax.div(x, 2)]
    for k in range(1, 16):
        ranks = ranks + r.plane_i[k, lax.div(x, 2)]
    r.ranks_v[...] = jnp.minimum(ranks, 31)
    spot = lax.broadcasted_iota(I32, (32, 128), 1)
    match = (ranks[0:1, :] == lax.broadcasted_iota(I32, (32, 128), 0)) & (spot < 32)
    found = [jnp.where(match, value, 0) for value in (lax.div(spot, 2), lax.rem(spot, 2))]
    for k in range(7):
        found = [value + pltpu.roll(value, 1 << k, 1) for value in found]
    r.order_v[...] = jnp.where(spot == 0, jnp.minimum(found[0], 15), jnp.minimum(found[1], 1))
    scalars = [
        pltpu.make_async_copy(r.ranks_v, r.ranks, r.here.at[5]),
        pltpu.make_async_copy(r.order_v, r.order, r.here.at[6]),
    ]
    for copy in scalars:
        copy.start()
    tokens.sent()
    for copy in scalars:
        copy.wait()
    sent.end()
    ff0.turn()

    sort_pairs(r.order, r.inbox0, r.kvs0, r.kvt0)
    sort_rows(r.order, lambda at: r.inbox0[at, 256:288, :], r.qs0, False, HEAD_DIM**-0.5)
    steps = {3: (), 2: (cots.pass_on,), 1: (), 0: (ff0.pass_line,)}
    for tile in (3, 2, 1, 0):
        mixed, lse = forward_tile(z, tile, r.qs0[tile_rows(tile), :], r.kvs0, r.kvt0, r.wide)
        r.lse0[tile] = jnp.broadcast_to(lse, (8, TILE))
        r.o0[tile] = mixed
        r.rows[tile * 8 : tile * 8 + 8] = mixed.T.reshape(8, 32, 128)
        for step in steps[tile]:
            step()

    def put_to(ref):
        def put(at, values):
            ref[at] = values

        return put

    put_back_rows(r.ranks, r.rows, put_to(r.m_out), 1)
    returned = exchange(1, r.m_out, r.m_in, 32)
    landed(3)
    in1.begin()
    landed(4)
    ff1.begin()
    sent.sent()
    ff0.end()
    expand(r.second, columns_of(r.ff0, WOUT, WFF), r.eb[2:3, :], r.inner0, r.act0)
    in1.pass_on()
    contract(r.act0, columns_of(r.ff0, WOUT + WFF, WFF), z_sum)

    def keep(ref):
        def put(s, c, k, values):
            ref[group_rows(s, c, k), :] = values.astype(ref.dtype)

        return put

    ff1.pass_on()
    returned.end()
    chips_to_heads(lambda at: r.m_in[at], keep(r.mixed0))
    total = ColumnSum(r.part, r.summed, where, True, column_sets[0])
    add_mixed(r.mixed0, columns_of(r.ff0, 0, WOUT), z_sum, r.part, core, total.begin)
    total.cross()
    in1.turn()
    ff1.turn()
    total.combine()
    in1.pass_line()
    total.relay()
    cots.end()
    in1.end()
    mix_back(lambda rows: r.cot[rows, :], columns_of(r.in1, WIN, WOUT), r.q_rows)
    heads_to_chips(lambda s, c, k: r.q_rows[group_rows(s, c, k), :], put_message(288))
    shift = r.vectors[14:15, :] + r.vectors[15:16, :]

    def hidden(index):
        return r.tok[rows_at(index, 32), :].astype(F32) + rows32(r.summed, index) + shift

    normalize_rows(hidden, r.normed1, r.inverse1, 8, lambda step: core_rows(step, core))
    ff1.pass_line()
    total.end()
    normalize_rows(hidden, r.normed1, r.inverse1, 8, lambda step: core_rows(step, 1 - core))
    scale_rows(r.normed1, r.vectors[2:3, :], r.vectors[6:7, :], r.first)
    project(r.first, r.in1, r.ib[3:6, :], tables, r.outbox, r.q_rows)
    heads_to_chips(lambda s, c, k: r.q_rows[group_rows(s, c, k), :], put_message(256))
    sent = exchange(2, r.outbox, r.inbox1, 320)

    def keep_own(index):
        r.own_hidden[rows_at(index, 32), :] = hidden(mine * 4 + index)

    loop(4, keep_own)
    scale_rows(r.normed1, r.vectors[3:4, :], r.vectors[7:8, :], r.second)
    ff1.end()
    expand(r.second, columns_of(r.ff1, 0, WFF), r.eb[3:4, :], r.inner1, r.act1)
    weight_grad(r.cot, r.act1, r.dw_ff, WFF, WFF)
    total.sent()
    sent.end()

    sort_pairs(r.order, r.inbox1, r.kvs1, r.kvt1)
    sort_rows(r.order, lambda at: r.inbox1[at, 256:288, :], r.qs1, False, HEAD_DIM**-0.5)
    sort_rows(r.order, lambda at: r.inbox1[at, 288:320, :], r.dos, True, 1.0)
    sent.sent()
    for tile in (3, 2, 1, 0):
        queries, outs = r.qs1[tile_rows(tile), :], r.dos[tile_rows(tile), :]
        mixed, lse = forward_tile(z, tile, queries, r.kvs1, r.kvt1, r.wide)
        r.rows[tile * 8 : tile * 8 + 8] = mixed.T.reshape(8, 32, 128)
        delta = jnp.sum(outs.astype(F32).T * mixed, axis=0, keepdims=True)
        query_grad = jnp.zeros((128, TILE), F32)
        for span in range(tile + 1):
            block = r.wide[span * SPAN : (span + 1) * SPAN, :]
            query_grad = query_grad + backward_span(
                tile, span, block, lse, delta, queries, outs, r.kvs1, r.kvt1, r.acc
            )
        r.o1[tile * 8 : tile * 8 + 8] = (query_grad.T * (HEAD_DIM**-0.5)).reshape(8, 32, 128)
    put_back_rows(r.ranks, r.rows, put_message(288), 1)
    put_back_rows(r.ranks, r.o1, put_message(256), 0)
    put_back_pairs(r.ranks, r.acc, r.outbox)
    sent = exchange(3, r.outbox, r.inbox0, 320)

    total1 = ColumnSum(r.part, r.summed2, where, False, column_sets[1])
    total2 = ColumnSum(r.part2, r.summed, where, True, column_sets[0])
    scatter_ff = Scatter(r.dw_ff, r.weights_out.at[1, :, :, pl.ds(PAIR, TWICE)], where, final(0), lines_ff)
    scatter_in = Scatter(r.dw_in, r.weights_out.at[1, :, :, pl.ds(0, PAIR)], where, final(1), lines_in)
    up, down = columns_of(r.ff1, 0, WFF), columns_of(r.ff1, WFF, WFF)
    expand_back(lambda rows: r.cot[rows, :], up, down, r.inner1, r.de, da2, r.eb_sums1)
    weight_grad(r.second, r.de, r.dw_ff, 0, WFF)
    contract(r.act1, columns_of(r.ff1, WFF, WFF), z_sum)
    sent.end()
    chips_to_heads(lambda at: r.inbox0[at, 256:288, :], keep(r.q_rows))
    project_back(r.inbox0, r.q_rows, tables, r.du, r.ib_sums1)
    join_back(
        r.du, r.in1, da2, r.normed1, r.vectors[2:3, :], r.vectors[3:4, :], r.sums1.at[pl.ds(0, 8)], r.part2,
        core, total2.begin,
    )
    total2.cross()
    scatter_ff.begin()
    chips_to_heads(lambda at: r.inbox0[at, 288:320, :], keep(r.mixed1))
    weight_grad(r.cot, r.mixed1, r.dw_in, WIN, WOUT)
    weight_grad(r.first, r.du, r.dw_in, 0, WIN)
    total2.combine()
    scatter_ff.pass_on()
    scatter_in.begin()
    total2.relay()
    r.sums1[8:16, :] = jnp.zeros((8, D), F32)
    r.sums0[8:16, :] = jnp.zeros((8, D), F32)

    def after(index):
        rows = rows_at(index, 32)
        before = r.cot[rows, :].astype(F32)
        return before, before + norm_back(
            rows32(r.summed, index), r.normed1[rows, :], r.inverse1[rows, 0:1]
        )

    def put_grad(index):
        before, values = after(index)
        r.sums1[8:9, :] += jnp.sum(before, axis=0, keepdims=True)
        r.sums0[8:9, :] += jnp.sum(values, axis=0, keepdims=True)
        dz_rows[rows_at(index, 32), :] = values.astype(BF16)

    loop(8, lambda step: put_grad(core_rows(step, core)), 4)
    total2.end()
    loop(8, lambda step: put_grad(core_rows(step, 1 - core)), 4)
    mix_back(lambda rows: dz_rows[rows, :], columns_of(r.ff0, 0, WOUT), r.q_rows)
    heads_to_chips(lambda s, c, k: r.q_rows[group_rows(s, c, k), :], put_to(r.dm_out))
    back = exchange(4, r.dm_out, r.dm_in, 32)
    sent.sent()
    scatter_ff.turn()
    scatter_in.pass_on()
    up, down = columns_of(r.ff0, WOUT, WFF), columns_of(r.ff0, WOUT + WFF, WFF)
    expand_back(lambda rows: dz_rows[rows, :], up, down, r.inner0, r.de, da2, r.eb_sums0)
    scatter_ff.pass_line()
    scatter_in.turn()
    scale_rows(r.normed0, r.vectors[1:2, :], r.vectors[5:6, :], r.second)

    def keep_grad(index):
        r.own_grad[rows_at(index, 32), :] = after(mine * 4 + index)[1]

    back.end()

    sort_rows(r.order, lambda at: r.dm_in[at], r.dos, True, 1.0)
    scatter_ff.deliver()
    scatter_ff0 = Scatter(r.dw_ff, r.weights_out.at[0, :, :, pl.ds(PAIR, TWICE)], where, final(2), lines_ff)
    scatter_in0 = Scatter(r.dw_in, r.weights_out.at[0, :, :, pl.ds(0, PAIR)], where, final(3), lines_in)

    def next_scatter():
        scatter_ff.end()
        weight_grad(r.second, r.de, r.dw_ff, 0, WFF)
        weight_grad(dz_rows, r.act0, r.dw_ff, WFF, WFF)
        scatter_ff0.begin()

    steps = {
        3: (scatter_in.pass_line, next_scatter),
        2: (scatter_in.deliver,),
        1: (),
        0: (scatter_ff0.pass_on,),
    }
    for tile in (3, 2, 1, 0):
        queries, outs = r.qs0[tile_rows(tile), :], r.dos[tile_rows(tile), :]
        delta = jnp.sum(outs.astype(F32).T * r.o0[tile], axis=0, keepdims=True)
        lse = r.lse0[tile][0:1, :]
        query_grad = jnp.zeros((128, TILE), F32)
        for span in range(tile + 1):
            block = score_span(z, tile, span, queries, r.kvs0)
            query_grad = query_grad + backward_span(
                tile, span, block, lse, delta, queries, outs, r.kvs0, r.kvt0, r.acc
            )
        r.o1[tile * 8 : tile * 8 + 8] = (query_grad.T * (HEAD_DIM**-0.5)).reshape(8, 32, 128)
        for step in steps[tile]:
            step()
    put_back_rows(r.ranks, r.o1, put_message(256), 0)
    put_back_pairs(r.ranks, r.acc, r.outbox)
    sent = exchange(5, r.outbox, r.inbox1, 288)
    total3 = ColumnSum(r.part, r.summed3, where, False, column_sets[0])
    add_mixed(r.mixed1, columns_of(r.in1, WIN, WOUT), z_sum, r.part, core, total1.begin)
    loop(4, keep_grad)
    scatter_in.end()
    total1.cross()
    weight_grad(dz_rows, r.mixed0, r.dw_in, WIN, WOUT)
    scatter_ff0.turn()
    scale_rows(r.normed0, r.vectors[0:1, :], r.vectors[4:5, :], r.first)
    total1.combine()
    scatter_ff0.pass_line()
    total1.sent()
    total2.sent()
    sent.end()
    chips_to_heads(lambda at: r.inbox1[at, 256:288, :], keep(r.q_rows))
    project_back(r.inbox1, r.q_rows, tables, r.du, r.ib_sums0)
    weight_grad(r.first, r.du, r.dw_in, 0, WIN)
    scatter_in0.begin()
    join_back(
        r.du, r.in0, da2, r.normed0, r.vectors[0:1, :], r.vectors[1:2, :], r.sums0.at[pl.ds(0, 8)], r.part,
        core, total3.begin,
    )
    scatter_in0.pass_on()
    total3.cross()

    once = jnp.where(place_in_column == 0, 1.0, 0.0)
    for half in range(2):
        for across in range(4):
            lanes = slice((half * 4 + across) * 128, (half * 4 + across + 1) * 128)
            at_home = jnp.where((tp == half) & (mine == across), 1.0, 0.0)
            for chip_z in range(4):
                cut = slice(chip_z * 128, (chip_z + 1) * 128)
                at = across * 4 + chip_z
                pieces = [
                    r.sums0[0:2, lanes], r.sums1[0:2, lanes], r.sums0[2:4, lanes], r.sums1[2:4, lanes],
                    r.ib_sums0[0:3, :] * at_home, r.ib_sums1[0:3, :] * at_home,
                    r.sums0[8:9, lanes] * once, r.sums0[8:9, lanes] * once,
                    r.sums1[8:9, lanes] * once, r.sums1[8:9, lanes] * once,
                    r.eb_sums0[0:1, cut] * at_home, r.eb_sums1[0:1, cut] * at_home,
                ]
                row = 0
                for piece in pieces:
                    count = piece.shape[0]
                    r.small[at, half, row : row + count, :] = piece
                    row += count
                r.small[at, half, 20:24, :] = jnp.zeros((4, 128), F32)
    around = []
    for k, (dx, dz) in enumerate(STEPS):
        copy = remote(
            r.small.at[ring(x, dx) * 4 + ring(z, dz)],
            r.gathered.at[k],
            r.send_s.at[k],
            r.recv_s.at[k],
            plane[k],
        )
        copy.start()
        around.append(copy)
    scatter_ff0.deliver()
    scatter_in0.turn()
    total3.combine()
    for copy in around:
        copy.wait_recv()
    r.total_s[...] = r.small[chip] + jnp.sum(r.gathered[...], axis=0)
    shared = []
    for k, peer in enumerate(column):
        copy = remote(r.total_s, r.others.at[k], r.send_d.at[k], r.recv_d.at[k], peer)
        copy.start()
        shared.append(copy)
    scatter_in0.pass_line()
    total1.end()
    shift = r.vectors[16:17, :] + r.vectors[17:18, :]
    for k in range(2):
        rows = pl.ds(k * 64, 64)
        r.act_out[rows, :] = (r.own_hidden[rows, :] + r.summed2[k].astype(F32) + shift).astype(BF16)

    total3.end()
    own = mine * ROWS
    for k in range(4):
        rows = pl.ds(pl.multiple_of(own + k * 32, 32), 32)
        summed = r.summed3[k // 2, (k % 2) * 32 : (k % 2 + 1) * 32, :].astype(F32)
        r.grad_out[k * 32 : (k + 1) * 32, :] = r.own_grad[k * 32 : (k + 1) * 32, :] + norm_back(
            summed, r.normed0[rows, :], r.inverse0[rows, 0:1]
        )
    scatter_in0.deliver()
    for copy in shared:
        copy.wait_recv()
    sums_here = r.total_s[...] + jnp.sum(r.others[...], axis=0)
    sums_here = jnp.where(seq == 0, sums_here[0], sums_here[1])
    line = lax.broadcasted_iota(I32, sums_here.shape, 0)
    r.small_out[...] = jnp.where(
        line < 18,
        pltpu.roll(sums_here, 128 - (z * 4 + core * 2 + tp) * 8, 1),
        pltpu.roll(sums_here, 128 - (core * 2 + tp) * 32, 1),
    )
    scatter_ff0.end()
    scatter_in0.end()
    for copies in arriving:
        for copy in copies:
            copy.wait_send()
    for copy in smalls + spread + ranks_here + ranks_there + around + shared:
        copy.wait_send()
    for one in (cots, in0, ff0, in1, ff1, returned, back, sent, total3):
        one.sent()


def whole(*operands):
    outs = tuple(v for v in NAMES.values() if v is not None)
    scratch = [*SCRATCH.values(), *ColumnSum.SCRATCH * 2, *Scatter.scratch(PAIR), *Scatter.scratch(TWICE)]
    return pl.pallas_call(
        whole_kernel,
        out_shape=outs,
        in_specs=[VMEM] * len(operands),
        out_specs=(VMEM,) * len(outs),
        scratch_shapes=scratch,
        compiler_params=pltpu.CompilerParams(
            collective_id=0, has_side_effects=True, vmem_limit_bytes=LIMIT * MIB
        ),
        name="whole",
    )(*operands)


def outputs_kernel(
    weights, small, input_out, output_out, expand_out, contract_out,
    gain_out, shift_out, input_shift_out, output_shift_out, expand_shift_out,
):
    for layer in range(LAYERS):
        for k in range(4):
            part = weights[layer, k].astype(F32)
            for t in range(3):
                at = t * 512 + k * 128
                input_out[layer, :, at : at + 128] = part[:, t * 128 : (t + 1) * 128]
            output_out[layer, :, k * WOUT : (k + 1) * WOUT] = part[:, WIN:PAIR]
            expand_out[layer, :, k * WFF : (k + 1) * WFF] = part[:, PAIR : PAIR + WFF]
            contract_out[layer, :, k * WFF : (k + 1) * WFF] = part[:, PAIR + WFF :]
        for k in range(2):
            row = layer * 2 + k
            gain_out[layer, k : k + 1, :] = small[row : row + 1, 0:8]
            shift_out[layer, k : k + 1, :] = small[row + 4 : row + 5, 0:8]
            output_shift_out[layer, k : k + 1, :] = small[row + 14 : row + 15, 0:8]
        input_shift_out[layer] = small[8 + layer * 3 : 11 + layer * 3, 0:8]
    expand_shift_out[...] = small[18:20, 0:32]


def outputs(*operands):
    outs = (
        f32(2, 16, 1536), f32(2, 16, 512), f32(2, 16, 2048), f32(2, 16, 2048),
        f32(2, 2, 8), f32(2, 2, 8), f32(2, 3, 8), f32(2, 2, 8), f32(2, 32),
    )
    return pl.pallas_call(
        outputs_kernel,
        out_shape=outs,
        in_specs=[VMEM] * len(operands),
        out_specs=(VMEM,) * len(outs),
        compiler_params=pltpu.CompilerParams(vmem_limit_bytes=8 * MIB),
        name="outputs",
    )(*operands)


def rotary_tables():
    half = ROT // 2
    freqs = 10000.0 ** (-(np.arange(half) * 2.0 / ROT))
    lane = np.arange(128) % HEAD_DIM
    every = np.where(lane < ROT, np.tile(freqs, 128 // half), 0.0)[None, :]
    start = np.arange(32)[:, None] * ROWS * every
    steps = np.arange(ROWS)[:, None] * every
    return np.concatenate([np.cos(start), np.sin(start), np.cos(steps), np.sin(steps)]).astype(np.float32)


def local(
    tokens, cotangent, group_order, input_weight, output_weight, expand_weight, contract_weight,
    norm_gain, norm_shift, input_bias, output_bias, expand_bias,
):
    eights = [norm_gain, norm_shift, input_bias, output_bias]
    raw = jnp.concatenate(
        [
            jnp.pad(jnp.concatenate([v.reshape(-1, 8) for v in eights], axis=0), ((0, 0), (0, 120))),
            jnp.pad(expand_bias, ((0, 4), (0, 96))),
        ],
        axis=0,
    )
    activations, input_gradient, weights_out, small = whole(
        input_weight.reshape(LAYERS, 16, 1536), output_weight, expand_weight, contract_weight, tokens, cotangent, raw,
        group_order, rotary_tables(),
    )
    input_out, *rest = outputs(weights_out, small)
    return (activations, input_gradient, input_out.reshape(2, 16, 3, 512), *rest)


def solution(mesh):
    rows, columns = P(("seq", "ctx"), None), P(None, None, ("seq", "ctx", "tp"))
    weight, flat = P(None, ("seq", "ctx"), "tp"), P(None, ("seq", "ctx", "tp"))
    first = P(None, ("seq", "ctx"), None, "tp")
    outs = (rows, rows, first, weight, weight, weight, columns, columns, columns, columns, flat)
    return jax.shard_map(
        local,
        mesh=mesh,
        in_specs=(rows, rows, P("seq", "ctx"), *outs[2:]),
        out_specs=outs,
        check_vma=False,
    )
```
